32 devices in a mesh: ctx: 16 (over z, x, core), tp: 2 (over y).
Axes of the slice: x: 2, y: 2, z: 4, core: 2. Of those that a mesh axis runs over, the one named last changes fastest.
Arguments:
- tokens: bfloat16 [1920, 8192], P('tp', 'ctx'), may hold values from -6 to 6
- norm_gain: float32 [1920], replicated, may hold values from 0.1 to 1.9
- w_in: bfloat16 [3, 1920, 1920], P(None, 'tp'), may hold values from -0.125 to 0.125
- w_short: float32 [3, 3, 1920], P(None, None, 'tp'), may hold values from -3 to 3
- decay_rate: float32 [16, 1920], P(None, 'tp'), as said below
- residue: float32 [16, 1920], P(None, 'tp'), may hold values from -1.5 to 1.5
- skip_gain: float32 [1920], P('tp'), may hold values from -3 to 3
- w_out: bfloat16 [1920, 1920], P('tp'), may hold values from -0.125 to 0.125
Outputs:
- mixed: bfloat16 [1920, 8192], P('tp', 'ctx')
The draws below stay inside these ranges and needn't reach their ends.
Inputs may be any that keep to these rules, and one draw needn't show every extreme that they name: `decay_rate`: every rate lies between 0.2 / 8192 and 1 / 30.
All inputs are finite; a program needn't handle non-finite values.
Results may differ from the reference program's by a relative error of at most 0.0077.
Values may be sent and summed in bfloat16 or wider, within the bound.
No kernel may reach another device: no remote copies, remote signals or barrier semaphores. Data moves between devices by JAX's collectives and lax.ppermute only.
A program may use at most 256 MiB of HBM per device.

```python
import math
import jax
import jax.numpy as jnp
from jax import lax

D = 1920
SHORT = 3
NMODES = 16
SEQ = 8192


def draw_decay_rate(key, part):
    first, second, third = jax.random.split(jax.random.fold_in(key, 17), 3)
    shape = (NMODES, D)
    slow_share = 0.5
    slow_pick = jax.random.uniform(first, shape, jnp.float32) < slow_share
    slow_rate = jnp.exp(jax.random.uniform(second, shape, jnp.float32, math.log(0.2 / SEQ), math.log(2.0 / SEQ)))
    fast_rate = jnp.exp(jax.random.uniform(third, shape, jnp.float32, math.log(1.0 / 50.0), math.log(1.0 / 30.0)))
    return jnp.where(slow_pick, slow_rate, fast_rate).astype(jnp.float32)


def shard_levels(stream_key, extent, cuts, least, high):
    level, own = 1.0, jax.random.fold_in(stream_key, 6)
    for axis_at, parts in cuts:
        draws = jnp.exp(jax.random.uniform(jax.random.fold_in(own, axis_at), (parts,), jnp.float32, least / len(cuts), high / len(cuts)))
        level = level * jnp.repeat(draws, extent[axis_at] // parts).reshape([-1 if axis == axis_at else 1 for axis in range(len(extent))])
    return level


def bell_draw(own_key, extent, scale, most, cuts=(), kind=jnp.bfloat16):
    entries = jax.random.normal(own_key, extent, jnp.float32) * scale
    if len(cuts) > 0:
        entries = shard_levels(own_key, extent, cuts, -0.22, 0.18) * entries
    return jnp.clip(entries, min=-most, max=most).astype(kind)


def setup_inputs(seed: int = 0) -> dict:
    key_of = jax.random.split(jax.random.key(seed), 9)
    return {
        "tokens": bell_draw(key_of[0], (D, SEQ), 1.0, 6.0, ((0, 2), (1, 16))),
        "norm_gain": jnp.clip(1.0 + 0.18 * jax.random.normal(key_of[1], (D,), jnp.float32), 0.1, 1.9),
        "w_in": bell_draw(key_of[2], (3, D, D), D ** -0.5, 0.125, ((1, 2),)),
        "w_short": bell_draw(key_of[3], (SHORT, 3, D), 0.5, 3.0, ((2, 2),), jnp.float32),
        "decay_rate": draw_decay_rate(jax.random.fold_in(key_of[8], 71), 0),
        "residue": bell_draw(key_of[5], (NMODES, D), NMODES ** -0.5, 1.5, ((1, 2),), jnp.float32),
        "skip_gain": bell_draw(key_of[6], (D,), 0.5, 3.0, ((0, 2),), jnp.float32),
        "w_out": bell_draw(key_of[7], (D, D), D ** -0.5, 0.125, ((0, 2),)),
    }


def reference(tokens, norm_gain, w_in, w_short, decay_rate, residue, skip_gain, w_out):
    features = tokens.astype(jnp.float32).T
    row_scale = lax.rsqrt(lax.optimization_barrier(jnp.mean(features * features, axis=1, keepdims=True)) + 1e-06)
    normed = (features * row_scale * norm_gain).astype(jnp.bfloat16)
    w_matrix = w_in.transpose(2, 0, 1).reshape(D, 3 * D).astype(jnp.float32)
    projected = jnp.dot(normed.astype(jnp.float32), w_matrix, precision=lax.Precision.HIGHEST).astype(jnp.bfloat16)
    streams = projected.reshape(SEQ, 3, D).astype(jnp.float32)
    short_mix = w_short[0] * streams
    for offset in range(1, SHORT):
        delayed = jnp.concatenate([jnp.zeros((offset, 3, D), jnp.float32), streams[:SEQ - offset]], axis=0)
        short_mix = short_mix + w_short[offset] * delayed
    signal = short_mix[:, 1] * short_mix[:, 2]
    mode_gains = residue * jnp.sqrt(-jnp.expm1(-2.0 * decay_rate))
    group = math.gcd(D, 128)
    block_count = D // group

    def one_block(pack):
        piece, rate, gain = pack
        positions = jnp.arange(SEQ).astype(rate.dtype)
        filter_time = lax.optimization_barrier(jnp.sum(gain[None] * jnp.exp(-rate[None] * positions[:, None, None]), axis=1))
        spectrum = jnp.fft.rfft(piece, n=2 * SEQ, axis=0) * jnp.fft.rfft(filter_time, n=2 * SEQ, axis=0)
        return jnp.fft.irfft(spectrum, n=2 * SEQ, axis=0)[:SEQ]
    pieces = signal.reshape(SEQ, block_count, group).transpose(1, 0, 2)
    rates = decay_rate.reshape(NMODES, block_count, group).transpose(1, 0, 2)
    gain_blocks = mode_gains.reshape(NMODES, block_count, group).transpose(1, 0, 2)
    long_conv = lax.map(one_block, (pieces, rates, gain_blocks)).transpose(1, 0, 2).reshape(SEQ, D)
    gated = (short_mix[:, 0] * (long_conv + skip_gain * signal)).astype(jnp.bfloat16)
    result = jnp.dot(gated.astype(jnp.float32), w_out.astype(jnp.float32), precision=lax.Precision.HIGHEST)
    return result.T.astype(jnp.bfloat16)
```

```python
import functools

import jax
import jax.numpy as jnp
from jax import lax
from jax.experimental import pallas as pl
from jax.experimental.pallas import tpu as pltpu
from jax.sharding import PartitionSpec as P

F32 = jnp.float32
BF16 = jnp.bfloat16
ROWS = 8
LANES = 128
CONTRACT_LAST = (((1,), (1,)), ((), ()))


def lane_groups(width):
    return [(start, min(LANES, width - start)) for start in range(0, width, LANES)]


def rows_as(row, width):
    return jnp.broadcast_to(row, (ROWS, width))


def interleave(rows, columns, length):
    row = lax.broadcasted_iota(jnp.int32, (rows, columns), 0)
    column = lax.broadcasted_iota(jnp.int32, (rows, columns), 1)
    wanted = lax.rem(row, ROWS) * length + lax.div(row, ROWS)
    return row, column, wanted


def first_stage(pieces, first, taps, *refs):
    refs = list(refs)
    me_ref = refs.pop(0)
    token_refs = [refs.pop(0) for _ in range(pieces)]
    edge_refs = [refs.pop(0) for _ in range(pieces)] if first else []
    tail_in = None if first else refs.pop(0)
    state_in = None if first else refs.pop(0)
    gain_ref, w_ref, short_ref, rate_ref, mode_ref, skip_ref = refs[:6]
    q_ref, local_ref, starts_ref, state_ref, tail_ref = refs[6:11]
    x_ref, normed_ref, p_ref, signal_ref = refs[11:]
    share, chunk = token_refs[0].shape
    length = chunk // ROWS
    modes, width = rate_ref.shape
    extra = 16 if first else 0
    total_rows = chunk + extra

    @pl.when(pl.program_id(0) == 0)
    def _():
        for s in range(pieces):
            rank = lax.rem(me_ref[0] + s, pieces)
            rows = pl.ds(pl.multiple_of(rank * share, 16), share)
            x_ref[rows, :chunk] = token_refs[s][...]
            if first:
                x_ref[rows, chunk:] = edge_refs[s][...]
        row, column, wanted = interleave(total_rows, x_ref.shape[1], length)
        if first:
            wanted = jnp.where(row < chunk, wanted, row)
        pick = jnp.where(column == wanted, 1.0, 0.0).astype(BF16)
        features = lax.dot_general(pick, x_ref[...], CONTRACT_LAST, preferred_element_type=F32)
        mean = jnp.mean(features * features, axis=1, keepdims=True)
        normed_ref[...] = (features * lax.rsqrt(mean + 1e-06) * gain_ref[...]).astype(BF16)

    segment = lax.broadcasted_iota(jnp.int32, (ROWS, width), 0)
    mixed = []
    for s in range(3):
        product = lax.dot_general(
            normed_ref[...], w_ref[s], CONTRACT_LAST, preferred_element_type=F32
        )
        p_ref[...] = product.astype(BF16).astype(F32)
        short = short_ref[0, s : s + 1, :] * p_ref[:chunk, :]
        heads = []
        for offset in range(1, taps):
            if first:
                before = p_ref[chunk + taps - 1 - offset : chunk + taps - offset, :]
            else:
                before = tail_in[s, taps - 1 - offset : taps - offset, :]
            low = chunk - ROWS * offset
            wrapped = pltpu.roll(p_ref[low : low + ROWS, :], 1, 0)
            heads.insert(0, jnp.where(segment == 0, rows_as(before, width), wrapped))
            delayed = jnp.concatenate(heads + [p_ref[:low, :]], axis=0)
            short = short + short_ref[offset, s : s + 1, :] * delayed
            tail_ref[s, taps - 1 - offset : taps - offset, :] = p_ref[
                low + ROWS - 1 : low + ROWS, :
            ]
        if s == 0:
            q_ref[...] = short
        elif s == 1:
            signal_ref[...] = short
        else:
            signal_ref[...] = signal_ref[...] * short

    for start, size in lane_groups(width):
        lanes = slice(start, start + size)
        rate = [rows_as(rate_ref[n : n + 1, lanes], size) for n in range(modes)]
        decay = [jnp.exp(-r) for r in rate]
        mode = [rows_as(mode_ref[n : n + 1, lanes], size) for n in range(modes)]
        skip = rows_as(skip_ref[:, lanes], size)

        def step(i, states):
            rows = pl.ds(pl.multiple_of(i * ROWS, ROWS), ROWS)
            now = signal_ref[rows, lanes]
            states = tuple(states[n] * decay[n] + now for n in range(modes))
            sums = [skip * now] + [mode[n] * states[n] for n in range(modes)]
            while len(sums) > 1:
                sums = [sum(sums[k : k + 2][1:], sums[k]) for k in range(0, len(sums), 2)]
            local_ref[rows, lanes] = sums[0]
            return states

        zero = jnp.zeros((ROWS, size), F32)
        ends = lax.fori_loop(0, length, step, (zero,) * modes, unroll=4)
        at = lax.broadcasted_iota(jnp.int32, (ROWS, size), 0)
        for n in range(modes):
            run = ends[n]
            for hop in (1, 2, 4):
                weight = jnp.where(at >= hop, jnp.exp(-rate[n] * (hop * length)), 0.0)
                run = run + weight * pltpu.roll(run, hop, 0)
            begin = jnp.where(at >= 1, pltpu.roll(run, 1, 0), 0.0)
            last = run[ROWS - 1 :, :]
            if not first:
                given = state_in[n : n + 1, lanes]
                begin = begin + jnp.exp(-rate[n] * (at * length).astype(F32)) * given
                last = last + jnp.exp(-rate_ref[n : n + 1, lanes] * chunk) * given
            starts_ref[n, :, lanes] = begin
            state_ref[n : n + 1, lanes] = last


def second_stage(pieces, begin_at, *refs):
    q_ref, local_ref, starts_ref, carry_ref, rate_ref, mode_ref, w_ref = refs[:7]
    send_ref, own_ref, gated_ref = refs[7:]
    chunk, width = q_ref.shape
    modes = rate_ref.shape[0]
    length = chunk // ROWS
    for start, size in lane_groups(width):
        lanes = slice(start, start + size)
        rate = [rows_as(rate_ref[n : n + 1, lanes], size) for n in range(modes)]
        decay = [jnp.exp(-r) for r in rate]
        at = lax.broadcasted_iota(jnp.int32, (ROWS, size), 0)
        past = (begin_at + at * length).astype(F32)
        states = tuple(
            mode_ref[n : n + 1, lanes]
            * (starts_ref[n, :, lanes] + jnp.exp(-rate[n] * past) * carry_ref[n : n + 1, lanes])
            for n in range(modes)
        )

        def step(i, states):
            rows = pl.ds(pl.multiple_of(i * ROWS, ROWS), ROWS)
            states = tuple(states[n] * decay[n] for n in range(modes))
            sums = [local_ref[rows, lanes]] + list(states)
            while len(sums) > 1:
                sums = [sum(sums[k : k + 2][1:], sums[k]) for k in range(0, len(sums), 2)]
            gated_ref[rows, lanes] = q_ref[rows, lanes] * sums[0]
            return states

        lax.fori_loop(0, length, step, states, unroll=4)
    row, column, wanted = interleave(chunk, chunk, length)
    pick = jnp.where(column == wanted, 1.0, 0.0).astype(BF16)
    gated = lax.dot_general(
        pick, gated_ref[...].astype(BF16), (((0,), (0,)), ((), ())), preferred_element_type=F32
    ).astype(BF16)
    share = own_ref.shape[0]
    away = (pieces - 1) * share
    if pieces > 1:
        send_ref[...] = lax.dot_general(
            w_ref[:away, :], gated, CONTRACT_LAST, preferred_element_type=F32
        ).astype(BF16)
    own_ref[...] = lax.dot_general(
        w_ref[away:, :], gated, CONTRACT_LAST, preferred_element_type=F32
    )


def run_first(pieces, first, me, tokens, edges, tail, state, gain, w_in, w_short, rate, mode, skip):
    share, chunk = tokens[0].shape
    streams, channels, features = w_in.shape
    taps = w_short.shape[0]
    modes = rate.shape[0]
    block = min(256, channels)
    grid = (channels + block - 1) // block
    whole = lambda a: pl.BlockSpec(a.shape, lambda b, *_: (0,) * a.ndim)
    by_last = lambda a: pl.BlockSpec(a.shape[:-1] + (block,), lambda b, *_: (0,) * (a.ndim - 1) + (b,))
    operands, specs = list(tokens), [whole(a) for a in tokens]
    if first:
        operands += edges
        specs += [whole(a) for a in edges]
    else:
        operands += [tail, state]
        specs += [by_last(tail), by_last(state)]
    operands += [gain, w_in, w_short, rate, mode, skip]
    specs += [whole(gain), pl.BlockSpec((streams, block, features), lambda b, *_: (0, b, 0))]
    specs += [by_last(a) for a in (w_short, rate, mode, skip)]
    outs = [
        jax.ShapeDtypeStruct((chunk, channels), F32),
        jax.ShapeDtypeStruct((chunk, channels), F32),
        jax.ShapeDtypeStruct((modes, ROWS, channels), F32),
        jax.ShapeDtypeStruct((modes, channels), F32),
        jax.ShapeDtypeStruct((streams, taps - 1, channels), F32),
    ]
    rows = chunk + (16 if first else 0)
    columns = chunk + (LANES if first else 0)
    flops = 2 * rows * features * streams * channels + 6 * chunk * channels * modes
    return pl.pallas_call(
        functools.partial(first_stage, pieces, first, taps),
        out_shape=outs,
        grid_spec=pltpu.PrefetchScalarGridSpec(
            num_scalar_prefetch=1,
            grid=(grid,),
            in_specs=specs,
            out_specs=[by_last(a) for a in outs],
            scratch_shapes=[
                pltpu.VMEM((features, columns), BF16),
                pltpu.VMEM((rows, features), BF16),
                pltpu.VMEM((rows, block), F32),
                pltpu.VMEM((chunk, block), F32),
            ],
        ),
        compiler_params=pltpu.CompilerParams(vmem_limit_bytes=28 * 2**20),
        cost_estimate=pl.CostEstimate(
            flops=flops,
            bytes_accessed=2 * w_in.size + 8 * chunk * channels,
            transcendentals=0,
        ),
        name="first_stage",
    )(me, *operands)


def run_second(pieces, begin_at, q, local, starts, carry, rate, mode, w):
    chunk, channels = q.shape
    features = w.shape[0]
    share = features // pieces
    vmem = pl.BlockSpec(memory_space=pltpu.VMEM)
    return pl.pallas_call(
        functools.partial(second_stage, pieces, begin_at),
        out_shape=[
            jax.ShapeDtypeStruct((max(1, pieces - 1) * share, chunk), BF16),
            jax.ShapeDtypeStruct((share, chunk), F32),
        ],
        in_specs=[vmem] * 7,
        out_specs=[vmem] * 2,
        scratch_shapes=[pltpu.VMEM((chunk, channels), F32)],
        compiler_params=pltpu.CompilerParams(vmem_limit_bytes=28 * 2**20),
        cost_estimate=pl.CostEstimate(
            flops=2 * features * channels * chunk,
            bytes_accessed=2 * w.size + 8 * chunk * channels,
            transcendentals=0,
        ),
        name="second_stage",
    )(q, local, starts, carry, rate, mode, w)


def rotate(value, axis, steps):
    count = lax.axis_size(axis)
    return lax.ppermute(value, axis, [((i + steps) % count, i) for i in range(count)])


def carried_in(state, rate, span, axis):
    count, position = lax.axis_size(axis), lax.axis_index(axis)
    carry, total, stride = jnp.zeros_like(state), state, 1
    while stride < count:
        radix = 4 if count % (stride * 4) == 0 else 2
        assert count % (stride * radix) == 0
        digit = lax.rem(lax.div(position, stride), radix)
        group = stride * radix
        others = []
        for shift in range(1, radix):
            pairs = []
            for i in range(count):
                place = (i // stride) % radix
                if group < count or place >= shift:
                    source = (i // group) * group + ((place - shift) % radix) * stride + i % stride
                    pairs.append((source, i))
            others.append(lax.ppermute(total, axis, pairs))
        unit = span * stride
        before = jnp.zeros_like(state)
        for shift in range(1, radix):
            reached = jnp.exp(-rate * (unit * (shift - 1))) * others[shift - 1]
            before = before + jnp.where(digit >= shift, reached, 0.0)
        inner = lax.rem(position, stride)
        carry = carry + jnp.exp(-rate * (span * inner).astype(F32)) * before
        if group < count:
            new = jnp.exp(-rate * (unit * (radix - 1 - digit)).astype(F32)) * total
            for shift in range(1, radix):
                place = lax.rem(digit - shift + radix, radix)
                weight = jnp.exp(-rate * (unit * (radix - 1 - place)).astype(F32))
                new = new + weight * others[shift - 1]
            total = new
        stride = group
    return carry


CHUNKS = 2


def body(tokens, norm_gain, w_in, w_short, decay_rate, residue, skip_gain, w_out):
    pieces, me = lax.axis_size("tp"), lax.axis_index("tp")
    count = lax.axis_size("ctx")
    share, rows = tokens.shape
    taps = w_short.shape[0]
    chunk = rows // CHUNKS
    parts = [tokens[:, j * chunk : (j + 1) * chunk] for j in range(CHUNKS)]
    gathered = [[part] + [rotate(part, "tp", s) for s in range(1, pieces)] for part in parts]
    last = tokens[:, rows - (taps - 1) :]
    edges = []
    for s in range(pieces):
        pairs = [
            (i * pieces + (t + s) % pieces, (i + 1) * pieces + t)
            for i in range(count - 1)
            for t in range(pieces)
        ]
        edge = lax.ppermute(last, ("ctx", "tp"), pairs)
        edges.append(jnp.pad(edge, ((0, 0), (0, LANES - (taps - 1)))))
    mode = residue * jnp.sqrt(-jnp.expm1(-2.0 * decay_rate))
    gain = norm_gain[None, :]
    skip = skip_gain[None, :]
    index = jnp.full((1,), me, jnp.int32)
    w_turned = jnp.roll(w_out.T, -(me + 1) * share, axis=0)

    tail = state = None
    kept = []
    for j in range(CHUNKS):
        q, local, starts, state, tail = run_first(
            pieces, j == 0, index, gathered[j], edges, tail, state, gain, w_in, w_short,
            decay_rate, mode, skip,
        )
        kept.append((q, local, starts))
    carry = carried_in(state, decay_rate, rows, "ctx")
    results = []
    for j, (q, local, starts) in enumerate(kept):
        send, own = run_second(
            pieces, j * chunk, q, local, starts, carry, decay_rate, mode, w_turned
        )
        for s in range(1, pieces):
            own = own + rotate(send[(s - 1) * share : s * share], "tp", -s).astype(F32)
        results.append(own.astype(BF16))
    return jnp.concatenate(results, axis=1)


def solution(mesh):
    placed = (
        P("tp", "ctx"),
        P(),
        P(None, "tp", None),
        P(None, None, "tp"),
        P(None, "tp"),
        P(None, "tp"),
        P("tp"),
        P("tp", None),
    )
    return jax.shard_map(
        body, mesh=mesh, in_specs=placed, out_specs=P("tp", "ctx"), check_vma=False
    )
```

```python
import functools

import jax
import jax.numpy as jnp
from jax import lax
from jax.experimental import pallas as pl
from jax.experimental.pallas import tpu as pltpu
from jax.sharding import PartitionSpec as P

F32 = jnp.float32
BF16 = jnp.bfloat16
ROWS = 8
LANES = 128
VMEM_LIMIT = 56 * 2**20
CONTRACT_LAST = (((1,), (1,)), ((), ()))


def lane_groups(width):
    return [(start, min(LANES, width - start)) for start in range(0, width, LANES)]


def rows_as(row, width):
    return jnp.broadcast_to(row, (ROWS, width))


def interleave(rows, columns, length):
    row = lax.broadcasted_iota(jnp.int32, (rows, columns), 0)
    column = lax.broadcasted_iota(jnp.int32, (rows, columns), 1)
    wanted = lax.rem(row, ROWS) * length + lax.div(row, ROWS)
    return row, column, wanted


def first_stage(pieces, first, taps, *refs):
    refs = list(refs)
    me_ref = refs.pop(0)
    token_refs = [refs.pop(0) for _ in range(pieces)]
    edge_refs = [refs.pop(0) for _ in range(pieces)] if first else []
    tail_in = None if first else refs.pop(0)
    state_in = None if first else refs.pop(0)
    gain_ref, w_ref, short_ref, rate_ref, mode_ref, skip_ref = refs[:6]
    q_ref, local_ref, starts_ref, state_ref, tail_ref = refs[6:11]
    x_ref, normed_ref, p_ref, signal_ref = refs[11:]
    share, chunk = token_refs[0].shape
    length = chunk // ROWS
    modes, width = rate_ref.shape
    extra = 16 if first else 0
    total_rows = chunk + extra

    @pl.when(pl.program_id(0) == 0)
    def _():
        for s in range(pieces):
            rank = lax.rem(me_ref[0] + s, pieces)
            rows = pl.ds(pl.multiple_of(rank * share, 16), share)
            x_ref[rows, :chunk] = token_refs[s][...]
            if first:
                x_ref[rows, chunk:] = edge_refs[s][...]
        row, column, wanted = interleave(total_rows, x_ref.shape[1], length)
        if first:
            wanted = jnp.where(row < chunk, wanted, row)
        pick = jnp.where(column == wanted, 1.0, 0.0).astype(BF16)
        features = lax.dot_general(pick, x_ref[...], CONTRACT_LAST, preferred_element_type=F32)
        mean = jnp.mean(features * features, axis=1, keepdims=True)
        normed_ref[...] = (features * lax.rsqrt(mean + 1e-06) * gain_ref[...]).astype(BF16)

    segment = lax.broadcasted_iota(jnp.int32, (ROWS, width), 0)
    mixed = []
    for s in range(3):
        product = lax.dot_general(
            normed_ref[...], w_ref[s], CONTRACT_LAST, preferred_element_type=F32
        )
        p_ref[...] = product.astype(BF16).astype(F32)
        short = short_ref[0, s : s + 1, :] * p_ref[:chunk, :]
        heads = []
        for offset in range(1, taps):
            if first:
                before = p_ref[chunk + taps - 1 - offset : chunk + taps - offset, :]
            else:
                before = tail_in[s, taps - 1 - offset : taps - offset, :]
            low = chunk - ROWS * offset
            wrapped = pltpu.roll(p_ref[low : low + ROWS, :], 1, 0)
            heads.insert(0, jnp.where(segment == 0, rows_as(before, width), wrapped))
            delayed = jnp.concatenate(heads + [p_ref[:low, :]], axis=0)
            short = short + short_ref[offset, s : s + 1, :] * delayed
            tail_ref[s, taps - 1 - offset : taps - offset, :] = p_ref[
                low + ROWS - 1 : low + ROWS, :
            ]
        if s == 0:
            q_ref[...] = short
        elif s == 1:
            signal_ref[...] = short
        else:
            signal_ref[...] = signal_ref[...] * short

    for start, size in lane_groups(width):
        lanes = slice(start, start + size)
        rate = [rows_as(rate_ref[n : n + 1, lanes], size) for n in range(modes)]
        decay = [jnp.exp(-r) for r in rate]
        mode = [rows_as(mode_ref[n : n + 1, lanes], size) for n in range(modes)]
        skip = rows_as(skip_ref[:, lanes], size)

        def step(i, states):
            rows = pl.ds(pl.multiple_of(i * ROWS, ROWS), ROWS)
            now = signal_ref[rows, lanes]
            states = tuple(states[n] * decay[n] + now for n in range(modes))
            sums = [skip * now] + [mode[n] * states[n] for n in range(modes)]
            while len(sums) > 1:
                sums = [sum(sums[k : k + 2][1:], sums[k]) for k in range(0, len(sums), 2)]
            local_ref[rows, lanes] = sums[0]
            return states

        zero = jnp.zeros((ROWS, size), F32)
        ends = lax.fori_loop(0, length, step, (zero,) * modes, unroll=4)
        at = lax.broadcasted_iota(jnp.int32, (ROWS, size), 0)
        for n in range(modes):
            run = ends[n]
            for hop in (1, 2, 4):
                weight = jnp.where(at >= hop, jnp.exp(-rate[n] * (hop * length)), 0.0)
                run = run + weight * pltpu.roll(run, hop, 0)
            begin = jnp.where(at >= 1, pltpu.roll(run, 1, 0), 0.0)
            last = run[ROWS - 1 :, :]
            if not first:
                given = state_in[n : n + 1, lanes]
                begin = begin + jnp.exp(-rate[n] * (at * length).astype(F32)) * given
                last = last + jnp.exp(-rate_ref[n : n + 1, lanes] * chunk) * given
            starts_ref[n, :, lanes] = begin
            state_ref[n : n + 1, lanes] = last


def second_stage(pieces, begin_at, channels, *refs):
    me_ref, q_ref, local_ref, starts_ref, carry_ref, rate_ref, mode_ref, w_hbm = refs[:8]
    send_ref, own_ref, gated_ref, w_ref, sem = refs[8:]
    chunk, width = q_ref.shape
    modes = rate_ref.shape[0]
    length = chunk // ROWS
    block = pl.program_id(0)
    fetch = pltpu.make_async_copy(w_hbm, w_ref, sem)

    @pl.when(block == 0)
    def _():
        fetch.start()

    for start, size in lane_groups(width):
        lanes = slice(start, start + size)
        rate = [rows_as(rate_ref[n : n + 1, lanes], size) for n in range(modes)]
        decay = [jnp.exp(-r) for r in rate]
        at = lax.broadcasted_iota(jnp.int32, (ROWS, size), 0)
        past = (begin_at + at * length).astype(F32)
        states = tuple(
            mode_ref[n : n + 1, lanes]
            * (starts_ref[n, :, lanes] + jnp.exp(-rate[n] * past) * carry_ref[n : n + 1, lanes])
            for n in range(modes)
        )

        def step(i, states):
            rows = pl.ds(pl.multiple_of(i * ROWS, ROWS), ROWS)
            states = tuple(states[n] * decay[n] for n in range(modes))
            sums = [local_ref[rows, lanes]] + list(states)
            while len(sums) > 1:
                sums = [sum(sums[k : k + 2][1:], sums[k]) for k in range(0, len(sums), 2)]
            gated_ref[block, rows, lanes] = q_ref[rows, lanes] * sums[0]
            return states

        lax.fori_loop(0, length, step, states, unroll=4)

    @pl.when(block == pl.num_programs(0) - 1)
    def _():
        row, column, wanted = interleave(chunk, chunk, length)
        pick = jnp.where(column == wanted, 1.0, 0.0).astype(BF16)
        gated = jnp.concatenate([gated_ref[b] for b in range(gated_ref.shape[0])], axis=1)
        gated = lax.dot_general(
            pick,
            gated[:, :channels].astype(BF16),
            (((0,), (0,)), ((), ())),
            preferred_element_type=F32,
        ).astype(BF16)
        fetch.wait()
        share = own_ref.shape[0]
        for s in range(pieces):
            rank = lax.rem(me_ref[0] + s, pieces)
            rows = pl.ds(pl.multiple_of(rank * share, 16), share)
            part = lax.dot_general(
                w_ref[rows, :], gated, CONTRACT_LAST, preferred_element_type=F32
            )
            if s == 0:
                own_ref[...] = part
            else:
                send_ref[(s - 1) * share : s * share, :] = part.astype(BF16)


def run_first(pieces, first, me, tokens, edges, tail, state, gain, w_in, w_short, rate, mode, skip):
    share, chunk = tokens[0].shape
    streams, channels, features = w_in.shape
    taps = w_short.shape[0]
    modes = rate.shape[0]
    block = min(256, channels)
    grid = (channels + block - 1) // block
    whole = lambda a: pl.BlockSpec(a.shape, lambda b, *_: (0,) * a.ndim)
    by_last = lambda a: pl.BlockSpec(a.shape[:-1] + (block,), lambda b, *_: (0,) * (a.ndim - 1) + (b,))
    operands, specs = list(tokens), [whole(a) for a in tokens]
    if first:
        operands += edges
        specs += [whole(a) for a in edges]
    else:
        operands += [tail, state]
        specs += [by_last(tail), by_last(state)]
    operands += [gain, w_in, w_short, rate, mode, skip]
    specs += [whole(gain), pl.BlockSpec((streams, block, features), lambda b, *_: (0, b, 0))]
    specs += [by_last(a) for a in (w_short, rate, mode, skip)]
    outs = [
        jax.ShapeDtypeStruct((chunk, channels), F32),
        jax.ShapeDtypeStruct((chunk, channels), F32),
        jax.ShapeDtypeStruct((modes, ROWS, channels), F32),
        jax.ShapeDtypeStruct((modes, channels), F32),
        jax.ShapeDtypeStruct((streams, taps - 1, channels), F32),
    ]
    rows = chunk + (16 if first else 0)
    columns = chunk + (LANES if first else 0)
    flops = 2 * rows * features * streams * channels + 6 * chunk * channels * modes
    return pl.pallas_call(
        functools.partial(first_stage, pieces, first, taps),
        out_shape=outs,
        grid_spec=pltpu.PrefetchScalarGridSpec(
            num_scalar_prefetch=1,
            grid=(grid,),
            in_specs=specs,
            out_specs=[by_last(a) for a in outs],
            scratch_shapes=[
                pltpu.VMEM((features, columns), BF16),
                pltpu.VMEM((rows, features), BF16),
                pltpu.VMEM((rows, block), F32),
                pltpu.VMEM((chunk, block), F32),
            ],
        ),
        compiler_params=pltpu.CompilerParams(vmem_limit_bytes=VMEM_LIMIT),
        cost_estimate=pl.CostEstimate(
            flops=flops,
            bytes_accessed=2 * w_in.size + 8 * chunk * channels,
            transcendentals=0,
        ),
        name="first_stage",
    )(me, *operands)


def run_second(pieces, begin_at, me, q, local, starts, carry, rate, mode, w):
    chunk, channels = q.shape
    features = w.shape[0]
    share = features // pieces
    block = min(256, channels)
    grid = (channels + block - 1) // block
    by_last = lambda a: pl.BlockSpec(a.shape[:-1] + (block,), lambda b, *_: (0,) * (a.ndim - 1) + (b,))
    whole = lambda a: pl.BlockSpec(a.shape, lambda b, *_: (0,) * a.ndim)
    outs = [
        jax.ShapeDtypeStruct((max(1, pieces - 1) * share, chunk), BF16),
        jax.ShapeDtypeStruct((share, chunk), F32),
    ]
    return pl.pallas_call(
        functools.partial(second_stage, pieces, begin_at, channels),
        out_shape=outs,
        grid_spec=pltpu.PrefetchScalarGridSpec(
            num_scalar_prefetch=1,
            grid=(grid,),
            in_specs=[by_last(a) for a in (q, local, starts, carry, rate, mode)]
            + [pl.BlockSpec(memory_space=pl.ANY)],
            out_specs=[whole(a) for a in outs],
            scratch_shapes=[
                pltpu.VMEM((grid, chunk, block), F32),
                pltpu.VMEM((features, channels), BF16),
                pltpu.SemaphoreType.DMA,
            ],
        ),
        compiler_params=pltpu.CompilerParams(vmem_limit_bytes=VMEM_LIMIT),
        cost_estimate=pl.CostEstimate(
            flops=2 * features * channels * chunk,
            bytes_accessed=2 * w.size + 8 * chunk * channels,
            transcendentals=0,
        ),
        name="second_stage",
    )(me, q, local, starts, carry, rate, mode, w)


def rotate(value, axis, steps):
    count = lax.axis_size(axis)
    return lax.ppermute(value, axis, [((i + steps) % count, i) for i in range(count)])


def carried_in(state, rate, span, axis):
    count, position = lax.axis_size(axis), lax.axis_index(axis)
    carry, total, stride = jnp.zeros_like(state), state, 1
    while stride < count:
        radix = 4 if count % (stride * 4) == 0 else 2
        assert count % (stride * radix) == 0
        digit = lax.rem(lax.div(position, stride), radix)
        group = stride * radix
        others = []
        for shift in range(1, radix):
            pairs = []
            for i in range(count):
                place = (i // stride) % radix
                if group < count or place >= shift:
                    source = (i // group) * group + ((place - shift) % radix) * stride + i % stride
                    pairs.append((source, i))
            others.append(lax.ppermute(total, axis, pairs))
        unit = span * stride
        before = jnp.zeros_like(state)
        for shift in range(1, radix):
            reached = jnp.exp(-rate * (unit * (shift - 1))) * others[shift - 1]
            before = before + jnp.where(digit >= shift, reached, 0.0)
        inner = lax.rem(position, stride)
        carry = carry + jnp.exp(-rate * (span * inner).astype(F32)) * before
        if group < count:
            new = jnp.exp(-rate * (unit * (radix - 1 - digit)).astype(F32)) * total
            for shift in range(1, radix):
                place = lax.rem(digit - shift + radix, radix)
                weight = jnp.exp(-rate * (unit * (radix - 1 - place)).astype(F32))
                new = new + weight * others[shift - 1]
            total = new
        stride = group
    return carry


CHUNKS = 4


def body(tokens, norm_gain, w_in, w_short, decay_rate, residue, skip_gain, w_out):
    pieces, me = lax.axis_size("tp"), lax.axis_index("tp")
    count = lax.axis_size("ctx")
    share, rows = tokens.shape
    taps = w_short.shape[0]
    chunk = rows // CHUNKS
    parts = [tokens[:, :chunk]]
    tokens, parts[0] = lax.optimization_barrier((tokens, parts[0]))
    parts += [tokens[:, j * chunk : (j + 1) * chunk] for j in range(1, CHUNKS)]
    gathered = [[part] + [rotate(part, "tp", s) for s in range(1, pieces)] for part in parts]
    last = tokens[:, rows - (taps - 1) :]
    edges = []
    for s in range(pieces):
        pairs = [
            (i * pieces + (t + s) % pieces, (i + 1) * pieces + t)
            for i in range(count - 1)
            for t in range(pieces)
        ]
        edge = lax.ppermute(last, ("ctx", "tp"), pairs)
        edges.append(jnp.pad(edge, ((0, 0), (0, LANES - (taps - 1)))))
    mode = residue * jnp.sqrt(-jnp.expm1(-2.0 * decay_rate))
    gain = norm_gain[None, :]
    skip = skip_gain[None, :]
    index = jnp.full((1,), me, jnp.int32)
    w_turned, index = lax.optimization_barrier((w_out.T, index))

    tail = state = None
    kept = []
    for j in range(CHUNKS):
        q, local, starts, state, tail = run_first(
            pieces, j == 0, index, gathered[j], edges, tail, state, gain, w_in, w_short,
            decay_rate, mode, skip,
        )
        kept.append((q, local, starts))
    carry = carried_in(state, decay_rate, rows, "ctx")
    result = jnp.zeros((share, rows), BF16)
    for j, (q, local, starts) in enumerate(kept):
        send, own = run_second(
            pieces, j * chunk, index, q, local, starts, carry, decay_rate, mode, w_turned
        )
        for s in range(1, pieces):
            own = own + rotate(send[(s - 1) * share : s * share], "tp", -s).astype(F32)
        result = lax.dynamic_update_slice(result, own.astype(BF16), (0, j * chunk))
    return result


def solution(mesh):
    placed = (
        P("tp", "ctx"),
        P(),
        P(None, "tp", None),
        P(None, None, "tp"),
        P(None, "tp"),
        P(None, "tp"),
        P("tp"),
        P("tp", None),
    )
    return jax.shard_map(
        body, mesh=mesh, in_specs=placed, out_specs=P("tp", "ctx"), check_vma=False
    )
```

```python
import functools

import jax
import jax.numpy as jnp
from jax import lax
from jax.experimental import pallas as pl
from jax.experimental.pallas import tpu as pltpu
from jax.sharding import PartitionSpec as P

F32 = jnp.float32
BF16 = jnp.bfloat16
ROWS = 8
LANES = 128
BLOCK = 256
VMEM_LIMIT = 24 * 2**20
CONTRACT_LAST = (((1,), (1,)), ((), ()))


def lane_groups(width):
    return [(start, min(LANES, width - start)) for start in range(0, width, LANES)]


def rows_as(row, width):
    return jnp.broadcast_to(row, (ROWS, width))


def tree_sum(terms):
    while len(terms) > 1:
        terms = [sum(terms[k + 1 : k + 2], terms[k]) for k in range(0, len(terms), 2)]
    return terms[0]


def interleave(rows, columns, length):
    row = lax.broadcasted_iota(jnp.int32, (rows, columns), 0)
    column = lax.broadcasted_iota(jnp.int32, (rows, columns), 1)
    wanted = lax.rem(row, ROWS) * length + lax.div(row, ROWS)
    return row, column, wanted


def first_stage(pieces, first, taps, *refs):
    refs = list(refs)
    me_ref = refs.pop(0)
    token_refs = [refs.pop(0) for _ in range(pieces)]
    edge_refs = [refs.pop(0) for _ in range(pieces)] if first else []
    tail_in = None if first else refs.pop(0)
    state_in = None if first else refs.pop(0)
    gain_ref, w_ref, short_ref, rate_ref, mode_ref, skip_ref = refs[:6]
    q_ref, local_ref, starts_ref, state_ref, tail_ref = refs[6:11]
    x_ref, normed_ref, p_ref, signal_ref = refs[11:]
    share, chunk = token_refs[0].shape
    length = chunk // ROWS
    modes, channels = rate_ref.shape
    extra = 16 if first else 0
    total_rows = chunk + extra

    for s in range(pieces):
        rank = lax.rem(me_ref[0] + s, pieces)
        rows = pl.ds(pl.multiple_of(rank * share, 16), share)
        x_ref[rows, :chunk] = token_refs[s][...]
        if first:
            x_ref[rows, chunk:] = edge_refs[s][...]
    row, column, wanted = interleave(total_rows, x_ref.shape[1], length)
    if first:
        wanted = jnp.where(row < chunk, wanted, row)
    pick = jnp.where(column == wanted, 1.0, 0.0).astype(BF16)
    features = lax.dot_general(pick, x_ref[...], CONTRACT_LAST, preferred_element_type=F32)
    mean = jnp.mean(features * features, axis=1, keepdims=True)
    normed_ref[...] = (features * lax.rsqrt(mean + 1e-06) * gain_ref[...]).astype(BF16)

    for low in range(0, channels, BLOCK):
        width = min(BLOCK, channels - low)
        part = slice(low, low + width)
        segment = lax.broadcasted_iota(jnp.int32, (ROWS, width), 0)
        for s in range(3):
            product = lax.dot_general(
                normed_ref[...], w_ref[s, part, :], CONTRACT_LAST, preferred_element_type=F32
            )
            p_ref[:, :width] = product.astype(BF16).astype(F32)
            short = short_ref[0, s : s + 1, part] * p_ref[:chunk, :width]
            heads = []
            for offset in range(1, taps):
                if first:
                    before = p_ref[chunk + taps - 1 - offset : chunk + taps - offset, :width]
                else:
                    before = tail_in[s, taps - 1 - offset : taps - offset, part]
                cut = chunk - ROWS * offset
                wrapped = pltpu.roll(p_ref[cut : cut + ROWS, :width], 1, 0)
                heads.insert(0, jnp.where(segment == 0, rows_as(before, width), wrapped))
                delayed = jnp.concatenate(heads + [p_ref[:cut, :width]], axis=0)
                short = short + short_ref[offset, s : s + 1, part] * delayed
                tail_ref[s, taps - 1 - offset : taps - offset, part] = p_ref[
                    cut + ROWS - 1 : cut + ROWS, :width
                ]
            if s == 0:
                q_ref[:, part] = short
            elif s == 1:
                signal_ref[:, :width] = short
            else:
                signal_ref[:, :width] = signal_ref[:, :width] * short

        for start, size in lane_groups(width):
            near = slice(start, start + size)
            lanes = slice(low + start, low + start + size)
            rate = [rows_as(rate_ref[n : n + 1, lanes], size) for n in range(modes)]
            decay = [jnp.exp(-r) for r in rate]
            mode = [rows_as(mode_ref[n : n + 1, lanes], size) for n in range(modes)]
            skip = rows_as(skip_ref[:, lanes], size)

            def step(i, states):
                rows = pl.ds(pl.multiple_of(i * ROWS, ROWS), ROWS)
                now = signal_ref[rows, near]
                states = tuple(states[n] * decay[n] + now for n in range(modes))
                local_ref[rows, lanes] = tree_sum(
                    [skip * now] + [mode[n] * states[n] for n in range(modes)]
                )
                return states

            zero = jnp.zeros((ROWS, size), F32)
            ends = lax.fori_loop(0, length, step, (zero,) * modes, unroll=4)
            at = lax.broadcasted_iota(jnp.int32, (ROWS, size), 0)
            for n in range(modes):
                run = ends[n]
                for hop in (1, 2, 4):
                    weight = jnp.where(at >= hop, jnp.exp(-rate[n] * (hop * length)), 0.0)
                    run = run + weight * pltpu.roll(run, hop, 0)
                begin = jnp.where(at >= 1, pltpu.roll(run, 1, 0), 0.0)
                last = run[ROWS - 1 :, :]
                if not first:
                    given = state_in[n : n + 1, lanes]
                    begin = begin + jnp.exp(-rate[n] * (at * length).astype(F32)) * given
                    last = last + jnp.exp(-rate_ref[n : n + 1, lanes] * chunk) * given
                starts_ref[n, :, lanes] = begin
                state_ref[n : n + 1, lanes] = last


def second_stage(pieces, begin_at, *refs):
    me_ref, q_ref, local_ref, starts_ref, carry_ref, rate_ref, mode_ref, w_ref = refs[:8]
    send_ref, own_ref, gated_ref = refs[8:]
    chunk, channels = q_ref.shape
    modes = rate_ref.shape[0]
    length = chunk // ROWS
    for start, size in lane_groups(channels):
        lanes = slice(start, start + size)
        rate = [rows_as(rate_ref[n : n + 1, lanes], size) for n in range(modes)]
        decay = [jnp.exp(-r) for r in rate]
        at = lax.broadcasted_iota(jnp.int32, (ROWS, size), 0)
        past = (begin_at + at * length).astype(F32)
        states = tuple(
            mode_ref[n : n + 1, lanes]
            * (starts_ref[n, :, lanes] + jnp.exp(-rate[n] * past) * carry_ref[n : n + 1, lanes])
            for n in range(modes)
        )

        def step(i, states):
            rows = pl.ds(pl.multiple_of(i * ROWS, ROWS), ROWS)
            states = tuple(states[n] * decay[n] for n in range(modes))
            gated_ref[rows, lanes] = q_ref[rows, lanes] * tree_sum(
                [local_ref[rows, lanes]] + list(states)
            )
            return states

        lax.fori_loop(0, length, step, states, unroll=4)

    row, column, wanted = interleave(chunk, chunk, length)
    pick = jnp.where(column == wanted, 1.0, 0.0).astype(BF16)
    gated = lax.dot_general(
        pick, gated_ref[...].astype(BF16), (((0,), (0,)), ((), ())), preferred_element_type=F32
    ).astype(BF16)
    share = own_ref.shape[0]
    for s in list(range(1, pieces)) + [0]:
        rank = lax.rem(me_ref[0] + s, pieces)
        rows = pl.ds(pl.multiple_of(rank * share, 16), share)
        part = lax.dot_general(w_ref[rows, :], gated, CONTRACT_LAST, preferred_element_type=F32)
        if s == 0:
            own_ref[...] = part
        else:
            send_ref[(s - 1) * share : s * share, :] = part.astype(BF16)


def run_first(pieces, first, me, tokens, edges, tail, state, gain, w_in, w_short, rate, mode, skip):
    share, chunk = tokens[0].shape
    streams, channels, features = w_in.shape
    taps = w_short.shape[0]
    modes = rate.shape[0]
    block = min(BLOCK, channels)
    vmem = pl.BlockSpec(memory_space=pltpu.VMEM)
    operands = list(tokens) + (list(edges) if first else [tail, state])
    operands += [gain, pltpu.with_memory_space_constraint(w_in, pltpu.VMEM)]
    operands += [w_short, rate, mode, skip]
    rows = chunk + (16 if first else 0)
    columns = chunk + (LANES if first else 0)
    return pl.pallas_call(
        functools.partial(first_stage, pieces, first, taps),
        out_shape=[
            jax.ShapeDtypeStruct((chunk, channels), F32),
            jax.ShapeDtypeStruct((chunk, channels), F32),
            jax.ShapeDtypeStruct((modes, ROWS, channels), F32),
            jax.ShapeDtypeStruct((modes, channels), F32),
            jax.ShapeDtypeStruct((streams, taps - 1, channels), F32),
        ],
        in_specs=[pl.BlockSpec(memory_space=pltpu.SMEM)] + [vmem] * len(operands),
        out_specs=[vmem] * 5,
        scratch_shapes=[
            pltpu.VMEM((features, columns), BF16),
            pltpu.VMEM((rows, features), BF16),
            pltpu.VMEM((rows, block), F32),
            pltpu.VMEM((chunk, block), F32),
        ],
        compiler_params=pltpu.CompilerParams(vmem_limit_bytes=VMEM_LIMIT),
        cost_estimate=pl.CostEstimate(
            flops=2 * rows * features * streams * channels,
            bytes_accessed=2 * w_in.size + 8 * chunk * channels,
            transcendentals=0,
        ),
        name="first_stage",
    )(me, *operands)


def run_second(pieces, begin_at, me, q, local, starts, carry, rate, mode, w):
    chunk, channels = q.shape
    features = w.shape[0]
    share = features // pieces
    vmem = pl.BlockSpec(memory_space=pltpu.VMEM)
    return pl.pallas_call(
        functools.partial(second_stage, pieces, begin_at),
        out_shape=[
            jax.ShapeDtypeStruct((max(1, pieces - 1) * share, chunk), BF16),
            jax.ShapeDtypeStruct((share, chunk), F32),
        ],
        in_specs=[pl.BlockSpec(memory_space=pltpu.SMEM)] + [vmem] * 7,
        out_specs=[vmem] * 2,
        scratch_shapes=[pltpu.VMEM((chunk, channels), F32)],
        compiler_params=pltpu.CompilerParams(vmem_limit_bytes=VMEM_LIMIT),
        cost_estimate=pl.CostEstimate(
            flops=2 * features * channels * chunk,
            bytes_accessed=2 * w.size + 8 * chunk * channels,
            transcendentals=0,
        ),
        name="second_stage",
    )(me, q, local, starts, carry, rate, mode, pltpu.with_memory_space_constraint(w, pltpu.VMEM))


def rotate(value, axis, steps):
    count = lax.axis_size(axis)
    return lax.ppermute(value, axis, [((i + steps) % count, i) for i in range(count)])


def carried_in(state, rate, span, axis):
    count, position = lax.axis_size(axis), lax.axis_index(axis)
    carry, total, stride = jnp.zeros_like(state), state, 1
    while stride < count:
        radix = 4 if count % (stride * 4) == 0 else 2
        assert count % (stride * radix) == 0
        digit = lax.rem(lax.div(position, stride), radix)
        group = stride * radix
        others = []
        for shift in range(1, radix):
            pairs = []
            for i in range(count):
                place = (i // stride) % radix
                if group < count or place >= shift:
                    source = (i // group) * group + ((place - shift) % radix) * stride + i % stride
                    pairs.append((source, i))
            others.append(lax.ppermute(total, axis, pairs))
        unit = span * stride
        before = jnp.zeros_like(state)
        for shift in range(1, radix):
            reached = jnp.exp(-rate * (unit * (shift - 1))) * others[shift - 1]
            before = before + jnp.where(digit >= shift, reached, 0.0)
        inner = lax.rem(position, stride)
        carry = carry + jnp.exp(-rate * (span * inner).astype(F32)) * before
        if group < count:
            new = jnp.exp(-rate * (unit * (radix - 1 - digit)).astype(F32)) * total
            for shift in range(1, radix):
                place = lax.rem(digit - shift + radix, radix)
                weight = jnp.exp(-rate * (unit * (radix - 1 - place)).astype(F32))
                new = new + weight * others[shift - 1]
            total = new
        stride = group
    return carry


CHUNKS = 4


def body(tokens, norm_gain, w_in, w_short, decay_rate, residue, skip_gain, w_out):
    pieces, me = lax.axis_size("tp"), lax.axis_index("tp")
    count = lax.axis_size("ctx")
    share, rows = tokens.shape
    taps = w_short.shape[0]
    chunk = rows // CHUNKS
    parts = [tokens[:, :chunk]]
    tokens, parts[0] = lax.optimization_barrier((tokens, parts[0]))
    parts += [tokens[:, j * chunk : (j + 1) * chunk] for j in range(1, CHUNKS)]
    gathered = [[part] + [rotate(part, "tp", s) for s in range(1, pieces)] for part in parts]
    last = tokens[:, rows - (taps - 1) :]
    edges = []
    for s in range(pieces):
        pairs = [
            (i * pieces + (t + s) % pieces, (i + 1) * pieces + t)
            for i in range(count - 1)
            for t in range(pieces)
        ]
        edge = lax.ppermute(last, ("ctx", "tp"), pairs)
        edges.append(jnp.pad(edge, ((0, 0), (0, LANES - (taps - 1)))))
    mode = residue * jnp.sqrt(-jnp.expm1(-2.0 * decay_rate))
    gain = norm_gain[None, :]
    skip = skip_gain[None, :]
    index = jnp.full((1,), me, jnp.int32)
    w_turned, index = lax.optimization_barrier((w_out.T, index))

    tail = state = None
    kept = []
    for j in range(CHUNKS):
        q, local, starts, state, tail = run_first(
            pieces, j == 0, index, gathered[j], edges, tail, state, gain, w_in, w_short,
            decay_rate, mode, skip,
        )
        kept.append((q, local, starts))
    carry = carried_in(state, decay_rate, rows, "ctx")
    result = jnp.zeros((share, rows), BF16)
    for j, (q, local, starts) in enumerate(kept):
        send, own = run_second(
            pieces, j * chunk, index, q, local, starts, carry, decay_rate, mode, w_turned
        )
        for s in range(1, pieces):
            own = own + rotate(send[(s - 1) * share : s * share], "tp", -s).astype(F32)
        result = lax.dynamic_update_slice(result, own.astype(BF16), (0, j * chunk))
    return result


def solution(mesh):
    placed = (
        P("tp", "ctx"),
        P(),
        P(None, "tp", None),
        P(None, None, "tp"),
        P(None, "tp"),
        P(None, "tp"),
        P("tp"),
        P("tp", None),
    )
    return jax.shard_map(
        body, mesh=mesh, in_specs=placed, out_specs=P("tp", "ctx"), check_vma=False
    )
```

```python
import functools

import jax
import jax.numpy as jnp
from jax import lax
from jax.experimental import pallas as pl
from jax.experimental.pallas import tpu as pltpu
from jax.sharding import PartitionSpec as P

F32 = jnp.float32
BF16 = jnp.bfloat16
ROWS = 8
LANES = 128
BLOCK = 256
VMEM_LIMIT = 10 * 2**20
CONTRACT_LAST = (((1,), (1,)), ((), ()))


def lane_groups(width):
    return [(start, min(LANES, width - start)) for start in range(0, width, LANES)]


def rows_as(row, width):
    return jnp.broadcast_to(row, (ROWS, width))


def tree_sum(terms):
    while len(terms) > 1:
        terms = [sum(terms[k + 1 : k + 2], terms[k]) for k in range(0, len(terms), 2)]
    return terms[0]


def interleave(rows, columns, length):
    row = lax.broadcasted_iota(jnp.int32, (rows, columns), 0)
    column = lax.broadcasted_iota(jnp.int32, (rows, columns), 1)
    wanted = lax.rem(row, ROWS) * length + lax.div(row, ROWS)
    return row, column, wanted


def delay_rows(p_ref, row_of, chunk, offset, heads, width):
    segment = lax.broadcasted_iota(jnp.int32, (ROWS, width), 0)
    cut = chunk - ROWS * offset
    wrapped = pltpu.roll(p_ref[cut : cut + ROWS, :width], 1, 0)
    heads.insert(0, jnp.where(segment == 0, rows_as(row_of(offset), width), wrapped))
    return jnp.concatenate(heads + [p_ref[:cut, :width]], axis=0)


def project(normed_ref, w_ref, s, part, p_ref, short_ref, tail_of, chunk, taps):
    width = part.stop - part.start
    product = lax.dot_general(
        normed_ref[...], w_ref[s, part, :], CONTRACT_LAST, preferred_element_type=F32
    )
    p_ref[:, :width] = product.astype(BF16).astype(F32)
    if tail_of is None:
        row_of = lambda offset: p_ref[chunk + taps - 1 - offset : chunk + taps - offset, :width]
    else:
        row_of = tail_of
    short = short_ref[0, s : s + 1, part] * p_ref[:chunk, :width]
    heads = []
    for offset in range(1, taps):
        delayed = delay_rows(p_ref, row_of, chunk, offset, heads, width)
        short = short + short_ref[offset, s : s + 1, part] * delayed
    return short


def last_rows(p_ref, chunk, offset, width):
    row = chunk - ROWS * offset + ROWS - 1
    return p_ref[row : row + 1, :width]


def signal_stage(pieces, first, taps, *refs):
    refs = list(refs)
    me_ref = refs.pop(0)
    token_refs = [refs.pop(0) for _ in range(pieces)]
    edge_refs = [refs.pop(0) for _ in range(pieces)] if first else []
    tail_in = None if first else refs.pop(0)
    state_in = None if first else refs.pop(0)
    gain_ref, w_ref, short_ref, rate_ref = refs[:4]
    normed_ref, signal_ref, ends_ref, state_ref, tail_ref = refs[4:9]
    x_ref, p_ref = refs[9:]
    share, chunk = token_refs[0].shape
    length = chunk // ROWS
    modes, channels = rate_ref.shape
    total_rows = normed_ref.shape[0]

    for s in range(pieces):
        rank = lax.rem(me_ref[0] + s, pieces)
        rows = pl.ds(pl.multiple_of(rank * share, 16), share)
        x_ref[rows, :chunk] = token_refs[s][...]
        if first:
            x_ref[rows, chunk:] = edge_refs[s][...]
    row, column, wanted = interleave(total_rows, x_ref.shape[1], length)
    if first:
        wanted = jnp.where(row < chunk, wanted, row)
    pick = jnp.where(column == wanted, 1.0, 0.0).astype(BF16)
    features = lax.dot_general(pick, x_ref[...], CONTRACT_LAST, preferred_element_type=F32)
    mean = jnp.mean(features * features, axis=1, keepdims=True)
    normed_ref[...] = (features * lax.rsqrt(mean + 1e-06) * gain_ref[...]).astype(BF16)

    for low in range(0, channels, BLOCK):
        width = min(BLOCK, channels - low)
        part = slice(low, low + width)
        for s in (1, 2):
            tail_of = None if first else (
                lambda offset: tail_in[s - 1, taps - 1 - offset : taps - offset, part]
            )
            short = project(normed_ref, w_ref, s, part, p_ref, short_ref, tail_of, chunk, taps)
            for offset in range(1, taps):
                tail_ref[s - 1, taps - 1 - offset : taps - offset, part] = last_rows(
                    p_ref, chunk, offset, width
                )
            signal_ref[:, part] = short if s == 1 else signal_ref[:, part] * short

        for start, size in lane_groups(width):
            lanes = slice(low + start, low + start + size)
            rate = [rows_as(rate_ref[n : n + 1, lanes], size) for n in range(modes)]
            decay = [jnp.exp(-r) for r in rate]

            def step(i, states):
                rows = pl.ds(pl.multiple_of(i * ROWS, ROWS), ROWS)
                now = signal_ref[rows, lanes]
                return tuple(states[n] * decay[n] + now for n in range(modes))

            zero = jnp.zeros((ROWS, size), F32)
            ends = lax.fori_loop(0, length, step, (zero,) * modes, unroll=8)
            left = lax.broadcasted_iota(jnp.int32, (ROWS, size), 0)
            left = ((ROWS - 1 - left) * length).astype(F32)
            for n in range(modes):
                ends_ref[n, :, lanes] = ends[n]
                last = jnp.sum(ends[n] * jnp.exp(-rate[n] * left), axis=0, keepdims=True)
                if not first:
                    past = jnp.exp(-rate_ref[n : n + 1, lanes] * chunk)
                    last = last + past * state_in[n : n + 1, lanes]
                state_ref[n : n + 1, lanes] = last


def local_stage(first, taps, *refs):
    refs = list(refs)
    normed_ref, signal_ref, ends_ref = refs[:3]
    refs = refs[3:]
    tail_in = None if first else refs.pop(0)
    state_in = None if first else refs.pop(0)
    w_ref, short_ref, rate_ref, mode_ref, skip_ref = refs[:5]
    q_ref, local_ref, tail_ref, p_ref = refs[5:]
    chunk, channels = signal_ref.shape
    modes = rate_ref.shape[0]
    length = chunk // ROWS
    for low in range(0, channels, BLOCK):
        width = min(BLOCK, channels - low)
        part = slice(low, low + width)
        tail_of = None if first else (
            lambda offset: tail_in[taps - 1 - offset : taps - offset, part]
        )
        q_ref[:, part] = project(
            normed_ref, w_ref, 0, part, p_ref, short_ref, tail_of, chunk, taps
        )
        for offset in range(1, taps):
            tail_ref[taps - 1 - offset : taps - offset, part] = last_rows(
                p_ref, chunk, offset, width
            )
        for start, size in lane_groups(width):
            lanes = slice(low + start, low + start + size)
            rate = [rows_as(rate_ref[n : n + 1, lanes], size) for n in range(modes)]
            decay = [jnp.exp(-r) for r in rate]
            mode = [rows_as(mode_ref[n : n + 1, lanes], size) for n in range(modes)]
            skip = rows_as(skip_ref[:, lanes], size)
            at = lax.broadcasted_iota(jnp.int32, (ROWS, size), 0)
            states = []
            for n in range(modes):
                run = ends_ref[n, :, lanes]
                for hop in (1, 2, 4):
                    weight = jnp.where(at >= hop, jnp.exp(-rate[n] * (hop * length)), 0.0)
                    run = run + weight * pltpu.roll(run, hop, 0)
                begin = jnp.where(at >= 1, pltpu.roll(run, 1, 0), 0.0)
                if not first:
                    begin = begin + jnp.exp(-rate[n] * (at * length).astype(F32)) * state_in[
                        n : n + 1, lanes
                    ]
                states.append(begin)

            def step(i, states):
                rows = pl.ds(pl.multiple_of(i * ROWS, ROWS), ROWS)
                now = signal_ref[rows, lanes]
                states = tuple(states[n] * decay[n] + now for n in range(modes))
                local_ref[rows, lanes] = tree_sum(
                    [skip * now] + [mode[n] * states[n] for n in range(modes)]
                )
                return states

            lax.fori_loop(0, length, step, tuple(states), unroll=4)


def second_stage(pieces, begin_at, *refs):
    me_ref, q_ref, local_ref, carry_ref, rate_ref, mode_ref, w_ref = refs[:7]
    send_ref, own_ref, gated_ref = refs[7:]
    chunk, channels = q_ref.shape
    modes = rate_ref.shape[0]
    length = chunk // ROWS
    for start, size in lane_groups(channels):
        lanes = slice(start, start + size)
        rate = [rows_as(rate_ref[n : n + 1, lanes], size) for n in range(modes)]
        decay = [jnp.exp(-r) for r in rate]
        at = lax.broadcasted_iota(jnp.int32, (ROWS, size), 0)
        past = (begin_at + at * length).astype(F32)
        states = tuple(
            jnp.exp(-rate[n] * past) * (mode_ref[n : n + 1, lanes] * carry_ref[n : n + 1, lanes])
            for n in range(modes)
        )

        def step(i, states):
            rows = pl.ds(pl.multiple_of(i * ROWS, ROWS), ROWS)
            states = tuple(states[n] * decay[n] for n in range(modes))
            gated_ref[rows, lanes] = q_ref[rows, lanes] * tree_sum(
                [local_ref[rows, lanes]] + list(states)
            )
            return states

        lax.fori_loop(0, length, step, states, unroll=4)

    row, column, wanted = interleave(chunk, chunk, length)
    pick = jnp.where(column == wanted, 1.0, 0.0).astype(BF16)
    gated = lax.dot_general(
        pick, gated_ref[...].astype(BF16), (((0,), (0,)), ((), ())), preferred_element_type=F32
    ).astype(BF16)
    share = own_ref.shape[0]
    for s in list(range(1, pieces)) + [0]:
        rank = lax.rem(me_ref[0] + s, pieces)
        rows = pl.ds(pl.multiple_of(rank * share, 16), share)
        part = lax.dot_general(w_ref[rows, :], gated, CONTRACT_LAST, preferred_element_type=F32)
        if s == 0:
            own_ref[...] = part
        else:
            send_ref[(s - 1) * share : s * share, :] = part.astype(BF16)


def call(kernel, name, scalars, operands, outs, scratch, flops):
    vmem = pl.BlockSpec(memory_space=pltpu.VMEM)
    smem = pl.BlockSpec(memory_space=pltpu.SMEM)
    size = lambda a: a.size * jnp.dtype(a.dtype).itemsize
    return pl.pallas_call(
        kernel,
        out_shape=outs,
        in_specs=[smem] * len(scalars) + [vmem] * len(operands),
        out_specs=[vmem] * len(outs),
        scratch_shapes=scratch,
        compiler_params=pltpu.CompilerParams(vmem_limit_bytes=VMEM_LIMIT),
        cost_estimate=pl.CostEstimate(
            flops=flops,
            bytes_accessed=sum(size(a) for a in list(operands) + list(outs)),
            transcendentals=0,
        ),
        name=name,
    )(*scalars, *operands)


def run_signal(pieces, first, me, tokens, edges, tail, state, gain, w_in, w_short, rate):
    share, chunk = tokens[0].shape
    streams, channels, features = w_in.shape
    taps = w_short.shape[0]
    modes = rate.shape[0]
    rows = chunk + (16 if first else 0)
    columns = chunk + (LANES if first else 0)
    return call(
        functools.partial(signal_stage, pieces, first, taps),
        "signal_stage",
        [me],
        list(tokens) + (list(edges) if first else [tail, state]) + [gain, w_in, w_short, rate],
        [
            jax.ShapeDtypeStruct((rows, features), BF16),
            jax.ShapeDtypeStruct((chunk, channels), F32),
            jax.ShapeDtypeStruct((modes, ROWS, channels), F32),
            jax.ShapeDtypeStruct((modes, channels), F32),
            jax.ShapeDtypeStruct((streams - 1, taps - 1, channels), F32),
        ],
        [pltpu.VMEM((features, columns), BF16), pltpu.VMEM((rows, min(BLOCK, channels)), F32)],
        4 * rows * features * channels,
    )


def run_local(first, normed, signal, ends, tail, state, w_in, w_short, rate, mode, skip):
    chunk, channels = signal.shape
    taps = w_short.shape[0]
    rows, features = normed.shape
    return call(
        functools.partial(local_stage, first, taps),
        "local_stage",
        [],
        [normed, signal, ends] + ([] if first else [tail, state]) + [w_in, w_short, rate, mode, skip],
        [
            jax.ShapeDtypeStruct((chunk, channels), F32),
            jax.ShapeDtypeStruct((chunk, channels), F32),
            jax.ShapeDtypeStruct((taps - 1, channels), F32),
        ],
        [pltpu.VMEM((rows, min(BLOCK, channels)), F32)],
        2 * rows * features * channels,
    )


def run_second(pieces, begin_at, me, q, local, carry, rate, mode, w):
    chunk, channels = q.shape
    features = w.shape[0]
    share = features // pieces
    return call(
        functools.partial(second_stage, pieces, begin_at),
        "second_stage",
        [me],
        [q, local, carry, rate, mode, w],
        [
            jax.ShapeDtypeStruct((max(1, pieces - 1) * share, chunk), BF16),
            jax.ShapeDtypeStruct((share, chunk), F32),
        ],
        [pltpu.VMEM((chunk, channels), F32)],
        2 * features * channels * chunk,
    )


def rotate(value, axis, steps):
    count = lax.axis_size(axis)
    return lax.ppermute(value, axis, [((i + steps) % count, i) for i in range(count)])


def carried_in(state, rate, span, axis, between):
    count, position = lax.axis_size(axis), lax.axis_index(axis)
    carry, total, stride = jnp.zeros_like(state), state, 1
    while stride < count:
        radix = 4 if count % (stride * 4) == 0 else 2
        assert count % (stride * radix) == 0
        digit = lax.rem(lax.div(position, stride), radix)
        group = stride * radix
        others = []
        for shift in range(1, radix):
            pairs = []
            for i in range(count):
                place = (i // stride) % radix
                if group < count or place >= shift:
                    source = (i // group) * group + ((place - shift) % radix) * stride + i % stride
                    pairs.append((source, i))
            others.append(lax.ppermute(total, axis, pairs))
        unit = span * stride
        others = between(stride, others)
        before = jnp.zeros_like(state)
        for shift in range(1, radix):
            reached = jnp.exp(-rate * (unit * (shift - 1))) * others[shift - 1]
            before = before + jnp.where(digit >= shift, reached, 0.0)
        inner = lax.rem(position, stride)
        carry = carry + jnp.exp(-rate * (span * inner).astype(F32)) * before
        if group < count:
            new = jnp.exp(-rate * (unit * (radix - 1 - digit)).astype(F32)) * total
            for shift in range(1, radix):
                place = lax.rem(digit - shift + radix, radix)
                weight = jnp.exp(-rate * (unit * (radix - 1 - place)).astype(F32))
                new = new + weight * others[shift - 1]
            total = new
        stride = group
    return carry


CHUNKS = 4


def body(tokens, norm_gain, w_in, w_short, decay_rate, residue, skip_gain, w_out):
    pieces, me = lax.axis_size("tp"), lax.axis_index("tp")
    count = lax.axis_size("ctx")
    share, rows = tokens.shape
    taps = w_short.shape[0]
    chunk = rows // CHUNKS
    parts = [tokens[:, :chunk]]
    tokens, parts[0] = lax.optimization_barrier((tokens, parts[0]))
    parts += [tokens[:, j * chunk : (j + 1) * chunk] for j in range(1, CHUNKS)]
    tokens, *parts[1:] = lax.optimization_barrier((tokens, *parts[1:]))
    gathered = [[part] + [rotate(part, "tp", s) for s in range(1, pieces)] for part in parts]
    last = tokens[:, rows - (taps - 1) :]
    edges = []
    for s in range(pieces):
        pairs = [
            (i * pieces + (t + s) % pieces, (i + 1) * pieces + t)
            for i in range(count - 1)
            for t in range(pieces)
        ]
        edge = lax.ppermute(last, ("ctx", "tp"), pairs)
        edges.append(jnp.pad(edge, ((0, 0), (0, LANES - (taps - 1)))))
    mode = residue * jnp.sqrt(-jnp.expm1(-2.0 * decay_rate))
    gain = norm_gain[None, :]
    skip = skip_gain[None, :]
    index = jnp.full((1,), me, jnp.int32)
    w_turned, index = lax.optimization_barrier((w_out.T, index))
    w_in = pltpu.with_memory_space_constraint(w_in, pltpu.VMEM)
    w_turned = pltpu.with_memory_space_constraint(w_turned, pltpu.VMEM)

    tail = state = None
    kept = []
    for j in range(CHUNKS):
        given = state
        normed, signal, ends, state, tail = run_signal(
            pieces, j == 0, index, gathered[j], edges, tail, state, gain, w_in, w_short, decay_rate
        )
        kept.append([normed, signal, ends, given])
    state, kept = lax.optimization_barrier((state, kept))
    done, query_tail = [], [None]

    def local_part(j):
        normed, signal, ends, given = kept[j]
        q, local, query_tail[0] = run_local(
            j == 0, normed, signal, ends, query_tail[0], given, w_in, w_short, decay_rate, mode, skip
        )
        done.append((q, local))

    def between(stride, others):
        if stride == 1:
            for j in range(CHUNKS // 2):
                local_part(j)
        elif len(done) < CHUNKS:
            for j in range(CHUNKS // 2, CHUNKS):
                local_part(j)
        others, done[:], query_tail[0] = lax.optimization_barrier(
            (others, done[:], query_tail[0])
        )
        return others

    carry = carried_in(state, decay_rate, rows, "ctx", between)
    result = jnp.zeros((share, rows), BF16)
    for j, (q, local) in enumerate(done):
        send, own = run_second(
            pieces, j * chunk, index, q, local, carry, decay_rate, mode, w_turned
        )
        for s in range(1, pieces):
            own = own + rotate(send[(s - 1) * share : s * share], "tp", -s).astype(F32)
        result = lax.dynamic_update_slice(result, own.astype(BF16), (0, j * chunk))
    return result


def solution(mesh):
    placed = (
        P("tp", "ctx"),
        P(),
        P(None, "tp", None),
        P(None, None, "tp"),
        P(None, "tp"),
        P(None, "tp"),
        P("tp"),
        P("tp", None),
    )
    return jax.shard_map(
        body, mesh=mesh, in_specs=placed, out_specs=P("tp", "ctx"), check_vma=False
    )
```

```python
import functools

import jax
import jax.numpy as jnp
from jax import lax
from jax.experimental import pallas as pl
from jax.experimental.pallas import tpu as pltpu
from jax.sharding import PartitionSpec as P


F32 = jnp.float32
BF16 = jnp.bfloat16
ROWS = 8
LANES = 128
BLOCK = 256
CHUNKS = 4
VMEM_LIMIT = 10 * 2**20
CONTRACT_LAST = (((1,), (1,)), ((), ()))
CONTRACT_FIRST = (((0,), (0,)), ((), ()))


def lane_groups(low, width):
    return [(start, min(LANES, low + width - start)) for start in range(low, low + width, LANES)]


def rows_as(row, width):
    return jnp.broadcast_to(row, (ROWS, width))


def tree_sum(terms):
    while len(terms) > 1:
        terms = [sum(terms[k + 1 : k + 2], terms[k]) for k in range(0, len(terms), 2)]
    return terms[0]


def token_picker(first_row, rows, tokens):
    length = tokens // ROWS
    row = lax.broadcasted_iota(jnp.int32, (rows, tokens), 0)
    column = lax.broadcasted_iota(jnp.int32, (rows, tokens), 1)
    wanted = lax.rem(row, ROWS) * length + lax.div(row, ROWS) + first_row // ROWS
    return jnp.where(column == wanted, 1.0, 0.0).astype(BF16)


def turned(pick, tokens):
    return lax.dot_general(pick, tokens, CONTRACT_LAST, preferred_element_type=F32).astype(BF16)


def first_rows(halo, tokens_ref, out_ref):
    rows, tokens = out_ref.shape[0], tokens_ref.shape[1]
    out_ref[...] = turned(token_picker(-halo, rows, tokens), tokens_ref[...])


def other_rows(halo, sizes, places, *refs):
    tokens_ref, w_hbm = refs[:2]
    chunk_refs, edge_ref, w_ref, sem = refs[2:-3], refs[-3], refs[-2], refs[-1]
    copies = [
        pltpu.make_async_copy(w_hbm.at[place], w_ref.at[place], sem.at[k])
        for k, place in enumerate(places)
    ]
    for copy in copies:
        copy.start()
    tokens = tokens_ref.shape[1]
    row = sizes[0]
    for ref in chunk_refs:
        ref[...] = turned(token_picker(row, ref.shape[0], tokens), tokens_ref[...])
        row += ref.shape[0]
    row = lax.broadcasted_iota(jnp.int32, (halo, tokens), 0)
    column = lax.broadcasted_iota(jnp.int32, (halo, tokens), 1)
    wanted = jnp.where(lax.rem(row, ROWS) == 0, tokens - halo // ROWS + lax.div(row, ROWS), -1)
    edge_ref[...] = turned(jnp.where(column == wanted, 1.0, 0.0).astype(BF16), tokens_ref[...])
    for copy in copies:
        copy.wait()


def short_conv(p_ref, short_ref, s, part, rows, taps):
    width = part.stop - part.start
    total = None
    for offset in range(taps):
        start = ROWS * (taps - 1 - offset)
        term = short_ref[offset, s : s + 1, part] * p_ref[start : start + rows, :width]
        total = term if total is None else total + term
    return total


def project(normed, w_ref, s, part):
    product = lax.dot_general(normed, w_ref[s, part, :], CONTRACT_LAST, preferred_element_type=F32)
    return product.astype(BF16).astype(F32)


def signal_stage(pieces, first, last, row, taps, *refs):
    refs = list(refs)
    me_ref = refs.pop(0)
    token_refs = [refs.pop(0) for _ in range(pieces)]
    edge_refs = [refs.pop(0) for _ in range(pieces)] if first else []
    normed_in, signal_in, states_in, tail_in = [None] * 4 if first else [refs.pop(0) for _ in range(4)]
    gain_ref, w_ref, short_ref, rate_ref = refs[:4]
    normed_ref, signal_ref, states_ref, tail_ref = refs[4:8]
    total_ref = refs[8] if last else None
    x_ref, p_ref = refs[-2:]
    halo = ROWS * (taps - 1)
    modes, channels = rate_ref.shape
    read, share = token_refs[0].shape
    rows = read - halo if first else read
    length = signal_ref.shape[0] // ROWS
    me = me_ref[0]

    values = []
    for s in range(pieces):
        value = token_refs[s][...].astype(F32)
        if first:
            edge = edge_refs[s][...].astype(F32)
            value = jnp.concatenate([value[:halo] + edge, value[halo:]], axis=0)
        values.append(value)
    for rank in range(pieces):
        chosen = values[0]
        for s in range(1, pieces):
            chosen = jnp.where(me == (rank - s) % pieces, values[s], chosen)
        x_ref[:, rank * share : (rank + 1) * share] = chosen
    features = x_ref[...]
    mean = jnp.mean(features * features, axis=1, keepdims=True)
    normed = (features * lax.rsqrt(mean + 1e-06) * gain_ref[...]).astype(BF16)
    begin = 0 if first else halo + row
    normed_ref[begin : begin + read, :] = normed

    for low in range(0, channels, BLOCK):
        width = min(BLOCK, channels - low)
        part = slice(low, low + width)
        for s in (1, 2):
            if not first:
                p_ref[:halo, :width] = tail_in[s - 1, :, part]
            p_ref[halo + rows - read :, :width] = project(
                normed_ref[begin : begin + read, :], w_ref, s, part
            )
            tail_ref[s - 1, :, part] = p_ref[rows:, :width]
            short = short_conv(p_ref, short_ref, s, part, rows, taps)
            if s == 1:
                signal_ref[row : row + rows, part] = short
            else:
                signal_ref[row : row + rows, part] = signal_ref[row : row + rows, part] * short
        for start, size in lane_groups(low, width):
            lanes = slice(start, start + size)
            rate = [rows_as(rate_ref[n : n + 1, lanes], size) for n in range(modes)]
            decay = [jnp.exp(-r) for r in rate]

            def step(i, states):
                here = pl.ds(pl.multiple_of(row + i * ROWS, ROWS), ROWS)
                now = signal_ref[here, lanes]
                return tuple(states[n] * decay[n] + now for n in range(modes))

            if first:
                states = (jnp.zeros((ROWS, size), F32),) * modes
            else:
                states = tuple(states_in[n, :, lanes] for n in range(modes))
            states = lax.fori_loop(0, rows // ROWS, step, states, unroll=8)
            for n in range(modes):
                states_ref[n, :, lanes] = states[n]
            if last:
                left = lax.broadcasted_iota(jnp.int32, (ROWS, size), 0)
                left = ((ROWS - 1 - left) * length).astype(F32)
                for n in range(modes):
                    total_ref[n : n + 1, lanes] = jnp.sum(
                        states[n] * jnp.exp(-rate[n] * left), axis=0, keepdims=True
                    )


def local_stage(low, high, taps, *refs):
    normed_ref, signal_ref, states_ref, w_ref, short_ref, rate_ref, mode_ref, skip_ref = refs[:8]
    q_ref, local_ref, p_ref = refs[8:]
    modes = rate_ref.shape[0]
    rows = signal_ref.shape[0]
    length = rows // ROWS
    for at in range(low, high, BLOCK):
        width = min(BLOCK, high - at)
        part = slice(at, at + width)
        p_ref[:, :width] = project(normed_ref[...], w_ref, 0, part)
        q_ref[:, at - low : at - low + width] = short_conv(p_ref, short_ref, 0, part, rows, taps)
        for start, size in lane_groups(at, width):
            lanes = slice(start, start + size)
            there = slice(start - low, start - low + size)
            rate = [rows_as(rate_ref[n : n + 1, lanes], size) for n in range(modes)]
            decay = [jnp.exp(-r) for r in rate]
            mode = [rows_as(mode_ref[n : n + 1, lanes], size) for n in range(modes)]
            skip = rows_as(skip_ref[:, lanes], size)
            segment = lax.broadcasted_iota(jnp.int32, (ROWS, size), 0)
            states = []
            for n in range(modes):
                run = states_ref[n, :, lanes]
                for hop in (1, 2, 4):
                    weight = jnp.where(segment >= hop, jnp.exp(-rate[n] * (hop * length)), 0.0)
                    run = run + weight * pltpu.roll(run, hop, 0)
                states.append(jnp.where(segment >= 1, pltpu.roll(run, 1, 0), 0.0))

            def step(i, states):
                here = pl.ds(pl.multiple_of(i * ROWS, ROWS), ROWS)
                now = signal_ref[here, lanes]
                states = tuple(states[n] * decay[n] + now for n in range(modes))
                local_ref[here, there] = tree_sum(
                    [skip * now] + [mode[n] * states[n] for n in range(modes)]
                )
                return states

            lax.fori_loop(0, length, step, tuple(states), unroll=4)


def second_stage(pieces, row, rows, bounds, *refs):
    count = len(bounds)
    me_ref = refs[0]
    q_refs, local_refs = refs[1 : 1 + count], refs[1 + count : 1 + 2 * count]
    carry_ref, rate_ref, mode_ref, w_ref = refs[1 + 2 * count : 5 + 2 * count]
    send_ref, own_ref, gated_ref = refs[5 + 2 * count :]
    modes = rate_ref.shape[0]
    length = q_refs[0].shape[0] // ROWS
    for (low, high), q_ref, local_ref in zip(bounds, q_refs, local_refs):
        for start, size in lane_groups(low, high - low):
            lanes = slice(start, start + size)
            there = slice(start - low, start - low + size)
            rate = [rows_as(rate_ref[n : n + 1, lanes], size) for n in range(modes)]
            decay = [jnp.exp(-r) for r in rate]
            segment = lax.broadcasted_iota(jnp.int32, (ROWS, size), 0)
            past = (segment * length + row // ROWS).astype(F32)
            states = tuple(
                jnp.exp(-rate[n] * past)
                * (mode_ref[n : n + 1, lanes] * carry_ref[n : n + 1, lanes])
                for n in range(modes)
            )

            def step(i, states):
                here = pl.ds(pl.multiple_of(i * ROWS, ROWS), ROWS)
                from_row = pl.ds(pl.multiple_of(row + i * ROWS, ROWS), ROWS)
                states = tuple(states[n] * decay[n] for n in range(modes))
                gated_ref[here, lanes] = q_ref[from_row, there] * tree_sum(
                    [local_ref[from_row, there]] + list(states)
                )
                return states

            lax.fori_loop(0, rows // ROWS, step, states, unroll=4)
    product = jnp.dot(gated_ref[...].astype(BF16), w_ref[...], preferred_element_type=F32)
    share = own_ref.shape[1]
    me = me_ref[0]
    columns = [product[:, rank * share : (rank + 1) * share] for rank in range(pieces)]
    for s in range(pieces):
        chosen = columns[0]
        for rank in range(1, pieces):
            chosen = jnp.where(me == (rank - s) % pieces, columns[rank], chosen)
        if s == 0:
            own_ref[...] = chosen
        else:
            send_ref[(s - 1) * rows : s * rows, :] = chosen.astype(BF16)


def last_stage(pieces, sizes, *refs):
    chunks = len(sizes)
    own_refs, came_refs = refs[:chunks], refs[chunks : chunks * pieces]
    out_ref, mixed_ref = refs[chunks * pieces :]
    row = 0
    for j, size in enumerate(sizes):
        total = own_refs[j][...]
        for s in range(pieces - 1):
            total = total + came_refs[j * (pieces - 1) + s][...].astype(F32)
        mixed_ref[row : row + size, :] = total.astype(BF16)
        row += size
    pick = token_picker(0, row, row)
    out_ref[...] = lax.dot_general(
        mixed_ref[...], pick, CONTRACT_FIRST, preferred_element_type=F32
    ).astype(BF16)


def call(kernel, name, scalars, operands, outs, scratch, flops, aliases={}, hbm=(), limit=VMEM_LIMIT):
    vmem = pl.BlockSpec(memory_space=pltpu.VMEM)
    smem = pl.BlockSpec(memory_space=pltpu.SMEM)
    any_space = pl.BlockSpec(memory_space=pl.ANY)
    size = lambda a: a.size * jnp.dtype(a.dtype).itemsize
    return pl.pallas_call(
        kernel,
        out_shape=outs,
        in_specs=[smem] * len(scalars)
        + [any_space if k in hbm else vmem for k in range(len(operands))],
        out_specs=[vmem] * len(outs),
        scratch_shapes=scratch,
        input_output_aliases=aliases,
        compiler_params=pltpu.CompilerParams(vmem_limit_bytes=limit),
        cost_estimate=pl.CostEstimate(
            flops=flops,
            bytes_accessed=sum(size(a) for a in operands),
            transcendentals=0,
        ),
        name=name,
    )(*scalars, *operands)


def run_rows(tokens, w_in, sizes, halo):
    share, count = tokens.shape
    (x0,) = call(
        functools.partial(first_rows, halo),
        "first_rows",
        [],
        [tokens],
        [jax.ShapeDtypeStruct((halo + sizes[0], share), BF16)],
        [],
        2 * (halo + sizes[0]) * count * share,
    )
    tokens, x0 = lax.optimization_barrier((tokens, x0))
    channels = w_in.shape[1]
    parts = next(k for k in (4, 3, 2, 1) if channels % (16 * k) == 0 or k == 1)
    size = channels // parts
    places = [
        (s, slice(p * size, (p + 1) * size)) for s in (1, 2, 0) for p in range(parts)
    ]
    *others, edge, w_in = call(
        functools.partial(other_rows, halo, sizes, places),
        "other_rows",
        [],
        [tokens, w_in],
        [jax.ShapeDtypeStruct((size, share), BF16) for size in sizes[1:]]
        + [jax.ShapeDtypeStruct((halo, share), BF16), pltpu.VMEM(w_in.shape, w_in.dtype)],
        [pltpu.SemaphoreType.DMA((len(places),))],
        2 * count * count * share,
        hbm=(1,),
        limit=46 * 2**20,
    )
    return [x0, *others], edge, w_in


def run_signal(pieces, row, sizes, j, taps, me, tokens, edges, before, gain, w_in, w_short, rate):
    first, last = j == 0, j == len(sizes) - 1
    read, share = tokens[0].shape
    streams, channels, features = w_in.shape
    modes = rate.shape[0]
    halo = ROWS * (taps - 1)
    count = sum(sizes)
    front = list(tokens) + (list(edges) if first else list(before))
    outs = [
        jax.ShapeDtypeStruct((halo + count, features), BF16),
        jax.ShapeDtypeStruct((count, channels), F32),
        jax.ShapeDtypeStruct((modes, ROWS, channels), F32),
        jax.ShapeDtypeStruct((streams - 1, halo, channels), F32),
    ]
    if last:
        outs.append(jax.ShapeDtypeStruct((modes, channels), F32))
    return call(
        functools.partial(signal_stage, pieces, first, last, row, taps),
        "signal_stage",
        [me],
        front + [gain, w_in, w_short, rate],
        outs,
        [
            pltpu.VMEM((read, features), F32),
            pltpu.VMEM((halo + sizes[j], min(BLOCK, channels)), F32),
        ],
        4 * read * features * channels,
        aliases={} if first else {1 + pieces: 0, 2 + pieces: 1},
    )


def run_local(low, high, taps, normed, signal, states, w_in, w_short, rate, mode, skip):
    count = signal.shape[0]
    rows, features = normed.shape
    out = jax.ShapeDtypeStruct((count, high - low), F32)
    return call(
        functools.partial(local_stage, low, high, taps),
        "local_stage",
        [],
        [normed, signal, states, w_in, w_short, rate, mode, skip],
        [out, out],
        [pltpu.VMEM((rows, min(BLOCK, high - low)), F32)],
        2 * rows * features * (high - low),
    )


def run_second(pieces, row, rows, bounds, me, q, local, carry, rate, mode, w):
    channels, features = w.shape
    share = features // pieces
    return call(
        functools.partial(second_stage, pieces, row, rows, bounds),
        "second_stage",
        [me],
        [*q, *local, carry, rate, mode, w],
        [
            jax.ShapeDtypeStruct((max(1, pieces - 1) * rows, share), BF16),
            jax.ShapeDtypeStruct((rows, share), F32),
        ],
        [pltpu.VMEM((rows, channels), F32)],
        2 * features * channels * rows,
    )


def run_last(pieces, sizes, own, came):
    count, share = sum(sizes), own[0].shape[1]
    (out,) = call(
        functools.partial(last_stage, pieces, sizes),
        "last_stage",
        [],
        [*own, *came],
        [jax.ShapeDtypeStruct((share, count), BF16)],
        [pltpu.VMEM((count, share), BF16)],
        2 * count * count * share,
    )
    return out


def rotate(value, axis, steps):
    count = lax.axis_size(axis)
    return lax.ppermute(value, axis, [((i + steps) % count, i) for i in range(count)])


def carried_in(state, rate, span, axis, between):
    count, position = lax.axis_size(axis), lax.axis_index(axis)
    carry, total, stride = jnp.zeros_like(state), state, 1
    while stride < count:
        radix = 4 if count % (stride * 4) == 0 else 2
        assert count % (stride * radix) == 0
        digit = lax.rem(lax.div(position, stride), radix)
        group = stride * radix
        others = []
        for shift in range(1, radix):
            pairs = []
            for i in range(count):
                place = (i // stride) % radix
                if group < count or place >= shift:
                    source = (i // group) * group + ((place - shift) % radix) * stride + i % stride
                    pairs.append((source, i))
            others.append(lax.ppermute(total, axis, pairs))
        unit = span * stride
        others = between(stride, others)
        before = jnp.zeros_like(state)
        for shift in range(1, radix):
            reached = jnp.exp(-rate * (unit * (shift - 1))) * others[shift - 1]
            before = before + jnp.where(digit >= shift, reached, 0.0)
        inner = lax.rem(position, stride)
        carry = carry + jnp.exp(-rate * (span * inner).astype(F32)) * before
        if group < count:
            new = jnp.exp(-rate * (unit * (radix - 1 - digit)).astype(F32)) * total
            for shift in range(1, radix):
                place = lax.rem(digit - shift + radix, radix)
                weight = jnp.exp(-rate * (unit * (radix - 1 - place)).astype(F32))
                new = new + weight * others[shift - 1]
            total = new
        stride = group
    return carry


def body(tokens, norm_gain, w_in, w_short, decay_rate, residue, skip_gain, w_out):
    pieces, me = lax.axis_size("tp"), lax.axis_index("tp")
    count = lax.axis_size("ctx")
    share, rows = tokens.shape
    channels = w_in.shape[1]
    taps = w_short.shape[0]
    halo = ROWS * (taps - 1)
    sizes = [rows // CHUNKS] * CHUNKS
    starts = [sum(sizes[:j]) for j in range(CHUNKS)]
    x, edge, w_in = run_rows(tokens, w_in, sizes, halo)
    w_in = pltpu.with_memory_space_constraint(w_in, pltpu.VMEM)
    gathered = [[part] + [rotate(part, "tp", s) for s in range(1, pieces)] for part in x]
    edge, gathered[0] = lax.optimization_barrier((edge, gathered[0]))
    edges = []
    for s in range(pieces):
        pairs = [
            (i * pieces + (t + s) % pieces, (i + 1) * pieces + t)
            for i in range(count - 1)
            for t in range(pieces)
        ]
        edges.append(lax.ppermute(edge, ("ctx", "tp"), pairs))
    mode = residue * jnp.sqrt(-jnp.expm1(-2.0 * decay_rate))
    gain = norm_gain[None, :]
    skip = skip_gain[None, :]
    index = jnp.full((1,), me, jnp.int32)

    before = []
    for j in range(CHUNKS):
        results = run_signal(
            pieces, starts[j], sizes, j, taps, index, gathered[j], edges, before, gain, w_in,
            w_short, decay_rate,
        )
        before = results[:4]
    normed, signal, states, _ = before
    state, normed, signal, states = lax.optimization_barrier((results[4], normed, signal, states))
    blocks = (channels + BLOCK - 1) // BLOCK
    middle = min(channels, (blocks + 1) // 2 * BLOCK)
    bounds = [b for b in ((0, middle), (middle, channels)) if b[0] < b[1]]
    done = []

    def between(stride, others):
        if len(done) < len(bounds):
            q, local = run_local(
                *bounds[len(done)], taps, normed, signal, states, w_in, w_short, decay_rate, mode, skip
            )
            done.append((q, local))
            others, done[-1] = lax.optimization_barrier((others, done[-1]))
        return others

    carry = carried_in(state, decay_rate, rows, "ctx", between)
    while len(done) < len(bounds):
        between(0, [])
    q, local = zip(*done)
    own, came = [], []
    for j in range(CHUNKS):
        if j == 2:
            carry, came[: pieces - 1] = lax.optimization_barrier((carry, came[: pieces - 1]))
        send, kept = run_second(
            pieces, starts[j], sizes[j], bounds, index, q, local, carry, decay_rate, mode, w_out
        )
        own.append(kept)
        for s in range(1, pieces):
            came.append(rotate(send[(s - 1) * sizes[j] : s * sizes[j]], "tp", -s))
    return run_last(pieces, sizes, own, came)


def solution(mesh):
    placed = (
        P("tp", "ctx"),
        P(),
        P(None, "tp", None),
        P(None, None, "tp"),
        P(None, "tp"),
        P(None, "tp"),
        P("tp"),
        P("tp", None),
    )
    return jax.shard_map(
        body, mesh=mesh, in_specs=placed, out_specs=P("tp", "ctx"), check_vma=False
    )
```

```python
import functools

import jax
import jax.numpy as jnp
from jax import lax
from jax.experimental import pallas as pl
from jax.experimental.pallas import tpu as pltpu
from jax.sharding import PartitionSpec as P


F32 = jnp.float32
BF16 = jnp.bfloat16
ROWS = 8
LANES = 128
BLOCK = 256
CHUNKS = 4
VMEM_LIMIT = 10 * 2**20
CONTRACT_LAST = (((1,), (1,)), ((), ()))
CONTRACT_FIRST = (((0,), (0,)), ((), ()))


def lane_groups(low, width):
    return [(start, min(LANES, low + width - start)) for start in range(low, low + width, LANES)]


def rows_as(row, width):
    return jnp.broadcast_to(row, (ROWS, width))


def tree_sum(terms):
    while len(terms) > 1:
        terms = [sum(terms[k + 1 : k + 2], terms[k]) for k in range(0, len(terms), 2)]
    return terms[0]


def token_picker(first_row, rows, tokens):
    length = tokens // ROWS
    row = lax.broadcasted_iota(jnp.int32, (rows, tokens), 0)
    column = lax.broadcasted_iota(jnp.int32, (rows, tokens), 1)
    wanted = lax.rem(row, ROWS) * length + lax.div(row, ROWS) + first_row // ROWS
    return jnp.where(column == wanted, 1.0, 0.0).astype(BF16)


def turned(pick, tokens):
    return lax.dot_general(pick, tokens, CONTRACT_LAST, preferred_element_type=F32).astype(BF16)


def first_rows(halo, tokens_ref, out_ref, edge_ref):
    tokens = tokens_ref.shape[1]
    out_ref[...] = turned(token_picker(-halo, out_ref.shape[0], tokens), tokens_ref[...])
    row = lax.broadcasted_iota(jnp.int32, (halo, tokens), 0)
    column = lax.broadcasted_iota(jnp.int32, (halo, tokens), 1)
    wanted = jnp.where(lax.rem(row, ROWS) == 0, tokens - halo // ROWS + lax.div(row, ROWS), -1)
    edge_ref[...] = turned(jnp.where(column == wanted, 1.0, 0.0).astype(BF16), tokens_ref[...])


def other_rows(halo, place_ref, tokens_ref, edge_ref, *chunk_refs):
    tokens = tokens_ref.shape[1]
    preceded = jnp.where(place_ref[1] > 0, 1.0, 0.0)
    row = tokens - sum(ref.shape[0] for ref in chunk_refs) + halo
    for k, ref in enumerate(chunk_refs):
        front = 0
        if k == 0:
            front = halo
            ref[:halo, :] = (edge_ref[...].astype(F32) * preceded).astype(BF16)
        rows = ref.shape[0] - front
        ref[front:, :] = turned(token_picker(row, rows, tokens), tokens_ref[...])
        row += rows


def load_weights(places, w_hbm, w_ref, sem):
    copies = [
        pltpu.make_async_copy(w_hbm.at[place], w_ref.at[place], sem.at[k])
        for k, place in enumerate(places)
    ]
    for copy in copies:
        copy.start()
    for copy in copies:
        copy.wait()


def short_conv(p_ref, short_ref, s, part, rows, taps):
    width = part.stop - part.start
    total = None
    for offset in range(taps):
        start = ROWS * (taps - 1 - offset)
        term = short_ref[offset, s : s + 1, part] * p_ref[start : start + rows, :width]
        total = term if total is None else total + term
    return total


def project(normed, w_ref, s, part):
    product = lax.dot_general(normed, w_ref[s, part, :], CONTRACT_LAST, preferred_element_type=F32)
    return product.astype(BF16).astype(F32)


def signal_stage(pieces, chunks, first, last, row, taps, *refs):
    refs = list(refs)
    me_ref = refs.pop(0)
    token_refs = [[refs.pop(0) for _ in range(pieces)] for _ in range(chunks)]
    normed_in, signal_in, states_in, tail_in = [None] * 4 if first else [refs.pop(0) for _ in range(4)]
    gain_ref, w_ref, short_ref, rate_ref = refs[:4]
    normed_ref, signal_ref, states_ref, tail_ref = refs[4:8]
    total_ref = refs[8] if last else None
    x_ref, p_ref = refs[-2:]
    halo = ROWS * (taps - 1)
    modes, channels = rate_ref.shape
    read, share = x_ref.shape[0], token_refs[0][0].shape[1]
    rows = read - halo if first else read
    length = signal_ref.shape[0] // ROWS
    me = me_ref[0]

    values = []
    for s in range(pieces):
        value = [refs_of[s][...].astype(F32) for refs_of in token_refs]
        if first:
            value = [value[0][:halo] + value[1][:halo]] + [v[halo:] for v in value[:2]] + value[2:]
        values.append(jnp.concatenate(value, axis=0) if len(value) > 1 else value[0])
    for rank in range(pieces):
        chosen = values[0]
        for s in range(1, pieces):
            chosen = jnp.where(me == (rank - s) % pieces, values[s], chosen)
        x_ref[:, rank * share : (rank + 1) * share] = chosen
    features = x_ref[...]
    mean = jnp.mean(features * features, axis=1, keepdims=True)
    normed = (features * lax.rsqrt(mean + 1e-06) * gain_ref[...]).astype(BF16)
    begin = 0 if first else halo + row
    normed_ref[begin : begin + read, :] = normed

    for low in range(0, channels, BLOCK):
        width = min(BLOCK, channels - low)
        part = slice(low, low + width)
        for s in (1, 2):
            if not first:
                p_ref[:halo, :width] = tail_in[s - 1, :, part]
            p_ref[halo + rows - read :, :width] = project(
                normed_ref[begin : begin + read, :], w_ref, s, part
            )
            tail_ref[s - 1, :, part] = p_ref[rows:, :width]
            short = short_conv(p_ref, short_ref, s, part, rows, taps)
            if s == 1:
                signal_ref[row : row + rows, part] = short
            else:
                signal_ref[row : row + rows, part] = signal_ref[row : row + rows, part] * short
        for start, size in lane_groups(low, width):
            lanes = slice(start, start + size)
            rate = [rows_as(rate_ref[n : n + 1, lanes], size) for n in range(modes)]
            decay = [jnp.exp(-r) for r in rate]

            def step(i, states):
                here = pl.ds(pl.multiple_of(row + i * ROWS, ROWS), ROWS)
                now = signal_ref[here, lanes]
                return tuple(states[n] * decay[n] + now for n in range(modes))

            if first:
                states = (jnp.zeros((ROWS, size), F32),) * modes
            else:
                states = tuple(states_in[n, :, lanes] for n in range(modes))
            states = lax.fori_loop(0, rows // ROWS, step, states, unroll=8)
            for n in range(modes):
                states_ref[n, :, lanes] = states[n]
            if last:
                left = lax.broadcasted_iota(jnp.int32, (ROWS, size), 0)
                left = ((ROWS - 1 - left) * length).astype(F32)
                for n in range(modes):
                    total_ref[n : n + 1, lanes] = jnp.sum(
                        states[n] * jnp.exp(-rate[n] * left), axis=0, keepdims=True
                    )


def local_stage(low, high, taps, *refs):
    normed_ref, signal_ref, states_ref, w_ref, short_ref, rate_ref, mode_ref, skip_ref = refs[:8]
    q_ref, local_ref, p_ref = refs[8:]
    modes = rate_ref.shape[0]
    rows = signal_ref.shape[0]
    length = rows // ROWS
    for at in range(low, high, BLOCK):
        width = min(BLOCK, high - at)
        part = slice(at, at + width)
        p_ref[:, :width] = project(normed_ref[...], w_ref, 0, part)
        q_ref[:, at - low : at - low + width] = short_conv(p_ref, short_ref, 0, part, rows, taps)
        for start, size in lane_groups(at, width):
            lanes = slice(start, start + size)
            there = slice(start - low, start - low + size)
            rate = [rows_as(rate_ref[n : n + 1, lanes], size) for n in range(modes)]
            decay = [jnp.exp(-r) for r in rate]
            mode = [rows_as(mode_ref[n : n + 1, lanes], size) for n in range(modes)]
            skip = rows_as(skip_ref[:, lanes], size)
            segment = lax.broadcasted_iota(jnp.int32, (ROWS, size), 0)
            states = []
            for n in range(modes):
                run = states_ref[n, :, lanes]
                for hop in (1, 2, 4):
                    weight = jnp.where(segment >= hop, jnp.exp(-rate[n] * (hop * length)), 0.0)
                    run = run + weight * pltpu.roll(run, hop, 0)
                states.append(jnp.where(segment >= 1, pltpu.roll(run, 1, 0), 0.0))

            half = (modes + 1) // 2
            for some in (range(half), range(half, modes)):

                def step(i, states):
                    here = pl.ds(pl.multiple_of(i * ROWS, ROWS), ROWS)
                    now = signal_ref[here, lanes]
                    states = [state * decay[n] + now for n, state in zip(some, states)]
                    rest = skip * now if some[0] == 0 else local_ref[here, there]
                    local_ref[here, there] = tree_sum(
                        [rest] + [mode[n] * state for n, state in zip(some, states)]
                    )
                    return tuple(states)

                lax.fori_loop(0, length, step, tuple(states[n] for n in some), unroll=8)


def second_stage(pieces, row, rows, bounds, *refs):
    count = len(bounds)
    me_ref = refs[0]
    q_refs, local_refs = refs[1 : 1 + count], refs[1 + count : 1 + 2 * count]
    carry_ref, rate_ref, mode_ref, w_ref = refs[1 + 2 * count : 5 + 2 * count]
    send_ref, own_ref, gated_ref = refs[5 + 2 * count :]
    modes = rate_ref.shape[0]
    length = q_refs[0].shape[0] // ROWS
    for (low, high), q_ref, local_ref in zip(bounds, q_refs, local_refs):
        for start, size in lane_groups(low, high - low):
            lanes = slice(start, start + size)
            there = slice(start - low, start - low + size)
            rate = [rows_as(rate_ref[n : n + 1, lanes], size) for n in range(modes)]
            decay = [jnp.exp(-r) for r in rate]
            segment = lax.broadcasted_iota(jnp.int32, (ROWS, size), 0)
            past = (segment * length + row // ROWS).astype(F32)
            states = tuple(
                jnp.exp(-rate[n] * past)
                * (mode_ref[n : n + 1, lanes] * carry_ref[n : n + 1, lanes])
                for n in range(modes)
            )

            def step(i, states):
                here = pl.ds(pl.multiple_of(i * ROWS, ROWS), ROWS)
                from_row = pl.ds(pl.multiple_of(row + i * ROWS, ROWS), ROWS)
                states = tuple(states[n] * decay[n] for n in range(modes))
                gated_ref[here, lanes] = q_ref[from_row, there] * tree_sum(
                    [local_ref[from_row, there]] + list(states)
                )
                return states

            lax.fori_loop(0, rows // ROWS, step, states, unroll=4)
    product = jnp.dot(gated_ref[...].astype(BF16), w_ref[...], preferred_element_type=F32)
    share = own_ref.shape[1]
    me = me_ref[0]
    columns = [product[:, rank * share : (rank + 1) * share] for rank in range(pieces)]
    for s in range(pieces):
        chosen = columns[0]
        for rank in range(1, pieces):
            chosen = jnp.where(me == (rank - s) % pieces, columns[rank], chosen)
        if s == 0:
            own_ref[...] = chosen
        else:
            send_ref[(s - 1) * rows : s * rows, :] = chosen.astype(BF16)


def last_stage(pieces, sizes, *refs):
    chunks = len(sizes)
    own_refs, came_refs = refs[:chunks], refs[chunks : chunks * pieces]
    out_ref, mixed_ref = refs[chunks * pieces :]
    row = 0
    for j, size in enumerate(sizes):
        total = own_refs[j][...]
        for s in range(pieces - 1):
            total = total + came_refs[j * (pieces - 1) + s][...].astype(F32)
        mixed_ref[row : row + size, :] = total.astype(BF16)
        row += size
    pick = token_picker(0, row, row)
    out_ref[...] = lax.dot_general(
        mixed_ref[...], pick, CONTRACT_FIRST, preferred_element_type=F32
    ).astype(BF16)


def call(kernel, name, scalars, operands, outs, scratch, flops, aliases={}):
    vmem = pl.BlockSpec(memory_space=pltpu.VMEM)
    smem = pl.BlockSpec(memory_space=pltpu.SMEM)
    size = lambda a: a.size * jnp.dtype(a.dtype).itemsize
    return pl.pallas_call(
        kernel,
        out_shape=outs,
        in_specs=[smem] * len(scalars) + [vmem] * len(operands),
        out_specs=[vmem] * len(outs),
        scratch_shapes=scratch,
        input_output_aliases=aliases,
        compiler_params=pltpu.CompilerParams(vmem_limit_bytes=VMEM_LIMIT),
        cost_estimate=pl.CostEstimate(
            flops=flops,
            bytes_accessed=sum(size(a) for a in operands),
            transcendentals=0,
        ),
        name=name,
    )(*scalars, *operands)


def in_vmem(w):
    streams, channels = w.shape[:2]
    parts = next(k for k in (4, 3, 2, 1) if channels % (16 * k) == 0 or k == 1)
    size = channels // parts
    places = [(s, slice(p * size, (p + 1) * size)) for s in range(streams) for p in range(parts)]
    return pl.pallas_call(
        functools.partial(load_weights, places),
        out_shape=pltpu.VMEM(w.shape, w.dtype),
        in_specs=[pl.BlockSpec(memory_space=pl.ANY)],
        out_specs=pl.BlockSpec(memory_space=pltpu.VMEM),
        scratch_shapes=[pltpu.SemaphoreType.DMA((len(places),))],
        compiler_params=pltpu.CompilerParams(vmem_limit_bytes=46 * 2**20),
        cost_estimate=pl.CostEstimate(
            flops=0, bytes_accessed=w.size * w.dtype.itemsize, transcendentals=0
        ),
        name="load_weights",
    )(w)


def run_signal(pieces, row, count, first, last, taps, place, tokens, before, gain, w_in, w_short, rate):
    streams, channels, features = w_in.shape
    modes = rate.shape[0]
    halo = ROWS * (taps - 1)
    read = sum(chunk[0].shape[0] for chunk in tokens) - (halo if first else 0)
    rows = read - halo if first else read
    outs = [
        jax.ShapeDtypeStruct((halo + count, features), BF16),
        jax.ShapeDtypeStruct((count, channels), F32),
        jax.ShapeDtypeStruct((modes, ROWS, channels), F32),
        jax.ShapeDtypeStruct((streams - 1, halo, channels), F32),
    ]
    if last:
        outs.append(jax.ShapeDtypeStruct((modes, channels), F32))
    inputs = 1 + len(tokens) * pieces
    return call(
        functools.partial(signal_stage, pieces, len(tokens), first, last, row, taps),
        "signal_stage",
        [place],
        [part for chunk in tokens for part in chunk] + list(before) + [gain, w_in, w_short, rate],
        outs,
        [
            pltpu.VMEM((read, features), F32),
            pltpu.VMEM((halo + rows, min(BLOCK, channels)), F32),
        ],
        4 * read * features * channels,
        aliases={} if first else {inputs: 0, inputs + 1: 1},
    )


def run_local(low, high, taps, normed, signal, states, w_in, w_short, rate, mode, skip):
    count = signal.shape[0]
    rows, features = normed.shape
    out = jax.ShapeDtypeStruct((count, high - low), F32)
    return call(
        functools.partial(local_stage, low, high, taps),
        "local_stage",
        [],
        [normed, signal, states, w_in, w_short, rate, mode, skip],
        [out, out],
        [pltpu.VMEM((rows, min(BLOCK, high - low)), F32)],
        2 * rows * features * (high - low),
    )


def run_second(pieces, row, rows, bounds, me, q, local, carry, rate, mode, w):
    channels, features = w.shape
    share = features // pieces
    return call(
        functools.partial(second_stage, pieces, row, rows, bounds),
        "second_stage",
        [me],
        [*q, *local, carry, rate, mode, w],
        [
            jax.ShapeDtypeStruct((max(1, pieces - 1) * rows, share), BF16),
            jax.ShapeDtypeStruct((rows, share), F32),
        ],
        [pltpu.VMEM((rows, channels), F32)],
        2 * features * channels * rows,
    )


def run_last(pieces, sizes, own, came):
    count, share = sum(sizes), own[0].shape[1]
    (out,) = call(
        functools.partial(last_stage, pieces, sizes),
        "last_stage",
        [],
        [*own, *came],
        [jax.ShapeDtypeStruct((share, count), BF16)],
        [pltpu.VMEM((count, share), BF16)],
        2 * count * count * share,
    )
    return out


def rotate(value, axis, steps):
    count = lax.axis_size(axis)
    return lax.ppermute(value, axis, [((i + steps) % count, i) for i in range(count)])


def combine_states(span, stride, radix, count, *refs):
    place_ref, rate_ref, total_ref = refs[:3]
    others = refs[3 : 2 + radix]
    refs = refs[2 + radix :]
    carry_in = refs[0] if stride > 1 else None
    carry_ref = refs[1] if stride > 1 else refs[0]
    position = place_ref[1]
    digit = lax.rem(lax.div(position, stride), radix)
    inner = lax.rem(position, stride)
    unit = span * stride
    rate = rate_ref[...]
    before = jnp.zeros(rate.shape, F32)
    for shift in range(1, radix):
        reached = jnp.where(digit >= shift, 1.0, 0.0)
        before = before + jnp.exp(-rate * (unit * (shift - 1))) * (others[shift - 1][...] * reached)
    if stride > 1:
        carry_ref[...] = carry_in[...] + jnp.exp(-rate * (span * inner).astype(F32)) * before
    else:
        carry_ref[...] = before
    if stride * radix < count:
        new = jnp.exp(-rate * (unit * (radix - 1 - digit)).astype(F32)) * total_ref[...]
        for shift in range(1, radix):
            at = lax.rem(digit - shift + radix, radix)
            weight = jnp.exp(-rate * (unit * (radix - 1 - at)).astype(F32))
            new = new + weight * others[shift - 1][...]
        refs[-1][...] = new


def carried_in(state, rate, span, axis, place, between):
    count = lax.axis_size(axis)
    total, stride, carry = state, 1, []
    while stride < count:
        radix = 4 if count % (stride * 4) == 0 else 2
        assert count % (stride * radix) == 0
        group = stride * radix
        others = []
        for shift in range(1, radix):
            pairs = []
            for i in range(count):
                digit = (i // stride) % radix
                pairs.append((i + ((digit - shift) % radix - digit) * stride, i))
            others.append(lax.ppermute(total, axis, pairs))
        others = between(others)
        shape = jax.ShapeDtypeStruct(state.shape, F32)
        carry = call(
            functools.partial(combine_states, span, stride, radix, count),
            "combine_states",
            [place],
            [rate, total, *others, *carry],
            [shape] * (2 if group < count else 1),
            [],
            0,
        )
        if group < count:
            *carry, total = carry
        stride = group
    return carry[0]


def body(tokens, norm_gain, w_in, w_short, decay_rate, residue, skip_gain, w_out):
    pieces, count = lax.axis_size("tp"), lax.axis_size("ctx")
    share, rows = tokens.shape
    channels = w_in.shape[1]
    taps = w_short.shape[0]
    halo = ROWS * (taps - 1)
    sizes = [rows // CHUNKS] * CHUNKS
    bf16_rows = lambda size: jax.ShapeDtypeStruct((size, share), BF16)

    x0, edge = call(
        functools.partial(first_rows, halo), "first_rows", [], [tokens],
        [bf16_rows(halo + sizes[0]), bf16_rows(halo)], [], 2 * (2 * halo + sizes[0]) * rows * share,
    )
    parts = [[x0] + [rotate(x0, "tp", s) for s in range(1, pieces)]]
    edge = rotate(edge, "ctx", -1)
    place = jnp.stack([lax.axis_index("tp"), lax.axis_index("ctx")]).astype(jnp.int32)
    mode = residue * jnp.sqrt(-jnp.expm1(-2.0 * decay_rate))
    gain = norm_gain[None, :]
    skip = skip_gain[None, :]
    tokens, edge, place, mode, gain, skip = lax.optimization_barrier(
        (tokens, edge, place, mode, gain, skip)
    )
    chunks = call(
        functools.partial(other_rows, halo), "other_rows", [place], [tokens, edge],
        [bf16_rows(halo + sizes[1])] + [bf16_rows(size) for size in sizes[2:]], [],
        2 * rows * rows * share,
    )
    parts += [[x] + [rotate(x, "tp", s) for s in range(1, pieces)] for x in chunks]
    w_in, chunks = lax.optimization_barrier((w_in, chunks))
    w_in = pltpu.with_memory_space_constraint(in_vmem(w_in), pltpu.VMEM)

    before, row = [], 0
    for group in [[0, 1]] + [[j] for j in range(2, CHUNKS)]:
        results = run_signal(
            pieces, row, rows, group[0] == 0, group[-1] == CHUNKS - 1, taps, place,
            [parts[j] for j in group], before, gain, w_in, w_short, decay_rate,
        )
        before = results[:4]
        row += sum(sizes[j] for j in group)
    normed, signal, states, _ = before
    state, normed, signal, states = lax.optimization_barrier((results[4], normed, signal, states))
    blocks = (channels + BLOCK - 1) // BLOCK
    middle = min(channels, (blocks + 1) // 2 * BLOCK)
    bounds = [b for b in ((0, middle), (middle, channels)) if b[0] < b[1]]
    done = []

    def between(others):
        if len(done) < len(bounds):
            q, local = run_local(
                *bounds[len(done)], taps, normed, signal, states, w_in, w_short, decay_rate, mode, skip
            )
            done.append((q, local))
            others, done[-1] = lax.optimization_barrier((others, done[-1]))
        return others

    carry = carried_in(state, decay_rate, rows, "ctx", place, between)
    while len(done) < len(bounds):
        between([])
    q, local = zip(*done)
    out_sizes = [rows // 4, rows // 2, rows // 4]
    own, came, row = [], [], 0
    for j, size in enumerate(out_sizes):
        if j == 2:
            carry, came[: pieces - 1] = lax.optimization_barrier((carry, came[: pieces - 1]))
        send, kept = run_second(
            pieces, row, size, bounds, place, q, local, carry, decay_rate, mode, w_out
        )
        own.append(kept)
        for s in range(1, pieces):
            came.append(rotate(send[(s - 1) * size : s * size], "tp", -s))
        row += size
    return run_last(pieces, out_sizes, own, came)


def solution(mesh):
    placed = (
        P("tp", "ctx"),
        P(),
        P(None, "tp", None),
        P(None, None, "tp"),
        P(None, "tp"),
        P(None, "tp"),
        P("tp"),
        P("tp", None),
    )
    return jax.shard_map(
        body, mesh=mesh, in_specs=placed, out_specs=P("tp", "ctx"), check_vma=False
    )
```

```python
import functools

import jax
import jax.numpy as jnp
from jax import lax
from jax.experimental import pallas as pl
from jax.experimental.pallas import tpu as pltpu
from jax.sharding import PartitionSpec as P


F32 = jnp.float32
BF16 = jnp.bfloat16
ROWS = 8
LANES = 128
BLOCK = 256
CHUNKS = 4
SPAN = 16
VMEM_LIMIT = 10 * 2**20
CONTRACT_LAST = (((1,), (1,)), ((), ()))
CONTRACT_FIRST = (((0,), (0,)), ((), ()))


def lane_groups(low, width):
    return [(start, min(LANES, low + width - start)) for start in range(low, low + width, LANES)]


def rows_as(row, width):
    return jnp.broadcast_to(row, (ROWS, width))


def tree_sum(terms):
    while len(terms) > 1:
        terms = [sum(terms[k + 1 : k + 2], terms[k]) for k in range(0, len(terms), 2)]
    return terms[0]


def token_picker(first_row, rows, tokens):
    length = tokens // ROWS
    row = lax.broadcasted_iota(jnp.int32, (rows, tokens), 0)
    column = lax.broadcasted_iota(jnp.int32, (rows, tokens), 1)
    wanted = lax.rem(row, ROWS) * length + lax.div(row, ROWS) + first_row // ROWS
    return jnp.where(column == wanted, 1.0, 0.0).astype(BF16)


def turned(pick, tokens):
    return lax.dot_general(pick, tokens, CONTRACT_LAST, preferred_element_type=F32).astype(BF16)


def first_rows(halo, tokens_ref, out_ref, edge_ref):
    tokens = tokens_ref.shape[1]
    out_ref[...] = turned(token_picker(-halo, out_ref.shape[0], tokens), tokens_ref[...])
    row = lax.broadcasted_iota(jnp.int32, (halo, tokens), 0)
    column = lax.broadcasted_iota(jnp.int32, (halo, tokens), 1)
    wanted = jnp.where(lax.rem(row, ROWS) == 0, tokens - halo // ROWS + lax.div(row, ROWS), -1)
    edge_ref[...] = turned(jnp.where(column == wanted, 1.0, 0.0).astype(BF16), tokens_ref[...])


def next_rows(row, tokens_ref, out_ref):
    rows, tokens = out_ref.shape[0], tokens_ref.shape[1]
    out_ref[...] = turned(token_picker(row, rows, tokens), tokens_ref[...])


def last_rows(halo, row, place_ref, tokens_ref, edge_ref, *chunk_refs):
    tokens = tokens_ref.shape[1]
    preceded = jnp.where(place_ref[1] > 0, 1.0, 0.0)
    for k, ref in enumerate(chunk_refs):
        front = 0
        if k == 0:
            front = halo
            ref[:halo, :] = (edge_ref[...].astype(F32) * preceded).astype(BF16)
        rows = ref.shape[0] - front
        ref[front:, :] = turned(token_picker(row, rows, tokens), tokens_ref[...])
        row += rows


def load_weights(places, w_hbm, w_ref, sem):
    copies = [
        pltpu.make_async_copy(w_hbm.at[place], w_ref.at[place], sem.at[k])
        for k, place in enumerate(places)
    ]
    for copy in copies:
        copy.start()
    for copy in copies:
        copy.wait()


def short_conv(p_ref, short_ref, s, part, rows, taps):
    width = part.stop - part.start
    total = None
    for offset in range(taps):
        start = ROWS * (taps - 1 - offset)
        term = short_ref[offset, s : s + 1, part] * p_ref[start : start + rows, :width]
        total = term if total is None else total + term
    return total


def project(normed, w_ref, s, part):
    product = lax.dot_general(normed, w_ref[s, part, :], CONTRACT_LAST, preferred_element_type=F32)
    return product.astype(BF16).astype(F32)


def signal_stage(pieces, chunks, first, last, row, taps, *refs):
    refs = list(refs)
    me_ref = refs.pop(0)
    token_refs = [[refs.pop(0) for _ in range(pieces)] for _ in range(chunks)]
    if not first:
        _, _, _, states_in, tail_in = [refs.pop(0) for _ in range(5)]
    gain_ref, w_ref, short_ref, rate_ref = refs[:4]
    normed_ref, signal_ref, marks_ref, states_ref, tail_ref = refs[4:9]
    total_ref = refs[9] if last else None
    x_ref, p_ref = refs[-2:]
    halo = ROWS * (taps - 1)
    modes, channels = rate_ref.shape
    read, share = x_ref.shape[0], token_refs[0][0].shape[1]
    rows = read - halo if first else read
    length = signal_ref.shape[0] // ROWS
    me = me_ref[0]

    values = []
    for s in range(pieces):
        value = [refs_of[s][...].astype(F32) for refs_of in token_refs]
        if first:
            front, edge = value[0][:halo], value[-1][:halo]
            value = [front + edge, value[0][halo:], *value[1:-1], value[-1][halo:]]
        values.append(jnp.concatenate(value, axis=0) if len(value) > 1 else value[0])
    for rank in range(pieces):
        chosen = values[0]
        for s in range(1, pieces):
            chosen = jnp.where(me == (rank - s) % pieces, values[s], chosen)
        x_ref[:, rank * share : (rank + 1) * share] = chosen
    features = x_ref[...]
    mean = jnp.mean(features * features, axis=1, keepdims=True)
    normed = (features * lax.rsqrt(mean + 1e-06) * gain_ref[...]).astype(BF16)
    begin = 0 if first else halo + row
    normed_ref[begin : begin + read, :] = normed

    for low in range(0, channels, BLOCK):
        width = min(BLOCK, channels - low)
        part = slice(low, low + width)
        for s in (1, 2):
            if not first:
                p_ref[:halo, :width] = tail_in[s - 1, :, part]
            p_ref[halo + rows - read :, :width] = project(
                normed_ref[begin : begin + read, :], w_ref, s, part
            )
            tail_ref[s - 1, :, part] = p_ref[rows:, :width]
            short = short_conv(p_ref, short_ref, s, part, rows, taps)
            if s == 1:
                signal_ref[row : row + rows, part] = short
            else:
                signal_ref[row : row + rows, part] = signal_ref[row : row + rows, part] * short
        for start, size in lane_groups(low, width):
            lanes = slice(start, start + size)
            rate = [rows_as(rate_ref[n : n + 1, lanes], size) for n in range(modes)]
            decay = [jnp.exp(-r) for r in rate]

            if first:
                states = (jnp.zeros((ROWS, size), F32),) * modes
            else:
                states = tuple(states_in[n, :, lanes] for n in range(modes))
            for at in range(row, row + rows, SPAN * ROWS):
                mark = at // (SPAN * ROWS)
                for n in range(modes):
                    marks_ref[mark, n, :, lanes] = states[n]

                def step(i, states):
                    here = pl.ds(pl.multiple_of(at + i * ROWS, ROWS), ROWS)
                    now = signal_ref[here, lanes]
                    return tuple(states[n] * decay[n] + now for n in range(modes))

                states = lax.fori_loop(0, SPAN, step, states, unroll=8)
            for n in range(modes):
                states_ref[n, :, lanes] = states[n]
            if last:
                left = lax.broadcasted_iota(jnp.int32, (ROWS, size), 0)
                left = ((ROWS - 1 - left) * length).astype(F32)
                for n in range(modes):
                    total_ref[n : n + 1, lanes] = jnp.sum(
                        states[n] * jnp.exp(-rate[n] * left), axis=0, keepdims=True
                    )


def local_stage(low, high, taps, *refs):
    normed_ref, signal_ref, states_ref, w_ref, short_ref, rate_ref, mode_ref, skip_ref = refs[:8]
    q_ref, local_ref, begin_ref, p_ref = refs[8:]
    modes = rate_ref.shape[0]
    rows = signal_ref.shape[0]
    length = rows // ROWS
    for at in range(low, high, BLOCK):
        width = min(BLOCK, high - at)
        part = slice(at, at + width)
        p_ref[:, :width] = project(normed_ref[...], w_ref, 0, part)
        q_ref[:, at - low : at - low + width] = short_conv(p_ref, short_ref, 0, part, rows, taps)
        for start, size in lane_groups(at, width):
            lanes = slice(start, start + size)
            there = slice(start - low, start - low + size)
            rate = [rows_as(rate_ref[n : n + 1, lanes], size) for n in range(modes)]
            segment = lax.broadcasted_iota(jnp.int32, (ROWS, size), 0)
            for n in range(modes):
                run = states_ref[n, :, lanes]
                for hop in (1, 2, 4):
                    weight = jnp.where(segment >= hop, jnp.exp(-rate[n] * (hop * length)), 0.0)
                    run = run + weight * pltpu.roll(run, hop, 0)
                begin_ref[n, :, there] = jnp.where(segment >= 1, pltpu.roll(run, 1, 0), 0.0)
            lag = segment.astype(F32)
            filters = []
            for first_lag in range(0, SPAN, ROWS):
                values = tree_sum(
                    [
                        rows_as(mode_ref[n : n + 1, lanes], size)
                        * jnp.exp(-rate[n] * (lag + first_lag))
                        for n in range(modes)
                    ]
                )
                filters += [rows_as(values[j : j + 1, :], size) for j in range(ROWS)]
            filters[0] = filters[0] + skip_ref[:, lanes]

            def span(i, carry):
                base = i * (SPAN * ROWS)
                here = [
                    pl.ds(pl.multiple_of(base + k * ROWS, ROWS), ROWS) for k in range(SPAN)
                ]
                now = [signal_ref[place, lanes] for place in here]
                for k in range(SPAN):
                    local_ref[here[k], there] = tree_sum(
                        [filters[j] * now[k - j] for j in range(k + 1)]
                    )
                return carry

            lax.fori_loop(0, length // SPAN, span, 0)


def second_stage(pieces, row, rows, bounds, *refs):
    count = len(bounds)
    me_ref = refs[0]
    q_refs, local_refs, begin_refs = [refs[1 + k * count : 1 + (k + 1) * count] for k in range(3)]
    refs = refs[1 + 3 * count :]
    marks_ref, carry_ref, rate_ref, mode_ref, w_ref, send_ref, own_ref, gated_ref = refs
    modes = rate_ref.shape[0]
    length = q_refs[0].shape[0] // ROWS
    for (low, high), q_ref, local_ref, begin_ref in zip(bounds, q_refs, local_refs, begin_refs):
        for start, size in lane_groups(low, high - low):
            lanes = slice(start, start + size)
            there = slice(start - low, start - low + size)
            rate = [rows_as(rate_ref[n : n + 1, lanes], size) for n in range(modes)]
            decay = [jnp.exp(-r) for r in rate]
            segment = lax.broadcasted_iota(jnp.int32, (ROWS, size), 0)
            past = (segment * length).astype(F32)
            for at in range(row, row + rows, SPAN * ROWS):
                mark = at // (SPAN * ROWS)
                states = []
                for n in range(modes):
                    state = begin_ref[n, :, there] + jnp.exp(-rate[n] * past) * carry_ref[
                        n : n + 1, lanes
                    ]
                    if mark > 0:
                        state = marks_ref[mark, n, :, lanes] + state * jnp.exp(
                            -rate[n] * (SPAN * mark)
                        )
                    states.append(mode_ref[n : n + 1, lanes] * state)

                def step(i, states):
                    here = pl.ds(pl.multiple_of(at - row + i * ROWS, ROWS), ROWS)
                    from_row = pl.ds(pl.multiple_of(at + i * ROWS, ROWS), ROWS)
                    states = tuple(states[n] * decay[n] for n in range(modes))
                    gated_ref[here, lanes] = q_ref[from_row, there] * tree_sum(
                        [local_ref[from_row, there]] + list(states)
                    )
                    return states

                lax.fori_loop(0, SPAN, step, tuple(states), unroll=4)
    product = jnp.dot(gated_ref[...].astype(BF16), w_ref[...], preferred_element_type=F32)
    share = own_ref.shape[1]
    me = me_ref[0]
    columns = [product[:, rank * share : (rank + 1) * share] for rank in range(pieces)]
    for s in range(pieces):
        chosen = columns[0]
        for rank in range(1, pieces):
            chosen = jnp.where(me == (rank - s) % pieces, columns[rank], chosen)
        if s == 0:
            own_ref[...] = chosen
        else:
            send_ref[(s - 1) * rows : s * rows, :] = chosen.astype(BF16)


def last_stage(pieces, sizes, *refs):
    chunks = len(sizes)
    own_refs, came_refs = refs[:chunks], refs[chunks : chunks * pieces]
    out_ref, mixed_ref = refs[chunks * pieces :]
    row = 0
    for j, size in enumerate(sizes):
        total = own_refs[j][...]
        for s in range(pieces - 1):
            total = total + came_refs[j * (pieces - 1) + s][...].astype(F32)
        mixed_ref[row : row + size, :] = total.astype(BF16)
        row += size
    pick = token_picker(0, row, row)
    out_ref[...] = lax.dot_general(
        mixed_ref[...], pick, CONTRACT_FIRST, preferred_element_type=F32
    ).astype(BF16)


def call(kernel, name, scalars, operands, outs, scratch, flops, aliases={}):
    vmem = pl.BlockSpec(memory_space=pltpu.VMEM)
    smem = pl.BlockSpec(memory_space=pltpu.SMEM)
    size = lambda a: a.size * jnp.dtype(a.dtype).itemsize
    return pl.pallas_call(
        kernel,
        out_shape=outs,
        in_specs=[smem] * len(scalars) + [vmem] * len(operands),
        out_specs=[vmem] * len(outs),
        scratch_shapes=scratch,
        input_output_aliases=aliases,
        compiler_params=pltpu.CompilerParams(vmem_limit_bytes=VMEM_LIMIT),
        cost_estimate=pl.CostEstimate(
            flops=flops,
            bytes_accessed=sum(size(a) for a in operands),
            transcendentals=0,
        ),
        name=name,
    )(*scalars, *operands)


def in_vmem(w):
    streams, channels = w.shape[:2]
    parts = next(k for k in (4, 3, 2, 1) if channels % (16 * k) == 0 or k == 1)
    size = channels // parts
    places = [(s, slice(p * size, (p + 1) * size)) for s in range(streams) for p in range(parts)]
    return pl.pallas_call(
        functools.partial(load_weights, places),
        out_shape=pltpu.VMEM(w.shape, w.dtype),
        in_specs=[pl.BlockSpec(memory_space=pl.ANY)],
        out_specs=pl.BlockSpec(memory_space=pltpu.VMEM),
        scratch_shapes=[pltpu.SemaphoreType.DMA((len(places),))],
        compiler_params=pltpu.CompilerParams(vmem_limit_bytes=46 * 2**20),
        cost_estimate=pl.CostEstimate(
            flops=0, bytes_accessed=w.size * w.dtype.itemsize, transcendentals=0
        ),
        name="load_weights",
    )(w)


def run_signal(pieces, row, count, first, last, taps, place, tokens, before, gain, w_in, w_short, rate):
    streams, channels, features = w_in.shape
    modes = rate.shape[0]
    halo = ROWS * (taps - 1)
    read = sum(chunk[0].shape[0] for chunk in tokens) - (halo if first else 0)
    rows = read - halo if first else read
    outs = [
        jax.ShapeDtypeStruct((halo + count, features), BF16),
        jax.ShapeDtypeStruct((count, channels), F32),
        jax.ShapeDtypeStruct((count // (SPAN * ROWS), modes, ROWS, channels), F32),
        jax.ShapeDtypeStruct((modes, ROWS, channels), F32),
        jax.ShapeDtypeStruct((streams - 1, halo, channels), F32),
    ]
    if last:
        outs.append(jax.ShapeDtypeStruct((modes, channels), F32))
    inputs = 1 + len(tokens) * pieces
    return call(
        functools.partial(signal_stage, pieces, len(tokens), first, last, row, taps),
        "signal_stage",
        [place],
        [part for chunk in tokens for part in chunk] + list(before) + [gain, w_in, w_short, rate],
        outs,
        [
            pltpu.VMEM((read, features), F32),
            pltpu.VMEM((halo + rows, min(BLOCK, channels)), F32),
        ],
        4 * read * features * channels,
        aliases={} if first else {inputs + k: k for k in range(3)},
    )


def run_local(low, high, taps, normed, signal, states, w_in, w_short, rate, mode, skip):
    count = signal.shape[0]
    rows, features = normed.shape
    modes = rate.shape[0]
    out = jax.ShapeDtypeStruct((count, high - low), F32)
    return call(
        functools.partial(local_stage, low, high, taps),
        "local_stage",
        [],
        [normed, signal, states, w_in, w_short, rate, mode, skip],
        [out, out, jax.ShapeDtypeStruct((modes, ROWS, high - low), F32)],
        [pltpu.VMEM((rows, min(BLOCK, high - low)), F32)],
        2 * rows * features * (high - low),
    )


def run_second(pieces, row, rows, bounds, place, done, marks, carry, rate, mode, w):
    channels, features = w.shape
    share = features // pieces
    return call(
        functools.partial(second_stage, pieces, row, rows, bounds),
        "second_stage",
        [place],
        [array for kind in zip(*done) for array in kind] + [marks, carry, rate, mode, w],
        [
            jax.ShapeDtypeStruct((max(1, pieces - 1) * rows, share), BF16),
            jax.ShapeDtypeStruct((rows, share), F32),
        ],
        [pltpu.VMEM((rows, channels), F32)],
        2 * features * channels * rows,
    )


def run_last(pieces, sizes, own, came):
    count, share = sum(sizes), own[0].shape[1]
    (out,) = call(
        functools.partial(last_stage, pieces, sizes),
        "last_stage",
        [],
        [*own, *came],
        [jax.ShapeDtypeStruct((share, count), BF16)],
        [pltpu.VMEM((count, share), BF16)],
        2 * count * count * share,
    )
    return out


def rotate(value, axis, steps):
    count = lax.axis_size(axis)
    return lax.ppermute(value, axis, [((i + steps) % count, i) for i in range(count)])


def combine_states(span, stride, radix, count, *refs):
    place_ref, rate_ref, total_ref = refs[:3]
    others = refs[3 : 2 + radix]
    refs = refs[2 + radix :]
    carry_in = refs[0] if stride > 1 else None
    carry_ref = refs[1] if stride > 1 else refs[0]
    position = place_ref[1]
    digit = lax.rem(lax.div(position, stride), radix)
    inner = lax.rem(position, stride)
    unit = span * stride
    rate = rate_ref[...]
    before = jnp.zeros(rate.shape, F32)
    for shift in range(1, radix):
        reached = jnp.where(digit >= shift, 1.0, 0.0)
        before = before + jnp.exp(-rate * (unit * (shift - 1))) * (others[shift - 1][...] * reached)
    if stride > 1:
        carry_ref[...] = carry_in[...] + jnp.exp(-rate * (span * inner).astype(F32)) * before
    else:
        carry_ref[...] = before
    if stride * radix < count:
        new = jnp.exp(-rate * (unit * (radix - 1 - digit)).astype(F32)) * total_ref[...]
        for shift in range(1, radix):
            at = lax.rem(digit - shift + radix, radix)
            weight = jnp.exp(-rate * (unit * (radix - 1 - at)).astype(F32))
            new = new + weight * others[shift - 1][...]
        refs[-1][...] = new


def carried_in(state, rate, span, axis, place, between):
    count = lax.axis_size(axis)
    total, stride, carry = state, 1, []
    while stride < count:
        radix = 4 if count % (stride * 4) == 0 else 2
        assert count % (stride * radix) == 0
        group = stride * radix
        others = []
        for shift in range(1, radix):
            pairs = []
            for i in range(count):
                digit = (i // stride) % radix
                pairs.append((i + ((digit - shift) % radix - digit) * stride, i))
            others.append(lax.ppermute(total, axis, pairs))
        others = between(others)
        shape = jax.ShapeDtypeStruct(state.shape, F32)
        carry = call(
            functools.partial(combine_states, span, stride, radix, count),
            "combine_states",
            [place],
            [rate, total, *others, *carry],
            [shape] * (2 if group < count else 1),
            [],
            0,
        )
        if group < count:
            *carry, total = carry
        stride = group
    return carry[0]


def body(tokens, norm_gain, w_in, w_short, decay_rate, residue, skip_gain, w_out):
    pieces, count = lax.axis_size("tp"), lax.axis_size("ctx")
    share, rows = tokens.shape
    channels = w_in.shape[1]
    taps = w_short.shape[0]
    halo = ROWS * (taps - 1)
    sizes = [rows // CHUNKS] * CHUNKS
    bf16_rows = lambda size: jax.ShapeDtypeStruct((size, share), BF16)

    place = jnp.stack([lax.axis_index("tp"), lax.axis_index("ctx")]).astype(jnp.int32)
    tokens, place = lax.optimization_barrier((tokens, place))
    x0, edge = call(
        functools.partial(first_rows, halo), "first_rows", [], [tokens],
        [bf16_rows(halo + sizes[0]), bf16_rows(halo)], [], 2 * (2 * halo + sizes[0]) * rows * share,
    )
    x = [x0]
    edge = rotate(edge, "ctx", -1)
    for j in range(1, CHUNKS - 2):
        x += call(
            functools.partial(next_rows, sum(sizes[:j])), "next_rows", [], [tokens],
            [bf16_rows(sizes[j])], [], 2 * sizes[j] * rows * share,
        )
    mode = residue * jnp.sqrt(-jnp.expm1(-2.0 * decay_rate))
    gain = norm_gain[None, :]
    skip = skip_gain[None, :]
    edge, mode, gain, skip, *_ = lax.optimization_barrier((edge, mode, gain, skip, *x))
    x += call(
        functools.partial(last_rows, halo, sum(sizes[:-2])), "last_rows", [place], [tokens, edge],
        [bf16_rows(halo + sizes[-2]), bf16_rows(sizes[-1])], [],
        2 * (sizes[-2] + sizes[-1]) * rows * share,
    )
    parts = [[part] + [rotate(part, "tp", s) for s in range(1, pieces)] for part in x]
    w_in, *_ = lax.optimization_barrier((w_in, *x))
    w_in = pltpu.with_memory_space_constraint(in_vmem(w_in), pltpu.VMEM)

    before, row = [], 0
    for group in [list(range(CHUNKS - 1)), [CHUNKS - 1]]:
        results = run_signal(
            pieces, row, rows, group[0] == 0, group[-1] == CHUNKS - 1, taps, place,
            [parts[j] for j in group], before, gain, w_in, w_short, decay_rate,
        )
        before = results[:5]
        row += sum(sizes[j] for j in group)
    normed, signal, marks, states, _ = before
    state, normed, signal, states = lax.optimization_barrier((results[5], normed, signal, states))
    blocks = (channels + BLOCK - 1) // BLOCK
    middle = min(channels, (blocks + 1) // 2 * BLOCK)
    bounds = [b for b in ((0, middle), (middle, channels)) if b[0] < b[1]]
    done = []

    def between(others):
        if len(done) < len(bounds):
            done.append(
                run_local(
                    *bounds[len(done)], taps, normed, signal, states, w_in, w_short, decay_rate,
                    mode, skip,
                )
            )
            others, done[-1] = lax.optimization_barrier((others, done[-1]))
        return others

    carry = carried_in(state, decay_rate, rows, "ctx", place, between)
    while len(done) < len(bounds):
        between([])
    out_sizes = [rows // 4, rows // 2, rows // 4]
    own, came, row = [], [], 0
    for j, size in enumerate(out_sizes):
        if j == 2:
            carry, came[: pieces - 1] = lax.optimization_barrier((carry, came[: pieces - 1]))
        send, kept = run_second(
            pieces, row, size, bounds, place, done, marks, carry, decay_rate, mode, w_out
        )
        own.append(kept)
        for s in range(1, pieces):
            came.append(rotate(send[(s - 1) * size : s * size], "tp", -s))
        row += size
    return run_last(pieces, out_sizes, own, came)


def solution(mesh):
    placed = (
        P("tp", "ctx"),
        P(),
        P(None, "tp", None),
        P(None, None, "tp"),
        P(None, "tp"),
        P(None, "tp"),
        P("tp"),
        P("tp", None),
    )
    return jax.shard_map(
        body, mesh=mesh, in_specs=placed, out_specs=P("tp", "ctx"), check_vma=False
    )
```

```python
import functools

import jax
import jax.numpy as jnp
from jax import lax
from jax.experimental import pallas as pl
from jax.experimental.pallas import tpu as pltpu
from jax.sharding import PartitionSpec as P


F32 = jnp.float32
BF16 = jnp.bfloat16
ROWS = 8
LANES = 128
BLOCK = 256
CHUNKS = 4
SPAN = 16
VMEM_LIMIT = 10 * 2**20
CONTRACT_LAST = (((1,), (1,)), ((), ()))
CONTRACT_FIRST = (((0,), (0,)), ((), ()))


def lane_groups(low, width):
    return [(start, min(LANES, low + width - start)) for start in range(low, low + width, LANES)]


def rows_as(row, width):
    return jnp.broadcast_to(row, (ROWS, width))


def tree_sum(terms):
    while len(terms) > 1:
        terms = [sum(terms[k + 1 : k + 2], terms[k]) for k in range(0, len(terms), 2)]
    return terms[0]


def token_picker(first_row, rows, tokens):
    length = tokens // ROWS
    row = lax.broadcasted_iota(jnp.int32, (rows, tokens), 0)
    column = lax.broadcasted_iota(jnp.int32, (rows, tokens), 1)
    wanted = lax.rem(row, ROWS) * length + lax.div(row, ROWS) + first_row // ROWS
    return jnp.where(column == wanted, 1.0, 0.0).astype(BF16)


def turned(pick, tokens):
    return lax.dot_general(pick, tokens, CONTRACT_LAST, preferred_element_type=F32).astype(BF16)


def first_rows(halo, tokens_ref, out_ref, edge_ref):
    tokens = tokens_ref.shape[1]
    out_ref[...] = turned(token_picker(-halo, out_ref.shape[0], tokens), tokens_ref[...])
    row = lax.broadcasted_iota(jnp.int32, (halo, tokens), 0)
    column = lax.broadcasted_iota(jnp.int32, (halo, tokens), 1)
    wanted = jnp.where(lax.rem(row, ROWS) == 0, tokens - halo // ROWS + lax.div(row, ROWS), -1)
    edge_ref[...] = turned(jnp.where(column == wanted, 1.0, 0.0).astype(BF16), tokens_ref[...])


def next_rows(row, tokens_ref, *chunk_refs):
    tokens = tokens_ref.shape[1]
    for ref in chunk_refs:
        ref[...] = turned(token_picker(row, ref.shape[0], tokens), tokens_ref[...])
        row += ref.shape[0]


def join_edge(place_ref, edge_ref, chunk_ref, out_ref):
    halo = edge_ref.shape[0]
    preceded = jnp.where(place_ref[1] > 0, 1.0, 0.0)
    out_ref[:halo, :] = (edge_ref[...].astype(F32) * preceded).astype(BF16)
    out_ref[halo:, :] = chunk_ref[...]


def load_weights(places, w_hbm, w_ref, sem):
    copies = [
        pltpu.make_async_copy(w_hbm.at[place], w_ref.at[place], sem.at[k])
        for k, place in enumerate(places)
    ]
    for copy in copies:
        copy.start()
    for copy in copies:
        copy.wait()


def short_conv(p_ref, short_ref, s, part, rows, taps):
    width = part.stop - part.start
    total = None
    for offset in range(taps):
        start = ROWS * (taps - 1 - offset)
        term = short_ref[offset, s : s + 1, part] * p_ref[start : start + rows, :width]
        total = term if total is None else total + term
    return total


def project(normed, w_ref, s, part):
    product = lax.dot_general(normed, w_ref[s, part, :], CONTRACT_LAST, preferred_element_type=F32)
    return product.astype(BF16).astype(F32)


def signal_stage(pieces, chunks, first, last, row, taps, *refs):
    refs = list(refs)
    me_ref = refs.pop(0)
    token_refs = [[refs.pop(0) for _ in range(pieces)] for _ in range(chunks)]
    if not first:
        _, _, _, states_in, tail_in = [refs.pop(0) for _ in range(5)]
    gain_ref, w_ref, short_ref, rate_ref = refs[:4]
    normed_ref, signal_ref, marks_ref, states_ref, tail_ref = refs[4:9]
    total_ref = refs[9] if last else None
    x_ref, p_ref = refs[-2:]
    halo = ROWS * (taps - 1)
    modes, channels = rate_ref.shape
    read, share = x_ref.shape[0], token_refs[0][0].shape[1]
    rows = read - halo if first else read
    length = signal_ref.shape[0] // ROWS
    me = me_ref[0]

    values = []
    for s in range(pieces):
        value = [refs_of[s][...].astype(F32) for refs_of in token_refs]
        if first:
            front, edge = value[0][:halo], value[-1][:halo]
            value = [front + edge, value[0][halo:], *value[1:-1], value[-1][halo:]]
        values.append(jnp.concatenate(value, axis=0) if len(value) > 1 else value[0])
    for rank in range(pieces):
        chosen = values[0]
        for s in range(1, pieces):
            chosen = jnp.where(me == (rank - s) % pieces, values[s], chosen)
        x_ref[:, rank * share : (rank + 1) * share] = chosen
    features = x_ref[...]
    mean = jnp.mean(features * features, axis=1, keepdims=True)
    normed = (features * lax.rsqrt(mean + 1e-06) * gain_ref[...]).astype(BF16)
    begin = 0 if first else halo + row
    normed_ref[begin : begin + read, :] = normed

    for low in range(0, channels, BLOCK):
        width = min(BLOCK, channels - low)
        part = slice(low, low + width)
        for s in (1, 2):
            if not first:
                p_ref[:halo, :width] = tail_in[s - 1, :, part]
            p_ref[halo + rows - read :, :width] = project(
                normed_ref[begin : begin + read, :], w_ref, s, part
            )
            tail_ref[s - 1, :, part] = p_ref[rows:, :width]
            short = short_conv(p_ref, short_ref, s, part, rows, taps)
            if s == 1:
                signal_ref[row : row + rows, part] = short
            else:
                signal_ref[row : row + rows, part] = signal_ref[row : row + rows, part] * short
        for start, size in lane_groups(low, width):
            lanes = slice(start, start + size)
            rate = [rows_as(rate_ref[n : n + 1, lanes], size) for n in range(modes)]
            decay = [jnp.exp(-r) for r in rate]

            if first:
                states = (jnp.zeros((ROWS, size), F32),) * modes
            else:
                states = tuple(states_in[n, :, lanes] for n in range(modes))
            for at in range(row, row + rows, SPAN * ROWS):
                mark = at // (SPAN * ROWS)
                for n in range(modes):
                    marks_ref[mark, n, :, lanes] = states[n]

                def step(i, states):
                    here = pl.ds(pl.multiple_of(at + i * ROWS, ROWS), ROWS)
                    now = signal_ref[here, lanes]
                    return tuple(states[n] * decay[n] + now for n in range(modes))

                states = lax.fori_loop(0, SPAN, step, states, unroll=8)
            for n in range(modes):
                states_ref[n, :, lanes] = states[n]
            if last:
                left = lax.broadcasted_iota(jnp.int32, (ROWS, size), 0)
                left = ((ROWS - 1 - left) * length).astype(F32)
                for n in range(modes):
                    total_ref[n : n + 1, lanes] = jnp.sum(
                        states[n] * jnp.exp(-rate[n] * left), axis=0, keepdims=True
                    )


def local_stage(low, high, taps, *refs):
    normed_ref, signal_ref, states_ref, w_ref, short_ref, rate_ref, mode_ref, skip_ref = refs[:8]
    q_ref, local_ref, begin_ref, p_ref = refs[8:]
    modes = rate_ref.shape[0]
    rows = signal_ref.shape[0]
    length = rows // ROWS
    for at in range(low, high, BLOCK):
        width = min(BLOCK, high - at)
        part = slice(at, at + width)
        p_ref[:, :width] = project(normed_ref[...], w_ref, 0, part)
        q_ref[:, at - low : at - low + width] = short_conv(p_ref, short_ref, 0, part, rows, taps)
        for start, size in lane_groups(at, width):
            lanes = slice(start, start + size)
            there = slice(start - low, start - low + size)
            rate = [rows_as(rate_ref[n : n + 1, lanes], size) for n in range(modes)]
            segment = lax.broadcasted_iota(jnp.int32, (ROWS, size), 0)
            for n in range(modes):
                run = states_ref[n, :, lanes]
                for hop in (1, 2, 4):
                    weight = jnp.where(segment >= hop, jnp.exp(-rate[n] * (hop * length)), 0.0)
                    run = run + weight * pltpu.roll(run, hop, 0)
                begin_ref[n, :, there] = jnp.where(segment >= 1, pltpu.roll(run, 1, 0), 0.0)
            lag = segment.astype(F32)
            filters = []
            for first_lag in range(0, SPAN, ROWS):
                values = tree_sum(
                    [
                        rows_as(mode_ref[n : n + 1, lanes], size)
                        * jnp.exp(-rate[n] * (lag + first_lag))
                        for n in range(modes)
                    ]
                )
                filters += [rows_as(values[j : j + 1, :], size) for j in range(ROWS)]
            filters[0] = filters[0] + skip_ref[:, lanes]

            def span(i, carry):
                base = i * (SPAN * ROWS)
                here = [
                    pl.ds(pl.multiple_of(base + k * ROWS, ROWS), ROWS) for k in range(SPAN)
                ]
                now = [signal_ref[place, lanes] for place in here]
                for k in range(SPAN):
                    local_ref[here[k], there] = tree_sum(
                        [filters[j] * now[k - j] for j in range(k + 1)]
                    )
                return carry

            lax.fori_loop(0, length // SPAN, span, 0)


def second_stage(pieces, row, rows, bounds, *refs):
    count = len(bounds)
    me_ref = refs[0]
    q_refs, local_refs, begin_refs = [refs[1 + k * count : 1 + (k + 1) * count] for k in range(3)]
    refs = refs[1 + 3 * count :]
    marks_ref, carry_ref, rate_ref, mode_ref, w_ref, send_ref, own_ref, gated_ref = refs
    modes = rate_ref.shape[0]
    length = q_refs[0].shape[0] // ROWS
    for (low, high), q_ref, local_ref, begin_ref in zip(bounds, q_refs, local_refs, begin_refs):
        for start, size in lane_groups(low, high - low):
            lanes = slice(start, start + size)
            there = slice(start - low, start - low + size)
            rate = [rows_as(rate_ref[n : n + 1, lanes], size) for n in range(modes)]
            decay = [jnp.exp(-r) for r in rate]
            segment = lax.broadcasted_iota(jnp.int32, (ROWS, size), 0)
            past = (segment * length).astype(F32)
            for at in range(row, row + rows, SPAN * ROWS):
                mark = at // (SPAN * ROWS)
                states = []
                for n in range(modes):
                    state = begin_ref[n, :, there] + jnp.exp(-rate[n] * past) * carry_ref[
                        n : n + 1, lanes
                    ]
                    if mark > 0:
                        state = marks_ref[mark, n, :, lanes] + state * jnp.exp(
                            -rate[n] * (SPAN * mark)
                        )
                    states.append(mode_ref[n : n + 1, lanes] * state)

                def step(i, states):
                    here = pl.ds(pl.multiple_of(at - row + i * ROWS, ROWS), ROWS)
                    from_row = pl.ds(pl.multiple_of(at + i * ROWS, ROWS), ROWS)
                    states = tuple(states[n] * decay[n] for n in range(modes))
                    gated_ref[here, lanes] = q_ref[from_row, there] * tree_sum(
                        [local_ref[from_row, there]] + list(states)
                    )
                    return states

                lax.fori_loop(0, SPAN, step, tuple(states), unroll=4)
    product = jnp.dot(gated_ref[...].astype(BF16), w_ref[...], preferred_element_type=F32)
    share = own_ref.shape[1]
    me = me_ref[0]
    columns = [product[:, rank * share : (rank + 1) * share] for rank in range(pieces)]
    for s in range(pieces):
        chosen = columns[0]
        for rank in range(1, pieces):
            chosen = jnp.where(me == (rank - s) % pieces, columns[rank], chosen)
        if s == 0:
            own_ref[...] = chosen
        else:
            send_ref[(s - 1) * rows : s * rows, :] = chosen.astype(BF16)


def last_stage(pieces, sizes, row, more, *refs):
    chunks = len(sizes)
    own_refs, came_refs = refs[:chunks], refs[chunks : chunks * pieces]
    done_ref = refs[chunks * pieces] if more else None
    out_ref, mixed_ref = refs[-2:]
    at = 0
    for j, size in enumerate(sizes):
        total = own_refs[j][...]
        for s in range(pieces - 1):
            total = total + came_refs[j * (pieces - 1) + s][...].astype(F32)
        mixed_ref[at : at + size, :] = total.astype(BF16)
        at += size
    pick = token_picker(row, at, out_ref.shape[1])
    out = lax.dot_general(mixed_ref[...], pick, CONTRACT_FIRST, preferred_element_type=F32)
    if more:
        out = out + done_ref[...]
    out_ref[...] = out.astype(out_ref.dtype)


def call(kernel, name, scalars, operands, outs, scratch, flops, aliases={}):
    vmem = pl.BlockSpec(memory_space=pltpu.VMEM)
    smem = pl.BlockSpec(memory_space=pltpu.SMEM)
    size = lambda a: a.size * jnp.dtype(a.dtype).itemsize
    return pl.pallas_call(
        kernel,
        out_shape=outs,
        in_specs=[smem] * len(scalars) + [vmem] * len(operands),
        out_specs=[vmem] * len(outs),
        scratch_shapes=scratch,
        input_output_aliases=aliases,
        compiler_params=pltpu.CompilerParams(vmem_limit_bytes=VMEM_LIMIT),
        cost_estimate=pl.CostEstimate(
            flops=flops,
            bytes_accessed=sum(size(a) for a in operands),
            transcendentals=0,
        ),
        name=name,
    )(*scalars, *operands)


def in_vmem(w):
    streams, channels = w.shape[:2]
    parts = next(k for k in (4, 3, 2, 1) if channels % (16 * k) == 0 or k == 1)
    size = channels // parts
    places = [(s, slice(p * size, (p + 1) * size)) for s in range(streams) for p in range(parts)]
    return pl.pallas_call(
        functools.partial(load_weights, places),
        out_shape=pltpu.VMEM(w.shape, w.dtype),
        in_specs=[pl.BlockSpec(memory_space=pl.ANY)],
        out_specs=pl.BlockSpec(memory_space=pltpu.VMEM),
        scratch_shapes=[pltpu.SemaphoreType.DMA((len(places),))],
        compiler_params=pltpu.CompilerParams(vmem_limit_bytes=46 * 2**20),
        cost_estimate=pl.CostEstimate(
            flops=0, bytes_accessed=w.size * w.dtype.itemsize, transcendentals=0
        ),
        name="load_weights",
    )(w)


def run_signal(pieces, row, count, first, last, taps, place, tokens, before, gain, w_in, w_short, rate):
    streams, channels, features = w_in.shape
    modes = rate.shape[0]
    halo = ROWS * (taps - 1)
    read = sum(chunk[0].shape[0] for chunk in tokens) - (halo if first else 0)
    rows = read - halo if first else read
    outs = [
        jax.ShapeDtypeStruct((halo + count, features), BF16),
        jax.ShapeDtypeStruct((count, channels), F32),
        jax.ShapeDtypeStruct((count // (SPAN * ROWS), modes, ROWS, channels), F32),
        jax.ShapeDtypeStruct((modes, ROWS, channels), F32),
        jax.ShapeDtypeStruct((streams - 1, halo, channels), F32),
    ]
    if last:
        outs.append(jax.ShapeDtypeStruct((modes, channels), F32))
    inputs = 1 + len(tokens) * pieces
    return call(
        functools.partial(signal_stage, pieces, len(tokens), first, last, row, taps),
        "signal_stage",
        [place],
        [part for chunk in tokens for part in chunk] + list(before) + [gain, w_in, w_short, rate],
        outs,
        [
            pltpu.VMEM((read, features), F32),
            pltpu.VMEM((halo + rows, min(BLOCK, channels)), F32),
        ],
        4 * read * features * channels,
        aliases={} if first else {inputs + k: k for k in range(3)},
    )


def run_local(low, high, taps, normed, signal, states, w_in, w_short, rate, mode, skip):
    count = signal.shape[0]
    rows, features = normed.shape
    modes = rate.shape[0]
    out = jax.ShapeDtypeStruct((count, high - low), F32)
    return call(
        functools.partial(local_stage, low, high, taps),
        "local_stage",
        [],
        [normed, signal, states, w_in, w_short, rate, mode, skip],
        [out, out, jax.ShapeDtypeStruct((modes, ROWS, high - low), F32)],
        [pltpu.VMEM((rows, min(BLOCK, high - low)), F32)],
        2 * rows * features * (high - low),
    )


def run_second(pieces, row, rows, bounds, place, done, marks, carry, rate, mode, w):
    channels, features = w.shape
    share = features // pieces
    return call(
        functools.partial(second_stage, pieces, row, rows, bounds),
        "second_stage",
        [place],
        [array for kind in zip(*done) for array in kind] + [marks, carry, rate, mode, w],
        [
            jax.ShapeDtypeStruct((max(1, pieces - 1) * rows, share), BF16),
            jax.ShapeDtypeStruct((rows, share), F32),
        ],
        [pltpu.VMEM((rows, channels), F32)],
        2 * features * channels * rows,
    )


def run_last(pieces, sizes, row, own, came, done, count):
    share = own[0].shape[1]
    rows = sum(sizes)
    (out,) = call(
        functools.partial(last_stage, pieces, sizes, row, bool(done)),
        "last_stage",
        [],
        [*own, *came, *done],
        [jax.ShapeDtypeStruct((share, count), BF16 if row + rows == count else F32)],
        [pltpu.VMEM((rows, share), BF16)],
        2 * rows * count * share,
    )
    return out


def rotate(value, axis, steps):
    count = lax.axis_size(axis)
    return lax.ppermute(value, axis, [((i + steps) % count, i) for i in range(count)])


def combine_states(span, stride, radix, count, *refs):
    place_ref, rate_ref, total_ref = refs[:3]
    others = refs[3 : 2 + radix]
    refs = refs[2 + radix :]
    carry_in = refs[0] if stride > 1 else None
    carry_ref = refs[1] if stride > 1 else refs[0]
    position = place_ref[1]
    digit = lax.rem(lax.div(position, stride), radix)
    inner = lax.rem(position, stride)
    unit = span * stride
    rate = rate_ref[...]
    before = jnp.zeros(rate.shape, F32)
    for shift in range(1, radix):
        reached = jnp.where(digit >= shift, 1.0, 0.0)
        before = before + jnp.exp(-rate * (unit * (shift - 1))) * (others[shift - 1][...] * reached)
    if stride > 1:
        carry_ref[...] = carry_in[...] + jnp.exp(-rate * (span * inner).astype(F32)) * before
    else:
        carry_ref[...] = before
    if stride * radix < count:
        new = jnp.exp(-rate * (unit * (radix - 1 - digit)).astype(F32)) * total_ref[...]
        for shift in range(1, radix):
            at = lax.rem(digit - shift + radix, radix)
            weight = jnp.exp(-rate * (unit * (radix - 1 - at)).astype(F32))
            new = new + weight * others[shift - 1][...]
        refs[-1][...] = new


def carried_in(state, rate, span, axis, place, between):
    count = lax.axis_size(axis)
    total, stride, carry = state, 1, []
    while stride < count:
        radix = 4 if count % (stride * 4) == 0 else 2
        assert count % (stride * radix) == 0
        group = stride * radix
        others = []
        for shift in range(1, radix):
            pairs = []
            for i in range(count):
                digit = (i // stride) % radix
                pairs.append((i + ((digit - shift) % radix - digit) * stride, i))
            others.append(lax.ppermute(total, axis, pairs))
        others = between(others)
        shape = jax.ShapeDtypeStruct(state.shape, F32)
        carry = call(
            functools.partial(combine_states, span, stride, radix, count),
            "combine_states",
            [place],
            [rate, total, *others, *carry],
            [shape] * (2 if group < count else 1),
            [],
            0,
        )
        if group < count:
            *carry, total = carry
        stride = group
    return carry[0]


def body(tokens, norm_gain, w_in, w_short, decay_rate, residue, skip_gain, w_out):
    pieces, count = lax.axis_size("tp"), lax.axis_size("ctx")
    share, rows = tokens.shape
    channels = w_in.shape[1]
    taps = w_short.shape[0]
    halo = ROWS * (taps - 1)
    sizes = [rows // CHUNKS] * CHUNKS
    bf16_rows = lambda size: jax.ShapeDtypeStruct((size, share), BF16)

    place = jnp.stack([lax.axis_index("tp"), lax.axis_index("ctx")]).astype(jnp.int32)
    tokens, place = lax.optimization_barrier((tokens, place))
    x0, edge = call(
        functools.partial(first_rows, halo), "first_rows", [], [tokens],
        [bf16_rows(halo + sizes[0]), bf16_rows(halo)], [], 2 * (2 * halo + sizes[0]) * rows * share,
    )
    edge = rotate(edge, "ctx", -1)
    x1, *others = call(
        functools.partial(next_rows, sizes[0]), "next_rows", [], [tokens],
        [bf16_rows(size) for size in sizes[1:]], [], 2 * rows * rows * share,
    )
    (x1,) = call(join_edge, "join_edge", [place], [edge, x1], [bf16_rows(halo + sizes[1])], [], 0)
    x1, others = lax.optimization_barrier((x1, others))
    x = [x0, x1, *others]
    residue, norm_gain, skip_gain, *_ = lax.optimization_barrier((residue, norm_gain, skip_gain, *x))
    mode = residue * jnp.sqrt(-jnp.expm1(-2.0 * decay_rate))
    gain = norm_gain[None, :]
    skip = skip_gain[None, :]
    parts = [[part] + [rotate(part, "tp", s) for s in range(1, pieces)] for part in x]
    w_in, mode, gain, skip, *_ = lax.optimization_barrier((w_in, mode, gain, skip, *x))
    w_in = pltpu.with_memory_space_constraint(in_vmem(w_in), pltpu.VMEM)

    before, row = [], 0
    for group in [[0, 1]] + [[j] for j in range(2, CHUNKS)]:
        results = run_signal(
            pieces, row, rows, group[0] == 0, group[-1] == CHUNKS - 1, taps, place,
            [parts[j] for j in group], before, gain, w_in, w_short, decay_rate,
        )
        before = results[:5]
        row += sum(sizes[j] for j in group)
    normed, signal, marks, states, _ = before
    state, normed, signal, states = lax.optimization_barrier((results[5], normed, signal, states))
    blocks = (channels + BLOCK - 1) // BLOCK
    middle = min(channels, (blocks + 1) // 2 * BLOCK)
    bounds = [b for b in ((0, middle), (middle, channels)) if b[0] < b[1]]
    done = []

    def between(others):
        if len(done) < len(bounds):
            done.append(
                run_local(
                    *bounds[len(done)], taps, normed, signal, states, w_in, w_short, decay_rate,
                    mode, skip,
                )
            )
            others, done[-1] = lax.optimization_barrier((others, done[-1]))
        return others

    carry = carried_in(state, decay_rate, rows, "ctx", place, between)
    while len(done) < len(bounds):
        between([])
    out_sizes = [rows // 4, rows // 2, rows // 4]
    own, came, row = [], [], 0
    for j, size in enumerate(out_sizes):
        if j == 2:
            carry, came[: pieces - 1] = lax.optimization_barrier((carry, came[: pieces - 1]))
        send, kept = run_second(
            pieces, row, size, bounds, place, done, marks, carry, decay_rate, mode, w_out
        )
        own.append(kept)
        for s in range(1, pieces):
            came.append(rotate(send[(s - 1) * size : s * size], "tp", -s))
        row += size
    early = sum(out_sizes[:-1])
    cut = (len(out_sizes) - 1) * (pieces - 1)
    done = run_last(pieces, out_sizes[:-1], 0, own[:-1], came[:cut], [], rows)
    return run_last(pieces, out_sizes[-1:], early, own[-1:], came[cut:], [done], rows)


def solution(mesh):
    placed = (
        P("tp", "ctx"),
        P(),
        P(None, "tp", None),
        P(None, None, "tp"),
        P(None, "tp"),
        P(None, "tp"),
        P("tp"),
        P("tp", None),
    )
    return jax.shard_map(
        body, mesh=mesh, in_specs=placed, out_specs=P("tp", "ctx"), check_vma=False
    )
```

```python
import functools

import jax
import jax.numpy as jnp
from jax import lax
from jax.experimental import pallas as pl
from jax.experimental.pallas import tpu as pltpu
from jax.sharding import PartitionSpec as P


F32 = jnp.float32
BF16 = jnp.bfloat16
ROWS = 8
LANES = 128
BLOCK = 256
CHUNKS = 4
SPAN = 16
VMEM_LIMIT = 10 * 2**20
CONTRACT_LAST = (((1,), (1,)), ((), ()))
CONTRACT_FIRST = (((0,), (0,)), ((), ()))


def lane_groups(low, width):
    return [(start, min(LANES, low + width - start)) for start in range(low, low + width, LANES)]


def rows_as(row, width):
    return jnp.broadcast_to(row, (ROWS, width))


def tree_sum(terms):
    while len(terms) > 1:
        terms = [sum(terms[k + 1 : k + 2], terms[k]) for k in range(0, len(terms), 2)]
    return terms[0]


def token_picker(first_row, rows, tokens):
    length = tokens // ROWS
    row = lax.broadcasted_iota(jnp.int32, (rows, tokens), 0)
    column = lax.broadcasted_iota(jnp.int32, (rows, tokens), 1)
    wanted = lax.rem(row, ROWS) * length + lax.div(row, ROWS) + first_row // ROWS
    return jnp.where(column == wanted, 1.0, 0.0).astype(BF16)


def turned(pick, tokens):
    return lax.dot_general(pick, tokens, CONTRACT_LAST, preferred_element_type=F32).astype(BF16)


def first_rows(halo, tokens_ref, out_ref, edge_ref):
    tokens = tokens_ref.shape[1]
    out_ref[...] = turned(token_picker(-halo, out_ref.shape[0], tokens), tokens_ref[...])
    row = lax.broadcasted_iota(jnp.int32, (halo, tokens), 0)
    column = lax.broadcasted_iota(jnp.int32, (halo, tokens), 1)
    wanted = jnp.where(lax.rem(row, ROWS) == 0, tokens - halo // ROWS + lax.div(row, ROWS), -1)
    edge_ref[...] = turned(jnp.where(column == wanted, 1.0, 0.0).astype(BF16), tokens_ref[...])


def next_rows(row, tokens_ref, *chunk_refs):
    tokens = tokens_ref.shape[1]
    for ref in chunk_refs:
        ref[...] = turned(token_picker(row, ref.shape[0], tokens), tokens_ref[...])
        row += ref.shape[0]


def join_edge(place_ref, edge_ref, chunk_ref, out_ref):
    halo = edge_ref.shape[0]
    preceded = jnp.where(place_ref[1] > 0, 1.0, 0.0)
    out_ref[:halo, :] = (edge_ref[...].astype(F32) * preceded).astype(BF16)
    out_ref[halo:, :] = chunk_ref[...]


def load_weights(places, w_hbm, w_ref, sem):
    copies = [
        pltpu.make_async_copy(w_hbm.at[place], w_ref.at[place], sem.at[k])
        for k, place in enumerate(places)
    ]
    for copy in copies:
        copy.start()
    for copy in copies:
        copy.wait()


def short_conv(p_ref, short_ref, s, part, rows, taps):
    width = part.stop - part.start
    total = None
    for offset in range(taps):
        start = ROWS * (taps - 1 - offset)
        term = short_ref[offset, s : s + 1, part] * p_ref[start : start + rows, :width]
        total = term if total is None else total + term
    return total


def project(normed, w_ref, s, part):
    product = lax.dot_general(normed, w_ref[s, part, :], CONTRACT_LAST, preferred_element_type=F32)
    return product.astype(BF16).astype(F32)


def signal_stage(pieces, chunks, first, last, row, taps, *refs):
    refs = list(refs)
    me_ref = refs.pop(0)
    token_refs = [[refs.pop(0) for _ in range(pieces)] for _ in range(chunks)]
    if not first:
        _, _, _, states_in, tail_in = [refs.pop(0) for _ in range(5)]
    gain_ref, w_ref, short_ref, rate_ref = refs[:4]
    normed_ref, signal_ref, marks_ref, states_ref, tail_ref = refs[4:9]
    total_ref = refs[9] if last else None
    x_ref, p_ref = refs[-2:]
    halo = ROWS * (taps - 1)
    modes, channels = rate_ref.shape
    read, share = x_ref.shape[0], token_refs[0][0].shape[1]
    rows = read - halo if first else read
    length = signal_ref.shape[0] // ROWS
    me = me_ref[0]

    values = []
    for s in range(pieces):
        value = [refs_of[s][...].astype(F32) for refs_of in token_refs]
        if first:
            front, edge = value[0][:halo], value[-1][:halo]
            value = [front + edge, value[0][halo:], *value[1:-1], value[-1][halo:]]
        values.append(jnp.concatenate(value, axis=0) if len(value) > 1 else value[0])
    for rank in range(pieces):
        chosen = values[0]
        for s in range(1, pieces):
            chosen = jnp.where(me == (rank - s) % pieces, values[s], chosen)
        x_ref[:, rank * share : (rank + 1) * share] = chosen
    features = x_ref[...]
    mean = jnp.mean(features * features, axis=1, keepdims=True)
    normed = (features * lax.rsqrt(mean + 1e-06) * gain_ref[...]).astype(BF16)
    begin = 0 if first else halo + row
    normed_ref[begin : begin + read, :] = normed

    for low in range(0, channels, BLOCK):
        width = min(BLOCK, channels - low)
        part = slice(low, low + width)
        for s in (1, 2):
            if not first:
                p_ref[:halo, :width] = tail_in[s - 1, :, part]
            p_ref[halo + rows - read :, :width] = project(
                normed_ref[begin : begin + read, :], w_ref, s, part
            )
            tail_ref[s - 1, :, part] = p_ref[rows:, :width]
            short = short_conv(p_ref, short_ref, s, part, rows, taps)
            if s == 1:
                signal_ref[row : row + rows, part] = short
            else:
                signal_ref[row : row + rows, part] = signal_ref[row : row + rows, part] * short
        for start, size in lane_groups(low, width):
            lanes = slice(start, start + size)
            rate = [rows_as(rate_ref[n : n + 1, lanes], size) for n in range(modes)]
            decay = [jnp.exp(-r) for r in rate]

            if first:
                states = (jnp.zeros((ROWS, size), F32),) * modes
            else:
                states = tuple(states_in[n, :, lanes] for n in range(modes))
            for at in range(row, row + rows, SPAN * ROWS):
                mark = at // (SPAN * ROWS)
                for n in range(modes):
                    marks_ref[mark, n, :, lanes] = states[n]

                def step(i, states):
                    here = pl.ds(pl.multiple_of(at + i * ROWS, ROWS), ROWS)
                    now = signal_ref[here, lanes]
                    return tuple(states[n] * decay[n] + now for n in range(modes))

                states = lax.fori_loop(0, SPAN, step, states, unroll=8)
            for n in range(modes):
                states_ref[n, :, lanes] = states[n]
            if last:
                left = lax.broadcasted_iota(jnp.int32, (ROWS, size), 0)
                left = ((ROWS - 1 - left) * length).astype(F32)
                for n in range(modes):
                    total_ref[n : n + 1, lanes] = jnp.sum(
                        states[n] * jnp.exp(-rate[n] * left), axis=0, keepdims=True
                    )


def local_stage(low, high, taps, *refs):
    normed_ref, signal_ref, states_ref, w_ref, short_ref, rate_ref, mode_ref, skip_ref = refs[:8]
    q_ref, local_ref, begin_ref, p_ref = refs[8:]
    modes = rate_ref.shape[0]
    rows = signal_ref.shape[0]
    length = rows // ROWS
    for at in range(low, high, BLOCK):
        width = min(BLOCK, high - at)
        part = slice(at, at + width)
        p_ref[:, :width] = project(normed_ref[...], w_ref, 0, part)
        q_ref[:, at - low : at - low + width] = short_conv(p_ref, short_ref, 0, part, rows, taps)
        for start, size in lane_groups(at, width):
            lanes = slice(start, start + size)
            there = slice(start - low, start - low + size)
            rate = [rows_as(rate_ref[n : n + 1, lanes], size) for n in range(modes)]
            segment = lax.broadcasted_iota(jnp.int32, (ROWS, size), 0)
            for n in range(modes):
                run = states_ref[n, :, lanes]
                for hop in (1, 2, 4):
                    weight = jnp.where(segment >= hop, jnp.exp(-rate[n] * (hop * length)), 0.0)
                    run = run + weight * pltpu.roll(run, hop, 0)
                begin_ref[n, :, there] = jnp.where(segment >= 1, pltpu.roll(run, 1, 0), 0.0)
            lag = segment.astype(F32)
            filters = []
            for first_lag in range(0, SPAN, ROWS):
                values = tree_sum(
                    [
                        rows_as(mode_ref[n : n + 1, lanes], size)
                        * jnp.exp(-rate[n] * (lag + first_lag))
                        for n in range(modes)
                    ]
                )
                filters += [rows_as(values[j : j + 1, :], size) for j in range(ROWS)]
            filters[0] = filters[0] + skip_ref[:, lanes]

            def span(i, carry):
                base = i * (SPAN * ROWS)
                here = [
                    pl.ds(pl.multiple_of(base + k * ROWS, ROWS), ROWS) for k in range(SPAN)
                ]
                now = [signal_ref[place, lanes] for place in here]
                for k in range(SPAN):
                    local_ref[here[k], there] = tree_sum(
                        [filters[j] * now[k - j] for j in range(k + 1)]
                    )
                return carry

            lax.fori_loop(0, length // SPAN, span, 0)


def second_stage(pieces, row, rows, bounds, *refs):
    count = len(bounds)
    me_ref = refs[0]
    q_refs, local_refs, begin_refs = [refs[1 + k * count : 1 + (k + 1) * count] for k in range(3)]
    refs = refs[1 + 3 * count :]
    marks_ref, carry_ref, rate_ref, mode_ref, w_ref, send_ref, own_ref, gated_ref = refs
    modes = rate_ref.shape[0]
    length = q_refs[0].shape[0] // ROWS
    for (low, high), q_ref, local_ref, begin_ref in zip(bounds, q_refs, local_refs, begin_refs):
        for start, size in lane_groups(low, high - low):
            lanes = slice(start, start + size)
            there = slice(start - low, start - low + size)
            rate = [rows_as(rate_ref[n : n + 1, lanes], size) for n in range(modes)]
            decay = [jnp.exp(-r) for r in rate]
            segment = lax.broadcasted_iota(jnp.int32, (ROWS, size), 0)
            past = (segment * length).astype(F32)
            for at in range(row, row + rows, SPAN * ROWS):
                mark = at // (SPAN * ROWS)
                states = []
                for n in range(modes):
                    state = begin_ref[n, :, there] + jnp.exp(-rate[n] * past) * carry_ref[
                        n : n + 1, lanes
                    ]
                    if mark > 0:
                        state = marks_ref[mark, n, :, lanes] + state * jnp.exp(
                            -rate[n] * (SPAN * mark)
                        )
                    states.append(mode_ref[n : n + 1, lanes] * state)

                def step(i, states):
                    here = pl.ds(pl.multiple_of(at - row + i * ROWS, ROWS), ROWS)
                    from_row = pl.ds(pl.multiple_of(at + i * ROWS, ROWS), ROWS)
                    states = tuple(states[n] * decay[n] for n in range(modes))
                    gated_ref[here, lanes] = q_ref[from_row, there] * tree_sum(
                        [local_ref[from_row, there]] + list(states)
                    )
                    return states

                lax.fori_loop(0, SPAN, step, tuple(states), unroll=4)
    product = jnp.dot(gated_ref[...].astype(BF16), w_ref[...], preferred_element_type=F32)
    share = own_ref.shape[1]
    me = me_ref[0]
    columns = [product[:, rank * share : (rank + 1) * share] for rank in range(pieces)]
    for s in range(pieces):
        chosen = columns[0]
        for rank in range(1, pieces):
            chosen = jnp.where(me == (rank - s) % pieces, columns[rank], chosen)
        if s == 0:
            own_ref[...] = chosen
        else:
            send_ref[(s - 1) * rows : s * rows, :] = chosen.astype(BF16)


def last_stage(pieces, sizes, row, more, *refs):
    chunks = len(sizes)
    own_refs, came_refs = refs[:chunks], refs[chunks : chunks * pieces]
    done_ref = refs[chunks * pieces] if more else None
    out_ref, mixed_ref = refs[-2:]
    at = 0
    for j, size in enumerate(sizes):
        total = own_refs[j][...]
        for s in range(pieces - 1):
            total = total + came_refs[j * (pieces - 1) + s][...].astype(F32)
        mixed_ref[at : at + size, :] = total.astype(BF16)
        at += size
    pick = token_picker(row, at, out_ref.shape[1])
    out = lax.dot_general(mixed_ref[...], pick, CONTRACT_FIRST, preferred_element_type=F32)
    if more:
        out = out + done_ref[...]
    out_ref[...] = out.astype(out_ref.dtype)


def call(kernel, name, scalars, operands, outs, scratch, flops, aliases={}):
    vmem = pl.BlockSpec(memory_space=pltpu.VMEM)
    smem = pl.BlockSpec(memory_space=pltpu.SMEM)
    size = lambda a: a.size * jnp.dtype(a.dtype).itemsize
    return pl.pallas_call(
        kernel,
        out_shape=outs,
        in_specs=[smem] * len(scalars) + [vmem] * len(operands),
        out_specs=[vmem] * len(outs),
        scratch_shapes=scratch,
        input_output_aliases=aliases,
        compiler_params=pltpu.CompilerParams(vmem_limit_bytes=VMEM_LIMIT),
        cost_estimate=pl.CostEstimate(
            flops=flops,
            bytes_accessed=sum(size(a) for a in operands),
            transcendentals=0,
        ),
        name=name,
    )(*scalars, *operands)


def in_vmem(w):
    streams, channels = w.shape[:2]
    parts = next(k for k in (4, 3, 2, 1) if channels % (16 * k) == 0 or k == 1)
    size = channels // parts
    places = [(s, slice(p * size, (p + 1) * size)) for s in range(streams) for p in range(parts)]
    return pl.pallas_call(
        functools.partial(load_weights, places),
        out_shape=pltpu.VMEM(w.shape, w.dtype),
        in_specs=[pl.BlockSpec(memory_space=pl.ANY)],
        out_specs=pl.BlockSpec(memory_space=pltpu.VMEM),
        scratch_shapes=[pltpu.SemaphoreType.DMA((len(places),))],
        compiler_params=pltpu.CompilerParams(vmem_limit_bytes=46 * 2**20),
        cost_estimate=pl.CostEstimate(
            flops=0, bytes_accessed=w.size * w.dtype.itemsize, transcendentals=0
        ),
        name="load_weights",
    )(w)


def run_signal(pieces, row, count, first, last, taps, place, tokens, before, gain, w_in, w_short, rate):
    streams, channels, features = w_in.shape
    modes = rate.shape[0]
    halo = ROWS * (taps - 1)
    read = sum(chunk[0].shape[0] for chunk in tokens) - (halo if first else 0)
    rows = read - halo if first else read
    outs = [
        jax.ShapeDtypeStruct((halo + count, features), BF16),
        jax.ShapeDtypeStruct((count, channels), F32),
        jax.ShapeDtypeStruct((count // (SPAN * ROWS), modes, ROWS, channels), F32),
        jax.ShapeDtypeStruct((modes, ROWS, channels), F32),
        jax.ShapeDtypeStruct((streams - 1, halo, channels), F32),
    ]
    if last:
        outs.append(jax.ShapeDtypeStruct((modes, channels), F32))
    inputs = 1 + len(tokens) * pieces
    return call(
        functools.partial(signal_stage, pieces, len(tokens), first, last, row, taps),
        "signal_stage",
        [place],
        [part for chunk in tokens for part in chunk] + list(before) + [gain, w_in, w_short, rate],
        outs,
        [
            pltpu.VMEM((read, features), F32),
            pltpu.VMEM((halo + rows, min(BLOCK, channels)), F32),
        ],
        4 * read * features * channels,
        aliases={} if first else {inputs + k: k for k in range(3)},
    )


def run_local(low, high, taps, normed, signal, states, w_in, w_short, rate, mode, skip):
    count = signal.shape[0]
    rows, features = normed.shape
    modes = rate.shape[0]
    out = jax.ShapeDtypeStruct((count, high - low), F32)
    return call(
        functools.partial(local_stage, low, high, taps),
        "local_stage",
        [],
        [normed, signal, states, w_in, w_short, rate, mode, skip],
        [out, out, jax.ShapeDtypeStruct((modes, ROWS, high - low), F32)],
        [pltpu.VMEM((rows, min(BLOCK, high - low)), F32)],
        2 * rows * features * (high - low),
    )


def run_second(pieces, row, rows, bounds, place, done, marks, carry, rate, mode, w):
    channels, features = w.shape
    share = features // pieces
    return call(
        functools.partial(second_stage, pieces, row, rows, bounds),
        "second_stage",
        [place],
        [array for kind in zip(*done) for array in kind] + [marks, carry, rate, mode, w],
        [
            jax.ShapeDtypeStruct((max(1, pieces - 1) * rows, share), BF16),
            jax.ShapeDtypeStruct((rows, share), F32),
        ],
        [pltpu.VMEM((rows, channels), F32)],
        2 * features * channels * rows,
    )


def run_last(pieces, sizes, row, own, came, done, count):
    share = own[0].shape[1]
    rows = sum(sizes)
    (out,) = call(
        functools.partial(last_stage, pieces, sizes, row, bool(done)),
        "last_stage",
        [],
        [*own, *came, *done],
        [jax.ShapeDtypeStruct((share, count), BF16 if row + rows == count else F32)],
        [pltpu.VMEM((rows, share), BF16)],
        2 * rows * count * share,
    )
    return out


def rotate(value, axis, steps):
    count = lax.axis_size(axis)
    return lax.ppermute(value, axis, [((i + steps) % count, i) for i in range(count)])


def combine_states(span, stride, radix, count, *refs):
    place_ref, rate_ref, total_ref = refs[:3]
    others = refs[3 : 2 + radix]
    refs = refs[2 + radix :]
    carry_in = refs[0] if stride > 1 else None
    carry_ref = refs[1] if stride > 1 else refs[0]
    position = place_ref[1]
    digit = lax.rem(lax.div(position, stride), radix)
    inner = lax.rem(position, stride)
    unit = span * stride
    rate = rate_ref[...]
    before = jnp.zeros(rate.shape, F32)
    for shift in range(1, radix):
        reached = jnp.where(digit >= shift, 1.0, 0.0)
        before = before + jnp.exp(-rate * (unit * (shift - 1))) * (others[shift - 1][...] * reached)
    if stride > 1:
        carry_ref[...] = carry_in[...] + jnp.exp(-rate * (span * inner).astype(F32)) * before
    else:
        carry_ref[...] = before
    if stride * radix < count:
        new = jnp.exp(-rate * (unit * (radix - 1 - digit)).astype(F32)) * total_ref[...]
        for shift in range(1, radix):
            at = lax.rem(digit - shift + radix, radix)
            weight = jnp.exp(-rate * (unit * (radix - 1 - at)).astype(F32))
            new = new + weight * others[shift - 1][...]
        refs[-1][...] = new


def carry_of_modes(span, count, place_ref, rate_ref, states_ref, carry_ref):
    kinds = states_ref.shape[0] // count
    for k in range(kinds):
        decay = jnp.exp(-rate_ref[pl.ds(place_ref[1] * kinds + k, 1), :] * span)
        carry = jnp.zeros(decay.shape, F32)
        for block in range(count):
            row = slice(block * kinds + k, block * kinds + k + 1)
            carry_ref[row, :] = carry
            carry = carry * decay + states_ref[row, :]


def carried_in(state, rate, span, axis, place, between):
    count = lax.axis_size(axis)
    if state.shape[0] % count == 0:
        states = lax.all_to_all(state, axis, 0, 0, tiled=True)
        (states,) = between([states])
        (carry,) = call(
            functools.partial(carry_of_modes, span, count),
            "carry_of_modes",
            [place],
            [rate, states],
            [jax.ShapeDtypeStruct(state.shape, F32)],
            [],
            0,
        )
        (carry,) = between([lax.all_to_all(carry, axis, 0, 0, tiled=True)])
        return carry
    total, stride, carry = state, 1, []
    while stride < count:
        radix = 4 if count % (stride * 4) == 0 else 2
        assert count % (stride * radix) == 0
        group = stride * radix
        others = []
        for shift in range(1, radix):
            pairs = []
            for i in range(count):
                digit = (i // stride) % radix
                pairs.append((i + ((digit - shift) % radix - digit) * stride, i))
            others.append(lax.ppermute(total, axis, pairs))
        others = between(others)
        shape = jax.ShapeDtypeStruct(state.shape, F32)
        carry = call(
            functools.partial(combine_states, span, stride, radix, count),
            "combine_states",
            [place],
            [rate, total, *others, *carry],
            [shape] * (2 if group < count else 1),
            [],
            0,
        )
        if group < count:
            *carry, total = carry
        stride = group
    return carry[0]


def body(tokens, norm_gain, w_in, w_short, decay_rate, residue, skip_gain, w_out):
    pieces, count = lax.axis_size("tp"), lax.axis_size("ctx")
    share, rows = tokens.shape
    channels = w_in.shape[1]
    taps = w_short.shape[0]
    halo = ROWS * (taps - 1)
    sizes = [rows // CHUNKS] * CHUNKS
    bf16_rows = lambda size: jax.ShapeDtypeStruct((size, share), BF16)

    place = jnp.stack([lax.axis_index("tp"), lax.axis_index("ctx")]).astype(jnp.int32)
    tokens, place = lax.optimization_barrier((tokens, place))
    x0, edge = call(
        functools.partial(first_rows, halo), "first_rows", [], [tokens],
        [bf16_rows(halo + sizes[0]), bf16_rows(halo)], [], 2 * (2 * halo + sizes[0]) * rows * share,
    )
    edge = rotate(edge, "ctx", -1)
    x1, *others = call(
        functools.partial(next_rows, sizes[0]), "next_rows", [], [tokens],
        [bf16_rows(size) for size in sizes[1:]], [], 2 * rows * rows * share,
    )
    (x1,) = call(join_edge, "join_edge", [place], [edge, x1], [bf16_rows(halo + sizes[1])], [], 0)
    x1, others = lax.optimization_barrier((x1, others))
    x = [x0, x1, *others]
    residue, norm_gain, skip_gain, *_ = lax.optimization_barrier((residue, norm_gain, skip_gain, *x))
    mode = residue * jnp.sqrt(-jnp.expm1(-2.0 * decay_rate))
    gain = norm_gain[None, :]
    skip = skip_gain[None, :]
    parts = [[part] + [rotate(part, "tp", s) for s in range(1, pieces)] for part in x]
    w_in, mode, gain, skip, *_ = lax.optimization_barrier((w_in, mode, gain, skip, *x))
    w_in = pltpu.with_memory_space_constraint(in_vmem(w_in), pltpu.VMEM)

    before, row = [], 0
    for group in [[0, 1]] + [[j] for j in range(2, CHUNKS)]:
        results = run_signal(
            pieces, row, rows, group[0] == 0, group[-1] == CHUNKS - 1, taps, place,
            [parts[j] for j in group], before, gain, w_in, w_short, decay_rate,
        )
        before = results[:5]
        row += sum(sizes[j] for j in group)
    normed, signal, marks, states, _ = before
    state, normed, signal, states = lax.optimization_barrier((results[5], normed, signal, states))
    blocks = (channels + BLOCK - 1) // BLOCK
    middle = min(channels, (blocks + 1) // 2 * BLOCK)
    bounds = [b for b in ((0, middle), (middle, channels)) if b[0] < b[1]]
    done = []

    def between(others):
        if len(done) < len(bounds):
            done.append(
                run_local(
                    *bounds[len(done)], taps, normed, signal, states, w_in, w_short, decay_rate,
                    mode, skip,
                )
            )
            others, done[-1] = lax.optimization_barrier((others, done[-1]))
        return others

    carry = carried_in(state, decay_rate, rows, "ctx", place, between)
    while len(done) < len(bounds):
        between([])
    out_sizes = [rows // 4, rows // 2, rows // 4]
    own, came, row = [], [], 0
    for j, size in enumerate(out_sizes):
        if j == 2:
            carry, came[: pieces - 1] = lax.optimization_barrier((carry, came[: pieces - 1]))
        send, kept = run_second(
            pieces, row, size, bounds, place, done, marks, carry, decay_rate, mode, w_out
        )
        own.append(kept)
        for s in range(1, pieces):
            came.append(rotate(send[(s - 1) * size : s * size], "tp", -s))
        row += size
    early = sum(out_sizes[:-1])
    cut = (len(out_sizes) - 1) * (pieces - 1)
    done = run_last(pieces, out_sizes[:-1], 0, own[:-1], came[:cut], [], rows)
    return run_last(pieces, out_sizes[-1:], early, own[-1:], came[cut:], [done], rows)


def solution(mesh):
    placed = (
        P("tp", "ctx"),
        P(),
        P(None, "tp", None),
        P(None, None, "tp"),
        P(None, "tp"),
        P(None, "tp"),
        P("tp"),
        P("tp", None),
    )
    return jax.shard_map(
        body, mesh=mesh, in_specs=placed, out_specs=P("tp", "ctx"), check_vma=False
    )
```

```python
import functools

import jax
import jax.numpy as jnp
from jax import lax
from jax.experimental import pallas as pl
from jax.experimental.pallas import tpu as pltpu
from jax.sharding import PartitionSpec as P


F32 = jnp.float32
BF16 = jnp.bfloat16
ROWS = 8
LANES = 128
BLOCK = 256
CHUNKS = 4
SPAN = 16
VMEM_LIMIT = 10 * 2**20
CONTRACT_LAST = (((1,), (1,)), ((), ()))
CONTRACT_FIRST = (((0,), (0,)), ((), ()))


def lane_groups(low, width):
    return [(start, min(LANES, low + width - start)) for start in range(low, low + width, LANES)]


def rows_as(row, width):
    return jnp.broadcast_to(row, (ROWS, width))


def tree_sum(terms):
    while len(terms) > 1:
        terms = [sum(terms[k + 1 : k + 2], terms[k]) for k in range(0, len(terms), 2)]
    return terms[0]


def token_picker(first_row, rows, tokens):
    length = tokens // ROWS
    row = lax.broadcasted_iota(jnp.int32, (rows, tokens), 0)
    column = lax.broadcasted_iota(jnp.int32, (rows, tokens), 1)
    wanted = lax.rem(row, ROWS) * length + lax.div(row, ROWS) + first_row // ROWS
    return jnp.where(column == wanted, 1.0, 0.0).astype(BF16)


def turned(pick, tokens):
    return lax.dot_general(pick, tokens, CONTRACT_LAST, preferred_element_type=F32).astype(BF16)


def first_rows(halo, tokens_ref, out_ref, edge_ref):
    tokens = tokens_ref.shape[1]
    out_ref[...] = turned(token_picker(-halo, out_ref.shape[0], tokens), tokens_ref[...])
    row = lax.broadcasted_iota(jnp.int32, (halo, tokens), 0)
    column = lax.broadcasted_iota(jnp.int32, (halo, tokens), 1)
    wanted = jnp.where(lax.rem(row, ROWS) == 0, tokens - halo // ROWS + lax.div(row, ROWS), -1)
    edge_ref[...] = turned(jnp.where(column == wanted, 1.0, 0.0).astype(BF16), tokens_ref[...])


def next_rows(row, tokens_ref, *chunk_refs):
    tokens = tokens_ref.shape[1]
    for ref in chunk_refs:
        ref[...] = turned(token_picker(row, ref.shape[0], tokens), tokens_ref[...])
        row += ref.shape[0]


def join_edge(place_ref, edge_ref, chunk_ref, out_ref):
    halo = edge_ref.shape[0]
    preceded = jnp.where(place_ref[1] > 0, 1.0, 0.0)
    out_ref[:halo, :] = (edge_ref[...].astype(F32) * preceded).astype(BF16)
    out_ref[halo:, :] = chunk_ref[...]


def load_weights(places, w_hbm, out_ref, w_ref, sem):
    copies = [
        pltpu.make_async_copy(w_hbm.at[place], w_ref.at[place], sem.at[k])
        for k, place in enumerate(places)
    ]
    for copy in copies:
        copy.start()
    for (s, part), copy in zip(places, copies):
        copy.wait()
        out_ref[s, :, part] = w_ref[s, part, :].T


def short_conv(p_ref, short_ref, s, part, rows, taps):
    width = part.stop - part.start
    total = None
    for offset in range(taps):
        start = ROWS * (taps - 1 - offset)
        term = short_ref[offset, s : s + 1, part] * p_ref[start : start + rows, :width]
        total = term if total is None else total + term
    return total


def project(normed, w_ref, s, part):
    product = jnp.dot(normed, w_ref[s, :, part], preferred_element_type=F32)
    return product.astype(BF16).astype(F32)


def signal_stage(pieces, chunks, first, last, row, taps, *refs):
    refs = list(refs)
    me_ref = refs.pop(0)
    token_refs = [[refs.pop(0) for _ in range(pieces)] for _ in range(chunks)]
    if not first:
        _, _, _, states_in, tail_in = [refs.pop(0) for _ in range(5)]
    gain_ref, w_ref, short_ref, rate_ref = refs[:4]
    normed_ref, signal_ref, marks_ref, states_ref, tail_ref = refs[4:9]
    total_ref = refs[9] if last else None
    x_ref, p_ref = refs[-2:]
    halo = ROWS * (taps - 1)
    modes, channels = rate_ref.shape
    read, share = x_ref.shape[0], token_refs[0][0].shape[1]
    rows = read - halo if first else read
    length = signal_ref.shape[0] // ROWS
    me = me_ref[0]

    values = []
    for s in range(pieces):
        value = [refs_of[s][...].astype(F32) for refs_of in token_refs]
        if first:
            front, edge = value[0][:halo], value[-1][:halo]
            value = [front + edge, value[0][halo:], *value[1:-1], value[-1][halo:]]
        values.append(jnp.concatenate(value, axis=0) if len(value) > 1 else value[0])
    for rank in range(pieces):
        chosen = values[0]
        for s in range(1, pieces):
            chosen = jnp.where(me == (rank - s) % pieces, values[s], chosen)
        x_ref[:, rank * share : (rank + 1) * share] = chosen
    features = x_ref[...]
    mean = jnp.mean(features * features, axis=1, keepdims=True)
    normed = (features * lax.rsqrt(mean + 1e-06) * gain_ref[...]).astype(BF16)
    begin = 0 if first else halo + row
    normed_ref[begin : begin + read, :] = normed

    for low in range(0, channels, BLOCK):
        width = min(BLOCK, channels - low)
        part = slice(low, low + width)
        for s in (1, 2):
            if not first:
                p_ref[:halo, :width] = tail_in[s - 1, :, part]
            p_ref[halo + rows - read :, :width] = project(
                normed_ref[begin : begin + read, :], w_ref, s, part
            )
            tail_ref[s - 1, :, part] = p_ref[rows:, :width]
            short = short_conv(p_ref, short_ref, s, part, rows, taps)
            if s == 1:
                signal_ref[row : row + rows, part] = short
            else:
                signal_ref[row : row + rows, part] = signal_ref[row : row + rows, part] * short
        for start, size in lane_groups(low, width):
            lanes = slice(start, start + size)
            rate = [rows_as(rate_ref[n : n + 1, lanes], size) for n in range(modes)]
            decay = [jnp.exp(-r) for r in rate]

            if first:
                states = (jnp.zeros((ROWS, size), F32),) * modes
            else:
                states = tuple(states_in[n, :, lanes] for n in range(modes))
            for at in range(row, row + rows, SPAN * ROWS):
                mark = at // (SPAN * ROWS)
                for n in range(modes):
                    marks_ref[mark, n, :, lanes] = states[n]

                def step(i, states):
                    here = pl.ds(pl.multiple_of(at + i * ROWS, ROWS), ROWS)
                    now = signal_ref[here, lanes]
                    return tuple(states[n] * decay[n] + now for n in range(modes))

                states = lax.fori_loop(0, SPAN, step, states, unroll=8)
            for n in range(modes):
                states_ref[n, :, lanes] = states[n]
            if last:
                left = lax.broadcasted_iota(jnp.int32, (ROWS, size), 0)
                left = ((ROWS - 1 - left) * length).astype(F32)
                for n in range(modes):
                    total_ref[n : n + 1, lanes] = jnp.sum(
                        states[n] * jnp.exp(-rate[n] * left), axis=0, keepdims=True
                    )


def local_stage(row, rows, taps, *refs):
    normed_ref, signal_ref, states_ref, w_ref, short_ref, rate_ref, mode_ref, skip_ref = refs[:8]
    q_ref, local_ref = refs[8:10]
    begin_ref = refs[10] if row == 0 else None
    p_ref = refs[-1]
    modes, channels = rate_ref.shape
    length = signal_ref.shape[0] // ROWS
    for low in range(0, channels, BLOCK):
        width = min(BLOCK, channels - low)
        part = slice(low, low + width)
        normed = normed_ref[row : row + p_ref.shape[0], :]
        p_ref[:, :width] = project(normed, w_ref, 0, part)
        q_ref[:, part] = short_conv(p_ref, short_ref, 0, part, rows, taps)
        for start, size in lane_groups(low, width):
            lanes = slice(start, start + size)
            rate = [rows_as(rate_ref[n : n + 1, lanes], size) for n in range(modes)]
            segment = lax.broadcasted_iota(jnp.int32, (ROWS, size), 0)
            if row == 0:
                for n in range(modes):
                    run = states_ref[n, :, lanes]
                    for hop in (1, 2, 4):
                        weight = jnp.where(segment >= hop, jnp.exp(-rate[n] * (hop * length)), 0.0)
                        run = run + weight * pltpu.roll(run, hop, 0)
                    begin_ref[n, :, lanes] = jnp.where(segment >= 1, pltpu.roll(run, 1, 0), 0.0)
            lag = segment.astype(F32)
            filters = []
            for first_lag in range(0, SPAN, ROWS):
                values = tree_sum(
                    [
                        rows_as(mode_ref[n : n + 1, lanes], size)
                        * jnp.exp(-rate[n] * (lag + first_lag))
                        for n in range(modes)
                    ]
                )
                filters += [rows_as(values[j : j + 1, :], size) for j in range(ROWS)]
            filters[0] = filters[0] + skip_ref[:, lanes]

            def span(i, carry):
                base = i * (SPAN * ROWS)
                now = [
                    signal_ref[pl.ds(pl.multiple_of(row + base + k * ROWS, ROWS), ROWS), lanes]
                    for k in range(SPAN)
                ]
                for k in range(SPAN):
                    local_ref[pl.ds(pl.multiple_of(base + k * ROWS, ROWS), ROWS), lanes] = tree_sum(
                        [filters[j] * now[k - j] for j in range(k + 1)]
                    )
                return carry

            lax.fori_loop(0, rows // (SPAN * ROWS), span, 0)


def second_stage(pieces, row, rows, shift, length, *refs):
    me_ref, q_ref, local_ref, begin_ref, marks_ref, carry_ref, rate_ref, mode_ref, w_ref = refs[:9]
    send_ref, own_ref, gated_ref = refs[9:]
    modes, channels = rate_ref.shape
    for start, size in lane_groups(0, channels):
        lanes = slice(start, start + size)
        rate = [rows_as(rate_ref[n : n + 1, lanes], size) for n in range(modes)]
        decay = [jnp.exp(-r) for r in rate]
        segment = lax.broadcasted_iota(jnp.int32, (ROWS, size), 0)
        past = (segment * length).astype(F32)
        for at in range(row, row + rows, SPAN * ROWS):
            mark = at // (SPAN * ROWS)
            states = []
            for n in range(modes):
                state = begin_ref[n, :, lanes] + jnp.exp(-rate[n] * past) * carry_ref[
                    n : n + 1, lanes
                ]
                if mark > 0:
                    state = marks_ref[mark, n, :, lanes] + state * jnp.exp(-rate[n] * (SPAN * mark))
                states.append(mode_ref[n : n + 1, lanes] * state)

            def step(i, states):
                here = pl.ds(pl.multiple_of(at - row + i * ROWS, ROWS), ROWS)
                there = pl.ds(pl.multiple_of(at - shift + i * ROWS, ROWS), ROWS)
                states = tuple(states[n] * decay[n] for n in range(modes))
                gated_ref[here, lanes] = q_ref[there, lanes] * tree_sum(
                    [local_ref[there, lanes]] + list(states)
                )
                return states

            lax.fori_loop(0, SPAN, step, tuple(states), unroll=4)
    product = jnp.dot(gated_ref[...].astype(BF16), w_ref[...], preferred_element_type=F32)
    share = own_ref.shape[1]
    me = me_ref[0]
    columns = [product[:, rank * share : (rank + 1) * share] for rank in range(pieces)]
    for s in range(pieces):
        chosen = columns[0]
        for rank in range(1, pieces):
            chosen = jnp.where(me == (rank - s) % pieces, columns[rank], chosen)
        if s == 0:
            own_ref[...] = chosen
        else:
            send_ref[(s - 1) * rows : s * rows, :] = chosen.astype(BF16)


def last_stage(pieces, sizes, row, more, *refs):
    chunks = len(sizes)
    own_refs, came_refs = refs[:chunks], refs[chunks : chunks * pieces]
    done_ref = refs[chunks * pieces] if more else None
    out_ref, mixed_ref = refs[-2:]
    at = 0
    for j, size in enumerate(sizes):
        total = own_refs[j][...]
        for s in range(pieces - 1):
            total = total + came_refs[j * (pieces - 1) + s][...].astype(F32)
        mixed_ref[at : at + size, :] = total.astype(BF16)
        at += size
    pick = token_picker(row, at, out_ref.shape[1])
    out = lax.dot_general(mixed_ref[...], pick, CONTRACT_FIRST, preferred_element_type=F32)
    if more:
        out = out + done_ref[...]
    out_ref[...] = out.astype(out_ref.dtype)


def call(kernel, name, scalars, operands, outs, scratch, aliases={}):
    vmem = pl.BlockSpec(memory_space=pltpu.VMEM)
    smem = pl.BlockSpec(memory_space=pltpu.SMEM)
    return pl.pallas_call(
        kernel,
        out_shape=outs,
        in_specs=[smem] * len(scalars) + [vmem] * len(operands),
        out_specs=[vmem] * len(outs),
        scratch_shapes=scratch,
        input_output_aliases=aliases,
        compiler_params=pltpu.CompilerParams(vmem_limit_bytes=VMEM_LIMIT),
        cost_estimate=pl.CostEstimate(flops=1, bytes_accessed=1, transcendentals=0),
        name=name,
    )(*scalars, *operands)


def in_vmem(w):
    streams, channels, features = w.shape
    block = min(BLOCK, channels)
    places = [
        (s, slice(low, min(low + block, channels)))
        for s in (1, 2, 0)
        for low in range(0, channels, block)
    ]
    return pl.pallas_call(
        functools.partial(load_weights, places),
        out_shape=pltpu.VMEM((streams, features, channels), w.dtype),
        in_specs=[pl.BlockSpec(memory_space=pl.ANY)],
        out_specs=pl.BlockSpec(memory_space=pltpu.VMEM),
        scratch_shapes=[
            pltpu.VMEM(w.shape, w.dtype),
            pltpu.SemaphoreType.DMA((len(places),)),
        ],
        compiler_params=pltpu.CompilerParams(vmem_limit_bytes=46 * 2**20),
        cost_estimate=pl.CostEstimate(flops=1, bytes_accessed=1, transcendentals=0),
        name="load_weights",
    )(w)


def run_signal(pieces, row, count, first, last, taps, place, tokens, before, gain, w_in, w_short, rate):
    streams, features, channels = w_in.shape
    modes = rate.shape[0]
    halo = ROWS * (taps - 1)
    read = sum(chunk[0].shape[0] for chunk in tokens) - (halo if first else 0)
    rows = read - halo if first else read
    outs = [
        jax.ShapeDtypeStruct((halo + count, features), BF16),
        jax.ShapeDtypeStruct((count, channels), F32),
        jax.ShapeDtypeStruct((count // (SPAN * ROWS), modes, ROWS, channels), F32),
        jax.ShapeDtypeStruct((modes, ROWS, channels), F32),
        jax.ShapeDtypeStruct((streams - 1, halo, channels), F32),
    ]
    if last:
        outs.append(jax.ShapeDtypeStruct((modes, channels), F32))
    inputs = 1 + len(tokens) * pieces
    return call(
        functools.partial(signal_stage, pieces, len(tokens), first, last, row, taps),
        "signal_stage",
        [place],
        [part for chunk in tokens for part in chunk] + list(before) + [gain, w_in, w_short, rate],
        outs,
        [
            pltpu.VMEM((read, features), F32),
            pltpu.VMEM((halo + rows, min(BLOCK, channels)), F32),
        ],
        aliases={} if first else {inputs + k: k for k in range(3)},
    )


def run_local(row, rows, taps, normed, signal, states, w_in, w_short, rate, mode, skip):
    channels = signal.shape[1]
    out = jax.ShapeDtypeStruct((rows, channels), F32)
    begin = jax.ShapeDtypeStruct(states.shape, F32)
    return call(
        functools.partial(local_stage, row, rows, taps),
        "local_stage",
        [],
        [normed, signal, states, w_in, w_short, rate, mode, skip],
        [out, out] + ([begin] if row == 0 else []),
        [pltpu.VMEM((rows + ROWS * (taps - 1), min(BLOCK, channels)), F32)],
    )


def run_second(pieces, row, rows, shift, count, place, q, local, begin, marks, carry, rate, mode, w):
    channels, features = w.shape
    share = features // pieces
    return call(
        functools.partial(second_stage, pieces, row, rows, shift, count // ROWS),
        "second_stage",
        [place],
        [q, local, begin, marks, carry, rate, mode, w],
        [
            jax.ShapeDtypeStruct((max(1, pieces - 1) * rows, share), BF16),
            jax.ShapeDtypeStruct((rows, share), F32),
        ],
        [pltpu.VMEM((rows, channels), F32)],
    )


def run_last(pieces, sizes, row, own, came, done, count):
    share = own[0].shape[1]
    rows = sum(sizes)
    (out,) = call(
        functools.partial(last_stage, pieces, sizes, row, bool(done)),
        "last_stage",
        [],
        [*own, *came, *done],
        [jax.ShapeDtypeStruct((share, count), BF16 if row + rows == count else F32)],
        [pltpu.VMEM((rows, share), BF16)],
    )
    return out


def rotate(value, axis, steps):
    count = lax.axis_size(axis)
    return lax.ppermute(value, axis, [((i + steps) % count, i) for i in range(count)])


def combine_states(span, stride, radix, count, *refs):
    place_ref, rate_ref, total_ref = refs[:3]
    others = refs[3 : 2 + radix]
    refs = refs[2 + radix :]
    carry_in = refs[0] if stride > 1 else None
    carry_ref = refs[1] if stride > 1 else refs[0]
    position = place_ref[1]
    digit = lax.rem(lax.div(position, stride), radix)
    inner = lax.rem(position, stride)
    unit = span * stride
    rate = rate_ref[...]
    before = jnp.zeros(rate.shape, F32)
    for shift in range(1, radix):
        reached = jnp.where(digit >= shift, 1.0, 0.0)
        before = before + jnp.exp(-rate * (unit * (shift - 1))) * (others[shift - 1][...] * reached)
    if stride > 1:
        carry_ref[...] = carry_in[...] + jnp.exp(-rate * (span * inner).astype(F32)) * before
    else:
        carry_ref[...] = before
    if stride * radix < count:
        new = jnp.exp(-rate * (unit * (radix - 1 - digit)).astype(F32)) * total_ref[...]
        for shift in range(1, radix):
            at = lax.rem(digit - shift + radix, radix)
            weight = jnp.exp(-rate * (unit * (radix - 1 - at)).astype(F32))
            new = new + weight * others[shift - 1][...]
        refs[-1][...] = new


def carried_in(state, rate, span, axis, place, between):
    count = lax.axis_size(axis)
    total, stride, carry = state, 1, []
    while stride < count:
        radix = 4 if count % (stride * 4) == 0 else 2
        assert count % (stride * radix) == 0
        group = stride * radix
        others = []
        for shift in range(1, radix):
            pairs = []
            for i in range(count):
                digit = (i // stride) % radix
                pairs.append((i + ((digit - shift) % radix - digit) * stride, i))
            others.append(lax.ppermute(total, axis, pairs))
        others = between(others)
        shape = jax.ShapeDtypeStruct(state.shape, F32)
        carry = call(
            functools.partial(combine_states, span, stride, radix, count),
            "combine_states",
            [place],
            [rate, total, *others, *carry],
            [shape] * (2 if group < count else 1),
            [],
        )
        if group < count:
            *carry, total = carry
        stride = group
    return carry[0]


def body(tokens, norm_gain, w_in, w_short, decay_rate, residue, skip_gain, w_out):
    pieces, count = lax.axis_size("tp"), lax.axis_size("ctx")
    share, rows = tokens.shape
    channels = w_in.shape[1]
    taps = w_short.shape[0]
    halo = ROWS * (taps - 1)
    sizes = [rows // CHUNKS] * CHUNKS
    bf16_rows = lambda size: jax.ShapeDtypeStruct((size, share), BF16)

    place = jnp.stack([lax.axis_index("tp"), lax.axis_index("ctx")]).astype(jnp.int32)
    tokens, place = lax.optimization_barrier((tokens, place))
    x0, edge = call(
        functools.partial(first_rows, halo), "first_rows", [], [tokens],
        [bf16_rows(halo + sizes[0]), bf16_rows(halo)], [],
    )
    edge = rotate(edge, "ctx", -1)
    x1, *others = call(
        functools.partial(next_rows, sizes[0]), "next_rows", [], [tokens],
        [bf16_rows(size) for size in sizes[1:]], [],
    )
    (x1,) = call(join_edge, "join_edge", [place], [edge, x1], [bf16_rows(halo + sizes[1])], [])
    x1, others = lax.optimization_barrier((x1, others))
    x = [x0, x1, *others]
    residue, norm_gain, skip_gain, *_ = lax.optimization_barrier((residue, norm_gain, skip_gain, *x))
    mode = residue * jnp.sqrt(-jnp.expm1(-2.0 * decay_rate))
    gain = norm_gain[None, :]
    skip = skip_gain[None, :]
    parts = [[part] + [rotate(part, "tp", s) for s in range(1, pieces)] for part in x]
    w_in, mode, gain, skip, *_ = lax.optimization_barrier((w_in, mode, gain, skip, *x))
    w_in = pltpu.with_memory_space_constraint(in_vmem(w_in), pltpu.VMEM)

    before, row = [], 0
    for group in [[0, 1]] + [[j] for j in range(2, CHUNKS)]:
        results = run_signal(
            pieces, row, rows, group[0] == 0, group[-1] == CHUNKS - 1, taps, place,
            [parts[j] for j in group], before, gain, w_in, w_short, decay_rate,
        )
        before = results[:5]
        row += sum(sizes[j] for j in group)
    normed, signal, marks, states, _ = before
    state, normed, signal, states = lax.optimization_barrier((results[5], normed, signal, states))
    out_sizes = [rows // 4, rows // 2, rows // 4]
    early = sum(out_sizes[:-1])
    small = [w_in, w_short, decay_rate, mode, skip]
    done, rounds = [], []

    def between(others):
        rounds.append(others)
        if len(rounds) == 2:
            done.extend(run_local(0, early, taps, normed, signal, states, *small))
            others, done[:] = lax.optimization_barrier((others, done[:]))
        return others

    carry = carried_in(state, decay_rate, rows, "ctx", place, between)
    if not done:
        done = run_local(0, early, taps, normed, signal, states, *small)
    q, local, begin = done
    own, came, row, shift = [], [], 0, 0
    for j, size in enumerate(out_sizes):
        if row == early:
            normed, signal, came[: pieces - 1] = lax.optimization_barrier(
                (normed, signal, came[: pieces - 1])
            )
            q, local = run_local(early, rows - early, taps, normed, signal, states, *small)
            shift = early
        send, kept = run_second(
            pieces, row, size, shift, rows, place, q, local, begin, marks, carry, decay_rate, mode,
            w_out,
        )
        own.append(kept)
        for s in range(1, pieces):
            came.append(rotate(send[(s - 1) * size : s * size], "tp", -s))
        row += size
    cut = (len(out_sizes) - 1) * (pieces - 1)
    done = run_last(pieces, out_sizes[:-1], 0, own[:-1], came[:cut], [], rows)
    return run_last(pieces, out_sizes[-1:], early, own[-1:], came[cut:], [done], rows)


def solution(mesh):
    placed = (
        P("tp", "ctx"),
        P(),
        P(None, "tp", None),
        P(None, None, "tp"),
        P(None, "tp"),
        P(None, "tp"),
        P("tp"),
        P("tp", None),
    )
    return jax.shard_map(
        body, mesh=mesh, in_specs=placed, out_specs=P("tp", "ctx"), check_vma=False
    )
```

```python
import functools

import jax
import jax.numpy as jnp
from jax import lax
from jax.experimental import pallas as pl
from jax.experimental.pallas import tpu as pltpu
from jax.sharding import PartitionSpec as P


F32 = jnp.float32
BF16 = jnp.bfloat16
ROWS = 8
LANES = 128
BLOCK = 256
CHUNKS = 4
SPAN = 16
VMEM_LIMIT = 10 * 2**20
CONTRACT_LAST = (((1,), (1,)), ((), ()))
CONTRACT_FIRST = (((0,), (0,)), ((), ()))


def lane_groups(low, width):
    return [(start, min(LANES, low + width - start)) for start in range(low, low + width, LANES)]


def rows_as(row, width):
    return jnp.broadcast_to(row, (ROWS, width))


def tree_sum(terms):
    while len(terms) > 1:
        terms = [sum(terms[k + 1 : k + 2], terms[k]) for k in range(0, len(terms), 2)]
    return terms[0]


def token_picker(first_row, rows, tokens):
    length = tokens // ROWS
    row = lax.broadcasted_iota(jnp.int32, (rows, tokens), 0)
    column = lax.broadcasted_iota(jnp.int32, (rows, tokens), 1)
    wanted = lax.rem(row, ROWS) * length + lax.div(row, ROWS) + first_row // ROWS
    return jnp.where(column == wanted, 1.0, 0.0).astype(BF16)


def turned(pick, tokens):
    return lax.dot_general(pick, tokens, CONTRACT_LAST, preferred_element_type=F32).astype(BF16)


def first_rows(halo, tokens_ref, out_ref, edge_ref):
    tokens = tokens_ref.shape[1]
    out_ref[...] = turned(token_picker(-halo, out_ref.shape[0], tokens), tokens_ref[...])
    row = lax.broadcasted_iota(jnp.int32, (halo, tokens), 0)
    column = lax.broadcasted_iota(jnp.int32, (halo, tokens), 1)
    wanted = jnp.where(lax.rem(row, ROWS) == 0, tokens - halo // ROWS + lax.div(row, ROWS), -1)
    edge_ref[...] = turned(jnp.where(column == wanted, 1.0, 0.0).astype(BF16), tokens_ref[...])


def next_rows(row, tokens_ref, *chunk_refs):
    tokens = tokens_ref.shape[1]
    for ref in chunk_refs:
        ref[...] = turned(token_picker(row, ref.shape[0], tokens), tokens_ref[...])
        row += ref.shape[0]


def join_edge(edge_ref, chunk_ref, out_ref):
    halo = edge_ref.shape[0]
    out_ref[:halo, :] = edge_ref[...]
    out_ref[halo:, :] = chunk_ref[...]


def load_weights(places, w_hbm, out_ref, w_ref, sem):
    copies = [
        pltpu.make_async_copy(w_hbm.at[place], w_ref.at[place], sem.at[k])
        for k, place in enumerate(places)
    ]
    for copy in copies:
        copy.start()
    for (s, part), copy in zip(places, copies):
        copy.wait()
        out_ref[s, :, part] = w_ref[s, part, :].T


def short_conv(p_ref, short_ref, s, part, rows, taps):
    width = part.stop - part.start
    total = None
    for offset in range(taps):
        start = ROWS * (taps - 1 - offset)
        term = short_ref[offset, s : s + 1, part] * p_ref[start : start + rows, :width]
        total = term if total is None else total + term
    return total


def project(normed, w_ref, s, part):
    product = jnp.dot(normed, w_ref[s, :, part], preferred_element_type=F32)
    return product.astype(BF16).astype(F32)


def signal_stage(pieces, chunks, first, last, row, taps, *refs):
    refs = list(refs)
    me_ref = refs.pop(0)
    token_refs = [[refs.pop(0) for _ in range(pieces)] for _ in range(chunks)]
    if not first:
        _, _, _, states_in, tail_in = [refs.pop(0) for _ in range(5)]
    gain_ref, w_ref, short_ref, rate_ref = refs[:4]
    normed_ref, signal_ref, marks_ref, states_ref, tail_ref = refs[4:9]
    total_ref = refs[9] if last else None
    x_ref, p_ref = refs[-2:]
    halo = ROWS * (taps - 1)
    modes, channels = rate_ref.shape
    read, share = x_ref.shape[0], token_refs[0][0].shape[1]
    rows = read - halo if first else read
    length = signal_ref.shape[0] // ROWS
    me = me_ref[0]

    values = []
    for s in range(pieces):
        value = [refs_of[s][...].astype(F32) for refs_of in token_refs]
        if first:
            front, edge = value[0][:halo], value[-1][:halo]
            value = [front + edge, value[0][halo:], *value[1:-1], value[-1][halo:]]
        values.append(jnp.concatenate(value, axis=0) if len(value) > 1 else value[0])
    for rank in range(pieces):
        chosen = values[0]
        for s in range(1, pieces):
            chosen = jnp.where(me == (rank - s) % pieces, values[s], chosen)
        x_ref[:, rank * share : (rank + 1) * share] = chosen
    features = x_ref[...]
    mean = jnp.mean(features * features, axis=1, keepdims=True)
    normed = (features * lax.rsqrt(mean + 1e-06) * gain_ref[...]).astype(BF16)
    begin = 0 if first else halo + row
    normed_ref[begin : begin + read, :] = normed

    for low in range(0, channels, BLOCK):
        width = min(BLOCK, channels - low)
        part = slice(low, low + width)
        for s in (1, 2):
            if not first:
                p_ref[:halo, :width] = tail_in[s - 1, :, part]
            p_ref[halo + rows - read :, :width] = project(
                normed_ref[begin : begin + read, :], w_ref, s, part
            )
            tail_ref[s - 1, :, part] = p_ref[rows:, :width]
            short = short_conv(p_ref, short_ref, s, part, rows, taps)
            if s == 1:
                signal_ref[row : row + rows, part] = short
            else:
                signal_ref[row : row + rows, part] = signal_ref[row : row + rows, part] * short
        for start, size in lane_groups(low, width):
            lanes = slice(start, start + size)
            rate = [rows_as(rate_ref[n : n + 1, lanes], size) for n in range(modes)]
            decay = [jnp.exp(-r) for r in rate]

            if first:
                states = (jnp.zeros((ROWS, size), F32),) * modes
            else:
                states = tuple(states_in[n, :, lanes] for n in range(modes))
            for at in range(row, row + rows, SPAN * ROWS):
                mark = at // (SPAN * ROWS)
                for n in range(modes):
                    marks_ref[mark, n, :, lanes] = states[n]

                def step(i, states):
                    here = pl.ds(pl.multiple_of(at + i * ROWS, ROWS), ROWS)
                    now = signal_ref[here, lanes]
                    return tuple(states[n] * decay[n] + now for n in range(modes))

                states = lax.fori_loop(0, SPAN, step, states, unroll=8)
            for n in range(modes):
                states_ref[n, :, lanes] = states[n]
            if last:
                left = lax.broadcasted_iota(jnp.int32, (ROWS, size), 0)
                left = ((ROWS - 1 - left) * length).astype(F32)
                for n in range(modes):
                    total_ref[n : n + 1, lanes] = jnp.sum(
                        states[n] * jnp.exp(-rate[n] * left), axis=0, keepdims=True
                    )


def local_stage(row, rows, taps, *refs):
    normed_ref, signal_ref, states_ref, w_ref, short_ref, rate_ref, mode_ref, skip_ref = refs[:8]
    q_ref, local_ref = refs[8:10]
    begin_ref = refs[10] if row == 0 else None
    p_ref = refs[-1]
    modes, channels = rate_ref.shape
    length = signal_ref.shape[0] // ROWS
    for low in range(0, channels, BLOCK):
        width = min(BLOCK, channels - low)
        part = slice(low, low + width)
        normed = normed_ref[row : row + p_ref.shape[0], :]
        p_ref[:, :width] = project(normed, w_ref, 0, part)
        q_ref[:, part] = short_conv(p_ref, short_ref, 0, part, rows, taps)
        for start, size in lane_groups(low, width):
            lanes = slice(start, start + size)
            rate = [rows_as(rate_ref[n : n + 1, lanes], size) for n in range(modes)]
            segment = lax.broadcasted_iota(jnp.int32, (ROWS, size), 0)
            if row == 0:
                for n in range(modes):
                    run = states_ref[n, :, lanes]
                    for hop in (1, 2, 4):
                        weight = jnp.where(segment >= hop, jnp.exp(-rate[n] * (hop * length)), 0.0)
                        run = run + weight * pltpu.roll(run, hop, 0)
                    begin_ref[n, :, lanes] = jnp.where(segment >= 1, pltpu.roll(run, 1, 0), 0.0)
            lag = segment.astype(F32)
            filters = []
            for first_lag in range(0, SPAN, ROWS):
                values = tree_sum(
                    [
                        rows_as(mode_ref[n : n + 1, lanes], size)
                        * jnp.exp(-rate[n] * (lag + first_lag))
                        for n in range(modes)
                    ]
                )
                filters += [rows_as(values[j : j + 1, :], size) for j in range(ROWS)]
            filters[0] = filters[0] + skip_ref[:, lanes]

            def span(i, carry):
                base = i * (SPAN * ROWS)
                now = [
                    signal_ref[pl.ds(pl.multiple_of(row + base + k * ROWS, ROWS), ROWS), lanes]
                    for k in range(SPAN)
                ]
                for k in range(SPAN):
                    local_ref[pl.ds(pl.multiple_of(base + k * ROWS, ROWS), ROWS), lanes] = tree_sum(
                        [filters[j] * now[k - j] for j in range(k + 1)]
                    )
                return carry

            lax.fori_loop(0, rows // (SPAN * ROWS), span, 0)


def second_stage(pieces, row, rows, length, *refs):
    me_ref, q_ref, local_ref, begin_ref, marks_ref, carry_ref, rate_ref, mode_ref, w_ref = refs[:9]
    send_ref, own_ref, gated_ref = refs[9:]
    modes, channels = rate_ref.shape
    for start, size in lane_groups(0, channels):
        lanes = slice(start, start + size)
        rate = [rows_as(rate_ref[n : n + 1, lanes], size) for n in range(modes)]
        decay = [jnp.exp(-r) for r in rate]
        segment = lax.broadcasted_iota(jnp.int32, (ROWS, size), 0)
        past = (segment * length).astype(F32)
        for at in range(row, row + rows, SPAN * ROWS):
            mark = at // (SPAN * ROWS)
            states = []
            for n in range(modes):
                state = begin_ref[n, :, lanes] + jnp.exp(-rate[n] * past) * carry_ref[
                    n : n + 1, lanes
                ]
                if mark > 0:
                    state = marks_ref[mark, n, :, lanes] + state * jnp.exp(-rate[n] * (SPAN * mark))
                states.append(mode_ref[n : n + 1, lanes] * state)

            def step(i, states):
                here = pl.ds(pl.multiple_of(at - row + i * ROWS, ROWS), ROWS)
                states = tuple(states[n] * decay[n] for n in range(modes))
                gated_ref[here, lanes] = q_ref[here, lanes] * tree_sum(
                    [local_ref[here, lanes]] + list(states)
                )
                return states

            lax.fori_loop(0, SPAN, step, tuple(states), unroll=4)
    product = jnp.dot(gated_ref[...].astype(BF16), w_ref[...], preferred_element_type=F32)
    share = own_ref.shape[1]
    me = me_ref[0]
    columns = [product[:, rank * share : (rank + 1) * share] for rank in range(pieces)]
    for s in range(pieces):
        chosen = columns[0]
        for rank in range(1, pieces):
            chosen = jnp.where(me == (rank - s) % pieces, columns[rank], chosen)
        if s == 0:
            own_ref[...] = chosen
        else:
            send_ref[(s - 1) * rows : s * rows, :] = chosen.astype(BF16)


def last_stage(pieces, sizes, row, more, *refs):
    chunks = len(sizes)
    own_refs, came_refs = refs[:chunks], refs[chunks : chunks * pieces]
    done_ref = refs[chunks * pieces] if more else None
    out_ref, mixed_ref = refs[-2:]
    at = 0
    for j, size in enumerate(sizes):
        total = own_refs[j][...]
        for s in range(pieces - 1):
            total = total + came_refs[j * (pieces - 1) + s][...].astype(F32)
        mixed_ref[at : at + size, :] = total.astype(BF16)
        at += size
    pick = token_picker(row, at, out_ref.shape[1])
    out = lax.dot_general(mixed_ref[...], pick, CONTRACT_FIRST, preferred_element_type=F32)
    if more:
        out = out + done_ref[...]
    out_ref[...] = out.astype(out_ref.dtype)


def call(kernel, name, scalars, operands, outs, scratch, aliases={}):
    vmem = pl.BlockSpec(memory_space=pltpu.VMEM)
    smem = pl.BlockSpec(memory_space=pltpu.SMEM)
    return pl.pallas_call(
        kernel,
        out_shape=outs,
        in_specs=[smem] * len(scalars) + [vmem] * len(operands),
        out_specs=[vmem] * len(outs),
        scratch_shapes=scratch,
        input_output_aliases=aliases,
        compiler_params=pltpu.CompilerParams(vmem_limit_bytes=VMEM_LIMIT),
        cost_estimate=pl.CostEstimate(flops=1, bytes_accessed=1, transcendentals=0),
        name=name,
    )(*scalars, *operands)


def in_vmem(w):
    streams, channels, features = w.shape
    block = min(BLOCK, channels)
    places = [
        (s, slice(low, min(low + block, channels)))
        for s in (1, 2, 0)
        for low in range(0, channels, block)
    ]
    return pl.pallas_call(
        functools.partial(load_weights, places),
        out_shape=pltpu.VMEM((streams, features, channels), w.dtype),
        in_specs=[pl.BlockSpec(memory_space=pl.ANY)],
        out_specs=pl.BlockSpec(memory_space=pltpu.VMEM),
        scratch_shapes=[
            pltpu.VMEM(w.shape, w.dtype),
            pltpu.SemaphoreType.DMA((len(places),)),
        ],
        compiler_params=pltpu.CompilerParams(vmem_limit_bytes=46 * 2**20),
        cost_estimate=pl.CostEstimate(flops=1, bytes_accessed=1, transcendentals=0),
        name="load_weights",
    )(w)


def run_signal(pieces, row, count, first, last, taps, place, tokens, before, gain, w_in, w_short, rate):
    streams, features, channels = w_in.shape
    modes = rate.shape[0]
    halo = ROWS * (taps - 1)
    read = sum(chunk[0].shape[0] for chunk in tokens) - (halo if first else 0)
    rows = read - halo if first else read
    outs = [
        jax.ShapeDtypeStruct((halo + count, features), BF16),
        jax.ShapeDtypeStruct((count, channels), F32),
        jax.ShapeDtypeStruct((count // (SPAN * ROWS), modes, ROWS, channels), F32),
        jax.ShapeDtypeStruct((modes, ROWS, channels), F32),
        jax.ShapeDtypeStruct((streams - 1, halo, channels), F32),
    ]
    if last:
        outs.append(jax.ShapeDtypeStruct((modes, channels), F32))
    inputs = 1 + len(tokens) * pieces
    return call(
        functools.partial(signal_stage, pieces, len(tokens), first, last, row, taps),
        "signal_stage",
        [place],
        [part for chunk in tokens for part in chunk] + list(before) + [gain, w_in, w_short, rate],
        outs,
        [
            pltpu.VMEM((read, features), F32),
            pltpu.VMEM((halo + rows, min(BLOCK, channels)), F32),
        ],
        aliases={} if first else {inputs + k: k for k in range(3)},
    )


def run_local(row, rows, taps, normed, signal, states, w_in, w_short, rate, mode, skip):
    channels = signal.shape[1]
    out = jax.ShapeDtypeStruct((rows, channels), F32)
    begin = jax.ShapeDtypeStruct(states.shape, F32)
    return call(
        functools.partial(local_stage, row, rows, taps),
        "local_stage",
        [],
        [normed, signal, states, w_in, w_short, rate, mode, skip],
        [out, out] + ([begin] if row == 0 else []),
        [pltpu.VMEM((rows + ROWS * (taps - 1), min(BLOCK, channels)), F32)],
    )


def run_second(pieces, row, rows, count, place, q, local, begin, marks, carry, rate, mode, w):
    channels, features = w.shape
    share = features // pieces
    return call(
        functools.partial(second_stage, pieces, row, rows, count // ROWS),
        "second_stage",
        [place],
        [q, local, begin, marks, carry, rate, mode, w],
        [
            jax.ShapeDtypeStruct((max(1, pieces - 1) * rows, share), BF16),
            jax.ShapeDtypeStruct((rows, share), F32),
        ],
        [pltpu.VMEM((rows, channels), F32)],
    )


def run_last(pieces, sizes, row, own, came, done, count):
    share = own[0].shape[1]
    rows = sum(sizes)
    (out,) = call(
        functools.partial(last_stage, pieces, sizes, row, bool(done)),
        "last_stage",
        [],
        [*own, *came, *done],
        [jax.ShapeDtypeStruct((share, count), BF16 if row + rows == count else F32)],
        [pltpu.VMEM((rows, share), BF16)],
    )
    return out


def rotate(value, axis, steps):
    count = lax.axis_size(axis)
    return lax.ppermute(value, axis, [((i + steps) % count, i) for i in range(count)])


def combine_states(span, stride, radix, count, *refs):
    place_ref, rate_ref, total_ref = refs[:3]
    others = refs[3 : 2 + radix]
    refs = refs[2 + radix :]
    carry_in = refs[0] if stride > 1 else None
    carry_ref = refs[1] if stride > 1 else refs[0]
    position = place_ref[1]
    digit = lax.rem(lax.div(position, stride), radix)
    inner = lax.rem(position, stride)
    unit = span * stride
    rate = rate_ref[...]
    before = jnp.zeros(rate.shape, F32)
    for shift in range(1, radix):
        reached = jnp.where(digit >= shift, 1.0, 0.0)
        before = before + jnp.exp(-rate * (unit * (shift - 1))) * (others[shift - 1][...] * reached)
    if stride > 1:
        carry_ref[...] = carry_in[...] + jnp.exp(-rate * (span * inner).astype(F32)) * before
    else:
        carry_ref[...] = before
    if stride * radix < count:
        new = jnp.exp(-rate * (unit * (radix - 1 - digit)).astype(F32)) * total_ref[...]
        for shift in range(1, radix):
            at = lax.rem(digit - shift + radix, radix)
            weight = jnp.exp(-rate * (unit * (radix - 1 - at)).astype(F32))
            new = new + weight * others[shift - 1][...]
        refs[-1][...] = new


def carried_in(state, rate, span, axis, place, between):
    count = lax.axis_size(axis)
    total, stride, carry = state, 1, []
    while stride < count:
        radix = 4 if count % (stride * 4) == 0 else 2
        assert count % (stride * radix) == 0
        group = stride * radix
        others = []
        for shift in range(1, radix):
            pairs = []
            for i in range(count):
                digit = (i // stride) % radix
                pairs.append((i + ((digit - shift) % radix - digit) * stride, i))
            others.append(lax.ppermute(total, axis, pairs))
        others = between(others)
        shape = jax.ShapeDtypeStruct(state.shape, F32)
        carry = call(
            functools.partial(combine_states, span, stride, radix, count),
            "combine_states",
            [place],
            [rate, total, *others, *carry],
            [shape] * (2 if group < count else 1),
            [],
        )
        if group < count:
            *carry, total = carry
        stride = group
    return carry[0]


def body(tokens, norm_gain, w_in, w_short, decay_rate, residue, skip_gain, w_out):
    pieces, count = lax.axis_size("tp"), lax.axis_size("ctx")
    share, rows = tokens.shape
    channels = w_in.shape[1]
    taps = w_short.shape[0]
    halo = ROWS * (taps - 1)
    sizes = [rows // CHUNKS] * CHUNKS
    bf16_rows = lambda size: jax.ShapeDtypeStruct((size, share), BF16)

    place = jnp.stack([lax.axis_index("tp"), lax.axis_index("ctx")]).astype(jnp.int32)
    tokens, place = lax.optimization_barrier((tokens, place))
    x0, edge = call(
        functools.partial(first_rows, halo), "first_rows", [], [tokens],
        [bf16_rows(halo + sizes[0]), bf16_rows(halo)], [],
    )
    edge = lax.ppermute(edge, "ctx", [(i, i + 1) for i in range(lax.axis_size("ctx") - 1)])
    x1, *others = call(
        functools.partial(next_rows, sizes[0]), "next_rows", [], [tokens],
        [bf16_rows(size) for size in sizes[1:]], [],
    )
    (x1,) = call(join_edge, "join_edge", [], [edge, x1], [bf16_rows(halo + sizes[1])], [])
    x1, others = lax.optimization_barrier((x1, others))
    x = [x0, x1, *others]
    residue, norm_gain, skip_gain, *_ = lax.optimization_barrier((residue, norm_gain, skip_gain, *x))
    mode = residue * jnp.sqrt(-jnp.expm1(-2.0 * decay_rate))
    gain = norm_gain[None, :]
    skip = skip_gain[None, :]
    parts = [[part] + [rotate(part, "tp", s) for s in range(1, pieces)] for part in x]
    w_in, mode, gain, skip, *_ = lax.optimization_barrier((w_in, mode, gain, skip, *x))
    w_in = pltpu.with_memory_space_constraint(in_vmem(w_in), pltpu.VMEM)

    before, row = [], 0
    for group in [[0, 1]] + [[j] for j in range(2, CHUNKS)]:
        results = run_signal(
            pieces, row, rows, group[0] == 0, group[-1] == CHUNKS - 1, taps, place,
            [parts[j] for j in group], before, gain, w_in, w_short, decay_rate,
        )
        before = results[:5]
        row += sum(sizes[j] for j in group)
    normed, signal, marks, states, _ = before
    state, normed, signal, states = lax.optimization_barrier((results[5], normed, signal, states))
    out_sizes = [rows // 4, rows // 2, rows // 4]
    out_rows = [0, rows // 4, 3 * rows // 4]
    small = [w_in, w_short, decay_rate, mode, skip]
    done = []

    def local_part():
        k = len(done)
        done.append(run_local(out_rows[k], out_sizes[k], taps, normed, signal, states, *small))

    def between(others):
        if len(done) < 2:
            local_part()
            others, done[-1] = lax.optimization_barrier((others, done[-1]))
        return others

    carry = carried_in(state, decay_rate, rows, "ctx", place, between)
    while len(done) < 2:
        local_part()
    begin = done[0][2]
    own, came = [], []
    for j in range(len(out_sizes)):
        if j == 2:
            normed, signal, came[: pieces - 1] = lax.optimization_barrier(
                (normed, signal, came[: pieces - 1])
            )
            local_part()
        send, kept = run_second(
            pieces, out_rows[j], out_sizes[j], rows, place, *done[j][:2], begin, marks, carry,
            decay_rate, mode, w_out,
        )
        own.append(kept)
        for s in range(1, pieces):
            came.append(rotate(send[(s - 1) * out_sizes[j] : s * out_sizes[j]], "tp", -s))
    early = out_rows[-1]
    cut = (len(out_sizes) - 1) * (pieces - 1)
    done = run_last(pieces, out_sizes[:-1], 0, own[:-1], came[:cut], [], rows)
    return run_last(pieces, out_sizes[-1:], early, own[-1:], came[cut:], [done], rows)


def solution(mesh):
    placed = (
        P("tp", "ctx"),
        P(),
        P(None, "tp", None),
        P(None, None, "tp"),
        P(None, "tp"),
        P(None, "tp"),
        P("tp"),
        P("tp", None),
    )
    return jax.shard_map(
        body, mesh=mesh, in_specs=placed, out_specs=P("tp", "ctx"), check_vma=False
    )
```

```python
import functools

import jax
import jax.numpy as jnp
from jax import lax
from jax.experimental import pallas as pl
from jax.experimental.pallas import tpu as pltpu
from jax.sharding import PartitionSpec as P


F32 = jnp.float32
BF16 = jnp.bfloat16
ROWS = 8
LANES = 128
BLOCK = 256
CHUNKS = 4
SPAN = 16
VMEM_LIMIT = 10 * 2**20
CONTRACT_LAST = (((1,), (1,)), ((), ()))
CONTRACT_FIRST = (((0,), (0,)), ((), ()))


def lane_groups(low, width):
    return [(start, min(LANES, low + width - start)) for start in range(low, low + width, LANES)]


def rows_as(row, width):
    return jnp.broadcast_to(row, (ROWS, width))


def tree_sum(terms):
    while len(terms) > 1:
        terms = [sum(terms[k + 1 : k + 2], terms[k]) for k in range(0, len(terms), 2)]
    return terms[0]


def token_picker(first_row, rows, tokens):
    length = tokens // ROWS
    row = lax.broadcasted_iota(jnp.int32, (rows, tokens), 0)
    column = lax.broadcasted_iota(jnp.int32, (rows, tokens), 1)
    wanted = lax.rem(row, ROWS) * length + lax.div(row, ROWS) + first_row // ROWS
    return jnp.where(column == wanted, 1.0, 0.0).astype(BF16)


def turned(pick, tokens):
    return lax.dot_general(pick, tokens, CONTRACT_LAST, preferred_element_type=F32).astype(BF16)


def first_rows(halo, tokens_hbm, out_ref, edge_ref, tokens_ref, sem):
    share, tokens = tokens_ref.shape
    parts = [slice(low, min(low + BLOCK, share)) for low in range(0, share, BLOCK)]
    copies = [
        pltpu.make_async_copy(tokens_hbm.at[part], tokens_ref.at[part], sem.at[k])
        for k, part in enumerate(parts)
    ]
    for copy in copies:
        copy.start()
    pick = token_picker(-halo, out_ref.shape[0], tokens)
    row = lax.broadcasted_iota(jnp.int32, (halo, tokens), 0)
    column = lax.broadcasted_iota(jnp.int32, (halo, tokens), 1)
    wanted = jnp.where(lax.rem(row, ROWS) == 0, tokens - halo // ROWS + lax.div(row, ROWS), -1)
    pick = jnp.concatenate([pick, jnp.where(column == wanted, 1.0, 0.0).astype(BF16)], axis=0)
    rows = out_ref.shape[0]
    for part, copy in zip(parts, copies):
        copy.wait()
        picked = turned(pick, tokens_ref[part, :])
        out_ref[:, part] = picked[:rows]
        edge_ref[:, part] = picked[rows:]


def next_rows(row, tokens_ref, *chunk_refs):
    tokens = tokens_ref.shape[1]
    for ref in chunk_refs:
        ref[...] = turned(token_picker(row, ref.shape[0], tokens), tokens_ref[...])
        row += ref.shape[0]


def join_edge(place_ref, edge_ref, chunk_ref, out_ref):
    halo = edge_ref.shape[0]
    preceded = jnp.where(place_ref[1] > 0, 1.0, 0.0)
    out_ref[:halo, :] = (edge_ref[...].astype(F32) * preceded).astype(BF16)
    out_ref[halo:, :] = chunk_ref[...]


def load_weights(places, w_hbm, out_ref, w_ref, sem):
    copies = [
        pltpu.make_async_copy(w_hbm.at[place], w_ref.at[place], sem.at[k])
        for k, place in enumerate(places)
    ]
    for copy in copies:
        copy.start()
    for (s, part), copy in zip(places, copies):
        copy.wait()
        out_ref[s, :, part] = w_ref[s, part, :].T


def short_conv(p_ref, short_ref, s, part, rows, taps):
    width = part.stop - part.start
    total = None
    for offset in range(taps):
        start = ROWS * (taps - 1 - offset)
        term = short_ref[offset, s : s + 1, part] * p_ref[start : start + rows, :width]
        total = term if total is None else total + term
    return total


def project(normed, w_ref, s, part):
    product = jnp.dot(normed, w_ref[s, :, part], preferred_element_type=F32)
    return product.astype(BF16).astype(F32)


def signal_stage(pieces, chunks, first, last, row, taps, *refs):
    refs = list(refs)
    me_ref = refs.pop(0)
    token_refs = [[refs.pop(0) for _ in range(pieces)] for _ in range(chunks)]
    if not first:
        _, _, _, states_in, tail_in = [refs.pop(0) for _ in range(5)]
    gain_ref, w_ref, short_ref, rate_ref = refs[:4]
    normed_ref, signal_ref, marks_ref, states_ref, tail_ref = refs[4:9]
    total_ref, sent_ref = refs[9:11] if last else (None, None)
    x_ref, p_ref = refs[-2:]
    halo = ROWS * (taps - 1)
    modes, channels = rate_ref.shape
    read, share = x_ref.shape[0], token_refs[0][0].shape[1]
    rows = read - halo if first else read
    length = signal_ref.shape[0] // ROWS
    me = me_ref[0]

    values = []
    for s in range(pieces):
        value = [refs_of[s][...].astype(F32) for refs_of in token_refs]
        if first:
            front, edge = value[0][:halo], value[-1][:halo]
            value = [front + edge, value[0][halo:], *value[1:-1], value[-1][halo:]]
        values.append(jnp.concatenate(value, axis=0) if len(value) > 1 else value[0])
    for rank in range(pieces):
        chosen = values[0]
        for s in range(1, pieces):
            chosen = jnp.where(me == (rank - s) % pieces, values[s], chosen)
        x_ref[:, rank * share : (rank + 1) * share] = chosen
    features = x_ref[...]
    mean = jnp.mean(features * features, axis=1, keepdims=True)
    normed = (features * lax.rsqrt(mean + 1e-06) * gain_ref[...]).astype(BF16)
    begin = 0 if first else halo + row
    normed_ref[begin : begin + read, :] = normed

    for low in range(0, channels, BLOCK):
        width = min(BLOCK, channels - low)
        part = slice(low, low + width)
        for s in (1, 2):
            if not first:
                p_ref[:halo, :width] = tail_in[s - 1, :, part]
            p_ref[halo + rows - read :, :width] = project(
                normed_ref[begin : begin + read, :], w_ref, s, part
            )
            tail_ref[s - 1, :, part] = p_ref[rows:, :width]
            short = short_conv(p_ref, short_ref, s, part, rows, taps)
            if s == 1:
                signal_ref[row : row + rows, part] = short
            else:
                signal_ref[row : row + rows, part] = signal_ref[row : row + rows, part] * short
        for start, size in lane_groups(low, width):
            lanes = slice(start, start + size)
            rate = [rows_as(rate_ref[n : n + 1, lanes], size) for n in range(modes)]
            decay = [jnp.exp(-r) for r in rate]

            if first:
                states = (jnp.zeros((ROWS, size), F32),) * modes
            else:
                states = tuple(states_in[n, :, lanes] for n in range(modes))
            for at in range(row, row + rows, SPAN * ROWS):
                mark = at // (SPAN * ROWS)
                for n in range(modes):
                    marks_ref[mark, n, :, lanes] = states[n]

                def step(i, states):
                    here = pl.ds(pl.multiple_of(at + i * ROWS, ROWS), ROWS)
                    now = signal_ref[here, lanes]
                    return tuple(states[n] * decay[n] + now for n in range(modes))

                states = lax.fori_loop(0, SPAN, step, states, unroll=8)
            for n in range(modes):
                states_ref[n, :, lanes] = states[n]
            if last:
                left = lax.broadcasted_iota(jnp.int32, (ROWS, size), 0)
                left = ((ROWS - 1 - left) * length).astype(F32)
                for n in range(modes):
                    total_ref[n : n + 1, lanes] = jnp.sum(
                        states[n] * jnp.exp(-rate[n] * left), axis=0, keepdims=True
                    )
                sent_ref[:, lanes] = total_ref[:, lanes].astype(BF16)


def local_stage(row, rows, taps, *refs):
    normed_ref, signal_ref, states_ref, w_ref, short_ref, rate_ref, mode_ref, skip_ref = refs[:8]
    q_ref, local_ref = refs[8:10]
    begin_ref = refs[10] if row == 0 else None
    p_ref = refs[-1]
    modes, channels = rate_ref.shape
    length = signal_ref.shape[0] // ROWS
    for low in range(0, channels, BLOCK):
        width = min(BLOCK, channels - low)
        part = slice(low, low + width)
        normed = normed_ref[row : row + p_ref.shape[0], :]
        p_ref[:, :width] = project(normed, w_ref, 0, part)
        q_ref[:, part] = short_conv(p_ref, short_ref, 0, part, rows, taps)
        for start, size in lane_groups(low, width):
            lanes = slice(start, start + size)
            rate = [rows_as(rate_ref[n : n + 1, lanes], size) for n in range(modes)]
            segment = lax.broadcasted_iota(jnp.int32, (ROWS, size), 0)
            if row == 0:
                for n in range(modes):
                    run = states_ref[n, :, lanes]
                    for hop in (1, 2, 4):
                        weight = jnp.where(segment >= hop, jnp.exp(-rate[n] * (hop * length)), 0.0)
                        run = run + weight * pltpu.roll(run, hop, 0)
                    begin_ref[n, :, lanes] = jnp.where(segment >= 1, pltpu.roll(run, 1, 0), 0.0)
            lag = segment.astype(F32)
            filters = []
            for first_lag in range(0, SPAN, ROWS):
                values = tree_sum(
                    [
                        rows_as(mode_ref[n : n + 1, lanes], size)
                        * jnp.exp(-rate[n] * (lag + first_lag))
                        for n in range(modes)
                    ]
                )
                filters += [rows_as(values[j : j + 1, :], size) for j in range(ROWS)]
            filters[0] = filters[0] + skip_ref[:, lanes]

            def span(i, carry):
                base = i * (SPAN * ROWS)
                now = [
                    signal_ref[pl.ds(pl.multiple_of(row + base + k * ROWS, ROWS), ROWS), lanes]
                    for k in range(SPAN)
                ]
                for k in range(SPAN):
                    local_ref[pl.ds(pl.multiple_of(base + k * ROWS, ROWS), ROWS), lanes] = tree_sum(
                        [filters[j] * now[k - j] for j in range(k + 1)]
                    )
                return carry

            lax.fori_loop(0, rows // (SPAN * ROWS), span, 0)


def second_stage(pieces, row, rows, length, *refs):
    me_ref, q_ref, local_ref, begin_ref, marks_ref, carry_ref, rate_ref, mode_ref, w_ref = refs[:9]
    send_ref, own_ref, gated_ref = refs[9:]
    modes, channels = rate_ref.shape
    for start, size in lane_groups(0, channels):
        lanes = slice(start, start + size)
        rate = [rows_as(rate_ref[n : n + 1, lanes], size) for n in range(modes)]
        decay = [jnp.exp(-r) for r in rate]
        segment = lax.broadcasted_iota(jnp.int32, (ROWS, size), 0)
        past = (segment * length).astype(F32)
        for at in range(row, row + rows, SPAN * ROWS):
            mark = at // (SPAN * ROWS)
            states = []
            for n in range(modes):
                state = begin_ref[n, :, lanes] + jnp.exp(-rate[n] * past) * carry_ref[
                    n : n + 1, lanes
                ]
                if mark > 0:
                    state = marks_ref[mark, n, :, lanes] + state * jnp.exp(-rate[n] * (SPAN * mark))
                states.append(mode_ref[n : n + 1, lanes] * state)

            def step(i, states):
                here = pl.ds(pl.multiple_of(at - row + i * ROWS, ROWS), ROWS)
                states = tuple(states[n] * decay[n] for n in range(modes))
                gated_ref[here, lanes] = q_ref[here, lanes] * tree_sum(
                    [local_ref[here, lanes]] + list(states)
                )
                return states

            lax.fori_loop(0, SPAN, step, tuple(states), unroll=4)
    product = jnp.dot(gated_ref[...].astype(BF16), w_ref[...], preferred_element_type=F32)
    share = own_ref.shape[1]
    me = me_ref[0]
    columns = [product[:, rank * share : (rank + 1) * share] for rank in range(pieces)]
    for s in range(pieces):
        chosen = columns[0]
        for rank in range(1, pieces):
            chosen = jnp.where(me == (rank - s) % pieces, columns[rank], chosen)
        if s == 0:
            own_ref[...] = chosen
        else:
            send_ref[(s - 1) * rows : s * rows, :] = chosen.astype(BF16)


def last_stage(pieces, sizes, row, more, *refs):
    chunks = len(sizes)
    own_refs, came_refs = refs[:chunks], refs[chunks : chunks * pieces]
    done_ref = refs[chunks * pieces] if more else None
    out_ref, mixed_ref = refs[-2:]
    at = 0
    for j, size in enumerate(sizes):
        total = own_refs[j][...]
        for s in range(pieces - 1):
            total = total + came_refs[j * (pieces - 1) + s][...].astype(F32)
        mixed_ref[at : at + size, :] = total.astype(BF16)
        at += size
    pick = token_picker(row, at, out_ref.shape[1])
    out = lax.dot_general(mixed_ref[...], pick, CONTRACT_FIRST, preferred_element_type=F32)
    if more:
        out = out + done_ref[...]
    out_ref[...] = out.astype(out_ref.dtype)


def call(kernel, name, scalars, operands, outs, scratch, aliases={}):
    vmem = pl.BlockSpec(memory_space=pltpu.VMEM)
    smem = pl.BlockSpec(memory_space=pltpu.SMEM)
    return pl.pallas_call(
        kernel,
        out_shape=outs,
        in_specs=[smem] * len(scalars) + [vmem] * len(operands),
        out_specs=[vmem] * len(outs),
        scratch_shapes=scratch,
        input_output_aliases=aliases,
        compiler_params=pltpu.CompilerParams(vmem_limit_bytes=VMEM_LIMIT),
        cost_estimate=pl.CostEstimate(flops=1, bytes_accessed=1, transcendentals=0),
        name=name,
    )(*scalars, *operands)


def run_first_rows(tokens, halo, size):
    share = tokens.shape[0]
    return pl.pallas_call(
        functools.partial(first_rows, halo),
        out_shape=[
            jax.ShapeDtypeStruct((halo + size, share), BF16),
            jax.ShapeDtypeStruct((halo, share), BF16),
        ],
        in_specs=[pl.BlockSpec(memory_space=pl.ANY)],
        out_specs=[pl.BlockSpec(memory_space=pltpu.VMEM)] * 2,
        scratch_shapes=[
            pltpu.VMEM(tokens.shape, BF16),
            pltpu.SemaphoreType.DMA((-(-share // BLOCK),)),
        ],
        compiler_params=pltpu.CompilerParams(vmem_limit_bytes=56 * 2**20),
        cost_estimate=pl.CostEstimate(flops=1, bytes_accessed=1, transcendentals=0),
        name="first_rows",
    )(tokens)


def in_vmem(w):
    streams, channels, features = w.shape
    block = min(BLOCK, channels)
    places = [
        (s, slice(low, min(low + block, channels)))
        for s in (1, 2, 0)
        for low in range(0, channels, block)
    ]
    return pl.pallas_call(
        functools.partial(load_weights, places),
        out_shape=pltpu.VMEM((streams, features, channels), w.dtype),
        in_specs=[pl.BlockSpec(memory_space=pl.ANY)],
        out_specs=pl.BlockSpec(memory_space=pltpu.VMEM),
        scratch_shapes=[
            pltpu.VMEM(w.shape, w.dtype),
            pltpu.SemaphoreType.DMA((len(places),)),
        ],
        compiler_params=pltpu.CompilerParams(vmem_limit_bytes=46 * 2**20),
        cost_estimate=pl.CostEstimate(flops=1, bytes_accessed=1, transcendentals=0),
        name="load_weights",
    )(w)


def run_signal(pieces, row, count, first, last, taps, place, tokens, before, gain, w_in, w_short, rate):
    streams, features, channels = w_in.shape
    modes = rate.shape[0]
    halo = ROWS * (taps - 1)
    read = sum(chunk[0].shape[0] for chunk in tokens) - (halo if first else 0)
    rows = read - halo if first else read
    outs = [
        jax.ShapeDtypeStruct((halo + count, features), BF16),
        jax.ShapeDtypeStruct((count, channels), F32),
        jax.ShapeDtypeStruct((count // (SPAN * ROWS), modes, ROWS, channels), F32),
        jax.ShapeDtypeStruct((modes, ROWS, channels), F32),
        jax.ShapeDtypeStruct((streams - 1, halo, channels), F32),
    ]
    if last:
        outs += [jax.ShapeDtypeStruct((modes, channels), kind) for kind in (F32, BF16)]
    inputs = 1 + len(tokens) * pieces
    return call(
        functools.partial(signal_stage, pieces, len(tokens), first, last, row, taps),
        "signal_stage",
        [place],
        [part for chunk in tokens for part in chunk] + list(before) + [gain, w_in, w_short, rate],
        outs,
        [
            pltpu.VMEM((read, features), F32),
            pltpu.VMEM((halo + rows, min(BLOCK, channels)), F32),
        ],
        aliases={} if first else {inputs + k: k for k in range(3)},
    )


def run_local(row, rows, taps, normed, signal, states, w_in, w_short, rate, mode, skip):
    channels = signal.shape[1]
    out = jax.ShapeDtypeStruct((rows, channels), F32)
    begin = jax.ShapeDtypeStruct(states.shape, F32)
    return call(
        functools.partial(local_stage, row, rows, taps),
        "local_stage",
        [],
        [normed, signal, states, w_in, w_short, rate, mode, skip],
        [out, out] + ([begin] if row == 0 else []),
        [pltpu.VMEM((rows + ROWS * (taps - 1), min(BLOCK, channels)), F32)],
    )


def run_second(pieces, row, rows, count, place, q, local, begin, marks, carry, rate, mode, w):
    channels, features = w.shape
    share = features // pieces
    return call(
        functools.partial(second_stage, pieces, row, rows, count // ROWS),
        "second_stage",
        [place],
        [q, local, begin, marks, carry, rate, mode, w],
        [
            jax.ShapeDtypeStruct((max(1, pieces - 1) * rows, share), BF16),
            jax.ShapeDtypeStruct((rows, share), F32),
        ],
        [pltpu.VMEM((rows, channels), F32)],
    )


def run_last(pieces, sizes, row, own, came, done, count):
    share = own[0].shape[1]
    rows = sum(sizes)
    (out,) = call(
        functools.partial(last_stage, pieces, sizes, row, bool(done)),
        "last_stage",
        [],
        [*own, *came, *done],
        [jax.ShapeDtypeStruct((share, count), BF16 if row + rows == count else F32)],
        [pltpu.VMEM((rows, share), BF16)],
    )
    return out


def rotate(value, axis, steps):
    count = lax.axis_size(axis)
    return lax.ppermute(value, axis, [((i + steps) % count, i) for i in range(count)])


def combine_states(span, stride, radix, count, *refs):
    place_ref, rate_ref, total_ref = refs[:3]
    others = refs[3 : 2 + radix]
    refs = refs[2 + radix :]
    carry_in = refs[0] if stride > 1 else None
    carry_ref = refs[1] if stride > 1 else refs[0]
    position = place_ref[1]
    digit = lax.rem(lax.div(position, stride), radix)
    inner = lax.rem(position, stride)
    unit = span * stride
    rate = rate_ref[...]
    before = jnp.zeros(rate.shape, F32)
    for shift in range(1, radix):
        reached = jnp.where(digit >= shift, 1.0, 0.0)
        other = others[shift - 1][...].astype(F32)
        before = before + jnp.exp(-rate * (unit * (shift - 1))) * (other * reached)
    if stride > 1:
        carry_ref[...] = carry_in[...] + jnp.exp(-rate * (span * inner).astype(F32)) * before
    else:
        carry_ref[...] = before
    if stride * radix < count:
        new = jnp.exp(-rate * (unit * (radix - 1 - digit)).astype(F32)) * total_ref[...]
        for shift in range(1, radix):
            at = lax.rem(digit - shift + radix, radix)
            weight = jnp.exp(-rate * (unit * (radix - 1 - at)).astype(F32))
            new = new + weight * others[shift - 1][...].astype(F32)
        refs[-2][...] = new
        refs[-1][...] = new.astype(BF16)


def carried_in(state, sent, rate, span, axis, place, between):
    count = lax.axis_size(axis)
    total, stride, carry = state, 1, []
    while stride < count:
        radix = 4 if count % (stride * 4) == 0 else 2
        assert count % (stride * radix) == 0
        group = stride * radix
        others = []
        for shift in range(1, radix):
            pairs = []
            for i in range(count):
                digit = (i // stride) % radix
                pairs.append((i + ((digit - shift) % radix - digit) * stride, i))
            others.append(lax.ppermute(sent, axis, pairs))
        others = between(stride, others)
        shape = jax.ShapeDtypeStruct(state.shape, F32)
        carry = call(
            functools.partial(combine_states, span, stride, radix, count),
            "combine_states",
            [place],
            [rate, total, *others, *carry],
            [shape, shape, jax.ShapeDtypeStruct(state.shape, BF16)] if group < count else [shape],
            [],
        )
        if group < count:
            *carry, total, sent = carry
        stride = group
    return carry[0]


def body(tokens, norm_gain, w_in, w_short, decay_rate, residue, skip_gain, w_out):
    pieces, count = lax.axis_size("tp"), lax.axis_size("ctx")
    share, rows = tokens.shape
    channels = w_in.shape[1]
    taps = w_short.shape[0]
    halo = ROWS * (taps - 1)
    sizes = [rows // CHUNKS] * CHUNKS
    bf16_rows = lambda size: jax.ShapeDtypeStruct((size, share), BF16)

    place = jnp.stack([lax.axis_index("tp"), lax.axis_index("ctx")]).astype(jnp.int32)
    tokens, place = lax.optimization_barrier((tokens, place))
    x0, edge = run_first_rows(tokens, halo, sizes[0])
    edge = rotate(edge, "ctx", -1)
    x1, *others = call(
        functools.partial(next_rows, sizes[0]), "next_rows", [], [tokens],
        [bf16_rows(size) for size in sizes[1:]], [],
    )
    (x1,) = call(join_edge, "join_edge", [place], [edge, x1], [bf16_rows(halo + sizes[1])], [])
    x1, others = lax.optimization_barrier((x1, others))
    x = [x0, x1, *others]
    residue, norm_gain, skip_gain, *_ = lax.optimization_barrier((residue, norm_gain, skip_gain, *x))
    mode = residue * jnp.sqrt(-jnp.expm1(-2.0 * decay_rate))
    gain = norm_gain[None, :]
    skip = skip_gain[None, :]
    parts = [[part] + [rotate(part, "tp", s) for s in range(1, pieces)] for part in x]
    w_in, mode, gain, skip, *_ = lax.optimization_barrier((w_in, mode, gain, skip, *x))
    w_in = pltpu.with_memory_space_constraint(in_vmem(w_in), pltpu.VMEM)

    before, row = [], 0
    for group in [[0, 1]] + [[j] for j in range(2, CHUNKS)]:
        results = run_signal(
            pieces, row, rows, group[0] == 0, group[-1] == CHUNKS - 1, taps, place,
            [parts[j] for j in group], before, gain, w_in, w_short, decay_rate,
        )
        before = results[:5]
        row += sum(sizes[j] for j in group)
    normed, signal, marks, states, _ = before
    state, sent, normed, signal, states = lax.optimization_barrier(
        (results[5], results[6], normed, signal, states)
    )
    out_sizes = [rows // 4] * 4
    out_rows = [sum(out_sizes[:j]) for j in range(4)]
    small = [w_in, w_short, decay_rate, mode, skip]
    done = []

    def local_part():
        k = len(done)
        done.append(run_local(out_rows[k], out_sizes[k], taps, normed, signal, states, *small))

    def between(stride, others):
        if stride > 1 and not done:
            local_part()
            others, done[-1] = lax.optimization_barrier((others, done[-1]))
        return others

    carry = carried_in(state, sent, decay_rate, rows, "ctx", place, between)
    if not done:
        local_part()
    begin = done[0][2]
    own, came = [], []
    for j in range(len(out_sizes)):
        if j >= 2:
            arrived = slice((j - 2) * (pieces - 1), (j - 1) * (pieces - 1))
            normed, signal, carry, came[arrived] = lax.optimization_barrier(
                (normed, signal, carry, came[arrived])
            )
        if j > 0:
            local_part()
        send, kept = run_second(
            pieces, out_rows[j], out_sizes[j], rows, place, *done[j][:2], begin, marks, carry,
            decay_rate, mode, w_out,
        )
        own.append(kept)
        for s in range(1, pieces):
            came.append(rotate(send[(s - 1) * out_sizes[j] : s * out_sizes[j]], "tp", -s))
    early = out_rows[-1]
    cut = (len(out_sizes) - 1) * (pieces - 1)
    done = run_last(pieces, out_sizes[:-1], 0, own[:-1], came[:cut], [], rows)
    return run_last(pieces, out_sizes[-1:], early, own[-1:], came[cut:], [done], rows)


def solution(mesh):
    placed = (
        P("tp", "ctx"),
        P(),
        P(None, "tp", None),
        P(None, None, "tp"),
        P(None, "tp"),
        P(None, "tp"),
        P("tp"),
        P("tp", None),
    )
    return jax.shard_map(
        body, mesh=mesh, in_specs=placed, out_specs=P("tp", "ctx"), check_vma=False
    )
```

```python
import functools

import jax
import jax.numpy as jnp
from jax import lax
from jax.experimental import pallas as pl
from jax.experimental.pallas import tpu as pltpu
from jax.sharding import PartitionSpec as P


F32 = jnp.float32
BF16 = jnp.bfloat16
ROWS = 8
LANES = 128
BLOCK = 256
CHUNKS = 4
SPAN = 16
VMEM_LIMIT = 10 * 2**20
CONTRACT_LAST = (((1,), (1,)), ((), ()))
CONTRACT_FIRST = (((0,), (0,)), ((), ()))


def lane_groups(low, width):
    return [(start, min(LANES, low + width - start)) for start in range(low, low + width, LANES)]


def rows_as(row, width):
    return jnp.broadcast_to(row, (ROWS, width))


def tree_sum(terms):
    while len(terms) > 1:
        terms = [sum(terms[k + 1 : k + 2], terms[k]) for k in range(0, len(terms), 2)]
    return terms[0]


def token_picker(first_row, rows, tokens):
    length = tokens // ROWS
    row = lax.broadcasted_iota(jnp.int32, (rows, tokens), 0)
    column = lax.broadcasted_iota(jnp.int32, (rows, tokens), 1)
    wanted = lax.rem(row, ROWS) * length + lax.div(row, ROWS) + first_row // ROWS
    return jnp.where(column == wanted, 1.0, 0.0).astype(BF16)


def turned(pick, tokens):
    return lax.dot_general(pick, tokens, CONTRACT_LAST, preferred_element_type=F32).astype(BF16)


def first_rows(halo, size, tokens_ref, out_ref, edge_ref):
    tokens = tokens_ref.shape[1]
    row = lax.broadcasted_iota(jnp.int32, (halo, tokens), 0)
    column = lax.broadcasted_iota(jnp.int32, (halo, tokens), 1)
    wanted = jnp.where(lax.rem(row, ROWS) == 0, tokens - halo // ROWS + lax.div(row, ROWS), -1)
    picks = [
        token_picker(-halo, halo, tokens),
        token_picker(size - halo, halo + size, tokens),
        jnp.where(column == wanted, 1.0, 0.0).astype(BF16),
    ]
    rows = turned(jnp.concatenate(picks, axis=0), tokens_ref[...])
    out_ref[...] = rows[: 2 * halo + size]
    edge_ref[...] = rows[2 * halo + size :]


def next_rows(firsts, tokens_ref, *chunk_refs):
    tokens = tokens_ref.shape[1]
    for row, ref in zip(firsts, chunk_refs):
        ref[...] = turned(token_picker(row, ref.shape[0], tokens), tokens_ref[...])


def load_weights(places, w_hbm, out_ref, w_ref, sem):
    copies = [
        pltpu.make_async_copy(w_hbm.at[place], w_ref.at[place], sem.at[k])
        for k, place in enumerate(places)
    ]
    for copy in copies:
        copy.start()
    for (s, part), copy in zip(places, copies):
        copy.wait()
        out_ref[s, :, part] = w_ref[s, part, :].T


def short_conv(p_ref, short_ref, s, part, rows, taps):
    width = part.stop - part.start
    total = None
    for offset in range(taps):
        start = ROWS * (taps - 1 - offset)
        term = short_ref[offset, s : s + 1, part] * p_ref[start : start + rows, :width]
        total = term if total is None else total + term
    return total


def project(normed, w_ref, s, part):
    product = jnp.dot(normed, w_ref[s, :, part], preferred_element_type=F32)
    return product.astype(BF16).astype(F32)


def signal_stage(pieces, row, taps, *refs):
    refs = list(refs)
    me_ref = refs.pop(0)
    token_refs = [refs.pop(0) for _ in range(pieces)]
    x_ref, p_ref = refs[-2:]
    halo = ROWS * (taps - 1)
    rows, share = p_ref.shape[0] - halo, token_refs[0].shape[1]
    last, start = row == 0, row == rows
    fresh = last or start
    read = rows + halo if fresh else rows
    halo_refs = [refs.pop(0) for _ in range(pieces)] if last else []
    edge_refs = [refs.pop(0) for _ in range(pieces)] if last else []
    if not start:
        _, _, _, states_in, tail_in = [refs.pop(0) for _ in range(5)]
    gain_ref, w_ref, short_ref, rate_ref = refs[:4]
    normed_ref, signal_ref, marks_ref, states_ref, tail_ref = refs[4:9]
    total_ref, sent_ref = refs[9:11] if last else (None, None)
    modes, channels = rate_ref.shape
    length = signal_ref.shape[0] // ROWS
    me = me_ref[0]

    values = [ref[halo if start else 0 :, :].astype(F32) for ref in token_refs]
    if last:
        preceded = jnp.where(me_ref[1] > 0, 1.0, 0.0)
        values = [
            jnp.concatenate(
                [near[:halo, :].astype(F32) + edge[...].astype(F32) * preceded, value], axis=0
            )
            for near, edge, value in zip(halo_refs, edge_refs, values)
        ]
    for rank in range(pieces):
        chosen = values[0]
        for s in range(1, pieces):
            chosen = jnp.where(me == (rank - s) % pieces, values[s], chosen)
        x_ref[:, rank * share : (rank + 1) * share] = chosen
    features = x_ref[...]
    mean = jnp.mean(features * features, axis=1, keepdims=True)
    normed = (features * lax.rsqrt(mean + 1e-06) * gain_ref[...]).astype(BF16)
    begin = row if fresh else halo + row
    normed_ref[begin : begin + read, :] = normed

    for low in range(0, channels, BLOCK):
        width = min(BLOCK, channels - low)
        part = slice(low, low + width)
        for s in (1, 2):
            if not fresh:
                p_ref[:halo, :width] = tail_in[s - 1, :, part]
            p_ref[halo + rows - read :, :width] = project(
                normed_ref[begin : begin + read, :], w_ref, s, part
            )
            tail_ref[s - 1, :, part] = p_ref[rows:, :width]
            short = short_conv(p_ref, short_ref, s, part, rows, taps)
            if s == 1:
                signal_ref[row : row + rows, part] = short
            else:
                signal_ref[row : row + rows, part] = signal_ref[row : row + rows, part] * short
        for start, size in lane_groups(low, width):
            lanes = slice(start, start + size)
            rate = [rows_as(rate_ref[n : n + 1, lanes], size) for n in range(modes)]
            decay = [jnp.exp(-r) for r in rate]

            if fresh:
                states = (jnp.zeros((ROWS, size), F32),) * modes
            else:
                states = tuple(states_in[n, :, lanes] for n in range(modes))
                for n in range(modes):
                    marks_ref[row // rows, n, :, lanes] = states[n]

            def step(i, states):
                here = pl.ds(pl.multiple_of(row + i * ROWS, ROWS), ROWS)
                now = signal_ref[here, lanes]
                return tuple(states[n] * decay[n] + now for n in range(modes))

            states = lax.fori_loop(0, rows // ROWS, step, states, unroll=8)
            if last:
                later = length - rows // ROWS
                for n in range(modes):
                    marks_ref[1, n, :, lanes] = states[n]
                states = tuple(
                    states_in[n, :, lanes] + jnp.exp(-rate[n] * later) * states[n]
                    for n in range(modes)
                )
            for n in range(modes):
                states_ref[n, :, lanes] = states[n]
            if last:
                left = lax.broadcasted_iota(jnp.int32, (ROWS, size), 0)
                left = ((ROWS - 1 - left) * length).astype(F32)
                for n in range(modes):
                    total_ref[n : n + 1, lanes] = jnp.sum(
                        states[n] * jnp.exp(-rate[n] * left), axis=0, keepdims=True
                    )
                sent_ref[:, lanes] = total_ref[:, lanes].astype(BF16)


def local_stage(row, rows, taps, *refs):
    normed_ref, signal_ref, states_ref, w_ref, short_ref, rate_ref, mode_ref, skip_ref = refs[:8]
    q_ref, local_ref = refs[8:10]
    begin_ref = refs[10] if row == 0 else None
    p_ref = refs[-1]
    modes, channels = rate_ref.shape
    length = signal_ref.shape[0] // ROWS
    for low in range(0, channels, BLOCK):
        width = min(BLOCK, channels - low)
        part = slice(low, low + width)
        normed = normed_ref[row : row + p_ref.shape[0], :]
        p_ref[:, :width] = project(normed, w_ref, 0, part)
        q_ref[:, part] = short_conv(p_ref, short_ref, 0, part, rows, taps)
        for start, size in lane_groups(low, width):
            lanes = slice(start, start + size)
            rate = [rows_as(rate_ref[n : n + 1, lanes], size) for n in range(modes)]
            segment = lax.broadcasted_iota(jnp.int32, (ROWS, size), 0)
            if row == 0:
                for n in range(modes):
                    run = states_ref[n, :, lanes]
                    for hop in (1, 2, 4):
                        weight = jnp.where(segment >= hop, jnp.exp(-rate[n] * (hop * length)), 0.0)
                        run = run + weight * pltpu.roll(run, hop, 0)
                    begin_ref[n, :, lanes] = jnp.where(segment >= 1, pltpu.roll(run, 1, 0), 0.0)
            lag = segment.astype(F32)
            filters = []
            for first_lag in range(0, SPAN, ROWS):
                values = tree_sum(
                    [
                        rows_as(mode_ref[n : n + 1, lanes], size)
                        * jnp.exp(-rate[n] * (lag + first_lag))
                        for n in range(modes)
                    ]
                )
                filters += [rows_as(values[j : j + 1, :], size) for j in range(ROWS)]
            filters[0] = filters[0] + skip_ref[:, lanes]

            def span(i, carry):
                base = i * (SPAN * ROWS)
                now = [
                    signal_ref[pl.ds(pl.multiple_of(row + base + k * ROWS, ROWS), ROWS), lanes]
                    for k in range(SPAN)
                ]
                for k in range(SPAN):
                    local_ref[pl.ds(pl.multiple_of(base + k * ROWS, ROWS), ROWS), lanes] = tree_sum(
                        [filters[j] * now[k - j] for j in range(k + 1)]
                    )
                return carry

            lax.fori_loop(0, rows // (SPAN * ROWS), span, 0)


def second_stage(pieces, row, rows, length, *refs):
    me_ref, q_ref, local_ref, begin_ref, marks_ref, carry_ref, rate_ref, mode_ref, w_ref = refs[:9]
    send_ref, own_ref, gated_ref = refs[9:]
    modes, channels = rate_ref.shape
    for start, size in lane_groups(0, channels):
        lanes = slice(start, start + size)
        rate = [rows_as(rate_ref[n : n + 1, lanes], size) for n in range(modes)]
        decay = [jnp.exp(-r) for r in rate]
        segment = lax.broadcasted_iota(jnp.int32, (ROWS, size), 0)
        past = (segment * length).astype(F32)
        for at in range(row, row + rows, SPAN * ROWS):
            mark = at // (SPAN * ROWS)
            states = []
            for n in range(modes):
                state = begin_ref[n, :, lanes] + jnp.exp(-rate[n] * past) * carry_ref[
                    n : n + 1, lanes
                ]
                if mark > 0:
                    state = marks_ref[1, n, :, lanes] + state * jnp.exp(-rate[n] * SPAN)
                if mark > 1:
                    state = marks_ref[mark, n, :, lanes] + state * jnp.exp(
                        -rate[n] * (SPAN * (mark - 1))
                    )
                states.append(mode_ref[n : n + 1, lanes] * state)

            def step(i, states):
                here = pl.ds(pl.multiple_of(at - row + i * ROWS, ROWS), ROWS)
                states = tuple(states[n] * decay[n] for n in range(modes))
                gated_ref[here, lanes] = q_ref[here, lanes] * tree_sum(
                    [local_ref[here, lanes]] + list(states)
                )
                return states

            lax.fori_loop(0, SPAN, step, tuple(states), unroll=4)
    product = jnp.dot(gated_ref[...].astype(BF16), w_ref[...], preferred_element_type=F32)
    share = own_ref.shape[1]
    me = me_ref[0]
    columns = [product[:, rank * share : (rank + 1) * share] for rank in range(pieces)]
    for s in range(pieces):
        chosen = columns[0]
        for rank in range(1, pieces):
            chosen = jnp.where(me == (rank - s) % pieces, columns[rank], chosen)
        if s == 0:
            own_ref[...] = chosen
        else:
            send_ref[(s - 1) * rows : s * rows, :] = chosen.astype(BF16)


def last_stage(pieces, sizes, row, more, *refs):
    chunks = len(sizes)
    own_refs, came_refs = refs[:chunks], refs[chunks : chunks * pieces]
    done_ref = refs[chunks * pieces] if more else None
    out_ref, mixed_ref = refs[-2:]
    at = 0
    for j, size in enumerate(sizes):
        total = own_refs[j][...]
        for s in range(pieces - 1):
            total = total + came_refs[j * (pieces - 1) + s][...].astype(F32)
        mixed_ref[at : at + size, :] = total.astype(BF16)
        at += size
    pick = token_picker(row, at, out_ref.shape[1])
    out = lax.dot_general(mixed_ref[...], pick, CONTRACT_FIRST, preferred_element_type=F32)
    if more:
        out = out + done_ref[...]
    out_ref[...] = out.astype(out_ref.dtype)


def call(kernel, name, scalars, operands, outs, scratch, aliases={}):
    vmem = pl.BlockSpec(memory_space=pltpu.VMEM)
    smem = pl.BlockSpec(memory_space=pltpu.SMEM)
    return pl.pallas_call(
        kernel,
        out_shape=outs,
        in_specs=[smem] * len(scalars) + [vmem] * len(operands),
        out_specs=[vmem] * len(outs),
        scratch_shapes=scratch,
        input_output_aliases=aliases,
        compiler_params=pltpu.CompilerParams(vmem_limit_bytes=VMEM_LIMIT),
        cost_estimate=pl.CostEstimate(flops=1, bytes_accessed=1, transcendentals=0),
        name=name,
    )(*scalars, *operands)


def in_vmem(w):
    streams, channels, features = w.shape
    block = min(BLOCK, channels)
    places = [
        (s, slice(low, min(low + block, channels)))
        for s in (1, 2, 0)
        for low in range(0, channels, block)
    ]
    return pl.pallas_call(
        functools.partial(load_weights, places),
        out_shape=pltpu.VMEM((streams, features, channels), w.dtype),
        in_specs=[pl.BlockSpec(memory_space=pl.ANY)],
        out_specs=pl.BlockSpec(memory_space=pltpu.VMEM),
        scratch_shapes=[
            pltpu.VMEM(w.shape, w.dtype),
            pltpu.SemaphoreType.DMA((len(places),)),
        ],
        compiler_params=pltpu.CompilerParams(vmem_limit_bytes=46 * 2**20),
        cost_estimate=pl.CostEstimate(flops=1, bytes_accessed=1, transcendentals=0),
        name="load_weights",
    )(w)


def run_signal(pieces, row, rows, count, taps, place, tokens, edges, before, gain, w_in, w_short, rate):
    streams, features, channels = w_in.shape
    modes = rate.shape[0]
    halo = ROWS * (taps - 1)
    outs = [
        jax.ShapeDtypeStruct((halo + count, features), BF16),
        jax.ShapeDtypeStruct((count, channels), F32),
        jax.ShapeDtypeStruct((count // rows, modes, ROWS, channels), F32),
        jax.ShapeDtypeStruct((modes, ROWS, channels), F32),
        jax.ShapeDtypeStruct((streams - 1, halo, channels), F32),
    ]
    if row == 0:
        outs += [jax.ShapeDtypeStruct((modes, channels), kind) for kind in (F32, BF16)]
    return call(
        functools.partial(signal_stage, pieces, row, taps),
        "signal_stage",
        [place],
        list(tokens) + list(edges) + list(before) + [gain, w_in, w_short, rate],
        outs,
        [
            pltpu.VMEM((rows + (halo if row in (0, rows) else 0), features), F32),
            pltpu.VMEM((halo + rows, min(BLOCK, channels)), F32),
        ],
        aliases={1 + len(tokens) + len(edges) + k: k for k in range(3)} if before else {},
    )


def run_local(row, rows, taps, normed, signal, states, w_in, w_short, rate, mode, skip):
    channels = signal.shape[1]
    out = jax.ShapeDtypeStruct((rows, channels), F32)
    begin = jax.ShapeDtypeStruct(states.shape, F32)
    return call(
        functools.partial(local_stage, row, rows, taps),
        "local_stage",
        [],
        [normed, signal, states, w_in, w_short, rate, mode, skip],
        [out, out] + ([begin] if row == 0 else []),
        [pltpu.VMEM((rows + ROWS * (taps - 1), min(BLOCK, channels)), F32)],
    )


def run_second(pieces, row, rows, count, place, q, local, begin, marks, carry, rate, mode, w):
    channels, features = w.shape
    share = features // pieces
    return call(
        functools.partial(second_stage, pieces, row, rows, count // ROWS),
        "second_stage",
        [place],
        [q, local, begin, marks, carry, rate, mode, w],
        [
            jax.ShapeDtypeStruct((max(1, pieces - 1) * rows, share), BF16),
            jax.ShapeDtypeStruct((rows, share), F32),
        ],
        [pltpu.VMEM((rows, channels), F32)],
    )


def run_last(pieces, sizes, row, own, came, done, count):
    share = own[0].shape[1]
    rows = sum(sizes)
    (out,) = call(
        functools.partial(last_stage, pieces, sizes, row, bool(done)),
        "last_stage",
        [],
        [*own, *came, *done],
        [jax.ShapeDtypeStruct((share, count), BF16 if row + rows == count else F32)],
        [pltpu.VMEM((rows, share), BF16)],
    )
    return out


def rotate(value, axis, steps):
    count = lax.axis_size(axis)
    return lax.ppermute(value, axis, [((i + steps) % count, i) for i in range(count)])


def combine_states(span, stride, radix, count, *refs):
    place_ref, rate_ref, total_ref = refs[:3]
    others = refs[3 : 2 + radix]
    refs = refs[2 + radix :]
    carry_in = refs[0] if stride > 1 else None
    carry_ref = refs[1] if stride > 1 else refs[0]
    position = place_ref[1]
    digit = lax.rem(lax.div(position, stride), radix)
    inner = lax.rem(position, stride)
    unit = span * stride
    rate = rate_ref[...]
    before = jnp.zeros(rate.shape, F32)
    for shift in range(1, radix):
        reached = jnp.where(digit >= shift, 1.0, 0.0)
        other = others[shift - 1][...].astype(F32)
        before = before + jnp.exp(-rate * (unit * (shift - 1))) * (other * reached)
    if stride > 1:
        carry_ref[...] = carry_in[...] + jnp.exp(-rate * (span * inner).astype(F32)) * before
    else:
        carry_ref[...] = before
    if stride * radix < count:
        new = jnp.exp(-rate * (unit * (radix - 1 - digit)).astype(F32)) * total_ref[...]
        for shift in range(1, radix):
            at = lax.rem(digit - shift + radix, radix)
            weight = jnp.exp(-rate * (unit * (radix - 1 - at)).astype(F32))
            new = new + weight * others[shift - 1][...].astype(F32)
        refs[-2][...] = new
        refs[-1][...] = new.astype(BF16)


def carried_in(state, sent, rate, span, axis, place, between):
    count = lax.axis_size(axis)
    total, stride, carry = state, 1, []
    while stride < count:
        radix = 4 if count % (stride * 4) == 0 else 2
        assert count % (stride * radix) == 0
        group = stride * radix
        others = []
        for shift in range(1, radix):
            pairs = []
            for i in range(count):
                digit = (i // stride) % radix
                pairs.append((i + ((digit - shift) % radix - digit) * stride, i))
            others.append(lax.ppermute(sent, axis, pairs))
        others = between(stride, others)
        shape = jax.ShapeDtypeStruct(state.shape, F32)
        carry = call(
            functools.partial(combine_states, span, stride, radix, count),
            "combine_states",
            [place],
            [rate, total, *others, *carry],
            [shape, shape, jax.ShapeDtypeStruct(state.shape, BF16)] if group < count else [shape],
            [],
        )
        if group < count:
            *carry, total, sent = carry
        stride = group
    return carry[0]


def body(tokens, norm_gain, w_in, w_short, decay_rate, residue, skip_gain, w_out):
    pieces, count = lax.axis_size("tp"), lax.axis_size("ctx")
    share, rows = tokens.shape
    channels = w_in.shape[1]
    taps = w_short.shape[0]
    halo = ROWS * (taps - 1)
    size = SPAN * ROWS
    assert rows == CHUNKS * size
    bf16_rows = lambda size: jax.ShapeDtypeStruct((size, share), BF16)

    place = jnp.stack([lax.axis_index("tp"), lax.axis_index("ctx")]).astype(jnp.int32)
    tokens, place = lax.optimization_barrier((tokens, place))
    x1, edge = call(
        functools.partial(first_rows, halo, size), "first_rows", [], [tokens],
        [bf16_rows(2 * halo + size), bf16_rows(halo)], [],
    )
    edge = rotate(edge, "ctx", -1)
    tokens, x1 = lax.optimization_barrier((tokens, x1))
    x0, *others = call(
        functools.partial(next_rows, [0] + [j * size for j in range(2, CHUNKS)]), "next_rows",
        [], [tokens], [bf16_rows(size)] * (CHUNKS - 1), [],
    )
    x = [x1, *others, x0]
    residue, norm_gain, skip_gain, *_ = lax.optimization_barrier((residue, norm_gain, skip_gain, *x))
    mode = residue * jnp.sqrt(-jnp.expm1(-2.0 * decay_rate))
    gain = norm_gain[None, :]
    skip = skip_gain[None, :]
    w_in, mode, gain, skip, *_ = lax.optimization_barrier((w_in, mode, gain, skip, *x))
    w_in = in_vmem(w_in)
    edge, w_in = lax.optimization_barrier((edge, w_in))
    w_in = pltpu.with_memory_space_constraint(w_in, pltpu.VMEM)
    *parts, edges = [[part] + [rotate(part, "tp", s) for s in range(1, pieces)] for part in x + [edge]]

    before = []
    for part, j in zip(parts, list(range(1, CHUNKS)) + [0]):
        results = run_signal(
            pieces, j * size, size, rows, taps, place, part, [] if j else parts[0] + edges, before, gain, w_in,
            w_short, decay_rate,
        )
        before = results[:5]
    normed, signal, marks, states, _ = before
    state, sent, normed, signal, states = lax.optimization_barrier(
        (results[5], results[6], normed, signal, states)
    )
    out_sizes = [rows // 4] * 4
    out_rows = [sum(out_sizes[:j]) for j in range(4)]
    small = [w_in, w_short, decay_rate, mode, skip]
    done = []

    def local_part():
        k = len(done)
        done.append(run_local(out_rows[k], out_sizes[k], taps, normed, signal, states, *small))

    def between(stride, others):
        if stride > 1 and not done:
            local_part()
            others, done[-1] = lax.optimization_barrier((others, done[-1]))
        return others

    carry = carried_in(state, sent, decay_rate, rows, "ctx", place, between)
    if not done:
        local_part()
    begin = done[0][2]
    own, came = [], []
    for j in range(len(out_sizes)):
        if j >= 2:
            arrived = slice((j - 2) * (pieces - 1), (j - 1) * (pieces - 1))
            normed, signal, carry, came[arrived] = lax.optimization_barrier(
                (normed, signal, carry, came[arrived])
            )
        if j > 0:
            local_part()
        send, kept = run_second(
            pieces, out_rows[j], out_sizes[j], rows, place, *done[j][:2], begin, marks, carry,
            decay_rate, mode, w_out,
        )
        own.append(kept)
        for s in range(1, pieces):
            came.append(rotate(send[(s - 1) * out_sizes[j] : s * out_sizes[j]], "tp", -s))
    early = out_rows[-1]
    cut = (len(out_sizes) - 1) * (pieces - 1)
    done = run_last(pieces, out_sizes[:-1], 0, own[:-1], came[:cut], [], rows)
    return run_last(pieces, out_sizes[-1:], early, own[-1:], came[cut:], [done], rows)


def solution(mesh):
    placed = (
        P("tp", "ctx"),
        P(),
        P(None, "tp", None),
        P(None, None, "tp"),
        P(None, "tp"),
        P(None, "tp"),
        P("tp"),
        P("tp", None),
    )
    return jax.shard_map(
        body, mesh=mesh, in_specs=placed, out_specs=P("tp", "ctx"), check_vma=False
    )
```

```python
import functools

import jax
import jax.numpy as jnp
from jax import lax
from jax.experimental import pallas as pl
from jax.experimental.pallas import tpu as pltpu
from jax.sharding import PartitionSpec as P


F32 = jnp.float32
BF16 = jnp.bfloat16
ROWS = 8
LANES = 128
BLOCK = 256
CHUNKS = 4
SPAN = 16
VMEM_LIMIT = 10 * 2**20
CONTRACT_LAST = (((1,), (1,)), ((), ()))
CONTRACT_FIRST = (((0,), (0,)), ((), ()))


def lane_groups(low, width):
    return [(start, min(LANES, low + width - start)) for start in range(low, low + width, LANES)]


def rows_as(row, width):
    return jnp.broadcast_to(row, (ROWS, width))


def tree_sum(terms):
    while len(terms) > 1:
        terms = [sum(terms[k + 1 : k + 2], terms[k]) for k in range(0, len(terms), 2)]
    return terms[0]


def token_picker(first_row, rows, tokens):
    length = tokens // ROWS
    row = lax.broadcasted_iota(jnp.int32, (rows, tokens), 0)
    column = lax.broadcasted_iota(jnp.int32, (rows, tokens), 1)
    wanted = lax.rem(row, ROWS) * length + lax.div(row, ROWS) + first_row // ROWS
    return jnp.where(column == wanted, 1.0, 0.0).astype(BF16)


def turned(pick, tokens):
    return lax.dot_general(pick, tokens, CONTRACT_LAST, preferred_element_type=F32).astype(BF16)


def first_rows(halo, size, tokens_ref, out_ref, edge_ref):
    tokens = tokens_ref.shape[1]
    row = lax.broadcasted_iota(jnp.int32, (halo, tokens), 0)
    column = lax.broadcasted_iota(jnp.int32, (halo, tokens), 1)
    wanted = jnp.where(lax.rem(row, ROWS) == 0, tokens - halo // ROWS + lax.div(row, ROWS), -1)
    picks = [
        token_picker(size - halo, halo + size, tokens),
        jnp.where(column == wanted, 1.0, 0.0).astype(BF16),
    ]
    rows = turned(jnp.concatenate(picks, axis=0), tokens_ref[...])
    out_ref[...] = rows[: halo + size]
    edge_ref[...] = rows[halo + size :]


def next_rows(firsts, tokens_ref, *chunk_refs):
    tokens = tokens_ref.shape[1]
    for row, ref in zip(firsts, chunk_refs):
        ref[...] = turned(token_picker(row, ref.shape[0], tokens), tokens_ref[...])


def load_weights(places, w_hbm, out_ref, w_ref, sem):
    copies = [
        pltpu.make_async_copy(w_hbm.at[place], w_ref.at[place], sem.at[k])
        for k, place in enumerate(places)
    ]
    for copy in copies:
        copy.start()
    for (s, part), copy in zip(places, copies):
        copy.wait()
        out_ref[s, :, part] = w_ref[s, part, :].T


def short_conv(p_ref, short_ref, s, part, rows, taps):
    width = part.stop - part.start
    total = None
    for offset in range(taps):
        start = ROWS * (taps - 1 - offset)
        term = short_ref[offset, s : s + 1, part] * p_ref[start : start + rows, :width]
        total = term if total is None else total + term
    return total


def project(normed, w_ref, s, part):
    product = jnp.dot(normed, w_ref[s, :, part], preferred_element_type=F32)
    return product.astype(BF16).astype(F32)


def signal_stage(pieces, row, taps, *refs):
    refs = list(refs)
    me_ref = refs.pop(0)
    token_refs = [refs.pop(0) for _ in range(pieces)]
    x_ref, p_ref = refs[-2:]
    halo = ROWS * (taps - 1)
    rows, share = p_ref.shape[0] - halo, token_refs[0].shape[1]
    last, start = row == 0, row == rows
    fresh = last or start
    read = rows + halo if fresh else rows
    edge_refs = [refs.pop(0) for _ in range(pieces)] if last else []
    if not start:
        normed_in, _, _, states_in, tail_in = [refs.pop(0) for _ in range(5)]
    gain_ref, w_ref, short_ref, rate_ref = refs[:4]
    normed_ref, signal_ref, marks_ref, states_ref, tail_ref = refs[4:9]
    total_ref, sent_ref = refs[9:11] if last else (None, None)
    modes, channels = rate_ref.shape
    length = signal_ref.shape[0] // ROWS
    me = me_ref[0]

    values = [ref[...].astype(F32) for ref in token_refs]
    if last:
        preceded = jnp.where(me_ref[1] > 0, 1.0, 0.0)
        values = [
            jnp.concatenate([edge[...].astype(F32) * preceded, value], axis=0)
            for edge, value in zip(edge_refs, values)
        ]
    for rank in range(pieces):
        chosen = values[0]
        for s in range(1, pieces):
            chosen = jnp.where(me == (rank - s) % pieces, values[s], chosen)
        x_ref[:, rank * share : (rank + 1) * share] = chosen
    features = x_ref[...]
    mean = jnp.mean(features * features, axis=1, keepdims=True)
    normed = features * lax.rsqrt(mean + 1e-06) * gain_ref[...]
    if last:
        ends = normed_in[normed_in.shape[0] - halo :, :].astype(F32)
        segment = lax.broadcasted_iota(jnp.int32, (ROWS, ends.shape[1]), 0)
        front = [
            jnp.where(segment >= 1, pltpu.roll(ends[at : at + ROWS], 1, 0), normed[at : at + ROWS])
            for at in range(0, halo, ROWS)
        ]
        normed = jnp.concatenate(front + [normed[halo:]], axis=0)
    normed = normed.astype(BF16)
    begin = row if fresh else halo + row
    normed_ref[begin : begin + read, :] = normed

    for low in range(0, channels, BLOCK):
        width = min(BLOCK, channels - low)
        part = slice(low, low + width)
        for s in (1, 2):
            if not fresh:
                p_ref[:halo, :width] = tail_in[s - 1, :, part]
            p_ref[halo + rows - read :, :width] = project(
                normed_ref[begin : begin + read, :], w_ref, s, part
            )
            tail_ref[s - 1, :, part] = p_ref[rows:, :width]
            short = short_conv(p_ref, short_ref, s, part, rows, taps)
            if s == 1:
                signal_ref[row : row + rows, part] = short
            else:
                signal_ref[row : row + rows, part] = signal_ref[row : row + rows, part] * short
        for start, size in lane_groups(low, width):
            lanes = slice(start, start + size)
            rate = [rows_as(rate_ref[n : n + 1, lanes], size) for n in range(modes)]
            decay = [jnp.exp(-r) for r in rate]

            if fresh:
                states = (jnp.zeros((ROWS, size), F32),) * modes
            else:
                states = tuple(states_in[n, :, lanes] for n in range(modes))
                for n in range(modes):
                    marks_ref[row // rows, n, :, lanes] = states[n]

            def step(i, states):
                here = pl.ds(pl.multiple_of(row + i * ROWS, ROWS), ROWS)
                now = signal_ref[here, lanes]
                return tuple(states[n] * decay[n] + now for n in range(modes))

            states = lax.fori_loop(0, rows // ROWS, step, states, unroll=8)
            if last:
                later = length - rows // ROWS
                for n in range(modes):
                    marks_ref[1, n, :, lanes] = states[n]
                states = tuple(
                    states_in[n, :, lanes] + jnp.exp(-rate[n] * later) * states[n]
                    for n in range(modes)
                )
            for n in range(modes):
                states_ref[n, :, lanes] = states[n]
            if last:
                left = lax.broadcasted_iota(jnp.int32, (ROWS, size), 0)
                left = ((ROWS - 1 - left) * length).astype(F32)
                for n in range(modes):
                    total_ref[n : n + 1, lanes] = jnp.sum(
                        states[n] * jnp.exp(-rate[n] * left), axis=0, keepdims=True
                    )
                sent_ref[:, lanes] = total_ref[:, lanes].astype(BF16)


def local_stage(row, rows, taps, *refs):
    normed_ref, signal_ref, states_ref, w_ref, short_ref, rate_ref, mode_ref, skip_ref = refs[:8]
    q_ref, local_ref = refs[8:10]
    begin_ref = refs[10] if row == 0 else None
    p_ref = refs[-1]
    modes, channels = rate_ref.shape
    length = signal_ref.shape[0] // ROWS
    for low in range(0, channels, BLOCK):
        width = min(BLOCK, channels - low)
        part = slice(low, low + width)
        normed = normed_ref[row : row + p_ref.shape[0], :]
        p_ref[:, :width] = project(normed, w_ref, 0, part)
        q_ref[:, part] = short_conv(p_ref, short_ref, 0, part, rows, taps)
        for start, size in lane_groups(low, width):
            lanes = slice(start, start + size)
            rate = [rows_as(rate_ref[n : n + 1, lanes], size) for n in range(modes)]
            segment = lax.broadcasted_iota(jnp.int32, (ROWS, size), 0)
            if row == 0:
                for n in range(modes):
                    run = states_ref[n, :, lanes]
                    for hop in (1, 2, 4):
                        weight = jnp.where(segment >= hop, jnp.exp(-rate[n] * (hop * length)), 0.0)
                        run = run + weight * pltpu.roll(run, hop, 0)
                    begin_ref[n, :, lanes] = jnp.where(segment >= 1, pltpu.roll(run, 1, 0), 0.0)
            lag = segment.astype(F32)
            filters = []
            for first_lag in range(0, SPAN, ROWS):
                values = tree_sum(
                    [
                        rows_as(mode_ref[n : n + 1, lanes], size)
                        * jnp.exp(-rate[n] * (lag + first_lag))
                        for n in range(modes)
                    ]
                )
                filters += [rows_as(values[j : j + 1, :], size) for j in range(ROWS)]
            filters[0] = filters[0] + skip_ref[:, lanes]

            def span(i, carry):
                base = i * (SPAN * ROWS)
                now = [
                    signal_ref[pl.ds(pl.multiple_of(row + base + k * ROWS, ROWS), ROWS), lanes]
                    for k in range(SPAN)
                ]
                for k in range(SPAN):
                    local_ref[pl.ds(pl.multiple_of(base + k * ROWS, ROWS), ROWS), lanes] = tree_sum(
                        [filters[j] * now[k - j] for j in range(k + 1)]
                    )
                return carry

            lax.fori_loop(0, rows // (SPAN * ROWS), span, 0)


def second_stage(pieces, row, rows, length, *refs):
    me_ref, q_ref, local_ref, begin_ref, marks_ref, carry_ref, rate_ref, mode_ref, w_ref = refs[:9]
    send_ref, own_ref, gated_ref = refs[9:]
    modes, channels = rate_ref.shape
    for start, size in lane_groups(0, channels):
        lanes = slice(start, start + size)
        rate = [rows_as(rate_ref[n : n + 1, lanes], size) for n in range(modes)]
        decay = [jnp.exp(-r) for r in rate]
        segment = lax.broadcasted_iota(jnp.int32, (ROWS, size), 0)
        past = (segment * length).astype(F32)
        for at in range(row, row + rows, SPAN * ROWS):
            mark = at // (SPAN * ROWS)
            states = []
            for n in range(modes):
                state = begin_ref[n, :, lanes] + jnp.exp(-rate[n] * past) * carry_ref[
                    n : n + 1, lanes
                ]
                if mark > 0:
                    state = marks_ref[1, n, :, lanes] + state * jnp.exp(-rate[n] * SPAN)
                if mark > 1:
                    state = marks_ref[mark, n, :, lanes] + state * jnp.exp(
                        -rate[n] * (SPAN * (mark - 1))
                    )
                states.append(mode_ref[n : n + 1, lanes] * state)

            def step(i, states):
                here = pl.ds(pl.multiple_of(at - row + i * ROWS, ROWS), ROWS)
                states = tuple(states[n] * decay[n] for n in range(modes))
                gated_ref[here, lanes] = q_ref[here, lanes] * tree_sum(
                    [local_ref[here, lanes]] + list(states)
                )
                return states

            lax.fori_loop(0, SPAN, step, tuple(states), unroll=4)
    product = jnp.dot(gated_ref[...].astype(BF16), w_ref[...], preferred_element_type=F32)
    share = own_ref.shape[1]
    me = me_ref[0]
    columns = [product[:, rank * share : (rank + 1) * share] for rank in range(pieces)]
    for s in range(pieces):
        chosen = columns[0]
        for rank in range(1, pieces):
            chosen = jnp.where(me == (rank - s) % pieces, columns[rank], chosen)
        if s == 0:
            own_ref[...] = chosen
        else:
            send_ref[(s - 1) * rows : s * rows, :] = chosen.astype(BF16)


def last_stage(pieces, sizes, row, more, *refs):
    chunks = len(sizes)
    own_refs, came_refs = refs[:chunks], refs[chunks : chunks * pieces]
    done_ref = refs[chunks * pieces] if more else None
    out_ref, mixed_ref = refs[-2:]
    at = 0
    for j, size in enumerate(sizes):
        total = own_refs[j][...]
        for s in range(pieces - 1):
            total = total + came_refs[j * (pieces - 1) + s][...].astype(F32)
        mixed_ref[at : at + size, :] = total.astype(BF16)
        at += size
    pick = token_picker(row, at, out_ref.shape[1])
    out = lax.dot_general(mixed_ref[...], pick, CONTRACT_FIRST, preferred_element_type=F32)
    if more:
        out = out + done_ref[...]
    out_ref[...] = out.astype(out_ref.dtype)


def call(kernel, name, scalars, operands, outs, scratch, aliases={}):
    vmem = pl.BlockSpec(memory_space=pltpu.VMEM)
    smem = pl.BlockSpec(memory_space=pltpu.SMEM)
    return pl.pallas_call(
        kernel,
        out_shape=outs,
        in_specs=[smem] * len(scalars) + [vmem] * len(operands),
        out_specs=[vmem] * len(outs),
        scratch_shapes=scratch,
        input_output_aliases=aliases,
        compiler_params=pltpu.CompilerParams(vmem_limit_bytes=VMEM_LIMIT),
        cost_estimate=pl.CostEstimate(flops=1, bytes_accessed=1, transcendentals=0),
        name=name,
    )(*scalars, *operands)


def in_vmem(w):
    streams, channels, features = w.shape
    block = min(BLOCK, channels)
    places = [
        (s, slice(low, min(low + block, channels)))
        for s in (1, 2, 0)
        for low in range(0, channels, block)
    ]
    return pl.pallas_call(
        functools.partial(load_weights, places),
        out_shape=pltpu.VMEM((streams, features, channels), w.dtype),
        in_specs=[pl.BlockSpec(memory_space=pl.ANY)],
        out_specs=pl.BlockSpec(memory_space=pltpu.VMEM),
        scratch_shapes=[
            pltpu.VMEM(w.shape, w.dtype),
            pltpu.SemaphoreType.DMA((len(places),)),
        ],
        compiler_params=pltpu.CompilerParams(vmem_limit_bytes=46 * 2**20),
        cost_estimate=pl.CostEstimate(flops=1, bytes_accessed=1, transcendentals=0),
        name="load_weights",
    )(w)


def run_signal(pieces, row, rows, count, taps, place, tokens, edges, before, gain, w_in, w_short, rate):
    streams, features, channels = w_in.shape
    modes = rate.shape[0]
    halo = ROWS * (taps - 1)
    outs = [
        jax.ShapeDtypeStruct((halo + count, features), BF16),
        jax.ShapeDtypeStruct((count, channels), F32),
        jax.ShapeDtypeStruct((count // rows, modes, ROWS, channels), F32),
        jax.ShapeDtypeStruct((modes, ROWS, channels), F32),
        jax.ShapeDtypeStruct((streams - 1, halo, channels), F32),
    ]
    if row == 0:
        outs += [jax.ShapeDtypeStruct((modes, channels), kind) for kind in (F32, BF16)]
    return call(
        functools.partial(signal_stage, pieces, row, taps),
        "signal_stage",
        [place],
        list(tokens) + list(edges) + list(before) + [gain, w_in, w_short, rate],
        outs,
        [
            pltpu.VMEM((rows + (halo if row in (0, rows) else 0), features), F32),
            pltpu.VMEM((halo + rows, min(BLOCK, channels)), F32),
        ],
        aliases={1 + len(tokens) + len(edges) + k: k for k in range(3)} if before else {},
    )


def run_local(row, rows, taps, normed, signal, states, w_in, w_short, rate, mode, skip):
    channels = signal.shape[1]
    out = jax.ShapeDtypeStruct((rows, channels), F32)
    begin = jax.ShapeDtypeStruct(states.shape, F32)
    return call(
        functools.partial(local_stage, row, rows, taps),
        "local_stage",
        [],
        [normed, signal, states, w_in, w_short, rate, mode, skip],
        [out, out] + ([begin] if row == 0 else []),
        [pltpu.VMEM((rows + ROWS * (taps - 1), min(BLOCK, channels)), F32)],
    )


def run_second(pieces, row, rows, count, place, q, local, begin, marks, carry, rate, mode, w):
    channels, features = w.shape
    share = features // pieces
    return call(
        functools.partial(second_stage, pieces, row, rows, count // ROWS),
        "second_stage",
        [place],
        [q, local, begin, marks, carry, rate, mode, w],
        [
            jax.ShapeDtypeStruct((max(1, pieces - 1) * rows, share), BF16),
            jax.ShapeDtypeStruct((rows, share), F32),
        ],
        [pltpu.VMEM((rows, channels), F32)],
    )


def run_last(pieces, sizes, row, own, came, done, count):
    share = own[0].shape[1]
    rows = sum(sizes)
    (out,) = call(
        functools.partial(last_stage, pieces, sizes, row, bool(done)),
        "last_stage",
        [],
        [*own, *came, *done],
        [jax.ShapeDtypeStruct((share, count), BF16 if row + rows == count else F32)],
        [pltpu.VMEM((rows, share), BF16)],
    )
    return out


def rotate(value, axis, steps):
    count = lax.axis_size(axis)
    return lax.ppermute(value, axis, [((i + steps) % count, i) for i in range(count)])


def combine_states(span, stride, radix, count, *refs):
    place_ref, rate_ref, total_ref = refs[:3]
    others = refs[3 : 2 + radix]
    refs = refs[2 + radix :]
    carry_in = refs[0] if stride > 1 else None
    carry_ref = refs[1] if stride > 1 else refs[0]
    position = place_ref[1]
    digit = lax.rem(lax.div(position, stride), radix)
    inner = lax.rem(position, stride)
    unit = span * stride
    rate = rate_ref[...]
    before = jnp.zeros(rate.shape, F32)
    for shift in range(1, radix):
        reached = jnp.where(digit >= shift, 1.0, 0.0)
        other = others[shift - 1][...].astype(F32)
        before = before + jnp.exp(-rate * (unit * (shift - 1))) * (other * reached)
    if stride > 1:
        carry_ref[...] = carry_in[...] + jnp.exp(-rate * (span * inner).astype(F32)) * before
    else:
        carry_ref[...] = before
    if stride * radix < count:
        new = jnp.exp(-rate * (unit * (radix - 1 - digit)).astype(F32)) * total_ref[...]
        for shift in range(1, radix):
            at = lax.rem(digit - shift + radix, radix)
            weight = jnp.exp(-rate * (unit * (radix - 1 - at)).astype(F32))
            new = new + weight * others[shift - 1][...].astype(F32)
        refs[-2][...] = new
        refs[-1][...] = new.astype(BF16)


def carried_in(state, sent, rate, span, axis, place, between):
    count = lax.axis_size(axis)
    total, stride, carry = state, 1, []
    while stride < count:
        radix = 4 if count % (stride * 4) == 0 else 2
        assert count % (stride * radix) == 0
        group = stride * radix
        others = []
        for shift in range(1, radix):
            pairs = []
            for i in range(count):
                digit = (i // stride) % radix
                if group < count or digit >= shift:
                    pairs.append((i + ((digit - shift) % radix - digit) * stride, i))
            others.append(lax.ppermute(sent, axis, pairs))
        others = between(stride, others)
        shape = jax.ShapeDtypeStruct(state.shape, F32)
        carry = call(
            functools.partial(combine_states, span, stride, radix, count),
            "combine_states",
            [place],
            [rate, total, *others, *carry],
            [shape, shape, jax.ShapeDtypeStruct(state.shape, BF16)] if group < count else [shape],
            [],
        )
        if group < count:
            *carry, total, sent = carry
        stride = group
    return carry[0]


def body(tokens, norm_gain, w_in, w_short, decay_rate, residue, skip_gain, w_out):
    pieces, count = lax.axis_size("tp"), lax.axis_size("ctx")
    share, rows = tokens.shape
    channels = w_in.shape[1]
    taps = w_short.shape[0]
    halo = ROWS * (taps - 1)
    size = SPAN * ROWS
    assert rows == CHUNKS * size
    bf16_rows = lambda size: jax.ShapeDtypeStruct((size, share), BF16)

    place = jnp.stack([lax.axis_index("tp"), lax.axis_index("ctx")]).astype(jnp.int32)
    tokens, place = lax.optimization_barrier((tokens, place))
    x1, edge = call(
        functools.partial(first_rows, halo, size), "first_rows", [], [tokens],
        [bf16_rows(halo + size), bf16_rows(halo)], [],
    )
    edge = rotate(edge, "ctx", -1)
    tokens, x1 = lax.optimization_barrier((tokens, x1))
    x0, *others = call(
        functools.partial(next_rows, [0] + [j * size for j in range(2, CHUNKS)]), "next_rows",
        [], [tokens], [bf16_rows(size)] * (CHUNKS - 1), [],
    )
    x = [x1, *others, x0]
    residue, norm_gain, skip_gain, *_ = lax.optimization_barrier((residue, norm_gain, skip_gain, *x))
    mode = residue * jnp.sqrt(-jnp.expm1(-2.0 * decay_rate))
    gain = norm_gain[None, :]
    skip = skip_gain[None, :]
    w_in, mode, gain, skip, *_ = lax.optimization_barrier((w_in, mode, gain, skip, *x))
    w_in = in_vmem(w_in)
    edge, w_in = lax.optimization_barrier((edge, w_in))
    w_in = pltpu.with_memory_space_constraint(w_in, pltpu.VMEM)
    *parts, edges = [[part] + [rotate(part, "tp", s) for s in range(1, pieces)] for part in x + [edge]]

    before = []
    for part, j in zip(parts, list(range(1, CHUNKS)) + [0]):
        results = run_signal(
            pieces, j * size, size, rows, taps, place, part, [] if j else edges, before, gain, w_in,
            w_short, decay_rate,
        )
        before = results[:5]
    normed, signal, marks, states, _ = before
    state, sent, normed, signal, states = lax.optimization_barrier(
        (results[5], results[6], normed, signal, states)
    )
    out_sizes = [rows // 4] * 4
    out_rows = [sum(out_sizes[:j]) for j in range(4)]
    small = [w_in, w_short, decay_rate, mode, skip]
    done = []

    def local_part():
        k = len(done)
        done.append(run_local(out_rows[k], out_sizes[k], taps, normed, signal, states, *small))

    def between(stride, others):
        if stride > 1 and not done:
            local_part()
            others, done[-1] = lax.optimization_barrier((others, done[-1]))
        return others

    carry = carried_in(state, sent, decay_rate, rows, "ctx", place, between)
    if not done:
        local_part()
    begin = done[0][2]
    own, came = [], []
    for j in range(len(out_sizes)):
        if j >= 2:
            arrived = slice((j - 2) * (pieces - 1), (j - 1) * (pieces - 1))
            normed, signal, carry, came[arrived] = lax.optimization_barrier(
                (normed, signal, carry, came[arrived])
            )
        if j > 0:
            local_part()
        send, kept = run_second(
            pieces, out_rows[j], out_sizes[j], rows, place, *done[j][:2], begin, marks, carry,
            decay_rate, mode, w_out,
        )
        own.append(kept)
        for s in range(1, pieces):
            came.append(rotate(send[(s - 1) * out_sizes[j] : s * out_sizes[j]], "tp", -s))
    early = out_rows[-1]
    cut = (len(out_sizes) - 1) * (pieces - 1)
    done = run_last(pieces, out_sizes[:-1], 0, own[:-1], came[:cut], [], rows)
    return run_last(pieces, out_sizes[-1:], early, own[-1:], came[cut:], [done], rows)


def solution(mesh):
    placed = (
        P("tp", "ctx"),
        P(),
        P(None, "tp", None),
        P(None, None, "tp"),
        P(None, "tp"),
        P(None, "tp"),
        P("tp"),
        P("tp", None),
    )
    return jax.shard_map(
        body, mesh=mesh, in_specs=placed, out_specs=P("tp", "ctx"), check_vma=False
    )
```

```python
import functools

import jax
import jax.numpy as jnp
from jax import lax
from jax.experimental import pallas as pl
from jax.experimental.pallas import tpu as pltpu
from jax.sharding import PartitionSpec as P


F32 = jnp.float32
BF16 = jnp.bfloat16
ROWS = 8
LANES = 128
BLOCK = 256
CHUNKS = 4
SPAN = 16
VMEM_LIMIT = 10 * 2**20
CONTRACT_LAST = (((1,), (1,)), ((), ()))
CONTRACT_FIRST = (((0,), (0,)), ((), ()))


def lane_groups(low, width):
    return [(start, min(LANES, low + width - start)) for start in range(low, low + width, LANES)]


def rows_as(row, width):
    return jnp.broadcast_to(row, (ROWS, width))


def tree_sum(terms):
    while len(terms) > 1:
        terms = [sum(terms[k + 1 : k + 2], terms[k]) for k in range(0, len(terms), 2)]
    return terms[0]


def token_picker(first_row, rows, tokens):
    length = tokens // ROWS
    row = lax.broadcasted_iota(jnp.int32, (rows, tokens), 0)
    column = lax.broadcasted_iota(jnp.int32, (rows, tokens), 1)
    wanted = lax.rem(row, ROWS) * length + lax.div(row, ROWS) + first_row // ROWS
    return jnp.where(column == wanted, 1.0, 0.0).astype(BF16)


def turned(pick, tokens):
    return lax.dot_general(pick, tokens, CONTRACT_LAST, preferred_element_type=F32).astype(BF16)


def first_rows(halo, size, tokens_ref, out_ref, edge_ref):
    tokens = tokens_ref.shape[1]
    row = lax.broadcasted_iota(jnp.int32, (halo, tokens), 0)
    column = lax.broadcasted_iota(jnp.int32, (halo, tokens), 1)
    last = edge_ref.shape[0]
    picks = [
        token_picker(size - halo, halo + size, tokens),
        jnp.where((row < last) & (column == tokens - last + row), 1.0, 0.0).astype(BF16),
    ]
    rows = turned(jnp.concatenate(picks, axis=0), tokens_ref[...])
    out_ref[...] = rows[: halo + size]
    edge_ref[...] = rows[halo + size : halo + size + last]


def next_rows(firsts, tokens_ref, *chunk_refs):
    tokens = tokens_ref.shape[1]
    for row, ref in zip(firsts, chunk_refs):
        ref[...] = turned(token_picker(row, ref.shape[0], tokens), tokens_ref[...])


def load_weights(places, w_hbm, out_ref, w_ref, sem):
    copies = [
        pltpu.make_async_copy(w_hbm.at[place], w_ref.at[place], sem.at[k])
        for k, place in enumerate(places)
    ]
    for copy in copies:
        copy.start()
    for (s, part), copy in zip(places, copies):
        copy.wait()
        out_ref[s, :, part] = w_ref[s, part, :].T


def short_conv(p_ref, short_ref, s, part, rows, taps):
    width = part.stop - part.start
    total = None
    for offset in range(taps):
        start = ROWS * (taps - 1 - offset)
        term = short_ref[offset, s : s + 1, part] * p_ref[start : start + rows, :width]
        total = term if total is None else total + term
    return total


def project(normed, w_ref, s, part):
    product = jnp.dot(normed, w_ref[s, :, part], preferred_element_type=F32)
    return product.astype(BF16).astype(F32)


def signal_stage(pieces, row, taps, *refs):
    refs = list(refs)
    me_ref = refs.pop(0)
    token_refs = [refs.pop(0) for _ in range(pieces)]
    x_ref, p_ref = refs[-2:]
    halo = ROWS * (taps - 1)
    rows, share = p_ref.shape[0] - halo, token_refs[0].shape[1]
    last, start = row == 0, row == rows
    fresh = last or start
    read = rows + halo if fresh else rows
    edge_refs = [refs.pop(0) for _ in range(pieces)] if last else []
    if not start:
        normed_in, _, _, states_in, tail_in = [refs.pop(0) for _ in range(5)]
    gain_ref, w_ref, short_ref, rate_ref = refs[:4]
    normed_ref, signal_ref, marks_ref, states_ref, tail_ref = refs[4:9]
    total_ref, sent_ref = refs[9:11] if last else (None, None)
    modes, channels = rate_ref.shape
    length = signal_ref.shape[0] // ROWS
    me = me_ref[0]

    values = [ref[...].astype(F32) for ref in token_refs]
    if last:
        preceded = jnp.where(me_ref[1] > 0, 1.0, 0.0)
        blank = jnp.zeros((ROWS - 1, share), F32)
        for s, ref in enumerate(edge_refs):
            edge = ref[...].astype(F32) * preceded
            front = [piece for k in range(taps - 1) for piece in (edge[k : k + 1], blank)]
            values[s] = jnp.concatenate(front + [values[s]], axis=0)
    for rank in range(pieces):
        chosen = values[0]
        for s in range(1, pieces):
            chosen = jnp.where(me == (rank - s) % pieces, values[s], chosen)
        x_ref[:, rank * share : (rank + 1) * share] = chosen
    features = x_ref[...]
    mean = jnp.mean(features * features, axis=1, keepdims=True)
    normed = features * lax.rsqrt(mean + 1e-06) * gain_ref[...]
    if last:
        ends = normed_in[normed_in.shape[0] - halo :, :].astype(F32)
        segment = lax.broadcasted_iota(jnp.int32, (ROWS, ends.shape[1]), 0)
        front = [
            jnp.where(segment >= 1, pltpu.roll(ends[at : at + ROWS], 1, 0), normed[at : at + ROWS])
            for at in range(0, halo, ROWS)
        ]
        normed = jnp.concatenate(front + [normed[halo:]], axis=0)
    normed = normed.astype(BF16)
    begin = row if fresh else halo + row
    normed_ref[begin : begin + read, :] = normed

    for low in range(0, channels, BLOCK):
        width = min(BLOCK, channels - low)
        part = slice(low, low + width)
        for s in (1, 2):
            if not fresh:
                p_ref[:halo, :width] = tail_in[s - 1, :, part]
            p_ref[halo + rows - read :, :width] = project(
                normed_ref[begin : begin + read, :], w_ref, s, part
            )
            tail_ref[s - 1, :, part] = p_ref[rows:, :width]
            short = short_conv(p_ref, short_ref, s, part, rows, taps)
            if s == 1:
                signal_ref[row : row + rows, part] = short
            else:
                signal_ref[row : row + rows, part] = signal_ref[row : row + rows, part] * short
        for start, size in lane_groups(low, width):
            lanes = slice(start, start + size)
            rate = [rows_as(rate_ref[n : n + 1, lanes], size) for n in range(modes)]
            decay = [jnp.exp(-r) for r in rate]

            if fresh:
                states = (jnp.zeros((ROWS, size), F32),) * modes
            else:
                states = tuple(states_in[n, :, lanes] for n in range(modes))
                for n in range(modes):
                    marks_ref[row // rows, n, :, lanes] = states[n]

            def step(i, states):
                here = pl.ds(pl.multiple_of(row + i * ROWS, ROWS), ROWS)
                now = signal_ref[here, lanes]
                return tuple(states[n] * decay[n] + now for n in range(modes))

            states = lax.fori_loop(0, rows // ROWS, step, states, unroll=8)
            if last:
                later = length - rows // ROWS
                for n in range(modes):
                    marks_ref[1, n, :, lanes] = states[n]
                states = tuple(
                    states_in[n, :, lanes] + jnp.exp(-rate[n] * later) * states[n]
                    for n in range(modes)
                )
            for n in range(modes):
                states_ref[n, :, lanes] = states[n]
            if last:
                left = lax.broadcasted_iota(jnp.int32, (ROWS, size), 0)
                left = ((ROWS - 1 - left) * length).astype(F32)
                for n in range(modes):
                    total_ref[n : n + 1, lanes] = jnp.sum(
                        states[n] * jnp.exp(-rate[n] * left), axis=0, keepdims=True
                    )
                sent_ref[:, lanes] = total_ref[:, lanes].astype(BF16)


def local_stage(row, rows, taps, *refs):
    normed_ref, signal_ref, states_ref, w_ref, short_ref, rate_ref, mode_ref, skip_ref = refs[:8]
    q_ref, local_ref = refs[8:10]
    begin_ref = refs[10] if row == 0 else None
    p_ref = refs[-1]
    modes, channels = rate_ref.shape
    length = signal_ref.shape[0] // ROWS
    for low in range(0, channels, BLOCK):
        width = min(BLOCK, channels - low)
        part = slice(low, low + width)
        normed = normed_ref[row : row + p_ref.shape[0], :]
        p_ref[:, :width] = project(normed, w_ref, 0, part)
        q_ref[:, part] = short_conv(p_ref, short_ref, 0, part, rows, taps)
        for start, size in lane_groups(low, width):
            lanes = slice(start, start + size)
            rate = [rows_as(rate_ref[n : n + 1, lanes], size) for n in range(modes)]
            segment = lax.broadcasted_iota(jnp.int32, (ROWS, size), 0)
            if row == 0:
                for n in range(modes):
                    run = states_ref[n, :, lanes]
                    for hop in (1, 2, 4):
                        weight = jnp.where(segment >= hop, jnp.exp(-rate[n] * (hop * length)), 0.0)
                        run = run + weight * pltpu.roll(run, hop, 0)
                    begin_ref[n, :, lanes] = jnp.where(segment >= 1, pltpu.roll(run, 1, 0), 0.0)
            lag = segment.astype(F32)
            filters = []
            for first_lag in range(0, SPAN, ROWS):
                values = tree_sum(
                    [
                        rows_as(mode_ref[n : n + 1, lanes], size)
                        * jnp.exp(-rate[n] * (lag + first_lag))
                        for n in range(modes)
                    ]
                )
                filters += [rows_as(values[j : j + 1, :], size) for j in range(ROWS)]
            filters[0] = filters[0] + skip_ref[:, lanes]

            def span(i, carry):
                base = i * (SPAN * ROWS)
                now = [
                    signal_ref[pl.ds(pl.multiple_of(row + base + k * ROWS, ROWS), ROWS), lanes]
                    for k in range(SPAN)
                ]
                for k in range(SPAN):
                    local_ref[pl.ds(pl.multiple_of(base + k * ROWS, ROWS), ROWS), lanes] = tree_sum(
                        [filters[j] * now[k - j] for j in range(k + 1)]
                    )
                return carry

            lax.fori_loop(0, rows // (SPAN * ROWS), span, 0)


def second_stage(pieces, row, rows, length, *refs):
    me_ref, q_ref, local_ref, begin_ref, marks_ref, carry_ref, rate_ref, mode_ref, w_ref = refs[:9]
    send_ref, own_ref, gated_ref = refs[9:]
    modes, channels = rate_ref.shape
    for start, size in lane_groups(0, channels):
        lanes = slice(start, start + size)
        rate = [rows_as(rate_ref[n : n + 1, lanes], size) for n in range(modes)]
        decay = [jnp.exp(-r) for r in rate]
        segment = lax.broadcasted_iota(jnp.int32, (ROWS, size), 0)
        past = (segment * length).astype(F32)
        for at in range(row, row + rows, SPAN * ROWS):
            mark = at // (SPAN * ROWS)
            states = []
            for n in range(modes):
                state = begin_ref[n, :, lanes] + jnp.exp(-rate[n] * past) * carry_ref[
                    n : n + 1, lanes
                ]
                if mark > 0:
                    state = marks_ref[1, n, :, lanes] + state * jnp.exp(-rate[n] * SPAN)
                if mark > 1:
                    state = marks_ref[mark, n, :, lanes] + state * jnp.exp(
                        -rate[n] * (SPAN * (mark - 1))
                    )
                states.append(mode_ref[n : n + 1, lanes] * state)

            def step(i, states):
                here = pl.ds(pl.multiple_of(at - row + i * ROWS, ROWS), ROWS)
                states = tuple(states[n] * decay[n] for n in range(modes))
                gated_ref[here, lanes] = q_ref[here, lanes] * tree_sum(
                    [local_ref[here, lanes]] + list(states)
                )
                return states

            lax.fori_loop(0, SPAN, step, tuple(states), unroll=4)
    product = jnp.dot(gated_ref[...].astype(BF16), w_ref[...], preferred_element_type=F32)
    share = own_ref.shape[1]
    me = me_ref[0]
    columns = [product[:, rank * share : (rank + 1) * share] for rank in range(pieces)]
    for s in range(pieces):
        chosen = columns[0]
        for rank in range(1, pieces):
            chosen = jnp.where(me == (rank - s) % pieces, columns[rank], chosen)
        if s == 0:
            own_ref[...] = chosen
        else:
            send_ref[(s - 1) * rows : s * rows, :] = chosen.astype(BF16)


def turned_back(rows, pick):
    return lax.dot_general(rows, pick, CONTRACT_FIRST, preferred_element_type=F32).astype(BF16)


def last_stage(pieces, sizes, row, more, *refs):
    chunks = len(sizes)
    own_refs, came_refs = refs[:chunks], refs[chunks : chunks * pieces]
    done_ref = refs[chunks * pieces] if more else None
    if more:
        out_ref, mixed_ref, rows_ref, sem = refs[-4:]
    else:
        out_ref, mixed_ref = refs[-2:]
    at = 0
    for j, size in enumerate(sizes):
        total = own_refs[j][...]
        for s in range(pieces - 1):
            total = total + came_refs[j * (pieces - 1) + s][...].astype(F32)
        mixed_ref[at : at + size, :] = total.astype(BF16)
        at += size
    if not more:
        pick = token_picker(row, at, out_ref.shape[1])
        out_ref[...] = turned_back(mixed_ref[...], pick)
        return
    share, tokens = rows_ref.shape
    pick = token_picker(row, at, tokens)
    copies = []
    for low in range(0, share, BLOCK):
        part = slice(low, min(low + BLOCK, share))
        rows_ref[part, :] = done_ref[part, :] + turned_back(mixed_ref[:, part], pick)
        copy = pltpu.make_async_copy(rows_ref.at[part], out_ref.at[part], sem.at[len(copies)])
        copy.start()
        copies.append(copy)
    for copy in copies:
        copy.wait()


def call(kernel, name, scalars, operands, outs, scratch, aliases={}, out_space=pltpu.VMEM):
    vmem = pl.BlockSpec(memory_space=pltpu.VMEM)
    smem = pl.BlockSpec(memory_space=pltpu.SMEM)
    return pl.pallas_call(
        kernel,
        out_shape=outs,
        in_specs=[smem] * len(scalars) + [vmem] * len(operands),
        out_specs=[pl.BlockSpec(memory_space=out_space)] * len(outs),
        scratch_shapes=scratch,
        input_output_aliases=aliases,
        compiler_params=pltpu.CompilerParams(vmem_limit_bytes=VMEM_LIMIT),
        cost_estimate=pl.CostEstimate(flops=1, bytes_accessed=1, transcendentals=0),
        name=name,
    )(*scalars, *operands)


def in_vmem(w):
    streams, channels, features = w.shape
    block = min(BLOCK, channels)
    places = [
        (s, slice(low, min(low + block, channels)))
        for s in (1, 2, 0)
        for low in range(0, channels, block)
    ]
    return pl.pallas_call(
        functools.partial(load_weights, places),
        out_shape=pltpu.VMEM((streams, features, channels), w.dtype),
        in_specs=[pl.BlockSpec(memory_space=pl.ANY)],
        out_specs=pl.BlockSpec(memory_space=pltpu.VMEM),
        scratch_shapes=[
            pltpu.VMEM(w.shape, w.dtype),
            pltpu.SemaphoreType.DMA((len(places),)),
        ],
        compiler_params=pltpu.CompilerParams(vmem_limit_bytes=46 * 2**20),
        cost_estimate=pl.CostEstimate(flops=1, bytes_accessed=1, transcendentals=0),
        name="load_weights",
    )(w)


def run_signal(pieces, row, rows, count, taps, place, tokens, edges, before, gain, w_in, w_short, rate):
    streams, features, channels = w_in.shape
    modes = rate.shape[0]
    halo = ROWS * (taps - 1)
    outs = [
        jax.ShapeDtypeStruct((halo + count, features), BF16),
        jax.ShapeDtypeStruct((count, channels), F32),
        jax.ShapeDtypeStruct((count // rows, modes, ROWS, channels), F32),
        jax.ShapeDtypeStruct((modes, ROWS, channels), F32),
        jax.ShapeDtypeStruct((streams - 1, halo, channels), F32),
    ]
    if row == 0:
        outs += [jax.ShapeDtypeStruct((modes, channels), kind) for kind in (F32, BF16)]
    return call(
        functools.partial(signal_stage, pieces, row, taps),
        "signal_stage",
        [place],
        list(tokens) + list(edges) + list(before) + [gain, w_in, w_short, rate],
        outs,
        [
            pltpu.VMEM((rows + (halo if row in (0, rows) else 0), features), F32),
            pltpu.VMEM((halo + rows, min(BLOCK, channels)), F32),
        ],
        aliases={1 + len(tokens) + len(edges) + k: k for k in range(3)} if before else {},
    )


def run_local(row, rows, taps, normed, signal, states, w_in, w_short, rate, mode, skip):
    channels = signal.shape[1]
    out = jax.ShapeDtypeStruct((rows, channels), F32)
    begin = jax.ShapeDtypeStruct(states.shape, F32)
    return call(
        functools.partial(local_stage, row, rows, taps),
        "local_stage",
        [],
        [normed, signal, states, w_in, w_short, rate, mode, skip],
        [out, out] + ([begin] if row == 0 else []),
        [pltpu.VMEM((rows + ROWS * (taps - 1), min(BLOCK, channels)), F32)],
    )


def run_second(pieces, row, rows, count, place, q, local, begin, marks, carry, rate, mode, w):
    channels, features = w.shape
    share = features // pieces
    return call(
        functools.partial(second_stage, pieces, row, rows, count // ROWS),
        "second_stage",
        [place],
        [q, local, begin, marks, carry, rate, mode, w],
        [
            jax.ShapeDtypeStruct((max(1, pieces - 1) * rows, share), BF16),
            jax.ShapeDtypeStruct((rows, share), F32),
        ],
        [pltpu.VMEM((rows, channels), F32)],
    )


def run_last(pieces, sizes, row, own, came, done, count):
    share = own[0].shape[1]
    scratch = [pltpu.VMEM((sum(sizes), share), BF16)]
    if done:
        scratch += [pltpu.VMEM((share, count), BF16), pltpu.SemaphoreType.DMA((-(-share // BLOCK),))]
    (out,) = call(
        functools.partial(last_stage, pieces, sizes, row, bool(done)),
        "last_stage",
        [],
        [*own, *came, *done],
        [jax.ShapeDtypeStruct((share, count), BF16)],
        scratch,
        out_space=pl.ANY if done else pltpu.VMEM,
    )
    return out


def rotate(value, axis, steps):
    count = lax.axis_size(axis)
    return lax.ppermute(value, axis, [((i + steps) % count, i) for i in range(count)])


def combine_states(span, stride, radix, count, *refs):
    place_ref, rate_ref, total_ref = refs[:3]
    others = refs[3 : 2 + radix]
    refs = refs[2 + radix :]
    carry_in = refs[0] if stride > 1 else None
    carry_ref = refs[1] if stride > 1 else refs[0]
    position = place_ref[1]
    digit = lax.rem(lax.div(position, stride), radix)
    inner = lax.rem(position, stride)
    unit = span * stride
    rate = rate_ref[...]
    before = jnp.zeros(rate.shape, F32)
    for shift in range(1, radix):
        reached = jnp.where(digit >= shift, 1.0, 0.0)
        other = others[shift - 1][...].astype(F32)
        before = before + jnp.exp(-rate * (unit * (shift - 1))) * (other * reached)
    if stride > 1:
        carry_ref[...] = carry_in[...] + jnp.exp(-rate * (span * inner).astype(F32)) * before
    else:
        carry_ref[...] = before
    if stride * radix < count:
        new = jnp.exp(-rate * (unit * (radix - 1 - digit)).astype(F32)) * total_ref[...]
        for shift in range(1, radix):
            at = lax.rem(digit - shift + radix, radix)
            weight = jnp.exp(-rate * (unit * (radix - 1 - at)).astype(F32))
            new = new + weight * others[shift - 1][...].astype(F32)
        refs[-2][...] = new
        refs[-1][...] = new.astype(BF16)


def carried_in(state, sent, rate, span, axis, place, between):
    count = lax.axis_size(axis)
    total, stride, carry = state, 1, []
    while stride < count:
        radix = 4 if count % (stride * 4) == 0 else 2
        assert count % (stride * radix) == 0
        group = stride * radix
        others = []
        for shift in range(1, radix):
            pairs = []
            for i in range(count):
                digit = (i // stride) % radix
                pairs.append((i + ((digit - shift) % radix - digit) * stride, i))
            others.append(lax.ppermute(sent, axis, pairs))
        others = between(stride, others)
        shape = jax.ShapeDtypeStruct(state.shape, F32)
        carry = call(
            functools.partial(combine_states, span, stride, radix, count),
            "combine_states",
            [place],
            [rate, total, *others, *carry],
            [shape, shape, jax.ShapeDtypeStruct(state.shape, BF16)] if group < count else [shape],
            [],
        )
        if group < count:
            *carry, total, sent = carry
        stride = group
    return carry[0]


def body(tokens, norm_gain, w_in, w_short, decay_rate, residue, skip_gain, w_out):
    pieces, count = lax.axis_size("tp"), lax.axis_size("ctx")
    share, rows = tokens.shape
    channels = w_in.shape[1]
    taps = w_short.shape[0]
    halo = ROWS * (taps - 1)
    size = SPAN * ROWS
    assert rows == CHUNKS * size
    bf16_rows = lambda size: jax.ShapeDtypeStruct((size, share), BF16)

    place = jnp.stack([lax.axis_index("tp"), lax.axis_index("ctx")]).astype(jnp.int32)
    tokens, place = lax.optimization_barrier((tokens, place))
    x1, edge = call(
        functools.partial(first_rows, halo, size), "first_rows", [], [tokens],
        [bf16_rows(halo + size), bf16_rows(taps - 1)], [],
    )
    edge = rotate(edge, "ctx", -1)
    tokens, x1 = lax.optimization_barrier((tokens, x1))
    x0, *others = call(
        functools.partial(next_rows, [0] + [j * size for j in range(2, CHUNKS)]), "next_rows",
        [], [tokens], [bf16_rows(size)] * (CHUNKS - 1), [],
    )
    x = [x1, *others, x0]
    residue, norm_gain, skip_gain, *_ = lax.optimization_barrier((residue, norm_gain, skip_gain, *x))
    mode = residue * jnp.sqrt(-jnp.expm1(-2.0 * decay_rate))
    gain = norm_gain[None, :]
    skip = skip_gain[None, :]
    w_in, mode, gain, skip, *_ = lax.optimization_barrier((w_in, mode, gain, skip, *x))
    w_in = in_vmem(w_in)
    edge, w_in = lax.optimization_barrier((edge, w_in))
    w_in = pltpu.with_memory_space_constraint(w_in, pltpu.VMEM)
    *parts, edges = [[part] + [rotate(part, "tp", s) for s in range(1, pieces)] for part in x + [edge]]

    before = []
    for part, j in zip(parts, list(range(1, CHUNKS)) + [0]):
        results = run_signal(
            pieces, j * size, size, rows, taps, place, part, [] if j else edges, before, gain, w_in,
            w_short, decay_rate,
        )
        before = results[:5]
    normed, signal, marks, states, _ = before
    state, sent, normed, signal, states = lax.optimization_barrier(
        (results[5], results[6], normed, signal, states)
    )
    out_sizes = [rows // 4] * 4
    out_rows = [sum(out_sizes[:j]) for j in range(4)]
    small = [w_in, w_short, decay_rate, mode, skip]
    done = []

    def local_part():
        k = len(done)
        done.append(run_local(out_rows[k], out_sizes[k], taps, normed, signal, states, *small))

    def between(stride, others):
        if stride > 1 and not done:
            local_part()
            others, done[-1] = lax.optimization_barrier((others, done[-1]))
        return others

    carry = carried_in(state, sent, decay_rate, rows, "ctx", place, between)
    if not done:
        local_part()
    begin = done[0][2]
    own, came = [], []
    for j in range(len(out_sizes)):
        if j >= 2:
            arrived = slice((j - 2) * (pieces - 1), (j - 1) * (pieces - 1))
            normed, signal, carry, came[arrived] = lax.optimization_barrier(
                (normed, signal, carry, came[arrived])
            )
        if j > 0:
            local_part()
        send, kept = run_second(
            pieces, out_rows[j], out_sizes[j], rows, place, *done[j][:2], begin, marks, carry,
            decay_rate, mode, w_out,
        )
        own.append(kept)
        for s in range(1, pieces):
            came.append(rotate(send[(s - 1) * out_sizes[j] : s * out_sizes[j]], "tp", -s))
    early = out_rows[-1]
    cut = (len(out_sizes) - 1) * (pieces - 1)
    done = run_last(pieces, out_sizes[:-1], 0, own[:-1], came[:cut], [], rows)
    return run_last(pieces, out_sizes[-1:], early, own[-1:], came[cut:], [done], rows)


def solution(mesh):
    placed = (
        P("tp", "ctx"),
        P(),
        P(None, "tp", None),
        P(None, None, "tp"),
        P(None, "tp"),
        P(None, "tp"),
        P("tp"),
        P("tp", None),
    )
    return jax.shard_map(
        body, mesh=mesh, in_specs=placed, out_specs=P("tp", "ctx"), check_vma=False
    )
```

```python
import functools

import jax
import jax.numpy as jnp
from jax import lax
from jax.experimental import pallas as pl
from jax.experimental.pallas import tpu as pltpu
from jax.sharding import PartitionSpec as P


F32 = jnp.float32
BF16 = jnp.bfloat16
ROWS = 8
LANES = 128
BLOCK = 256
CHUNKS = 4
SPAN = 16
VMEM_LIMIT = 10 * 2**20
CONTRACT_LAST = (((1,), (1,)), ((), ()))
CONTRACT_FIRST = (((0,), (0,)), ((), ()))


def lane_groups(low, width):
    return [(start, min(LANES, low + width - start)) for start in range(low, low + width, LANES)]


def rows_as(row, width):
    return jnp.broadcast_to(row, (ROWS, width))


def decays(rate_ref, lanes, size, steps):
    values = jnp.exp(-rate_ref[:, lanes] * steps)
    return [rows_as(values[n : n + 1, :], size) for n in range(values.shape[0])]


def sums_of_rows(values):
    row = lax.broadcasted_iota(jnp.int32, values[0].shape, 0)
    count = len(values)
    values = list(values) + [jnp.zeros_like(values[0])] * (ROWS - count)
    for hop in (4, 2, 1):
        low = lax.rem(row, 2 * hop) < hop
        joined = []
        for a, b in zip(values[:hop], values[hop:]):
            other = jnp.where(low, b, a)
            if 2 * hop == ROWS:
                other = pltpu.roll(other, hop, 0)
            else:
                other = jnp.where(low, pltpu.roll(other, ROWS - hop, 0), pltpu.roll(other, hop, 0))
            joined.append(jnp.where(low, a, b) + other)
        values = joined
    return values[0][:count]


def tree_sum(terms):
    while len(terms) > 1:
        terms = [sum(terms[k + 1 : k + 2], terms[k]) for k in range(0, len(terms), 2)]
    return terms[0]


def token_picker(first_row, rows, tokens):
    length = tokens // ROWS
    row = lax.broadcasted_iota(jnp.int32, (rows, tokens), 0)
    column = lax.broadcasted_iota(jnp.int32, (rows, tokens), 1)
    wanted = lax.rem(row, ROWS) * length + lax.div(row, ROWS) + first_row // ROWS
    return jnp.where(column == wanted, 1.0, 0.0).astype(BF16)


def turned(pick, tokens):
    return lax.dot_general(pick, tokens, CONTRACT_LAST, preferred_element_type=F32).astype(BF16)


def first_rows(halo, size, tokens_ref, out_ref, edge_ref):
    tokens = tokens_ref.shape[1]
    row = lax.broadcasted_iota(jnp.int32, (halo, tokens), 0)
    column = lax.broadcasted_iota(jnp.int32, (halo, tokens), 1)
    last = edge_ref.shape[0]
    picks = [
        token_picker(size - halo, halo + size, tokens),
        jnp.where((row < last) & (column == tokens - last + row), 1.0, 0.0).astype(BF16),
    ]
    rows = turned(jnp.concatenate(picks, axis=0), tokens_ref[...])
    out_ref[...] = rows[: halo + size]
    edge_ref[...] = rows[halo + size : halo + size + last]


def next_rows(firsts, tokens_ref, *chunk_refs):
    tokens = tokens_ref.shape[1]
    for row, ref in zip(firsts, chunk_refs):
        ref[...] = turned(token_picker(row, ref.shape[0], tokens), tokens_ref[...])


def load_weights(places, w_hbm, out_ref, w_ref, sem):
    copies = [
        pltpu.make_async_copy(w_hbm.at[place], w_ref.at[place], sem.at[k])
        for k, place in enumerate(places)
    ]
    for copy in copies:
        copy.start()
    for (s, part), copy in zip(places, copies):
        copy.wait()
        out_ref[s, :, part] = w_ref[s, part, :].T


def short_conv(p_ref, short_ref, s, part, rows, taps):
    width = part.stop - part.start
    total = None
    for offset in range(taps):
        start = ROWS * (taps - 1 - offset)
        term = short_ref[offset, s : s + 1, part] * p_ref[start : start + rows, :width]
        total = term if total is None else total + term
    return total


def project(normed, w_ref, s, part):
    product = jnp.dot(normed, w_ref[s, :, part], preferred_element_type=F32)
    return product.astype(BF16).astype(F32)


def signal_stage(pieces, row, taps, *refs):
    refs = list(refs)
    me_ref = refs.pop(0)
    token_refs = [refs.pop(0) for _ in range(pieces)]
    x_ref, p_ref = refs[-2:]
    halo = ROWS * (taps - 1)
    rows, share = p_ref.shape[0] - halo, token_refs[0].shape[1]
    last, start = row == 0, row == rows
    fresh = last or start
    read = rows + halo if fresh else rows
    edge_refs = [refs.pop(0) for _ in range(pieces)] if last else []
    if not start:
        normed_in, _, _, states_in, tail_in = [refs.pop(0) for _ in range(5)]
    gain_ref, w_ref, short_ref, rate_ref = refs[:4]
    normed_ref, signal_ref, marks_ref, states_ref, tail_ref = refs[4:9]
    total_ref, sent_ref = refs[9:11] if last else (None, None)
    modes, channels = rate_ref.shape
    length = signal_ref.shape[0] // ROWS
    me = me_ref[0]

    values = [ref[...].astype(F32) for ref in token_refs]
    if last:
        preceded = jnp.where(me_ref[1] > 0, 1.0, 0.0)
        blank = jnp.zeros((ROWS - 1, share), F32)
        for s, ref in enumerate(edge_refs):
            edge = ref[...].astype(F32) * preceded
            front = [piece for k in range(taps - 1) for piece in (edge[k : k + 1], blank)]
            values[s] = jnp.concatenate(front + [values[s]], axis=0)
    for rank in range(pieces):
        chosen = values[0]
        for s in range(1, pieces):
            chosen = jnp.where(me == (rank - s) % pieces, values[s], chosen)
        x_ref[:, rank * share : (rank + 1) * share] = chosen
    features = x_ref[...]
    mean = jnp.mean(features * features, axis=1, keepdims=True)
    normed = features * lax.rsqrt(mean + 1e-06) * gain_ref[...]
    if last:
        ends = normed_in[normed_in.shape[0] - halo :, :].astype(F32)
        segment = lax.broadcasted_iota(jnp.int32, (ROWS, ends.shape[1]), 0)
        front = [
            jnp.where(segment >= 1, pltpu.roll(ends[at : at + ROWS], 1, 0), normed[at : at + ROWS])
            for at in range(0, halo, ROWS)
        ]
        normed = jnp.concatenate(front + [normed[halo:]], axis=0)
    normed = normed.astype(BF16)
    begin = row if fresh else halo + row
    normed_ref[begin : begin + read, :] = normed

    for low in range(0, channels, BLOCK):
        width = min(BLOCK, channels - low)
        part = slice(low, low + width)
        for s in (1, 2):
            if not fresh:
                p_ref[:halo, :width] = tail_in[s - 1, :, part]
            p_ref[halo + rows - read :, :width] = project(
                normed_ref[begin : begin + read, :], w_ref, s, part
            )
            tail_ref[s - 1, :, part] = p_ref[rows:, :width]
            short = short_conv(p_ref, short_ref, s, part, rows, taps)
            if s == 1:
                signal_ref[row : row + rows, part] = short
            else:
                signal_ref[row : row + rows, part] = signal_ref[row : row + rows, part] * short
        for start, size in lane_groups(low, width):
            lanes = slice(start, start + size)
            decay = decays(rate_ref, lanes, size, 1.0)

            if fresh:
                states = (jnp.zeros((ROWS, size), F32),) * modes
            else:
                states = tuple(states_in[n, :, lanes] for n in range(modes))
                for n in range(modes):
                    marks_ref[row // rows, n, :, lanes] = states[n]

            def step(i, states):
                here = pl.ds(pl.multiple_of(row + i * ROWS, ROWS), ROWS)
                now = signal_ref[here, lanes]
                return tuple(states[n] * decay[n] + now for n in range(modes))

            states = lax.fori_loop(0, rows // ROWS, step, states, unroll=8)
            if last:
                for n in range(modes):
                    marks_ref[1, n, :, lanes] = states[n]
                later = decays(rate_ref, lanes, size, float(length - rows // ROWS))
                states = tuple(states_in[n, :, lanes] + later[n] * states[n] for n in range(modes))
            for n in range(modes):
                states_ref[n, :, lanes] = states[n]
            if last:
                left = lax.broadcasted_iota(jnp.int32, (ROWS, size), 0)
                left = ((ROWS - 1 - left) * length).astype(F32)
                for low_mode in range(0, modes, ROWS):
                    some = range(low_mode, min(low_mode + ROWS, modes))
                    total_ref[low_mode : low_mode + len(some), lanes] = sums_of_rows(
                        [
                            states[n] * jnp.exp(-rows_as(rate_ref[n : n + 1, lanes], size) * left)
                            for n in some
                        ]
                    )
                sent_ref[:, lanes] = total_ref[:, lanes].astype(BF16)


def local_stage(row, rows, taps, *refs):
    normed_ref, signal_ref, states_ref, w_ref, short_ref, rate_ref, mode_ref, skip_ref = refs[:8]
    q_ref, local_ref = refs[8:10]
    begin_ref, past_ref = refs[10:12] if row == 0 else (None, None)
    p_ref = refs[-1]
    modes, channels = rate_ref.shape
    length = signal_ref.shape[0] // ROWS
    for low in range(0, channels, BLOCK):
        width = min(BLOCK, channels - low)
        part = slice(low, low + width)
        normed = normed_ref[row : row + p_ref.shape[0], :]
        p_ref[:, :width] = project(normed, w_ref, 0, part)
        q_ref[:, part] = short_conv(p_ref, short_ref, 0, part, rows, taps)
        for start, size in lane_groups(low, width):
            lanes = slice(start, start + size)
            rate = [rows_as(rate_ref[n : n + 1, lanes], size) for n in range(modes)]
            segment = lax.broadcasted_iota(jnp.int32, (ROWS, size), 0)
            if row == 0:
                for n in range(modes):
                    run = states_ref[n, :, lanes]
                    for hop in (1, 2, 4):
                        weight = jnp.where(segment >= hop, jnp.exp(-rate[n] * (hop * length)), 0.0)
                        run = run + weight * pltpu.roll(run, hop, 0)
                    mode = rows_as(mode_ref[n : n + 1, lanes], size)
                    begin = jnp.where(segment >= 1, pltpu.roll(run, 1, 0), 0.0)
                    begin_ref[n, :, lanes] = mode * begin
                    past = (segment * length).astype(F32)
                    past_ref[n, :, lanes] = mode * jnp.exp(-rate[n] * past)
            lag = segment.astype(F32)
            filters = []
            for first_lag in range(0, SPAN, ROWS):
                values = tree_sum(
                    [
                        rows_as(mode_ref[n : n + 1, lanes], size)
                        * jnp.exp(-rate[n] * (lag + first_lag))
                        for n in range(modes)
                    ]
                )
                filters += [rows_as(values[j : j + 1, :], size) for j in range(ROWS)]
            filters[0] = filters[0] + skip_ref[:, lanes]

            def span(i, carry):
                base = i * (SPAN * ROWS)
                now = [
                    signal_ref[pl.ds(pl.multiple_of(row + base + k * ROWS, ROWS), ROWS), lanes]
                    for k in range(SPAN)
                ]
                for k in range(SPAN):
                    local_ref[pl.ds(pl.multiple_of(base + k * ROWS, ROWS), ROWS), lanes] = tree_sum(
                        [filters[j] * now[k - j] for j in range(k + 1)]
                    )
                return carry

            lax.fori_loop(0, rows // (SPAN * ROWS), span, 0)


def second_stage(pieces, row, rows, *refs):
    me_ref, q_ref, local_ref, begin_ref, past_ref, marks_ref, carry_ref = refs[:7]
    rate_ref, mode_ref, w_ref, send_ref, own_ref, gated_ref = refs[7:]
    modes, channels = rate_ref.shape
    for start, size in lane_groups(0, channels):
        lanes = slice(start, start + size)
        decay = decays(rate_ref, lanes, size, 1.0)
        for at in range(row, row + rows, SPAN * ROWS):
            mark = at // (SPAN * ROWS)
            states = [
                begin_ref[n, :, lanes] + past_ref[n, :, lanes] * carry_ref[n : n + 1, lanes]
                for n in range(modes)
            ]
            for known, steps in ((1, SPAN), (mark, SPAN * (mark - 1))):
                if mark >= max(known, 1) and steps > 0:
                    less = decays(rate_ref, lanes, size, float(steps))
                    states = [
                        mode_ref[n : n + 1, lanes] * marks_ref[known, n, :, lanes]
                        + states[n] * less[n]
                        for n in range(modes)
                    ]

            def step(i, states):
                here = pl.ds(pl.multiple_of(at - row + i * ROWS, ROWS), ROWS)
                states = tuple(states[n] * decay[n] for n in range(modes))
                gated_ref[here, lanes] = q_ref[here, lanes] * tree_sum(
                    [local_ref[here, lanes]] + list(states)
                )
                return states

            lax.fori_loop(0, SPAN, step, tuple(states), unroll=4)
    product = jnp.dot(gated_ref[...].astype(BF16), w_ref[...], preferred_element_type=F32)
    share = own_ref.shape[1]
    me = me_ref[0]
    columns = [product[:, rank * share : (rank + 1) * share] for rank in range(pieces)]
    for s in range(pieces):
        chosen = columns[0]
        for rank in range(1, pieces):
            chosen = jnp.where(me == (rank - s) % pieces, columns[rank], chosen)
        if s == 0:
            own_ref[...] = chosen
        else:
            send_ref[(s - 1) * rows : s * rows, :] = chosen.astype(BF16)


def turned_back(rows, pick):
    return lax.dot_general(rows, pick, CONTRACT_FIRST, preferred_element_type=F32).astype(BF16)


def last_stage(pieces, sizes, row, more, *refs):
    chunks = len(sizes)
    own_refs, came_refs = refs[:chunks], refs[chunks : chunks * pieces]
    done_ref = refs[chunks * pieces] if more else None
    if more:
        out_ref, mixed_ref, rows_ref, sem = refs[-4:]
    else:
        out_ref, mixed_ref = refs[-2:]
    at = 0
    for j, size in enumerate(sizes):
        total = own_refs[j][...]
        for s in range(pieces - 1):
            total = total + came_refs[j * (pieces - 1) + s][...].astype(F32)
        mixed_ref[at : at + size, :] = total.astype(BF16)
        at += size
    if not more:
        pick = token_picker(row, at, out_ref.shape[1])
        out_ref[...] = turned_back(mixed_ref[...], pick)
        return
    share, tokens = rows_ref.shape
    pick = token_picker(row, at, tokens)
    copies = []
    for low in range(0, share, BLOCK):
        part = slice(low, min(low + BLOCK, share))
        rows_ref[part, :] = done_ref[part, :] + turned_back(mixed_ref[:, part], pick)
        copy = pltpu.make_async_copy(rows_ref.at[part], out_ref.at[part], sem.at[len(copies)])
        copy.start()
        copies.append(copy)
    for copy in copies:
        copy.wait()


def call(kernel, name, scalars, operands, outs, scratch, aliases={}, out_space=pltpu.VMEM):
    vmem = pl.BlockSpec(memory_space=pltpu.VMEM)
    smem = pl.BlockSpec(memory_space=pltpu.SMEM)
    return pl.pallas_call(
        kernel,
        out_shape=outs,
        in_specs=[smem] * len(scalars) + [vmem] * len(operands),
        out_specs=[pl.BlockSpec(memory_space=out_space)] * len(outs),
        scratch_shapes=scratch,
        input_output_aliases=aliases,
        compiler_params=pltpu.CompilerParams(vmem_limit_bytes=VMEM_LIMIT),
        cost_estimate=pl.CostEstimate(flops=1, bytes_accessed=1, transcendentals=0),
        name=name,
    )(*scalars, *operands)


def in_vmem(w):
    streams, channels, features = w.shape
    block = min(BLOCK, channels)
    places = [
        (s, slice(low, min(low + block, channels)))
        for s in (1, 2, 0)
        for low in range(0, channels, block)
    ]
    return pl.pallas_call(
        functools.partial(load_weights, places),
        out_shape=pltpu.VMEM((streams, features, channels), w.dtype),
        in_specs=[pl.BlockSpec(memory_space=pl.ANY)],
        out_specs=pl.BlockSpec(memory_space=pltpu.VMEM),
        scratch_shapes=[
            pltpu.VMEM(w.shape, w.dtype),
            pltpu.SemaphoreType.DMA((len(places),)),
        ],
        compiler_params=pltpu.CompilerParams(vmem_limit_bytes=46 * 2**20),
        cost_estimate=pl.CostEstimate(flops=1, bytes_accessed=1, transcendentals=0),
        name="load_weights",
    )(w)


def run_signal(pieces, row, rows, count, taps, place, tokens, edges, before, gain, w_in, w_short, rate):
    streams, features, channels = w_in.shape
    modes = rate.shape[0]
    halo = ROWS * (taps - 1)
    outs = [
        jax.ShapeDtypeStruct((halo + count, features), BF16),
        jax.ShapeDtypeStruct((count, channels), F32),
        jax.ShapeDtypeStruct((count // rows, modes, ROWS, channels), F32),
        jax.ShapeDtypeStruct((modes, ROWS, channels), F32),
        jax.ShapeDtypeStruct((streams - 1, halo, channels), F32),
    ]
    if row == 0:
        outs += [jax.ShapeDtypeStruct((modes, channels), kind) for kind in (F32, BF16)]
    return call(
        functools.partial(signal_stage, pieces, row, taps),
        "signal_stage",
        [place],
        list(tokens) + list(edges) + list(before) + [gain, w_in, w_short, rate],
        outs,
        [
            pltpu.VMEM((rows + (halo if row in (0, rows) else 0), features), F32),
            pltpu.VMEM((halo + rows, min(BLOCK, channels)), F32),
        ],
        aliases={1 + len(tokens) + len(edges) + k: k for k in range(3)} if before else {},
    )


def run_local(row, rows, taps, normed, signal, states, w_in, w_short, rate, mode, skip):
    channels = signal.shape[1]
    out = jax.ShapeDtypeStruct((rows, channels), F32)
    begin = jax.ShapeDtypeStruct(states.shape, F32)
    return call(
        functools.partial(local_stage, row, rows, taps),
        "local_stage",
        [],
        [normed, signal, states, w_in, w_short, rate, mode, skip],
        [out, out] + ([begin, begin] if row == 0 else []),
        [pltpu.VMEM((rows + ROWS * (taps - 1), min(BLOCK, channels)), F32)],
    )


def run_second(pieces, row, rows, place, q, local, begin, past, marks, carry, rate, mode, w):
    channels, features = w.shape
    share = features // pieces
    return call(
        functools.partial(second_stage, pieces, row, rows),
        "second_stage",
        [place],
        [q, local, begin, past, marks, carry, rate, mode, w],
        [
            jax.ShapeDtypeStruct((max(1, pieces - 1) * rows, share), BF16),
            jax.ShapeDtypeStruct((rows, share), F32),
        ],
        [pltpu.VMEM((rows, channels), F32)],
    )


def run_last(pieces, sizes, row, own, came, done, count):
    share = own[0].shape[1]
    scratch = [pltpu.VMEM((sum(sizes), share), BF16)]
    if done:
        scratch += [pltpu.VMEM((share, count), BF16), pltpu.SemaphoreType.DMA((-(-share // BLOCK),))]
    (out,) = call(
        functools.partial(last_stage, pieces, sizes, row, bool(done)),
        "last_stage",
        [],
        [*own, *came, *done],
        [jax.ShapeDtypeStruct((share, count), BF16)],
        scratch,
        out_space=pl.ANY if done else pltpu.VMEM,
    )
    return out


def rotate(value, axis, steps):
    count = lax.axis_size(axis)
    return lax.ppermute(value, axis, [((i + steps) % count, i) for i in range(count)])


def combine_states(span, stride, radix, count, *refs):
    place_ref, rate_ref, total_ref = refs[:3]
    others = refs[3 : 2 + radix]
    refs = refs[2 + radix :]
    carry_in = refs[0] if stride > 1 else None
    carry_ref = refs[1] if stride > 1 else refs[0]
    position = place_ref[1]
    digit = lax.rem(lax.div(position, stride), radix)
    inner = lax.rem(position, stride)
    unit = span * stride
    rate = rate_ref[...]
    before = jnp.zeros(rate.shape, F32)
    for shift in range(1, radix):
        reached = jnp.where(digit >= shift, 1.0, 0.0)
        other = others[shift - 1][...].astype(F32)
        before = before + jnp.exp(-rate * (unit * (shift - 1))) * (other * reached)
    if stride > 1:
        carry_ref[...] = carry_in[...] + jnp.exp(-rate * (span * inner).astype(F32)) * before
    else:
        carry_ref[...] = before
    if stride * radix < count:
        new = jnp.exp(-rate * (unit * (radix - 1 - digit)).astype(F32)) * total_ref[...]
        for shift in range(1, radix):
            at = lax.rem(digit - shift + radix, radix)
            weight = jnp.exp(-rate * (unit * (radix - 1 - at)).astype(F32))
            new = new + weight * others[shift - 1][...].astype(F32)
        refs[-2][...] = new
        refs[-1][...] = new.astype(BF16)


def carried_in(state, sent, rate, span, axis, place, between):
    count = lax.axis_size(axis)
    total, stride, carry = state, 1, []
    while stride < count:
        radix = 4 if count % (stride * 4) == 0 else 2
        assert count % (stride * radix) == 0
        group = stride * radix
        others = []
        for shift in reversed(range(1, radix)):
            pairs = []
            for i in range(count):
                digit = (i // stride) % radix
                pairs.append((i + ((digit - shift) % radix - digit) * stride, i))
            others.append(lax.ppermute(sent, axis, pairs))
        others = between(stride, others[::-1])
        shape = jax.ShapeDtypeStruct(state.shape, F32)
        carry = call(
            functools.partial(combine_states, span, stride, radix, count),
            "combine_states",
            [place],
            [rate, total, *others, *carry],
            [shape, shape, jax.ShapeDtypeStruct(state.shape, BF16)] if group < count else [shape],
            [],
        )
        if group < count:
            *carry, total, sent = carry
        stride = group
    return carry[0]


def body(tokens, norm_gain, w_in, w_short, decay_rate, residue, skip_gain, w_out):
    pieces, count = lax.axis_size("tp"), lax.axis_size("ctx")
    share, rows = tokens.shape
    channels = w_in.shape[1]
    taps = w_short.shape[0]
    halo = ROWS * (taps - 1)
    size = SPAN * ROWS
    assert rows == CHUNKS * size
    bf16_rows = lambda size: jax.ShapeDtypeStruct((size, share), BF16)

    place = jnp.stack([lax.axis_index("tp"), lax.axis_index("ctx")]).astype(jnp.int32)
    tokens, place = lax.optimization_barrier((tokens, place))
    x1, edge = call(
        functools.partial(first_rows, halo, size), "first_rows", [], [tokens],
        [bf16_rows(halo + size), bf16_rows(taps - 1)], [],
    )
    edge = rotate(edge, "ctx", -1)
    tokens, x1 = lax.optimization_barrier((tokens, x1))
    x0, *others = call(
        functools.partial(next_rows, [0] + [j * size for j in range(2, CHUNKS)]), "next_rows",
        [], [tokens], [bf16_rows(size)] * (CHUNKS - 1), [],
    )
    x = [x1, *others, x0]
    residue, norm_gain, skip_gain, *_ = lax.optimization_barrier((residue, norm_gain, skip_gain, *x))
    mode = residue * jnp.sqrt(-jnp.expm1(-2.0 * decay_rate))
    gain = norm_gain[None, :]
    skip = skip_gain[None, :]
    w_in, mode, gain, skip, *_ = lax.optimization_barrier((w_in, mode, gain, skip, *x))
    w_in = in_vmem(w_in)
    edge, w_in = lax.optimization_barrier((edge, w_in))
    w_in = pltpu.with_memory_space_constraint(w_in, pltpu.VMEM)
    *parts, edges = [[part] + [rotate(part, "tp", s) for s in range(1, pieces)] for part in x + [edge]]

    before = []
    for part, j in zip(parts, list(range(1, CHUNKS)) + [0]):
        results = run_signal(
            pieces, j * size, size, rows, taps, place, part, [] if j else edges, before, gain, w_in,
            w_short, decay_rate,
        )
        before = results[:5]
    normed, signal, marks, states, _ = before
    state, sent, normed, signal, states = lax.optimization_barrier(
        (results[5], results[6], normed, signal, states)
    )
    out_sizes = [rows // 4] * 4
    out_rows = [sum(out_sizes[:j]) for j in range(4)]
    small = [w_in, w_short, decay_rate, mode, skip]
    done = []

    def local_part():
        k = len(done)
        done.append(run_local(out_rows[k], out_sizes[k], taps, normed, signal, states, *small))

    def between(stride, others):
        if stride > 1 and not done:
            local_part()
            others, done[-1] = lax.optimization_barrier((others, done[-1]))
        return others

    carry = carried_in(state, sent, decay_rate, rows, "ctx", place, between)
    if not done:
        local_part()
    begin, past = done[0][2:]
    own, came = [], []
    for j in range(len(out_sizes)):
        if j >= 2:
            arrived = slice((j - 2) * (pieces - 1), (j - 1) * (pieces - 1))
            normed, signal, carry, came[arrived] = lax.optimization_barrier(
                (normed, signal, carry, came[arrived])
            )
        if j > 0:
            local_part()
        send, kept = run_second(
            pieces, out_rows[j], out_sizes[j], place, *done[j][:2], begin, past, marks, carry,
            decay_rate, mode, w_out,
        )
        own.append(kept)
        for s in range(1, pieces):
            came.append(rotate(send[(s - 1) * out_sizes[j] : s * out_sizes[j]], "tp", -s))
    early = out_rows[-1]
    cut = (len(out_sizes) - 1) * (pieces - 1)
    done = run_last(pieces, out_sizes[:-1], 0, own[:-1], came[:cut], [], rows)
    return run_last(pieces, out_sizes[-1:], early, own[-1:], came[cut:], [done], rows)


def solution(mesh):
    placed = (
        P("tp", "ctx"),
        P(),
        P(None, "tp", None),
        P(None, None, "tp"),
        P(None, "tp"),
        P(None, "tp"),
        P("tp"),
        P("tp", None),
    )
    return jax.shard_map(
        body, mesh=mesh, in_specs=placed, out_specs=P("tp", "ctx"), check_vma=False
    )
```

```python
import functools

import jax
import jax.numpy as jnp
from jax import lax
from jax.experimental import pallas as pl
from jax.experimental.pallas import tpu as pltpu
from jax.sharding import PartitionSpec as P


F32 = jnp.float32
BF16 = jnp.bfloat16
ROWS = 8
LANES = 128
BLOCK = 256
CHUNKS = 4
SPAN = 16
VMEM_LIMIT = 10 * 2**20
CONTRACT_LAST = (((1,), (1,)), ((), ()))
CONTRACT_FIRST = (((0,), (0,)), ((), ()))


def lane_groups(low, width):
    return [(start, min(LANES, low + width - start)) for start in range(low, low + width, LANES)]


def rows_as(row, width):
    return jnp.broadcast_to(row, (ROWS, width))


def decays(rate_ref, lanes, size, steps):
    values = jnp.exp(-rate_ref[:, lanes] * steps)
    return [rows_as(values[n : n + 1, :], size) for n in range(values.shape[0])]


def sums_of_rows(values):
    row = lax.broadcasted_iota(jnp.int32, values[0].shape, 0)
    count = len(values)
    values = list(values) + [jnp.zeros_like(values[0])] * (ROWS - count)
    for hop in (4, 2, 1):
        low = lax.rem(row, 2 * hop) < hop
        joined = []
        for a, b in zip(values[:hop], values[hop:]):
            other = jnp.where(low, b, a)
            if 2 * hop == ROWS:
                other = pltpu.roll(other, hop, 0)
            else:
                other = jnp.where(low, pltpu.roll(other, ROWS - hop, 0), pltpu.roll(other, hop, 0))
            joined.append(jnp.where(low, a, b) + other)
        values = joined
    return values[0][:count]


def tree_sum(terms):
    while len(terms) > 1:
        terms = [sum(terms[k + 1 : k + 2], terms[k]) for k in range(0, len(terms), 2)]
    return terms[0]


def token_picker(first_row, rows, tokens):
    length = tokens // ROWS
    row = lax.broadcasted_iota(jnp.int32, (rows, tokens), 0)
    column = lax.broadcasted_iota(jnp.int32, (rows, tokens), 1)
    wanted = lax.rem(row, ROWS) * length + lax.div(row, ROWS) + first_row // ROWS
    return jnp.where(column == wanted, 1.0, 0.0).astype(BF16)


def turned(pick, tokens):
    return lax.dot_general(pick, tokens, CONTRACT_LAST, preferred_element_type=F32).astype(BF16)


def first_rows(halo, size, tokens_ref, out_ref, edge_ref):
    tokens = tokens_ref.shape[1]
    row = lax.broadcasted_iota(jnp.int32, (halo, tokens), 0)
    column = lax.broadcasted_iota(jnp.int32, (halo, tokens), 1)
    last = edge_ref.shape[0]
    picks = [
        token_picker(size - halo, halo + size, tokens),
        jnp.where((row < last) & (column == tokens - last + row), 1.0, 0.0).astype(BF16),
    ]
    rows = turned(jnp.concatenate(picks, axis=0), tokens_ref[...])
    out_ref[...] = rows[: halo + size]
    edge_ref[...] = rows[halo + size : halo + size + last]


def next_rows(firsts, tokens_ref, *chunk_refs):
    tokens = tokens_ref.shape[1]
    for row, ref in zip(firsts, chunk_refs):
        ref[...] = turned(token_picker(row, ref.shape[0], tokens), tokens_ref[...])


def load_weights(places, w_hbm, out_ref, w_ref, sem):
    copies = [
        pltpu.make_async_copy(w_hbm.at[place], w_ref.at[place], sem.at[k])
        for k, place in enumerate(places)
    ]
    for copy in copies:
        copy.start()
    for (s, part), copy in zip(places, copies):
        copy.wait()
        out_ref[s, :, part] = w_ref[s, part, :].T


def short_conv(p_ref, short_ref, s, part, rows, taps):
    width = part.stop - part.start
    total = None
    for offset in range(taps):
        start = ROWS * (taps - 1 - offset)
        term = short_ref[offset, s : s + 1, part] * p_ref[start : start + rows, :width]
        total = term if total is None else total + term
    return total


def project(normed, w_ref, s, part):
    product = jnp.dot(normed, w_ref[s, :, part], preferred_element_type=F32)
    return product.astype(BF16).astype(F32)


def signal_stage(pieces, row, taps, *refs):
    refs = list(refs)
    me_ref = refs.pop(0)
    token_refs = [refs.pop(0) for _ in range(pieces)]
    x_ref, p_ref = refs[-2:]
    halo = ROWS * (taps - 1)
    rows, share = p_ref.shape[0] - halo, token_refs[0].shape[1]
    last, start = row == 0, row == rows
    fresh = last or start
    read = rows + halo if fresh else rows
    edge_refs = [refs.pop(0) for _ in range(pieces)] if last else []
    if not start:
        normed_in, _, _, states_in, tail_in = [refs.pop(0) for _ in range(5)]
    gain_ref, w_ref, short_ref, rate_ref = refs[:4]
    normed_ref, signal_ref, marks_ref, states_ref, tail_ref = refs[4:9]
    total_ref, sent_ref = refs[9:11] if last else (None, None)
    modes, channels = rate_ref.shape
    length = signal_ref.shape[0] // ROWS
    me = me_ref[0]

    values = [ref[...].astype(F32) for ref in token_refs]
    if last:
        preceded = jnp.where(me_ref[1] > 0, 1.0, 0.0)
        blank = jnp.zeros((ROWS - 1, share), F32)
        for s, ref in enumerate(edge_refs):
            edge = ref[...].astype(F32) * preceded
            front = [piece for k in range(taps - 1) for piece in (edge[k : k + 1], blank)]
            values[s] = jnp.concatenate(front + [values[s]], axis=0)
    for rank in range(pieces):
        chosen = values[0]
        for s in range(1, pieces):
            chosen = jnp.where(me == (rank - s) % pieces, values[s], chosen)
        x_ref[:, rank * share : (rank + 1) * share] = chosen
    features = x_ref[...]
    mean = jnp.mean(features * features, axis=1, keepdims=True)
    normed = features * lax.rsqrt(mean + 1e-06) * gain_ref[...]
    if last:
        ends = normed_in[normed_in.shape[0] - halo :, :].astype(F32)
        segment = lax.broadcasted_iota(jnp.int32, (ROWS, ends.shape[1]), 0)
        front = [
            jnp.where(segment >= 1, pltpu.roll(ends[at : at + ROWS], 1, 0), normed[at : at + ROWS])
            for at in range(0, halo, ROWS)
        ]
        normed = jnp.concatenate(front + [normed[halo:]], axis=0)
    normed = normed.astype(BF16)
    begin = row if fresh else halo + row
    normed_ref[begin : begin + read, :] = normed

    for low in range(0, channels, BLOCK):
        width = min(BLOCK, channels - low)
        part = slice(low, low + width)
        for s in (1, 2):
            if not fresh:
                p_ref[:halo, :width] = tail_in[s - 1, :, part]
            p_ref[halo + rows - read :, :width] = project(
                normed_ref[begin : begin + read, :], w_ref, s, part
            )
            tail_ref[s - 1, :, part] = p_ref[rows:, :width]
            short = short_conv(p_ref, short_ref, s, part, rows, taps)
            if s == 1:
                signal_ref[row : row + rows, part] = short
            else:
                signal_ref[row : row + rows, part] = signal_ref[row : row + rows, part] * short
        for start, size in lane_groups(low, width):
            lanes = slice(start, start + size)
            decay = decays(rate_ref, lanes, size, 1.0)

            if fresh:
                states = (jnp.zeros((ROWS, size), F32),) * modes
            else:
                states = tuple(states_in[n, :, lanes] for n in range(modes))
                for n in range(modes):
                    marks_ref[row // rows, n, :, lanes] = states[n]

            def step(i, states):
                here = pl.ds(pl.multiple_of(row + i * ROWS, ROWS), ROWS)
                now = signal_ref[here, lanes]
                return tuple(states[n] * decay[n] + now for n in range(modes))

            states = lax.fori_loop(0, rows // ROWS, step, states, unroll=8)
            if last:
                for n in range(modes):
                    marks_ref[1, n, :, lanes] = states[n]
                later = decays(rate_ref, lanes, size, float(length - rows // ROWS))
                states = tuple(states_in[n, :, lanes] + later[n] * states[n] for n in range(modes))
            for n in range(modes):
                states_ref[n, :, lanes] = states[n]
            if last:
                left = lax.broadcasted_iota(jnp.int32, (ROWS, size), 0)
                left = ((ROWS - 1 - left) * length).astype(F32)
                for low_mode in range(0, modes, ROWS):
                    some = range(low_mode, min(low_mode + ROWS, modes))
                    total_ref[low_mode : low_mode + len(some), lanes] = sums_of_rows(
                        [
                            states[n] * jnp.exp(-rows_as(rate_ref[n : n + 1, lanes], size) * left)
                            for n in some
                        ]
                    )
                sent_ref[:, lanes] = total_ref[:, lanes].astype(BF16)


def local_stage(row, rows, taps, *refs):
    normed_ref, signal_ref, states_ref, w_ref, short_ref, rate_ref, mode_ref, skip_ref = refs[:8]
    q_ref, local_ref = refs[8:10]
    begin_ref, past_ref = refs[10:12] if row == 0 else (None, None)
    p_ref = refs[-1]
    modes, channels = rate_ref.shape
    length = signal_ref.shape[0] // ROWS
    for low in range(0, channels, BLOCK):
        width = min(BLOCK, channels - low)
        part = slice(low, low + width)
        normed = normed_ref[row : row + p_ref.shape[0], :]
        p_ref[:, :width] = project(normed, w_ref, 0, part)
        q_ref[:, part] = short_conv(p_ref, short_ref, 0, part, rows, taps)
        for start, size in lane_groups(low, width):
            lanes = slice(start, start + size)
            rate = [rows_as(rate_ref[n : n + 1, lanes], size) for n in range(modes)]
            segment = lax.broadcasted_iota(jnp.int32, (ROWS, size), 0)
            if row == 0:
                for n in range(modes):
                    run = states_ref[n, :, lanes]
                    for hop in (1, 2, 4):
                        weight = jnp.where(segment >= hop, jnp.exp(-rate[n] * (hop * length)), 0.0)
                        run = run + weight * pltpu.roll(run, hop, 0)
                    mode = rows_as(mode_ref[n : n + 1, lanes], size)
                    begin = jnp.where(segment >= 1, pltpu.roll(run, 1, 0), 0.0)
                    begin_ref[n, :, lanes] = mode * begin
                    past = (segment * length).astype(F32)
                    past_ref[n, :, lanes] = mode * jnp.exp(-rate[n] * past)
            lag = segment.astype(F32)
            filters = []
            for first_lag in range(0, SPAN, ROWS):
                values = tree_sum(
                    [
                        rows_as(mode_ref[n : n + 1, lanes], size)
                        * jnp.exp(-rate[n] * (lag + first_lag))
                        for n in range(modes)
                    ]
                )
                filters += [rows_as(values[j : j + 1, :], size) for j in range(ROWS)]
            filters[0] = filters[0] + skip_ref[:, lanes]

            def span(i, carry):
                base = i * (SPAN * ROWS)
                now = [
                    signal_ref[pl.ds(pl.multiple_of(row + base + k * ROWS, ROWS), ROWS), lanes]
                    for k in range(SPAN)
                ]
                for k in range(SPAN):
                    local_ref[pl.ds(pl.multiple_of(base + k * ROWS, ROWS), ROWS), lanes] = tree_sum(
                        [filters[j] * now[k - j] for j in range(k + 1)]
                    )
                return carry

            lax.fori_loop(0, rows // (SPAN * ROWS), span, 0)


def second_stage(pieces, row, rows, *refs):
    me_ref, q_ref, local_ref, begin_ref, past_ref, marks_ref, carry_ref = refs[:7]
    rate_ref, mode_ref, w_ref, send_ref, own_ref, gated_ref = refs[7:]
    modes, channels = rate_ref.shape
    for start, size in lane_groups(0, channels):
        lanes = slice(start, start + size)
        decay = decays(rate_ref, lanes, size, 1.0)
        for at in range(row, row + rows, SPAN * ROWS):
            mark = at // (SPAN * ROWS)
            states = [
                begin_ref[n, :, lanes] + past_ref[n, :, lanes] * carry_ref[n : n + 1, lanes]
                for n in range(modes)
            ]
            for known, steps in ((1, SPAN), (mark, SPAN * (mark - 1))):
                if mark >= max(known, 1) and steps > 0:
                    less = decays(rate_ref, lanes, size, float(steps))
                    states = [
                        mode_ref[n : n + 1, lanes] * marks_ref[known, n, :, lanes]
                        + states[n] * less[n]
                        for n in range(modes)
                    ]

            def step(i, states):
                here = pl.ds(pl.multiple_of(at - row + i * ROWS, ROWS), ROWS)
                states = tuple(states[n] * decay[n] for n in range(modes))
                gated_ref[here, lanes] = q_ref[here, lanes] * tree_sum(
                    [local_ref[here, lanes]] + list(states)
                )
                return states

            lax.fori_loop(0, SPAN, step, tuple(states), unroll=4)
    product = jnp.dot(gated_ref[...].astype(BF16), w_ref[...], preferred_element_type=F32)
    share = own_ref.shape[1]
    me = me_ref[0]
    columns = [product[:, rank * share : (rank + 1) * share] for rank in range(pieces)]
    for s in range(pieces):
        chosen = columns[0]
        for rank in range(1, pieces):
            chosen = jnp.where(me == (rank - s) % pieces, columns[rank], chosen)
        if s == 0:
            own_ref[...] = chosen
        else:
            send_ref[(s - 1) * rows : s * rows, :] = chosen.astype(BF16)


def turned_back(rows, pick):
    return lax.dot_general(rows, pick, CONTRACT_FIRST, preferred_element_type=F32).astype(BF16)


def last_stage(pieces, sizes, row, more, *refs):
    chunks = len(sizes)
    own_refs, came_refs = refs[:chunks], refs[chunks : chunks * pieces]
    done_ref = refs[chunks * pieces] if more else None
    if more:
        out_ref, mixed_ref, rows_ref, sem = refs[-4:]
    else:
        out_ref, mixed_ref = refs[-2:]
    at = 0
    for j, size in enumerate(sizes):
        total = own_refs[j][...]
        for s in range(pieces - 1):
            total = total + came_refs[j * (pieces - 1) + s][...].astype(F32)
        mixed_ref[at : at + size, :] = total.astype(BF16)
        at += size
    if not more:
        pick = token_picker(row, at, out_ref.shape[1])
        out_ref[...] = turned_back(mixed_ref[...], pick)
        return
    share, tokens = rows_ref.shape
    pick = token_picker(row, at, tokens)
    copies = []
    for low in range(0, share, BLOCK):
        part = slice(low, min(low + BLOCK, share))
        rows_ref[part, :] = done_ref[part, :] + turned_back(mixed_ref[:, part], pick)
        copy = pltpu.make_async_copy(rows_ref.at[part], out_ref.at[part], sem.at[len(copies)])
        copy.start()
        copies.append(copy)
    for copy in copies:
        copy.wait()


def call(kernel, name, scalars, operands, outs, scratch, aliases={}, out_space=pltpu.VMEM):
    vmem = pl.BlockSpec(memory_space=pltpu.VMEM)
    smem = pl.BlockSpec(memory_space=pltpu.SMEM)
    return pl.pallas_call(
        kernel,
        out_shape=outs,
        in_specs=[smem] * len(scalars) + [vmem] * len(operands),
        out_specs=[pl.BlockSpec(memory_space=out_space)] * len(outs),
        scratch_shapes=scratch,
        input_output_aliases=aliases,
        compiler_params=pltpu.CompilerParams(vmem_limit_bytes=VMEM_LIMIT),
        cost_estimate=pl.CostEstimate(flops=1, bytes_accessed=1, transcendentals=0),
        name=name,
    )(*scalars, *operands)


def in_vmem(w):
    streams, channels, features = w.shape
    block = min(BLOCK, channels)
    places = [
        (s, slice(low, min(low + block, channels)))
        for s in (1, 2, 0)
        for low in range(0, channels, block)
    ]
    return pl.pallas_call(
        functools.partial(load_weights, places),
        out_shape=pltpu.VMEM((streams, features, channels), w.dtype),
        in_specs=[pl.BlockSpec(memory_space=pl.ANY)],
        out_specs=pl.BlockSpec(memory_space=pltpu.VMEM),
        scratch_shapes=[
            pltpu.VMEM(w.shape, w.dtype),
            pltpu.SemaphoreType.DMA((len(places),)),
        ],
        compiler_params=pltpu.CompilerParams(vmem_limit_bytes=46 * 2**20),
        cost_estimate=pl.CostEstimate(flops=1, bytes_accessed=1, transcendentals=0),
        name="load_weights",
    )(w)


def run_signal(pieces, row, rows, count, taps, place, tokens, edges, before, gain, w_in, w_short, rate):
    streams, features, channels = w_in.shape
    modes = rate.shape[0]
    halo = ROWS * (taps - 1)
    outs = [
        jax.ShapeDtypeStruct((halo + count, features), BF16),
        jax.ShapeDtypeStruct((count, channels), F32),
        jax.ShapeDtypeStruct((count // rows, modes, ROWS, channels), F32),
        jax.ShapeDtypeStruct((modes, ROWS, channels), F32),
        jax.ShapeDtypeStruct((streams - 1, halo, channels), F32),
    ]
    if row == 0:
        outs += [jax.ShapeDtypeStruct((modes, channels), kind) for kind in (F32, BF16)]
    return call(
        functools.partial(signal_stage, pieces, row, taps),
        "signal_stage",
        [place],
        list(tokens) + list(edges) + list(before) + [gain, w_in, w_short, rate],
        outs,
        [
            pltpu.VMEM((rows + (halo if row in (0, rows) else 0), features), F32),
            pltpu.VMEM((halo + rows, min(BLOCK, channels)), F32),
        ],
        aliases={1 + len(tokens) + len(edges) + k: k for k in range(3)} if before else {},
    )


def run_local(row, rows, taps, normed, signal, states, w_in, w_short, rate, mode, skip):
    channels = signal.shape[1]
    out = jax.ShapeDtypeStruct((rows, channels), F32)
    begin = jax.ShapeDtypeStruct(states.shape, F32)
    return call(
        functools.partial(local_stage, row, rows, taps),
        "local_stage",
        [],
        [normed, signal, states, w_in, w_short, rate, mode, skip],
        [out, out] + ([begin, begin] if row == 0 else []),
        [pltpu.VMEM((rows + ROWS * (taps - 1), min(BLOCK, channels)), F32)],
    )


def run_second(pieces, row, rows, place, q, local, begin, past, marks, carry, rate, mode, w):
    channels, features = w.shape
    share = features // pieces
    return call(
        functools.partial(second_stage, pieces, row, rows),
        "second_stage",
        [place],
        [q, local, begin, past, marks, carry, rate, mode, w],
        [
            jax.ShapeDtypeStruct((max(1, pieces - 1) * rows, share), BF16),
            jax.ShapeDtypeStruct((rows, share), F32),
        ],
        [pltpu.VMEM((rows, channels), F32)],
    )


def run_last(pieces, sizes, row, own, came, done, count):
    share = own[0].shape[1]
    scratch = [pltpu.VMEM((sum(sizes), share), BF16)]
    if done:
        scratch += [pltpu.VMEM((share, count), BF16), pltpu.SemaphoreType.DMA((-(-share // BLOCK),))]
    (out,) = call(
        functools.partial(last_stage, pieces, sizes, row, bool(done)),
        "last_stage",
        [],
        [*own, *came, *done],
        [jax.ShapeDtypeStruct((share, count), BF16)],
        scratch,
        out_space=pl.ANY if done else pltpu.VMEM,
    )
    return out


def rotate(value, axis, steps):
    count = lax.axis_size(axis)
    return lax.ppermute(value, axis, [((i + steps) % count, i) for i in range(count)])


def combine_states(span, stride, radix, count, *refs):
    place_ref, rate_ref, total_ref = refs[:3]
    others = refs[3 : 2 + radix]
    refs = refs[2 + radix :]
    carry_in = refs[0] if stride > 1 else None
    carry_ref = refs[1] if stride > 1 else refs[0]
    position = place_ref[1]
    digit = lax.rem(lax.div(position, stride), radix)
    inner = lax.rem(position, stride)
    unit = span * stride
    rate = rate_ref[...]
    before = jnp.zeros(rate.shape, F32)
    for shift in range(1, radix):
        reached = jnp.where(digit >= shift, 1.0, 0.0)
        other = others[shift - 1][: rate.shape[0], :].astype(F32)
        before = before + jnp.exp(-rate * (unit * (shift - 1))) * (other * reached)
    if stride > 1:
        carry_ref[...] = carry_in[...] + jnp.exp(-rate * (span * inner).astype(F32)) * before
    else:
        carry_ref[...] = before
    if stride * radix < count:
        new = jnp.exp(-rate * (unit * (radix - 1 - digit)).astype(F32)) * total_ref[...]
        for shift in range(1, radix):
            at = lax.rem(digit - shift + radix, radix)
            weight = jnp.exp(-rate * (unit * (radix - 1 - at)).astype(F32))
            new = new + weight * others[shift - 1][: rate.shape[0], :].astype(F32)
        refs[-3][...] = new
        refs[-2][...] = new.astype(BF16)
        modes = new.shape[0]
        refs[-1][:modes, :] = new.astype(BF16)
        refs[-1][modes:, :] = jnp.zeros((refs[-1].shape[0] - modes, new.shape[1]), BF16)


def carried_in(state, sent, rate, span, axis, place, between):
    count = lax.axis_size(axis)
    total, stride, carry, longer = state, 1, [], None
    modes, channels = state.shape
    while stride < count:
        radix = 4 if count % (stride * 4) == 0 else 2
        assert count % (stride * radix) == 0
        group = stride * radix
        others = []
        for shift in reversed(range(1, radix)):
            pairs = []
            for i in range(count):
                digit = (i // stride) % radix
                pairs.append((i + ((digit - shift) % radix - digit) * stride, i))
            first = shift == 1 and longer is not None
            others.append(lax.ppermute(longer if first else sent, axis, pairs))
        others = between(stride, others[::-1])
        shape = jax.ShapeDtypeStruct(state.shape, F32)
        carry = call(
            functools.partial(combine_states, span, stride, radix, count),
            "combine_states",
            [place],
            [rate, total, *others, *carry],
            [shape] if group == count else [shape, shape]
            + [jax.ShapeDtypeStruct((rows, channels), BF16) for rows in (modes, modes + ROWS)],
            [],
        )
        if group < count:
            *carry, total, sent, longer = carry
        stride = group
    return carry[0]


def body(tokens, norm_gain, w_in, w_short, decay_rate, residue, skip_gain, w_out):
    pieces, count = lax.axis_size("tp"), lax.axis_size("ctx")
    share, rows = tokens.shape
    channels = w_in.shape[1]
    taps = w_short.shape[0]
    halo = ROWS * (taps - 1)
    size = SPAN * ROWS
    assert rows == CHUNKS * size
    bf16_rows = lambda size: jax.ShapeDtypeStruct((size, share), BF16)

    place = jnp.stack([lax.axis_index("tp"), lax.axis_index("ctx")]).astype(jnp.int32)
    tokens, place = lax.optimization_barrier((tokens, place))
    x1, edge = call(
        functools.partial(first_rows, halo, size), "first_rows", [], [tokens],
        [bf16_rows(halo + size), bf16_rows(taps - 1)], [],
    )
    edge = rotate(edge, "ctx", -1)
    tokens, x1 = lax.optimization_barrier((tokens, x1))
    x0, *others = call(
        functools.partial(next_rows, [0] + [j * size for j in range(2, CHUNKS)]), "next_rows",
        [], [tokens], [bf16_rows(size)] * (CHUNKS - 1), [],
    )
    x = [x1, *others, x0]
    residue, norm_gain, skip_gain, *_ = lax.optimization_barrier((residue, norm_gain, skip_gain, *x))
    mode = residue * jnp.sqrt(-jnp.expm1(-2.0 * decay_rate))
    gain = norm_gain[None, :]
    skip = skip_gain[None, :]
    w_in, mode, gain, skip, *_ = lax.optimization_barrier((w_in, mode, gain, skip, *x))
    w_in = in_vmem(w_in)
    edge, w_in = lax.optimization_barrier((edge, w_in))
    w_in = pltpu.with_memory_space_constraint(w_in, pltpu.VMEM)
    *parts, edges = [[part] + [rotate(part, "tp", s) for s in range(1, pieces)] for part in x + [edge]]

    before = []
    for part, j in zip(parts, list(range(1, CHUNKS)) + [0]):
        results = run_signal(
            pieces, j * size, size, rows, taps, place, part, [] if j else edges, before, gain, w_in,
            w_short, decay_rate,
        )
        before = results[:5]
    normed, signal, marks, states, _ = before
    state, sent, normed, signal, states = lax.optimization_barrier(
        (results[5], results[6], normed, signal, states)
    )
    out_sizes = [rows // 4] * 4
    out_rows = [sum(out_sizes[:j]) for j in range(4)]
    small = [w_in, w_short, decay_rate, mode, skip]
    done = []

    def local_part():
        k = len(done)
        done.append(run_local(out_rows[k], out_sizes[k], taps, normed, signal, states, *small))

    def between(stride, others):
        if stride > 1 and not done:
            local_part()
            others, done[-1] = lax.optimization_barrier((others, done[-1]))
        return others

    carry = carried_in(state, sent, decay_rate, rows, "ctx", place, between)
    if not done:
        local_part()
    begin, past = done[0][2:]
    own, came = [], []
    for j in range(len(out_sizes)):
        if j >= 2:
            arrived = slice((j - 2) * (pieces - 1), (j - 1) * (pieces - 1))
            normed, signal, carry, came[arrived] = lax.optimization_barrier(
                (normed, signal, carry, came[arrived])
            )
        if j > 0:
            local_part()
        send, kept = run_second(
            pieces, out_rows[j], out_sizes[j], place, *done[j][:2], begin, past, marks, carry,
            decay_rate, mode, w_out,
        )
        own.append(kept)
        for s in range(1, pieces):
            came.append(rotate(send[(s - 1) * out_sizes[j] : s * out_sizes[j]], "tp", -s))
    early = out_rows[-1]
    cut = (len(out_sizes) - 1) * (pieces - 1)
    done = run_last(pieces, out_sizes[:-1], 0, own[:-1], came[:cut], [], rows)
    return run_last(pieces, out_sizes[-1:], early, own[-1:], came[cut:], [done], rows)


def solution(mesh):
    placed = (
        P("tp", "ctx"),
        P(),
        P(None, "tp", None),
        P(None, None, "tp"),
        P(None, "tp"),
        P(None, "tp"),
        P("tp"),
        P("tp", None),
    )
    return jax.shard_map(
        body, mesh=mesh, in_specs=placed, out_specs=P("tp", "ctx"), check_vma=False
    )
```

```python
import functools

import jax
import jax.numpy as jnp
from jax import lax
from jax.experimental import pallas as pl
from jax.experimental.pallas import tpu as pltpu
from jax.sharding import PartitionSpec as P


F32 = jnp.float32
BF16 = jnp.bfloat16
ROWS = 8
LANES = 128
BLOCK = 256
CHUNKS = 4
SPAN = 16
VMEM_LIMIT = 10 * 2**20
CONTRACT_LAST = (((1,), (1,)), ((), ()))
CONTRACT_FIRST = (((0,), (0,)), ((), ()))


def lane_groups(low, width):
    return [(start, min(LANES, low + width - start)) for start in range(low, low + width, LANES)]


def rows_as(row, width):
    return jnp.broadcast_to(row, (ROWS, width))


def decays(rate_ref, lanes, size, steps):
    values = jnp.exp(-rate_ref[:, lanes] * steps)
    return [rows_as(values[n : n + 1, :], size) for n in range(values.shape[0])]


def sums_of_rows(values):
    row = lax.broadcasted_iota(jnp.int32, values[0].shape, 0)
    count = len(values)
    values = list(values) + [jnp.zeros_like(values[0])] * (ROWS - count)
    for hop in (4, 2, 1):
        low = lax.rem(row, 2 * hop) < hop
        joined = []
        for a, b in zip(values[:hop], values[hop:]):
            other = jnp.where(low, b, a)
            if 2 * hop == ROWS:
                other = pltpu.roll(other, hop, 0)
            else:
                other = jnp.where(low, pltpu.roll(other, ROWS - hop, 0), pltpu.roll(other, hop, 0))
            joined.append(jnp.where(low, a, b) + other)
        values = joined
    return values[0][:count]


def tree_sum(terms):
    while len(terms) > 1:
        terms = [sum(terms[k + 1 : k + 2], terms[k]) for k in range(0, len(terms), 2)]
    return terms[0]


def token_picker(first_row, rows, tokens):
    length = tokens // ROWS
    row = lax.broadcasted_iota(jnp.int32, (rows, tokens), 0)
    column = lax.broadcasted_iota(jnp.int32, (rows, tokens), 1)
    wanted = lax.rem(row, ROWS) * length + lax.div(row, ROWS) + first_row // ROWS
    return jnp.where(column == wanted, 1.0, 0.0).astype(BF16)


def turned(pick, tokens):
    return lax.dot_general(pick, tokens, CONTRACT_LAST, preferred_element_type=F32).astype(BF16)


def first_rows(halo, size, tokens_ref, out_ref, edge_ref):
    tokens = tokens_ref.shape[1]
    row = lax.broadcasted_iota(jnp.int32, (halo, tokens), 0)
    column = lax.broadcasted_iota(jnp.int32, (halo, tokens), 1)
    last = edge_ref.shape[0]
    picks = [
        token_picker(size - halo, halo + size, tokens),
        jnp.where((row < last) & (column == tokens - last + row), 1.0, 0.0).astype(BF16),
    ]
    rows = turned(jnp.concatenate(picks, axis=0), tokens_ref[...])
    out_ref[...] = rows[: halo + size]
    edge_ref[...] = rows[halo + size : halo + size + last]


def next_rows(firsts, tokens_ref, *chunk_refs):
    tokens = tokens_ref.shape[1]
    for row, ref in zip(firsts, chunk_refs):
        ref[...] = turned(token_picker(row, ref.shape[0], tokens), tokens_ref[...])


def load_weights(places, w_hbm, out_ref, w_ref, sem):
    copies = [
        pltpu.make_async_copy(w_hbm.at[place], w_ref.at[place], sem.at[k])
        for k, place in enumerate(places)
    ]
    for copy in copies:
        copy.start()
    for (s, part), copy in zip(places, copies):
        copy.wait()
        out_ref[s, :, part] = w_ref[s, part, :].T


def short_conv(p_ref, short_ref, s, part, rows, taps):
    width = part.stop - part.start
    total = None
    for offset in range(taps):
        start = ROWS * (taps - 1 - offset)
        term = short_ref[offset, s : s + 1, part] * p_ref[start : start + rows, :width]
        total = term if total is None else total + term
    return total


def project(normed, w_ref, s, part):
    product = jnp.dot(normed, w_ref[s, :, part], preferred_element_type=F32)
    return product.astype(BF16).astype(F32)


def signal_stage(pieces, row, taps, *refs):
    refs = list(refs)
    me_ref = refs.pop(0)
    token_refs = [refs.pop(0) for _ in range(pieces)]
    x_ref, p_ref = refs[-2:]
    halo = ROWS * (taps - 1)
    rows, share = p_ref.shape[0] - halo, token_refs[0].shape[1]
    last, start = row == 0, row == rows
    fresh = last or start
    read = rows + halo if fresh else rows
    edge_refs = [refs.pop(0) for _ in range(pieces)] if last else []
    if not start:
        normed_in, _, _, states_in, tail_in = [refs.pop(0) for _ in range(5)]
    gain_ref, w_ref, short_ref, rate_ref = refs[:4]
    normed_ref, signal_ref, marks_ref, states_ref, tail_ref = refs[4:9]
    total_ref, sent_ref = refs[9:11] if last else (None, None)
    modes, channels = rate_ref.shape
    length = signal_ref.shape[0] // ROWS
    me = me_ref[0]

    values = [ref[...].astype(F32) for ref in token_refs]
    if last:
        preceded = jnp.where(me_ref[1] > 0, 1.0, 0.0)
        blank = jnp.zeros((ROWS - 1, share), F32)
        for s, ref in enumerate(edge_refs):
            edge = ref[...].astype(F32) * preceded
            front = [piece for k in range(taps - 1) for piece in (edge[k : k + 1], blank)]
            values[s] = jnp.concatenate(front + [values[s]], axis=0)
    for rank in range(pieces):
        chosen = values[0]
        for s in range(1, pieces):
            chosen = jnp.where(me == (rank - s) % pieces, values[s], chosen)
        x_ref[:, rank * share : (rank + 1) * share] = chosen
    features = x_ref[...]
    mean = jnp.mean(features * features, axis=1, keepdims=True)
    normed = features * lax.rsqrt(mean + 1e-06) * gain_ref[...]
    if last:
        ends = normed_in[normed_in.shape[0] - halo :, :].astype(F32)
        segment = lax.broadcasted_iota(jnp.int32, (ROWS, ends.shape[1]), 0)
        front = [
            jnp.where(segment >= 1, pltpu.roll(ends[at : at + ROWS], 1, 0), normed[at : at + ROWS])
            for at in range(0, halo, ROWS)
        ]
        normed = jnp.concatenate(front + [normed[halo:]], axis=0)
    normed = normed.astype(BF16)
    begin = row if fresh else halo + row
    normed_ref[begin : begin + read, :] = normed

    for low in range(0, channels, BLOCK):
        width = min(BLOCK, channels - low)
        part = slice(low, low + width)
        for s in (1, 2):
            if not fresh:
                p_ref[:halo, :width] = tail_in[s - 1, :, part]
            p_ref[halo + rows - read :, :width] = project(
                normed_ref[begin : begin + read, :], w_ref, s, part
            )
            tail_ref[s - 1, :, part] = p_ref[rows:, :width]
            short = short_conv(p_ref, short_ref, s, part, rows, taps)
            if s == 1:
                signal_ref[row : row + rows, part] = short
            else:
                signal_ref[row : row + rows, part] = signal_ref[row : row + rows, part] * short
        for start, size in lane_groups(low, width):
            lanes = slice(start, start + size)
            decay = decays(rate_ref, lanes, size, 1.0)

            if fresh:
                states = (jnp.zeros((ROWS, size), F32),) * modes
            else:
                states = tuple(states_in[n, :, lanes] for n in range(modes))
                for n in range(modes):
                    marks_ref[row // rows, n, :, lanes] = states[n]

            def step(i, states):
                here = pl.ds(pl.multiple_of(row + i * ROWS, ROWS), ROWS)
                now = signal_ref[here, lanes]
                return tuple(states[n] * decay[n] + now for n in range(modes))

            states = lax.fori_loop(0, rows // ROWS, step, states, unroll=8)
            if last:
                for n in range(modes):
                    marks_ref[1, n, :, lanes] = states[n]
                later = decays(rate_ref, lanes, size, float(length - rows // ROWS))
                states = tuple(states_in[n, :, lanes] + later[n] * states[n] for n in range(modes))
            for n in range(modes):
                states_ref[n, :, lanes] = states[n]
            if last:
                left = lax.broadcasted_iota(jnp.int32, (ROWS, size), 0)
                left = ((ROWS - 1 - left) * length).astype(F32)
                for low_mode in range(0, modes, ROWS):
                    some = range(low_mode, min(low_mode + ROWS, modes))
                    total_ref[low_mode : low_mode + len(some), lanes] = sums_of_rows(
                        [
                            states[n] * jnp.exp(-rows_as(rate_ref[n : n + 1, lanes], size) * left)
                            for n in some
                        ]
                    )
                sent_ref[:, lanes] = total_ref[:, lanes].astype(BF16)


def local_stage(row, rows, taps, *refs):
    normed_ref, signal_ref, states_ref, w_ref, short_ref, rate_ref, mode_ref, skip_ref = refs[:8]
    q_ref, local_ref = refs[8:10]
    begin_ref, past_ref = refs[10:12] if row == 0 else (None, None)
    p_ref = refs[-1]
    modes, channels = rate_ref.shape
    length = signal_ref.shape[0] // ROWS
    for low in range(0, channels, BLOCK):
        width = min(BLOCK, channels - low)
        part = slice(low, low + width)
        normed = normed_ref[row : row + p_ref.shape[0], :]
        p_ref[:, :width] = project(normed, w_ref, 0, part)
        q_ref[:, part] = short_conv(p_ref, short_ref, 0, part, rows, taps)
        for start, size in lane_groups(low, width):
            lanes = slice(start, start + size)
            rate = [rows_as(rate_ref[n : n + 1, lanes], size) for n in range(modes)]
            segment = lax.broadcasted_iota(jnp.int32, (ROWS, size), 0)
            if row == 0:
                for n in range(modes):
                    run = states_ref[n, :, lanes]
                    for hop in (1, 2, 4):
                        weight = jnp.where(segment >= hop, jnp.exp(-rate[n] * (hop * length)), 0.0)
                        run = run + weight * pltpu.roll(run, hop, 0)
                    mode = rows_as(mode_ref[n : n + 1, lanes], size)
                    begin = jnp.where(segment >= 1, pltpu.roll(run, 1, 0), 0.0)
                    begin_ref[n, :, lanes] = mode * begin
                    past = (segment * length).astype(F32)
                    past_ref[n, :, lanes] = mode * jnp.exp(-rate[n] * past)
            lag = segment.astype(F32)
            filters = []
            for first_lag in range(0, SPAN, ROWS):
                values = tree_sum(
                    [
                        rows_as(mode_ref[n : n + 1, lanes], size)
                        * jnp.exp(-rate[n] * (lag + first_lag))
                        for n in range(modes)
                    ]
                )
                filters += [rows_as(values[j : j + 1, :], size) for j in range(ROWS)]
            filters[0] = filters[0] + skip_ref[:, lanes]

            def span(i, carry):
                base = i * (SPAN * ROWS)
                now = [
                    signal_ref[pl.ds(pl.multiple_of(row + base + k * ROWS, ROWS), ROWS), lanes]
                    for k in range(SPAN)
                ]
                for k in range(SPAN):
                    local_ref[pl.ds(pl.multiple_of(base + k * ROWS, ROWS), ROWS), lanes] = tree_sum(
                        [filters[j] * now[k - j] for j in range(k + 1)]
                    )
                return carry

            lax.fori_loop(0, rows // (SPAN * ROWS), span, 0)


def second_stage(pieces, row, rows, *refs):
    me_ref, q_ref, local_ref, begin_ref, past_ref, marks_ref, carry_ref = refs[:7]
    rate_ref, mode_ref, w_ref, send_ref, own_ref, gated_ref = refs[7:]
    modes, channels = rate_ref.shape
    for start, size in lane_groups(0, channels):
        lanes = slice(start, start + size)
        decay = decays(rate_ref, lanes, size, 1.0)
        for at in range(row, row + rows, SPAN * ROWS):
            mark = at // (SPAN * ROWS)
            states = [
                begin_ref[n, :, lanes] + past_ref[n, :, lanes] * carry_ref[n : n + 1, lanes]
                for n in range(modes)
            ]
            for known, steps in ((1, SPAN), (mark, SPAN * (mark - 1))):
                if mark >= max(known, 1) and steps > 0:
                    less = decays(rate_ref, lanes, size, float(steps))
                    states = [
                        mode_ref[n : n + 1, lanes] * marks_ref[known, n, :, lanes]
                        + states[n] * less[n]
                        for n in range(modes)
                    ]

            def step(i, states):
                here = pl.ds(pl.multiple_of(at - row + i * ROWS, ROWS), ROWS)
                states = tuple(states[n] * decay[n] for n in range(modes))
                gated_ref[here, lanes] = q_ref[here, lanes] * tree_sum(
                    [local_ref[here, lanes]] + list(states)
                )
                return states

            lax.fori_loop(0, SPAN, step, tuple(states), unroll=4)
    product = jnp.dot(gated_ref[...].astype(BF16), w_ref[...], preferred_element_type=F32)
    share = own_ref.shape[1]
    me = me_ref[0]
    columns = [product[:, rank * share : (rank + 1) * share] for rank in range(pieces)]
    for s in range(pieces):
        chosen = columns[0]
        for rank in range(1, pieces):
            chosen = jnp.where(me == (rank - s) % pieces, columns[rank], chosen)
        if s == 0:
            own_ref[...] = chosen
        else:
            send_ref[(s - 1) * rows : s * rows, :] = chosen.astype(BF16)


def turned_back(rows, pick):
    return lax.dot_general(rows, pick, CONTRACT_FIRST, preferred_element_type=F32).astype(BF16)


def last_stage(pieces, sizes, row, more, *refs):
    chunks = len(sizes)
    own_refs, came_refs = refs[:chunks], refs[chunks : chunks * pieces]
    done_ref = refs[chunks * pieces] if more else None
    if more:
        out_ref, mixed_ref, rows_ref, sem = refs[-4:]
    else:
        out_ref, mixed_ref = refs[-2:]
    at = 0
    for j, size in enumerate(sizes):
        total = own_refs[j][...]
        for s in range(pieces - 1):
            total = total + came_refs[j * (pieces - 1) + s][...].astype(F32)
        mixed_ref[at : at + size, :] = total.astype(BF16)
        at += size
    if not more:
        pick = token_picker(row, at, out_ref.shape[1])
        out_ref[...] = turned_back(mixed_ref[...], pick)
        return
    share, tokens = rows_ref.shape
    pick = token_picker(row, at, tokens)
    copies = []
    for low in range(0, share, BLOCK):
        part = slice(low, min(low + BLOCK, share))
        rows_ref[part, :] = done_ref[part, :] + turned_back(mixed_ref[:, part], pick)
        copy = pltpu.make_async_copy(rows_ref.at[part], out_ref.at[part], sem.at[len(copies)])
        copy.start()
        copies.append(copy)
    for copy in copies:
        copy.wait()


def call(kernel, name, scalars, operands, outs, scratch, aliases={}, out_space=pltpu.VMEM):
    vmem = pl.BlockSpec(memory_space=pltpu.VMEM)
    smem = pl.BlockSpec(memory_space=pltpu.SMEM)
    return pl.pallas_call(
        kernel,
        out_shape=outs,
        in_specs=[smem] * len(scalars) + [vmem] * len(operands),
        out_specs=[pl.BlockSpec(memory_space=out_space)] * len(outs),
        scratch_shapes=scratch,
        input_output_aliases=aliases,
        compiler_params=pltpu.CompilerParams(vmem_limit_bytes=VMEM_LIMIT),
        cost_estimate=pl.CostEstimate(flops=1, bytes_accessed=1, transcendentals=0),
        name=name,
    )(*scalars, *operands)


def in_vmem(w):
    streams, channels, features = w.shape
    block = min(BLOCK, channels)
    places = [
        (s, slice(low, min(low + block, channels)))
        for s in (1, 2, 0)
        for low in range(0, channels, block)
    ]
    return pl.pallas_call(
        functools.partial(load_weights, places),
        out_shape=pltpu.VMEM((streams, features, channels), w.dtype),
        in_specs=[pl.BlockSpec(memory_space=pl.ANY)],
        out_specs=pl.BlockSpec(memory_space=pltpu.VMEM),
        scratch_shapes=[
            pltpu.VMEM(w.shape, w.dtype),
            pltpu.SemaphoreType.DMA((len(places),)),
        ],
        compiler_params=pltpu.CompilerParams(vmem_limit_bytes=46 * 2**20),
        cost_estimate=pl.CostEstimate(flops=1, bytes_accessed=1, transcendentals=0),
        name="load_weights",
    )(w)


def run_signal(pieces, row, rows, count, taps, place, tokens, edges, before, gain, w_in, w_short, rate):
    streams, features, channels = w_in.shape
    modes = rate.shape[0]
    halo = ROWS * (taps - 1)
    outs = [
        jax.ShapeDtypeStruct((halo + count, features), BF16),
        jax.ShapeDtypeStruct((count, channels), F32),
        jax.ShapeDtypeStruct((count // rows, modes, ROWS, channels), F32),
        jax.ShapeDtypeStruct((modes, ROWS, channels), F32),
        jax.ShapeDtypeStruct((streams - 1, halo, channels), F32),
    ]
    if row == 0:
        outs += [jax.ShapeDtypeStruct((modes, channels), kind) for kind in (F32, BF16)]
    return call(
        functools.partial(signal_stage, pieces, row, taps),
        "signal_stage",
        [place],
        list(tokens) + list(edges) + list(before) + [gain, w_in, w_short, rate],
        outs,
        [
            pltpu.VMEM((rows + (halo if row in (0, rows) else 0), features), F32),
            pltpu.VMEM((halo + rows, min(BLOCK, channels)), F32),
        ],
        aliases={1 + len(tokens) + len(edges) + k: k for k in range(3)} if before else {},
    )


def run_local(row, rows, taps, normed, signal, states, w_in, w_short, rate, mode, skip):
    channels = signal.shape[1]
    out = jax.ShapeDtypeStruct((rows, channels), F32)
    begin = jax.ShapeDtypeStruct(states.shape, F32)
    return call(
        functools.partial(local_stage, row, rows, taps),
        "local_stage",
        [],
        [normed, signal, states, w_in, w_short, rate, mode, skip],
        [out, out] + ([begin, begin] if row == 0 else []),
        [pltpu.VMEM((rows + ROWS * (taps - 1), min(BLOCK, channels)), F32)],
    )


def run_second(pieces, row, rows, place, q, local, begin, past, marks, carry, rate, mode, w):
    channels, features = w.shape
    share = features // pieces
    return call(
        functools.partial(second_stage, pieces, row, rows),
        "second_stage",
        [place],
        [q, local, begin, past, marks, carry, rate, mode, w],
        [
            jax.ShapeDtypeStruct((max(1, pieces - 1) * rows, share), BF16),
            jax.ShapeDtypeStruct((rows, share), F32),
        ],
        [pltpu.VMEM((rows, channels), F32)],
    )


def run_last(pieces, sizes, row, own, came, done, count):
    share = own[0].shape[1]
    scratch = [pltpu.VMEM((sum(sizes), share), BF16)]
    if done:
        scratch += [pltpu.VMEM((share, count), BF16), pltpu.SemaphoreType.DMA((-(-share // BLOCK),))]
    (out,) = call(
        functools.partial(last_stage, pieces, sizes, row, bool(done)),
        "last_stage",
        [],
        [*own, *came, *done],
        [jax.ShapeDtypeStruct((share, count), BF16)],
        scratch,
        out_space=pl.ANY if done else pltpu.VMEM,
    )
    return out


def rotate(value, axis, steps):
    count = lax.axis_size(axis)
    return lax.ppermute(value, axis, [((i + steps) % count, i) for i in range(count)])


def combine_states(span, stride, radix, count, *refs):
    place_ref, rate_ref, total_ref = refs[:3]
    others = refs[3 : 2 + radix]
    refs = refs[2 + radix :]
    carry_in = refs[0] if stride > 1 else None
    carry_ref = refs[1] if stride > 1 else refs[0]
    position = place_ref[1]
    digit = lax.rem(lax.div(position, stride), radix)
    inner = lax.rem(position, stride)
    unit = span * stride
    rate = rate_ref[...]
    before = jnp.zeros(rate.shape, F32)
    for shift in range(1, radix):
        reached = jnp.where(digit >= shift, 1.0, 0.0)
        other = others[shift - 1][: rate.shape[0], :].astype(F32)
        before = before + jnp.exp(-rate * (unit * (shift - 1))) * (other * reached)
    if stride > 1:
        carry_ref[...] = carry_in[...] + jnp.exp(-rate * (span * inner).astype(F32)) * before
    else:
        carry_ref[...] = before
    if stride * radix < count:
        new = jnp.exp(-rate * (unit * (radix - 1 - digit)).astype(F32)) * total_ref[...]
        for shift in range(1, radix):
            at = lax.rem(digit - shift + radix, radix)
            weight = jnp.exp(-rate * (unit * (radix - 1 - at)).astype(F32))
            new = new + weight * others[shift - 1][: rate.shape[0], :].astype(F32)
        refs[-3][...] = new
        refs[-2][...] = new.astype(BF16)
        modes = new.shape[0]
        refs[-1][:modes, :] = new.astype(BF16)
        refs[-1][modes:, :] = jnp.zeros((refs[-1].shape[0] - modes, new.shape[1]), BF16)


def carried_in(state, sent, rate, span, axis, place, between):
    count = lax.axis_size(axis)
    total, stride, carry, longer = state, 1, [], None
    modes, channels = state.shape
    while stride < count:
        radix = 4 if count % (stride * 4) == 0 else 2
        assert count % (stride * radix) == 0
        group = stride * radix
        others = []
        for shift in reversed(range(1, radix)):
            pairs = []
            for i in range(count):
                digit = (i // stride) % radix
                pairs.append((i + ((digit - shift) % radix - digit) * stride, i))
            first = shift == 1 and longer is not None
            others.append(lax.ppermute(longer if first else sent, axis, pairs))
        others = between(others[::-1])
        shape = jax.ShapeDtypeStruct(state.shape, F32)
        carry = call(
            functools.partial(combine_states, span, stride, radix, count),
            "combine_states",
            [place],
            [rate, total, *others, *carry],
            [shape] if group == count else [shape, shape]
            + [jax.ShapeDtypeStruct((rows, channels), BF16) for rows in (modes, modes + ROWS)],
            [],
        )
        if group < count:
            *carry, total, sent, longer = carry
        stride = group
    return carry[0]


def body(tokens, norm_gain, w_in, w_short, decay_rate, residue, skip_gain, w_out):
    pieces, count = lax.axis_size("tp"), lax.axis_size("ctx")
    share, rows = tokens.shape
    channels = w_in.shape[1]
    taps = w_short.shape[0]
    halo = ROWS * (taps - 1)
    size = SPAN * ROWS
    assert rows == CHUNKS * size
    bf16_rows = lambda size: jax.ShapeDtypeStruct((size, share), BF16)

    place = jnp.stack([lax.axis_index("tp"), lax.axis_index("ctx")]).astype(jnp.int32)
    tokens, place = lax.optimization_barrier((tokens, place))
    x1, edge = call(
        functools.partial(first_rows, halo, size), "first_rows", [], [tokens],
        [bf16_rows(halo + size), bf16_rows(taps - 1)], [],
    )
    edge = rotate(edge, "ctx", -1)
    tokens, x1 = lax.optimization_barrier((tokens, x1))
    x0, *others = call(
        functools.partial(next_rows, [0] + [j * size for j in range(2, CHUNKS)]), "next_rows",
        [], [tokens], [bf16_rows(size)] * (CHUNKS - 1), [],
    )
    x = [x1, *others, x0]
    residue, norm_gain, skip_gain, *_ = lax.optimization_barrier((residue, norm_gain, skip_gain, *x))
    mode = residue * jnp.sqrt(-jnp.expm1(-2.0 * decay_rate))
    gain = norm_gain[None, :]
    skip = skip_gain[None, :]
    w_in, mode, gain, skip, *_ = lax.optimization_barrier((w_in, mode, gain, skip, *x))
    w_in = in_vmem(w_in)
    edge, w_in = lax.optimization_barrier((edge, w_in))
    w_in = pltpu.with_memory_space_constraint(w_in, pltpu.VMEM)
    *parts, edges = [[part] + [rotate(part, "tp", s) for s in range(1, pieces)] for part in x + [edge]]

    before = []
    for part, j in zip(parts, list(range(1, CHUNKS)) + [0]):
        results = run_signal(
            pieces, j * size, size, rows, taps, place, part, [] if j else edges, before, gain, w_in,
            w_short, decay_rate,
        )
        before = results[:5]
    normed, signal, marks, states, _ = before
    state, sent, normed, signal, states = lax.optimization_barrier(
        (results[5], results[6], normed, signal, states)
    )
    out_sizes = [rows // 4] * 4
    out_rows = [sum(out_sizes[:j]) for j in range(4)]
    small = [w_in, w_short, decay_rate, mode, skip]
    done = []

    def local_part():
        k = len(done)
        done.append(run_local(out_rows[k], out_sizes[k], taps, normed, signal, states, *small))

    def between(others):
        if not done:
            local_part()
            others, done[-1] = lax.optimization_barrier((others, done[-1]))
        return others

    carry = carried_in(state, sent, decay_rate, rows, "ctx", place, between)
    if not done:
        local_part()
    begin, past = done[0][2:]
    own, came = [], []
    for j in range(len(out_sizes)):
        if j >= 2:
            arrived = slice((j - 2) * (pieces - 1), (j - 1) * (pieces - 1))
            normed, signal, carry, came[arrived] = lax.optimization_barrier(
                (normed, signal, carry, came[arrived])
            )
        if j > 0:
            local_part()
        send, kept = run_second(
            pieces, out_rows[j], out_sizes[j], place, *done[j][:2], begin, past, marks, carry,
            decay_rate, mode, w_out,
        )
        own.append(kept)
        for s in range(1, pieces):
            came.append(rotate(send[(s - 1) * out_sizes[j] : s * out_sizes[j]], "tp", -s))
    early = out_rows[-1]
    cut = (len(out_sizes) - 1) * (pieces - 1)
    done = run_last(pieces, out_sizes[:-1], 0, own[:-1], came[:cut], [], rows)
    return run_last(pieces, out_sizes[-1:], early, own[-1:], came[cut:], [done], rows)


def solution(mesh):
    placed = (
        P("tp", "ctx"),
        P(),
        P(None, "tp", None),
        P(None, None, "tp"),
        P(None, "tp"),
        P(None, "tp"),
        P("tp"),
        P("tp", None),
    )
    return jax.shard_map(
        body, mesh=mesh, in_specs=placed, out_specs=P("tp", "ctx"), check_vma=False
    )
```

```python
import functools

import jax
import jax.numpy as jnp
from jax import lax
from jax.experimental import pallas as pl
from jax.experimental.pallas import tpu as pltpu
from jax.sharding import PartitionSpec as P


F32 = jnp.float32
BF16 = jnp.bfloat16
ROWS = 8
LANES = 128
BLOCK = 256
CHUNKS = 4
SPAN = 16
VMEM_LIMIT = 10 * 2**20
CONTRACT_LAST = (((1,), (1,)), ((), ()))
CONTRACT_FIRST = (((0,), (0,)), ((), ()))


def lane_groups(low, width):
    return [(start, min(LANES, low + width - start)) for start in range(low, low + width, LANES)]


def rows_as(row, width):
    return jnp.broadcast_to(row, (ROWS, width))


def decays(rate_ref, lanes, size, steps):
    values = jnp.exp(-rate_ref[:, lanes] * steps)
    return [rows_as(values[n : n + 1, :], size) for n in range(values.shape[0])]


def sums_of_rows(values):
    row = lax.broadcasted_iota(jnp.int32, values[0].shape, 0)
    count = len(values)
    values = list(values) + [jnp.zeros_like(values[0])] * (ROWS - count)
    for hop in (4, 2, 1):
        low = lax.rem(row, 2 * hop) < hop
        joined = []
        for a, b in zip(values[:hop], values[hop:]):
            other = jnp.where(low, b, a)
            if 2 * hop == ROWS:
                other = pltpu.roll(other, hop, 0)
            else:
                other = jnp.where(low, pltpu.roll(other, ROWS - hop, 0), pltpu.roll(other, hop, 0))
            joined.append(jnp.where(low, a, b) + other)
        values = joined
    return values[0][:count]


def tree_sum(terms):
    while len(terms) > 1:
        terms = [sum(terms[k + 1 : k + 2], terms[k]) for k in range(0, len(terms), 2)]
    return terms[0]


def token_picker(first_row, rows, tokens):
    length = tokens // ROWS
    row = lax.broadcasted_iota(jnp.int32, (rows, tokens), 0)
    column = lax.broadcasted_iota(jnp.int32, (rows, tokens), 1)
    wanted = lax.rem(row, ROWS) * length + lax.div(row, ROWS) + first_row // ROWS
    return jnp.where(column == wanted, 1.0, 0.0).astype(BF16)


def turned(pick, tokens):
    return lax.dot_general(pick, tokens, CONTRACT_LAST, preferred_element_type=F32).astype(BF16)


def first_rows(halo, size, tokens_ref, out_ref, edge_ref):
    tokens = tokens_ref.shape[1]
    row = lax.broadcasted_iota(jnp.int32, (halo, tokens), 0)
    column = lax.broadcasted_iota(jnp.int32, (halo, tokens), 1)
    last = edge_ref.shape[0]
    picks = [
        token_picker(size, size, tokens),
        jnp.where((row < last) & (column == tokens - last + row), 1.0, 0.0).astype(BF16),
    ]
    rows = turned(jnp.concatenate(picks, axis=0), tokens_ref[...])
    out_ref[...] = rows[:size]
    edge_ref[...] = rows[size : size + last]


def next_rows(firsts, tokens_ref, *chunk_refs):
    tokens = tokens_ref.shape[1]
    for row, ref in zip(firsts, chunk_refs):
        ref[...] = turned(token_picker(row, ref.shape[0], tokens), tokens_ref[...])


def load_weights(places, w_hbm, out_ref, w_ref, sem):
    copies = [
        pltpu.make_async_copy(w_hbm.at[place], w_ref.at[place], sem.at[k])
        for k, place in enumerate(places)
    ]
    for copy in copies:
        copy.start()
    for (s, part), copy in zip(places, copies):
        copy.wait()
        out_ref[s, :, part] = w_ref[s, part, :].T


def short_conv(p_ref, short_ref, s, part, rows, taps):
    width = part.stop - part.start
    total = None
    for offset in range(taps):
        start = ROWS * (taps - 1 - offset)
        term = short_ref[offset, s : s + 1, part] * p_ref[start : start + rows, :width]
        total = term if total is None else total + term
    return total


def project(normed, w_ref, s, part):
    product = jnp.dot(normed, w_ref[s, :, part], preferred_element_type=F32)
    return product.astype(BF16).astype(F32)


def signal_stage(pieces, row, taps, *refs):
    refs = list(refs)
    me_ref = refs.pop(0)
    token_refs = [refs.pop(0) for _ in range(pieces)]
    x_ref, p_ref = refs[-2:]
    halo = ROWS * (taps - 1)
    rows, share = token_refs[0].shape
    last, start = row == 0, row == rows
    fresh = last or start
    read = rows + halo if last else rows
    edge_refs = [refs.pop(0) for _ in range(pieces)] if last else []
    if not start:
        normed_in, _, _, states_in, tail_in = [refs.pop(0) for _ in range(5)]
    heads_in = refs.pop(0) if last else None
    gain_ref, w_ref, short_ref, rate_ref = refs[:4]
    normed_ref, signal_ref, marks_ref, states_ref, tail_ref = refs[4:9]
    heads_ref = refs[9] if start else None
    total_ref, sent_ref = refs[9:11] if last else (None, None)
    modes, channels = rate_ref.shape
    length = signal_ref.shape[0] // ROWS
    me = me_ref[0]

    values = [ref[...].astype(F32) for ref in token_refs]
    if last:
        preceded = jnp.where(me_ref[1] > 0, 1.0, 0.0)
        blank = jnp.zeros((ROWS - 1, share), F32)
        for s, ref in enumerate(edge_refs):
            edge = ref[...].astype(F32) * preceded
            front = [piece for k in range(taps - 1) for piece in (edge[k : k + 1], blank)]
            values[s] = jnp.concatenate(front + [values[s]], axis=0)
    for rank in range(pieces):
        chosen = values[0]
        for s in range(1, pieces):
            chosen = jnp.where(me == (rank - s) % pieces, values[s], chosen)
        x_ref[:, rank * share : (rank + 1) * share] = chosen
    features = x_ref[...]
    mean = jnp.mean(features * features, axis=1, keepdims=True)
    normed = features * lax.rsqrt(mean + 1e-06) * gain_ref[...]
    if last:
        ends = normed_in[normed_in.shape[0] - halo :, :].astype(F32)
        segment = lax.broadcasted_iota(jnp.int32, (ROWS, ends.shape[1]), 0)
        front = [
            jnp.where(segment >= 1, pltpu.roll(ends[at : at + ROWS], 1, 0), normed[at : at + ROWS])
            for at in range(0, halo, ROWS)
        ]
        normed = jnp.concatenate(front + [normed[halo:]], axis=0)
    normed = normed.astype(BF16)
    begin = 0 if last else halo + row
    normed_ref[begin : begin + read, :] = normed

    for low in range(0, channels, BLOCK):
        width = min(BLOCK, channels - low)
        part = slice(low, low + width)
        for s in (1, 2):
            if start:
                p_ref[:halo, :width] = jnp.zeros((halo, width), F32)
            elif not last:
                p_ref[:halo, :width] = tail_in[s - 1, :, part]
            p_ref[halo + rows - read : halo + rows, :width] = project(
                normed_ref[begin : begin + read, :], w_ref, s, part
            )
            if last:
                p_ref[halo + rows :, :width] = heads_in[s - 1, :, part]
            if start:
                heads_ref[s - 1, :, part] = p_ref[halo : 2 * halo, :width]
            tail_ref[s - 1, :, part] = p_ref[rows : rows + halo, :width]
            short = short_conv(p_ref, short_ref, s, part, p_ref.shape[0] - halo, taps)
            front = halo if start else 0
            there = slice(row + front, row + short.shape[0])
            if s == 1:
                signal_ref[there, part] = short[front:]
            else:
                signal_ref[there, part] = signal_ref[there, part] * short[front:]
        for lane, size in lane_groups(low, width):
            lanes = slice(lane, lane + size)
            decay = decays(rate_ref, lanes, size, 1.0)

            if fresh:
                states = (jnp.zeros((ROWS, size), F32),) * modes
            else:
                states = tuple(states_in[n, :, lanes] for n in range(modes))
                for n in range(modes):
                    marks_ref[row // rows, n, :, lanes] = states[n]

            def step(i, states):
                here = pl.ds(pl.multiple_of(row + i * ROWS, ROWS), ROWS)
                now = signal_ref[here, lanes]
                return tuple(states[n] * decay[n] + now for n in range(modes))

            steps = rows // ROWS
            skipped = taps - 1 if start else 0
            unroll = next(k for k in (8, 7, 4, 2, 1) if (steps - skipped) % k == 0)
            states = lax.fori_loop(skipped, steps, step, states, unroll=unroll)
            if last:
                for n in range(modes):
                    marks_ref[1, n, :, lanes] = states[n]
                for at in range(rows, rows + halo, ROWS):
                    now = signal_ref[at : at + ROWS, lanes]
                    states = tuple(states[n] * decay[n] + now for n in range(modes))
                for n in range(modes):
                    marks_ref[0, n, :, lanes] = states[n]
                later = decays(rate_ref, lanes, size, float(length - steps - (taps - 1)))
                states = tuple(states_in[n, :, lanes] + later[n] * states[n] for n in range(modes))
            for n in range(modes):
                states_ref[n, :, lanes] = states[n]
            if last:
                left = lax.broadcasted_iota(jnp.int32, (ROWS, size), 0)
                left = ((ROWS - 1 - left) * length).astype(F32)
                for low_mode in range(0, modes, ROWS):
                    some = range(low_mode, min(low_mode + ROWS, modes))
                    total_ref[low_mode : low_mode + len(some), lanes] = sums_of_rows(
                        [
                            states[n] * jnp.exp(-rows_as(rate_ref[n : n + 1, lanes], size) * left)
                            for n in some
                        ]
                    )
                sent_ref[:, lanes] = total_ref[:, lanes].astype(BF16)


def local_stage(row, rows, taps, *refs):
    normed_ref, signal_ref, states_ref, w_ref, short_ref, rate_ref, mode_ref, skip_ref = refs[:8]
    q_ref, local_ref = refs[8:10]
    begin_ref, past_ref = refs[10:12] if row == 0 else (None, None)
    p_ref = refs[-1]
    modes, channels = rate_ref.shape
    length = signal_ref.shape[0] // ROWS
    for low in range(0, channels, BLOCK):
        width = min(BLOCK, channels - low)
        part = slice(low, low + width)
        normed = normed_ref[row : row + p_ref.shape[0], :]
        p_ref[:, :width] = project(normed, w_ref, 0, part)
        q_ref[:, part] = short_conv(p_ref, short_ref, 0, part, rows, taps)
        for start, size in lane_groups(low, width):
            lanes = slice(start, start + size)
            rate = [rows_as(rate_ref[n : n + 1, lanes], size) for n in range(modes)]
            segment = lax.broadcasted_iota(jnp.int32, (ROWS, size), 0)
            if row == 0:
                for n in range(modes):
                    run = states_ref[n, :, lanes]
                    for hop in (1, 2, 4):
                        weight = jnp.where(segment >= hop, jnp.exp(-rate[n] * (hop * length)), 0.0)
                        run = run + weight * pltpu.roll(run, hop, 0)
                    mode = rows_as(mode_ref[n : n + 1, lanes], size)
                    begin = jnp.where(segment >= 1, pltpu.roll(run, 1, 0), 0.0)
                    begin_ref[n, :, lanes] = mode * begin
                    past = (segment * length).astype(F32)
                    past_ref[n, :, lanes] = mode * jnp.exp(-rate[n] * past)
            lag = segment.astype(F32)
            filters = []
            for first_lag in range(0, SPAN, ROWS):
                values = tree_sum(
                    [
                        rows_as(mode_ref[n : n + 1, lanes], size)
                        * jnp.exp(-rate[n] * (lag + first_lag))
                        for n in range(modes)
                    ]
                )
                filters += [rows_as(values[j : j + 1, :], size) for j in range(ROWS)]
            filters[0] = filters[0] + skip_ref[:, lanes]

            def span(i, carry):
                base = i * (SPAN * ROWS)
                now = [
                    signal_ref[pl.ds(pl.multiple_of(row + base + k * ROWS, ROWS), ROWS), lanes]
                    for k in range(SPAN)
                ]
                for k in range(SPAN):
                    local_ref[pl.ds(pl.multiple_of(base + k * ROWS, ROWS), ROWS), lanes] = tree_sum(
                        [filters[j] * now[k - j] for j in range(k + 1)]
                    )
                return carry

            lax.fori_loop(0, rows // (SPAN * ROWS), span, 0)


def second_stage(pieces, row, rows, ahead, *refs):
    me_ref, q_ref, local_ref, begin_ref, past_ref, marks_ref, carry_ref = refs[:7]
    rate_ref, mode_ref, w_ref, send_ref, own_ref, gated_ref = refs[7:]
    modes, channels = rate_ref.shape
    for start, size in lane_groups(0, channels):
        lanes = slice(start, start + size)
        decay = decays(rate_ref, lanes, size, 1.0)
        for at in range(row, row + rows, SPAN * ROWS):
            mark = at // (SPAN * ROWS)
            states = [
                begin_ref[n, :, lanes] + past_ref[n, :, lanes] * carry_ref[n : n + 1, lanes]
                for n in range(modes)
            ]
            for known, steps in ((mark, SPAN * mark), (0, SPAN * (mark - 1) - ahead)):
                if steps <= 0:
                    continue
                less = decays(rate_ref, lanes, size, float(steps))
                mode = [mode_ref[n : n + 1, lanes] for n in range(modes)]
                if known:
                    states = [
                        mode[n] * marks_ref[known, n, :, lanes] + states[n] * less[n]
                        for n in range(modes)
                    ]
                else:
                    states = [
                        states[n] + mode[n] * marks_ref[0, n, :, lanes] * less[n]
                        for n in range(modes)
                    ]

            def step(i, states):
                here = pl.ds(pl.multiple_of(at - row + i * ROWS, ROWS), ROWS)
                states = tuple(states[n] * decay[n] for n in range(modes))
                gated_ref[here, lanes] = q_ref[here, lanes] * tree_sum(
                    [local_ref[here, lanes]] + list(states)
                )
                return states

            lax.fori_loop(0, SPAN, step, tuple(states), unroll=4)
    product = jnp.dot(gated_ref[...].astype(BF16), w_ref[...], preferred_element_type=F32)
    share = own_ref.shape[1]
    me = me_ref[0]
    columns = [product[:, rank * share : (rank + 1) * share] for rank in range(pieces)]
    for s in range(pieces):
        chosen = columns[0]
        for rank in range(1, pieces):
            chosen = jnp.where(me == (rank - s) % pieces, columns[rank], chosen)
        if s == 0:
            own_ref[...] = chosen
        else:
            send_ref[(s - 1) * rows : s * rows, :] = chosen.astype(BF16)


def turned_back(rows, pick):
    return lax.dot_general(rows, pick, CONTRACT_FIRST, preferred_element_type=F32).astype(BF16)


def last_stage(pieces, sizes, row, more, *refs):
    chunks = len(sizes)
    own_refs, came_refs = refs[:chunks], refs[chunks : chunks * pieces]
    done_ref = refs[chunks * pieces] if more else None
    if more:
        out_ref, mixed_ref, rows_ref, sem = refs[-4:]
    else:
        out_ref, mixed_ref = refs[-2:]
    at = 0
    for j, size in enumerate(sizes):
        total = own_refs[j][...]
        for s in range(pieces - 1):
            total = total + came_refs[j * (pieces - 1) + s][...].astype(F32)
        mixed_ref[at : at + size, :] = total.astype(BF16)
        at += size
    if not more:
        pick = token_picker(row, at, out_ref.shape[1])
        out_ref[...] = turned_back(mixed_ref[...], pick)
        return
    share, tokens = rows_ref.shape
    pick = token_picker(row, at, tokens)
    copies = []
    for low in range(0, share, BLOCK):
        part = slice(low, min(low + BLOCK, share))
        rows_ref[part, :] = done_ref[part, :] + turned_back(mixed_ref[:, part], pick)
        copy = pltpu.make_async_copy(rows_ref.at[part], out_ref.at[part], sem.at[len(copies)])
        copy.start()
        copies.append(copy)
    for copy in copies:
        copy.wait()


def call(kernel, name, scalars, operands, outs, scratch, aliases={}, out_space=pltpu.VMEM):
    vmem = pl.BlockSpec(memory_space=pltpu.VMEM)
    smem = pl.BlockSpec(memory_space=pltpu.SMEM)
    return pl.pallas_call(
        kernel,
        out_shape=outs,
        in_specs=[smem] * len(scalars) + [vmem] * len(operands),
        out_specs=[pl.BlockSpec(memory_space=out_space)] * len(outs),
        scratch_shapes=scratch,
        input_output_aliases=aliases,
        compiler_params=pltpu.CompilerParams(vmem_limit_bytes=VMEM_LIMIT),
        cost_estimate=pl.CostEstimate(flops=1, bytes_accessed=1, transcendentals=0),
        name=name,
    )(*scalars, *operands)


def in_vmem(w):
    streams, channels, features = w.shape
    block = min(BLOCK, channels)
    places = [
        (s, slice(low, min(low + block, channels)))
        for s in (1, 2, 0)
        for low in range(0, channels, block)
    ]
    return pl.pallas_call(
        functools.partial(load_weights, places),
        out_shape=pltpu.VMEM((streams, features, channels), w.dtype),
        in_specs=[pl.BlockSpec(memory_space=pl.ANY)],
        out_specs=pl.BlockSpec(memory_space=pltpu.VMEM),
        scratch_shapes=[
            pltpu.VMEM(w.shape, w.dtype),
            pltpu.SemaphoreType.DMA((len(places),)),
        ],
        compiler_params=pltpu.CompilerParams(vmem_limit_bytes=46 * 2**20),
        cost_estimate=pl.CostEstimate(flops=1, bytes_accessed=1, transcendentals=0),
        name="load_weights",
    )(w)


def run_signal(pieces, row, rows, count, taps, place, tokens, edges, before, gain, w_in, w_short, rate):
    streams, features, channels = w_in.shape
    modes = rate.shape[0]
    halo = ROWS * (taps - 1)
    outs = [
        jax.ShapeDtypeStruct((halo + count, features), BF16),
        jax.ShapeDtypeStruct((count, channels), F32),
        jax.ShapeDtypeStruct((count // rows, modes, ROWS, channels), F32),
        jax.ShapeDtypeStruct((modes, ROWS, channels), F32),
        jax.ShapeDtypeStruct((streams - 1, halo, channels), F32),
    ]
    if row == rows:
        outs.append(outs[-1])
    if row == 0:
        outs += [jax.ShapeDtypeStruct((modes, channels), kind) for kind in (F32, BF16)]
    return call(
        functools.partial(signal_stage, pieces, row, taps),
        "signal_stage",
        [place],
        list(tokens) + list(edges) + list(before) + [gain, w_in, w_short, rate],
        outs,
        [
            pltpu.VMEM((rows + (halo if row == 0 else 0), features), F32),
            pltpu.VMEM((rows + halo * (2 if row == 0 else 1), min(BLOCK, channels)), F32),
        ],
        aliases={1 + len(tokens) + len(edges) + k: k for k in range(3)} if before else {},
    )


def run_local(row, rows, taps, normed, signal, states, w_in, w_short, rate, mode, skip):
    channels = signal.shape[1]
    out = jax.ShapeDtypeStruct((rows, channels), F32)
    begin = jax.ShapeDtypeStruct(states.shape, F32)
    return call(
        functools.partial(local_stage, row, rows, taps),
        "local_stage",
        [],
        [normed, signal, states, w_in, w_short, rate, mode, skip],
        [out, out] + ([begin, begin] if row == 0 else []),
        [pltpu.VMEM((rows + ROWS * (taps - 1), min(BLOCK, channels)), F32)],
    )


def run_second(pieces, row, rows, ahead, place, q, local, begin, past, marks, carry, rate, mode, w):
    channels, features = w.shape
    share = features // pieces
    return call(
        functools.partial(second_stage, pieces, row, rows, ahead),
        "second_stage",
        [place],
        [q, local, begin, past, marks, carry, rate, mode, w],
        [
            jax.ShapeDtypeStruct((max(1, pieces - 1) * rows, share), BF16),
            jax.ShapeDtypeStruct((rows, share), F32),
        ],
        [pltpu.VMEM((rows, channels), F32)],
    )


def run_last(pieces, sizes, row, own, came, done, count):
    share = own[0].shape[1]
    scratch = [pltpu.VMEM((sum(sizes), share), BF16)]
    if done:
        scratch += [pltpu.VMEM((share, count), BF16), pltpu.SemaphoreType.DMA((-(-share // BLOCK),))]
    (out,) = call(
        functools.partial(last_stage, pieces, sizes, row, bool(done)),
        "last_stage",
        [],
        [*own, *came, *done],
        [jax.ShapeDtypeStruct((share, count), BF16)],
        scratch,
        out_space=pl.ANY if done else pltpu.VMEM,
    )
    return out


def rotate(value, axis, steps):
    count = lax.axis_size(axis)
    return lax.ppermute(value, axis, [((i + steps) % count, i) for i in range(count)])


def combine_states(span, stride, radix, count, *refs):
    place_ref, rate_ref, total_ref = refs[:3]
    others = refs[3 : 2 + radix]
    refs = refs[2 + radix :]
    carry_in = refs[0] if stride > 1 else None
    carry_ref = refs[1] if stride > 1 else refs[0]
    position = place_ref[1]
    digit = lax.rem(lax.div(position, stride), radix)
    inner = lax.rem(position, stride)
    unit = span * stride
    rate = rate_ref[...]
    before = jnp.zeros(rate.shape, F32)
    for shift in range(1, radix):
        reached = jnp.where(digit >= shift, 1.0, 0.0)
        other = others[shift - 1][: rate.shape[0], :].astype(F32)
        before = before + jnp.exp(-rate * (unit * (shift - 1))) * (other * reached)
    if stride > 1:
        carry_ref[...] = carry_in[...] + jnp.exp(-rate * (span * inner).astype(F32)) * before
    else:
        carry_ref[...] = before
    if stride * radix < count:
        new = jnp.exp(-rate * (unit * (radix - 1 - digit)).astype(F32)) * total_ref[...]
        for shift in range(1, radix):
            at = lax.rem(digit - shift + radix, radix)
            weight = jnp.exp(-rate * (unit * (radix - 1 - at)).astype(F32))
            new = new + weight * others[shift - 1][: rate.shape[0], :].astype(F32)
        refs[-3][...] = new
        refs[-2][...] = new.astype(BF16)
        modes = new.shape[0]
        refs[-1][:modes, :] = new.astype(BF16)
        refs[-1][modes:, :] = jnp.zeros((refs[-1].shape[0] - modes, new.shape[1]), BF16)


def carried_in(state, sent, rate, span, axis, place, between):
    count = lax.axis_size(axis)
    total, stride, carry, longer = state, 1, [], None
    modes, channels = state.shape
    while stride < count:
        radix = 4 if count % (stride * 4) == 0 else 2
        assert count % (stride * radix) == 0
        group = stride * radix
        others = []
        for shift in reversed(range(1, radix)):
            pairs = []
            for i in range(count):
                digit = (i // stride) % radix
                pairs.append((i + ((digit - shift) % radix - digit) * stride, i))
            first = shift == 1 and longer is not None
            others.append(lax.ppermute(longer if first else sent, axis, pairs))
        others = between(others[::-1])
        shape = jax.ShapeDtypeStruct(state.shape, F32)
        carry = call(
            functools.partial(combine_states, span, stride, radix, count),
            "combine_states",
            [place],
            [rate, total, *others, *carry],
            [shape] if group == count else [shape, shape]
            + [jax.ShapeDtypeStruct((rows, channels), BF16) for rows in (modes, modes + ROWS)],
            [],
        )
        if group < count:
            *carry, total, sent, longer = carry
        stride = group
    return carry[0]


def body(tokens, norm_gain, w_in, w_short, decay_rate, residue, skip_gain, w_out):
    pieces, count = lax.axis_size("tp"), lax.axis_size("ctx")
    share, rows = tokens.shape
    channels = w_in.shape[1]
    taps = w_short.shape[0]
    halo = ROWS * (taps - 1)
    size = SPAN * ROWS
    assert rows == CHUNKS * size
    bf16_rows = lambda size: jax.ShapeDtypeStruct((size, share), BF16)

    place = jnp.stack([lax.axis_index("tp"), lax.axis_index("ctx")]).astype(jnp.int32)
    tokens, place = lax.optimization_barrier((tokens, place))
    x1, edge = call(
        functools.partial(first_rows, halo, size), "first_rows", [], [tokens],
        [bf16_rows(size), bf16_rows(taps - 1)], [],
    )
    edge = rotate(edge, "ctx", -1)
    tokens, x1 = lax.optimization_barrier((tokens, x1))
    x0, *others = call(
        functools.partial(next_rows, [0] + [j * size for j in range(2, CHUNKS)]), "next_rows",
        [], [tokens], [bf16_rows(size)] * (CHUNKS - 1), [],
    )
    x = [x1, *others, x0]
    residue, norm_gain, skip_gain, *_ = lax.optimization_barrier((residue, norm_gain, skip_gain, *x))
    mode = residue * jnp.sqrt(-jnp.expm1(-2.0 * decay_rate))
    gain = norm_gain[None, :]
    skip = skip_gain[None, :]
    w_in, mode, gain, skip, *_ = lax.optimization_barrier((w_in, mode, gain, skip, *x))
    w_in = in_vmem(w_in)
    edge, w_in = lax.optimization_barrier((edge, w_in))
    w_in = pltpu.with_memory_space_constraint(w_in, pltpu.VMEM)
    *parts, edges = [[part] + [rotate(part, "tp", s) for s in range(1, pieces)] for part in x + [edge]]

    before = []
    for part, j in zip(parts, list(range(1, CHUNKS)) + [0]):
        results = run_signal(
            pieces, j * size, size, rows, taps, place, part, [] if j else edges,
            before if j else [*before, heads], gain, w_in,
            w_short, decay_rate,
        )
        before = results[:5]
        if j == 1:
            heads = results[5]
    normed, signal, marks, states, _ = before
    state, sent, normed, signal, states = lax.optimization_barrier(
        (results[5], results[6], normed, signal, states)
    )
    out_sizes = [rows // 4] * 4
    out_rows = [sum(out_sizes[:j]) for j in range(4)]
    small = [w_in, w_short, decay_rate, mode, skip]
    done = []

    def local_part():
        k = len(done)
        done.append(run_local(out_rows[k], out_sizes[k], taps, normed, signal, states, *small))

    def between(others):
        if not done:
            local_part()
            others, done[-1] = lax.optimization_barrier((others, done[-1]))
        return others

    carry = carried_in(state, sent, decay_rate, rows, "ctx", place, between)
    if not done:
        local_part()
    begin, past = done[0][2:]
    own, came = [], []
    for j in range(len(out_sizes)):
        if j >= 2:
            arrived = slice((j - 2) * (pieces - 1), (j - 1) * (pieces - 1))
            normed, signal, carry, came[arrived] = lax.optimization_barrier(
                (normed, signal, carry, came[arrived])
            )
        if j > 0:
            local_part()
        send, kept = run_second(
            pieces, out_rows[j], out_sizes[j], taps - 1, place, *done[j][:2], begin, past, marks, carry,
            decay_rate, mode, w_out,
        )
        own.append(kept)
        for s in range(1, pieces):
            came.append(rotate(send[(s - 1) * out_sizes[j] : s * out_sizes[j]], "tp", -s))
    early = out_rows[-1]
    cut = (len(out_sizes) - 1) * (pieces - 1)
    done = run_last(pieces, out_sizes[:-1], 0, own[:-1], came[:cut], [], rows)
    return run_last(pieces, out_sizes[-1:], early, own[-1:], came[cut:], [done], rows)


def solution(mesh):
    placed = (
        P("tp", "ctx"),
        P(),
        P(None, "tp", None),
        P(None, None, "tp"),
        P(None, "tp"),
        P(None, "tp"),
        P("tp"),
        P("tp", None),
    )
    return jax.shard_map(
        body, mesh=mesh, in_specs=placed, out_specs=P("tp", "ctx"), check_vma=False
    )
```

```python
import functools

import jax
import jax.numpy as jnp
from jax import lax
from jax.experimental import pallas as pl
from jax.experimental.pallas import tpu as pltpu
from jax.sharding import PartitionSpec as P


F32 = jnp.float32
BF16 = jnp.bfloat16
ROWS = 8
LANES = 128
BLOCK = 256
CHUNKS = 4
SPAN = 16
VMEM_LIMIT = 10 * 2**20
CONTRACT_LAST = (((1,), (1,)), ((), ()))
CONTRACT_FIRST = (((0,), (0,)), ((), ()))


def lane_groups(low, width):
    return [(start, min(LANES, low + width - start)) for start in range(low, low + width, LANES)]


def rows_as(row, width):
    return jnp.broadcast_to(row, (ROWS, width))


def decays(rate_ref, lanes, size, steps):
    values = jnp.exp(-rate_ref[:, lanes] * steps)
    return [rows_as(values[n : n + 1, :], size) for n in range(values.shape[0])]


def sums_of_rows(values):
    row = lax.broadcasted_iota(jnp.int32, values[0].shape, 0)
    count = len(values)
    values = list(values) + [jnp.zeros_like(values[0])] * (ROWS - count)
    for hop in (4, 2, 1):
        low = lax.rem(row, 2 * hop) < hop
        joined = []
        for a, b in zip(values[:hop], values[hop:]):
            other = jnp.where(low, b, a)
            if 2 * hop == ROWS:
                other = pltpu.roll(other, hop, 0)
            else:
                other = jnp.where(low, pltpu.roll(other, ROWS - hop, 0), pltpu.roll(other, hop, 0))
            joined.append(jnp.where(low, a, b) + other)
        values = joined
    return values[0][:count]


def tree_sum(terms):
    while len(terms) > 1:
        terms = [sum(terms[k + 1 : k + 2], terms[k]) for k in range(0, len(terms), 2)]
    return terms[0]


def token_picker(first_row, rows, tokens):
    length = tokens // ROWS
    row = lax.broadcasted_iota(jnp.int32, (rows, tokens), 0)
    column = lax.broadcasted_iota(jnp.int32, (rows, tokens), 1)
    wanted = lax.rem(row, ROWS) * length + lax.div(row, ROWS) + first_row // ROWS
    return jnp.where(column == wanted, 1.0, 0.0).astype(BF16)


def turned(pick, tokens):
    return lax.dot_general(pick, tokens, CONTRACT_LAST, preferred_element_type=F32).astype(BF16)


def first_rows(halo, size, tokens_ref, out_ref, edge_ref):
    tokens = tokens_ref.shape[1]
    row = lax.broadcasted_iota(jnp.int32, (halo, tokens), 0)
    column = lax.broadcasted_iota(jnp.int32, (halo, tokens), 1)
    last = edge_ref.shape[0]
    picks = [
        token_picker(size, size, tokens),
        jnp.where((row < last) & (column == tokens - last + row), 1.0, 0.0).astype(BF16),
    ]
    rows = turned(jnp.concatenate(picks, axis=0), tokens_ref[...])
    out_ref[...] = rows[:size]
    edge_ref[...] = rows[size : size + last]


def next_rows(firsts, tokens_ref, *chunk_refs):
    tokens = tokens_ref.shape[1]
    for row, ref in zip(firsts, chunk_refs):
        ref[...] = turned(token_picker(row, ref.shape[0], tokens), tokens_ref[...])


def load_weights(places, w_hbm, out_ref, w_ref, sem):
    copies = [
        pltpu.make_async_copy(w_hbm.at[place], w_ref.at[place], sem.at[k])
        for k, place in enumerate(places)
    ]
    for copy in copies:
        copy.start()
    for (s, part), copy in zip(places, copies):
        copy.wait()
        out_ref[s, :, part] = w_ref[s, part, :].T


def short_conv(p_ref, short_ref, s, part, rows, taps):
    width = part.stop - part.start
    total = None
    for offset in range(taps):
        start = ROWS * (taps - 1 - offset)
        term = short_ref[offset, s : s + 1, part] * p_ref[start : start + rows, :width]
        total = term if total is None else total + term
    return total


def project(normed, w_ref, s, part):
    product = jnp.dot(normed, w_ref[s, :, part], preferred_element_type=F32)
    return product.astype(BF16).astype(F32)


def signal_stage(pieces, row, taps, *refs):
    refs = list(refs)
    me_ref = refs.pop(0)
    token_refs = [refs.pop(0) for _ in range(pieces)]
    x_ref, p_ref = refs[-2:]
    halo = ROWS * (taps - 1)
    rows, share = token_refs[0].shape
    last, start = row == 0, row == rows
    fresh = last or start
    read = rows + halo if last else rows
    edge_refs = [refs.pop(0) for _ in range(pieces)] if last else []
    if not start:
        normed_in, _, _, states_in, tail_in = [refs.pop(0) for _ in range(5)]
    heads_in = refs.pop(0) if last else None
    gain_ref, w_ref, short_ref, rate_ref = refs[:4]
    normed_ref, signal_ref, marks_ref, states_ref, tail_ref = refs[4:9]
    heads_ref = refs[9] if start else None
    total_ref, sent_ref = refs[9:11] if last else (None, None)
    modes, channels = rate_ref.shape
    length = signal_ref.shape[0] // ROWS
    me = me_ref[0]

    values = [ref[...].astype(F32) for ref in token_refs]
    if last:
        preceded = jnp.where(me_ref[1] > 0, 1.0, 0.0)
        blank = jnp.zeros((ROWS - 1, share), F32)
        for s, ref in enumerate(edge_refs):
            edge = ref[...].astype(F32) * preceded
            front = [piece for k in range(taps - 1) for piece in (edge[k : k + 1], blank)]
            values[s] = jnp.concatenate(front + [values[s]], axis=0)
    for rank in range(pieces):
        chosen = values[0]
        for s in range(1, pieces):
            chosen = jnp.where(me == (rank - s) % pieces, values[s], chosen)
        x_ref[:, rank * share : (rank + 1) * share] = chosen
    features = x_ref[...]
    mean = jnp.mean(features * features, axis=1, keepdims=True)
    normed = features * lax.rsqrt(mean + 1e-06) * gain_ref[...]
    if last:
        ends = normed_in[normed_in.shape[0] - halo :, :].astype(F32)
        segment = lax.broadcasted_iota(jnp.int32, (ROWS, ends.shape[1]), 0)
        front = [
            jnp.where(segment >= 1, pltpu.roll(ends[at : at + ROWS], 1, 0), normed[at : at + ROWS])
            for at in range(0, halo, ROWS)
        ]
        normed = jnp.concatenate(front + [normed[halo:]], axis=0)
    normed = normed.astype(BF16)
    begin = 0 if last else halo + row
    normed_ref[begin : begin + read, :] = normed

    for low in range(0, channels, BLOCK):
        width = min(BLOCK, channels - low)
        part = slice(low, low + width)
        for s in (1, 2):
            if start:
                p_ref[:halo, :width] = jnp.zeros((halo, width), F32)
            elif not last:
                p_ref[:halo, :width] = tail_in[s - 1, :, part]
            p_ref[halo + rows - read : halo + rows, :width] = project(
                normed_ref[begin : begin + read, :], w_ref, s, part
            )
            if last:
                p_ref[halo + rows :, :width] = heads_in[s - 1, :, part]
            if start:
                heads_ref[s - 1, :, part] = p_ref[halo : 2 * halo, :width]
            tail_ref[s - 1, :, part] = p_ref[rows : rows + halo, :width]
            short = short_conv(p_ref, short_ref, s, part, p_ref.shape[0] - halo, taps)
            front = halo if start else 0
            there = slice(row + front, row + short.shape[0])
            if s == 1:
                signal_ref[there, part] = short[front:]
            else:
                signal_ref[there, part] = signal_ref[there, part] * short[front:]
        for lane, size in lane_groups(low, width):
            lanes = slice(lane, lane + size)
            decay = decays(rate_ref, lanes, size, 1.0)

            if fresh:
                states = (jnp.zeros((ROWS, size), F32),) * modes
            else:
                states = tuple(states_in[n, :, lanes] for n in range(modes))
                for n in range(modes):
                    marks_ref[row // rows, n, :, lanes] = states[n]

            def step(i, states):
                here = pl.ds(pl.multiple_of(row + i * ROWS, ROWS), ROWS)
                now = signal_ref[here, lanes]
                return tuple(states[n] * decay[n] + now for n in range(modes))

            steps = rows // ROWS
            skipped = taps - 1 if start else 0
            states = lax.fori_loop(skipped, steps, step, states, unroll=steps - skipped)
            if last:
                for n in range(modes):
                    marks_ref[1, n, :, lanes] = states[n]
                for at in range(rows, rows + halo, ROWS):
                    now = signal_ref[at : at + ROWS, lanes]
                    states = tuple(states[n] * decay[n] + now for n in range(modes))
                for n in range(modes):
                    marks_ref[0, n, :, lanes] = states[n]
                later = decays(rate_ref, lanes, size, float(length - steps - (taps - 1)))
                states = tuple(states_in[n, :, lanes] + later[n] * states[n] for n in range(modes))
            for n in range(modes):
                states_ref[n, :, lanes] = states[n]
            if last:
                left = lax.broadcasted_iota(jnp.int32, (ROWS, size), 0)
                left = ((ROWS - 1 - left) * length).astype(F32)
                for low_mode in range(0, modes, ROWS):
                    some = range(low_mode, min(low_mode + ROWS, modes))
                    total_ref[low_mode : low_mode + len(some), lanes] = sums_of_rows(
                        [
                            states[n] * jnp.exp(-rows_as(rate_ref[n : n + 1, lanes], size) * left)
                            for n in some
                        ]
                    )
                sent_ref[:, lanes] = total_ref[:, lanes].astype(BF16)


def local_stage(row, rows, taps, *refs):
    normed_ref, signal_ref, states_ref, w_ref, short_ref, rate_ref, mode_ref, skip_ref = refs[:8]
    q_ref, local_ref = refs[8:10]
    begin_ref, past_ref = refs[10:12] if row == 0 else (None, None)
    p_ref = refs[-1]
    modes, channels = rate_ref.shape
    length = signal_ref.shape[0] // ROWS
    for low in range(0, channels, BLOCK):
        width = min(BLOCK, channels - low)
        part = slice(low, low + width)
        normed = normed_ref[row : row + p_ref.shape[0], :]
        p_ref[:, :width] = project(normed, w_ref, 0, part)
        q_ref[:, part] = short_conv(p_ref, short_ref, 0, part, rows, taps)
        for start, size in lane_groups(low, width):
            lanes = slice(start, start + size)
            rate = [rows_as(rate_ref[n : n + 1, lanes], size) for n in range(modes)]
            segment = lax.broadcasted_iota(jnp.int32, (ROWS, size), 0)
            if row == 0:
                for n in range(modes):
                    run = states_ref[n, :, lanes]
                    for hop in (1, 2, 4):
                        weight = jnp.where(segment >= hop, jnp.exp(-rate[n] * (hop * length)), 0.0)
                        run = run + weight * pltpu.roll(run, hop, 0)
                    mode = rows_as(mode_ref[n : n + 1, lanes], size)
                    begin = jnp.where(segment >= 1, pltpu.roll(run, 1, 0), 0.0)
                    begin_ref[n, :, lanes] = mode * begin
                    past = (segment * length).astype(F32)
                    past_ref[n, :, lanes] = mode * jnp.exp(-rate[n] * past)
            lag = segment.astype(F32)
            filters = []
            for first_lag in range(0, SPAN, ROWS):
                values = tree_sum(
                    [
                        rows_as(mode_ref[n : n + 1, lanes], size)
                        * jnp.exp(-rate[n] * (lag + first_lag))
                        for n in range(modes)
                    ]
                )
                filters += [rows_as(values[j : j + 1, :], size) for j in range(ROWS)]
            filters[0] = filters[0] + skip_ref[:, lanes]

            def span(i, carry):
                base = i * (SPAN * ROWS)
                now = [
                    signal_ref[pl.ds(pl.multiple_of(row + base + k * ROWS, ROWS), ROWS), lanes]
                    for k in range(SPAN)
                ]
                for k in range(SPAN):
                    local_ref[pl.ds(pl.multiple_of(base + k * ROWS, ROWS), ROWS), lanes] = tree_sum(
                        [filters[j] * now[k - j] for j in range(k + 1)]
                    )
                return carry

            lax.fori_loop(0, rows // (SPAN * ROWS), span, 0)


def second_stage(pieces, row, rows, ahead, *refs):
    me_ref, q_ref, local_ref, begin_ref, past_ref, marks_ref, carry_ref = refs[:7]
    rate_ref, mode_ref, w_ref, send_ref, own_ref, gated_ref = refs[7:]
    modes, channels = rate_ref.shape
    for start, size in lane_groups(0, channels):
        lanes = slice(start, start + size)
        decay = decays(rate_ref, lanes, size, 1.0)
        for at in range(row, row + rows, SPAN * ROWS):
            mark = at // (SPAN * ROWS)
            states = [
                begin_ref[n, :, lanes] + past_ref[n, :, lanes] * carry_ref[n : n + 1, lanes]
                for n in range(modes)
            ]
            for known, steps in ((mark, SPAN * mark), (0, SPAN * (mark - 1) - ahead)):
                if steps <= 0:
                    continue
                less = decays(rate_ref, lanes, size, float(steps))
                mode = [mode_ref[n : n + 1, lanes] for n in range(modes)]
                if known:
                    states = [
                        mode[n] * marks_ref[known, n, :, lanes] + states[n] * less[n]
                        for n in range(modes)
                    ]
                else:
                    states = [
                        states[n] + mode[n] * marks_ref[0, n, :, lanes] * less[n]
                        for n in range(modes)
                    ]

            def step(i, states):
                here = pl.ds(pl.multiple_of(at - row + i * ROWS, ROWS), ROWS)
                states = tuple(states[n] * decay[n] for n in range(modes))
                gated_ref[here, lanes] = q_ref[here, lanes] * tree_sum(
                    [local_ref[here, lanes]] + list(states)
                )
                return states

            lax.fori_loop(0, SPAN, step, tuple(states), unroll=SPAN)
    product = jnp.dot(gated_ref[...].astype(BF16), w_ref[...], preferred_element_type=F32)
    share = own_ref.shape[1]
    me = me_ref[0]
    columns = [product[:, rank * share : (rank + 1) * share] for rank in range(pieces)]
    for s in range(pieces):
        chosen = columns[0]
        for rank in range(1, pieces):
            chosen = jnp.where(me == (rank - s) % pieces, columns[rank], chosen)
        if s == 0:
            own_ref[...] = chosen
        else:
            send_ref[(s - 1) * rows : s * rows, :] = chosen.astype(BF16)


def turned_back(rows, pick):
    return lax.dot_general(rows, pick, CONTRACT_FIRST, preferred_element_type=F32).astype(BF16)


def last_stage(pieces, sizes, row, more, *refs):
    chunks = len(sizes)
    own_refs, came_refs = refs[:chunks], refs[chunks : chunks * pieces]
    done_ref = refs[chunks * pieces] if more else None
    if more:
        out_ref, mixed_ref, rows_ref, sem = refs[-4:]
    else:
        out_ref, mixed_ref = refs[-2:]
    at = 0
    for j, size in enumerate(sizes):
        total = own_refs[j][...]
        for s in range(pieces - 1):
            total = total + came_refs[j * (pieces - 1) + s][...].astype(F32)
        mixed_ref[at : at + size, :] = total.astype(BF16)
        at += size
    if not more:
        pick = token_picker(row, at, out_ref.shape[1])
        out_ref[...] = turned_back(mixed_ref[...], pick)
        return
    share, tokens = rows_ref.shape
    pick = token_picker(row, at, tokens)
    copies = []
    for low in range(0, share, BLOCK):
        part = slice(low, min(low + BLOCK, share))
        rows_ref[part, :] = done_ref[part, :] + turned_back(mixed_ref[:, part], pick)
        copy = pltpu.make_async_copy(rows_ref.at[part], out_ref.at[part], sem.at[len(copies)])
        copy.start()
        copies.append(copy)
    for copy in copies:
        copy.wait()


def call(kernel, name, scalars, operands, outs, scratch, aliases={}, out_space=pltpu.VMEM):
    vmem = pl.BlockSpec(memory_space=pltpu.VMEM)
    smem = pl.BlockSpec(memory_space=pltpu.SMEM)
    return pl.pallas_call(
        kernel,
        out_shape=outs,
        in_specs=[smem] * len(scalars) + [vmem] * len(operands),
        out_specs=[pl.BlockSpec(memory_space=out_space)] * len(outs),
        scratch_shapes=scratch,
        input_output_aliases=aliases,
        compiler_params=pltpu.CompilerParams(vmem_limit_bytes=VMEM_LIMIT),
        cost_estimate=pl.CostEstimate(flops=1, bytes_accessed=1, transcendentals=0),
        name=name,
    )(*scalars, *operands)


def in_vmem(w):
    streams, channels, features = w.shape
    block = min(BLOCK, channels)
    places = [
        (s, slice(low, min(low + block, channels)))
        for s in (1, 2, 0)
        for low in range(0, channels, block)
    ]
    return pl.pallas_call(
        functools.partial(load_weights, places),
        out_shape=pltpu.VMEM((streams, features, channels), w.dtype),
        in_specs=[pl.BlockSpec(memory_space=pl.ANY)],
        out_specs=pl.BlockSpec(memory_space=pltpu.VMEM),
        scratch_shapes=[
            pltpu.VMEM(w.shape, w.dtype),
            pltpu.SemaphoreType.DMA((len(places),)),
        ],
        compiler_params=pltpu.CompilerParams(vmem_limit_bytes=46 * 2**20),
        cost_estimate=pl.CostEstimate(flops=1, bytes_accessed=1, transcendentals=0),
        name="load_weights",
    )(w)


def run_signal(pieces, row, rows, count, taps, place, tokens, edges, before, gain, w_in, w_short, rate):
    streams, features, channels = w_in.shape
    modes = rate.shape[0]
    halo = ROWS * (taps - 1)
    outs = [
        jax.ShapeDtypeStruct((halo + count, features), BF16),
        jax.ShapeDtypeStruct((count, channels), F32),
        jax.ShapeDtypeStruct((count // rows, modes, ROWS, channels), F32),
        jax.ShapeDtypeStruct((modes, ROWS, channels), F32),
        jax.ShapeDtypeStruct((streams - 1, halo, channels), F32),
    ]
    if row == rows:
        outs.append(outs[-1])
    if row == 0:
        outs += [jax.ShapeDtypeStruct((modes, channels), kind) for kind in (F32, BF16)]
    return call(
        functools.partial(signal_stage, pieces, row, taps),
        "signal_stage",
        [place],
        list(tokens) + list(edges) + list(before) + [gain, w_in, w_short, rate],
        outs,
        [
            pltpu.VMEM((rows + (halo if row == 0 else 0), features), F32),
            pltpu.VMEM((rows + halo * (2 if row == 0 else 1), min(BLOCK, channels)), F32),
        ],
        aliases={1 + len(tokens) + len(edges) + k: k for k in range(3)} if before else {},
    )


def run_local(row, rows, taps, normed, signal, states, w_in, w_short, rate, mode, skip):
    channels = signal.shape[1]
    out = jax.ShapeDtypeStruct((rows, channels), F32)
    begin = jax.ShapeDtypeStruct(states.shape, F32)
    return call(
        functools.partial(local_stage, row, rows, taps),
        "local_stage",
        [],
        [normed, signal, states, w_in, w_short, rate, mode, skip],
        [out, out] + ([begin, begin] if row == 0 else []),
        [pltpu.VMEM((rows + ROWS * (taps - 1), min(BLOCK, channels)), F32)],
    )


def run_second(pieces, row, rows, ahead, place, q, local, begin, past, marks, carry, rate, mode, w):
    channels, features = w.shape
    share = features // pieces
    return call(
        functools.partial(second_stage, pieces, row, rows, ahead),
        "second_stage",
        [place],
        [q, local, begin, past, marks, carry, rate, mode, w],
        [
            jax.ShapeDtypeStruct((max(1, pieces - 1) * rows, share), BF16),
            jax.ShapeDtypeStruct((rows, share), F32),
        ],
        [pltpu.VMEM((rows, channels), F32)],
    )


def run_last(pieces, sizes, row, own, came, done, count):
    share = own[0].shape[1]
    scratch = [pltpu.VMEM((sum(sizes), share), BF16)]
    if done:
        scratch += [pltpu.VMEM((share, count), BF16), pltpu.SemaphoreType.DMA((-(-share // BLOCK),))]
    (out,) = call(
        functools.partial(last_stage, pieces, sizes, row, bool(done)),
        "last_stage",
        [],
        [*own, *came, *done],
        [jax.ShapeDtypeStruct((share, count), BF16)],
        scratch,
        out_space=pl.ANY if done else pltpu.VMEM,
    )
    return out


def rotate(value, axis, steps):
    count = lax.axis_size(axis)
    return lax.ppermute(value, axis, [((i + steps) % count, i) for i in range(count)])


def combine_states(span, stride, radix, count, *refs):
    place_ref, rate_ref, total_ref = refs[:3]
    others = refs[3 : 2 + radix]
    refs = refs[2 + radix :]
    carry_in = refs[0] if stride > 1 else None
    carry_ref = refs[1] if stride > 1 else refs[0]
    position = place_ref[1]
    digit = lax.rem(lax.div(position, stride), radix)
    inner = lax.rem(position, stride)
    unit = span * stride
    rate = rate_ref[...]
    before = jnp.zeros(rate.shape, F32)
    for shift in range(1, radix):
        reached = jnp.where(digit >= shift, 1.0, 0.0)
        other = others[shift - 1][: rate.shape[0], :].astype(F32)
        before = before + jnp.exp(-rate * (unit * (shift - 1))) * (other * reached)
    if stride > 1:
        carry_ref[...] = carry_in[...] + jnp.exp(-rate * (span * inner).astype(F32)) * before
    else:
        carry_ref[...] = before
    if stride * radix < count:
        new = jnp.exp(-rate * (unit * (radix - 1 - digit)).astype(F32)) * total_ref[...]
        for shift in range(1, radix):
            at = lax.rem(digit - shift + radix, radix)
            weight = jnp.exp(-rate * (unit * (radix - 1 - at)).astype(F32))
            new = new + weight * others[shift - 1][: rate.shape[0], :].astype(F32)
        refs[-3][...] = new
        refs[-2][...] = new.astype(BF16)
        modes = new.shape[0]
        refs[-1][:modes, :] = new.astype(BF16)
        refs[-1][modes:, :] = jnp.zeros((refs[-1].shape[0] - modes, new.shape[1]), BF16)


def carried_in(state, sent, rate, span, axis, place, between):
    count = lax.axis_size(axis)
    total, stride, carry, longer = state, 1, [], None
    modes, channels = state.shape
    while stride < count:
        radix = 4 if count % (stride * 4) == 0 else 2
        assert count % (stride * radix) == 0
        group = stride * radix
        others = []
        for shift in reversed(range(1, radix)):
            pairs = []
            for i in range(count):
                digit = (i // stride) % radix
                pairs.append((i + ((digit - shift) % radix - digit) * stride, i))
            first = shift == 1 and longer is not None
            others.append(lax.ppermute(longer if first else sent, axis, pairs))
        others = between(others[::-1])
        shape = jax.ShapeDtypeStruct(state.shape, F32)
        carry = call(
            functools.partial(combine_states, span, stride, radix, count),
            "combine_states",
            [place],
            [rate, total, *others, *carry],
            [shape] if group == count else [shape, shape]
            + [jax.ShapeDtypeStruct((rows, channels), BF16) for rows in (modes, modes + ROWS)],
            [],
        )
        if group < count:
            *carry, total, sent, longer = carry
        stride = group
    return carry[0]


def body(tokens, norm_gain, w_in, w_short, decay_rate, residue, skip_gain, w_out):
    pieces, count = lax.axis_size("tp"), lax.axis_size("ctx")
    share, rows = tokens.shape
    channels = w_in.shape[1]
    taps = w_short.shape[0]
    halo = ROWS * (taps - 1)
    size = SPAN * ROWS
    assert rows == CHUNKS * size
    bf16_rows = lambda size: jax.ShapeDtypeStruct((size, share), BF16)

    place = jnp.stack([lax.axis_index("tp"), lax.axis_index("ctx")]).astype(jnp.int32)
    tokens, place = lax.optimization_barrier((tokens, place))
    x1, edge = call(
        functools.partial(first_rows, halo, size), "first_rows", [], [tokens],
        [bf16_rows(size), bf16_rows(taps - 1)], [],
    )
    edge = rotate(edge, "ctx", -1)
    tokens, x1 = lax.optimization_barrier((tokens, x1))
    x0, *others = call(
        functools.partial(next_rows, [0] + [j * size for j in range(2, CHUNKS)]), "next_rows",
        [], [tokens], [bf16_rows(size)] * (CHUNKS - 1), [],
    )
    x = [x1, *others, x0]
    residue, norm_gain, skip_gain, *_ = lax.optimization_barrier((residue, norm_gain, skip_gain, *x))
    mode = residue * jnp.sqrt(-jnp.expm1(-2.0 * decay_rate))
    gain = norm_gain[None, :]
    skip = skip_gain[None, :]
    w_in, mode, gain, skip, *_ = lax.optimization_barrier((w_in, mode, gain, skip, *x))
    w_in = in_vmem(w_in)
    edge, w_in = lax.optimization_barrier((edge, w_in))
    w_in = pltpu.with_memory_space_constraint(w_in, pltpu.VMEM)
    *parts, edges = [[part] + [rotate(part, "tp", s) for s in range(1, pieces)] for part in x + [edge]]

    before = []
    for part, j in zip(parts, list(range(1, CHUNKS)) + [0]):
        results = run_signal(
            pieces, j * size, size, rows, taps, place, part, [] if j else edges,
            before if j else [*before, heads], gain, w_in,
            w_short, decay_rate,
        )
        before = results[:5]
        if j == 1:
            heads = results[5]
    normed, signal, marks, states, _ = before
    state, sent, normed, signal, states = lax.optimization_barrier(
        (results[5], results[6], normed, signal, states)
    )
    out_sizes = [rows // 4] * 4
    out_rows = [sum(out_sizes[:j]) for j in range(4)]
    small = [w_in, w_short, decay_rate, mode, skip]
    done = []

    def local_part():
        k = len(done)
        done.append(run_local(out_rows[k], out_sizes[k], taps, normed, signal, states, *small))

    def between(others):
        if not done:
            local_part()
            others, done[-1] = lax.optimization_barrier((others, done[-1]))
        return others

    carry = carried_in(state, sent, decay_rate, rows, "ctx", place, between)
    if not done:
        local_part()
    begin, past = done[0][2:]
    own, came = [], []
    for j in range(len(out_sizes)):
        if j >= 2:
            arrived = slice((j - 2) * (pieces - 1), (j - 1) * (pieces - 1))
            normed, signal, carry, came[arrived] = lax.optimization_barrier(
                (normed, signal, carry, came[arrived])
            )
        if j > 0:
            local_part()
        send, kept = run_second(
            pieces, out_rows[j], out_sizes[j], taps - 1, place, *done[j][:2], begin, past, marks, carry,
            decay_rate, mode, w_out,
        )
        own.append(kept)
        for s in range(1, pieces):
            came.append(rotate(send[(s - 1) * out_sizes[j] : s * out_sizes[j]], "tp", -s))
    early = out_rows[-1]
    cut = (len(out_sizes) - 1) * (pieces - 1)
    done = run_last(pieces, out_sizes[:-1], 0, own[:-1], came[:cut], [], rows)
    return run_last(pieces, out_sizes[-1:], early, own[-1:], came[cut:], [done], rows)


def solution(mesh):
    placed = (
        P("tp", "ctx"),
        P(),
        P(None, "tp", None),
        P(None, None, "tp"),
        P(None, "tp"),
        P(None, "tp"),
        P("tp"),
        P("tp", None),
    )
    return jax.shard_map(
        body, mesh=mesh, in_specs=placed, out_specs=P("tp", "ctx"), check_vma=False
    )
```

```python
import functools

import jax
import jax.numpy as jnp
from jax import lax
from jax.experimental import pallas as pl
from jax.experimental.pallas import tpu as pltpu
from jax.sharding import PartitionSpec as P


F32 = jnp.float32
BF16 = jnp.bfloat16
ROWS = 8
LANES = 128
BLOCK = 512
CHUNKS = 4
SPAN = 16
VMEM_LIMIT = 10 * 2**20
CONTRACT_LAST = (((1,), (1,)), ((), ()))
CONTRACT_FIRST = (((0,), (0,)), ((), ()))


def lane_groups(low, width):
    return [(start, min(LANES, low + width - start)) for start in range(low, low + width, LANES)]


def rows_as(row, width):
    return jnp.broadcast_to(row, (ROWS, width))


def decays(rate_ref, lanes, size, steps):
    values = jnp.exp(-rate_ref[:, lanes] * steps)
    return [rows_as(values[n : n + 1, :], size) for n in range(values.shape[0])]


def sums_of_rows(values):
    row = lax.broadcasted_iota(jnp.int32, values[0].shape, 0)
    count = len(values)
    values = list(values) + [jnp.zeros_like(values[0])] * (ROWS - count)
    for hop in (4, 2, 1):
        low = lax.rem(row, 2 * hop) < hop
        joined = []
        for a, b in zip(values[:hop], values[hop:]):
            other = jnp.where(low, b, a)
            if 2 * hop == ROWS:
                other = pltpu.roll(other, hop, 0)
            else:
                other = jnp.where(low, pltpu.roll(other, ROWS - hop, 0), pltpu.roll(other, hop, 0))
            joined.append(jnp.where(low, a, b) + other)
        values = joined
    return values[0][:count]


def tree_sum(terms):
    while len(terms) > 1:
        terms = [sum(terms[k + 1 : k + 2], terms[k]) for k in range(0, len(terms), 2)]
    return terms[0]


def token_picker(first_row, rows, tokens):
    length = tokens // ROWS
    row = lax.broadcasted_iota(jnp.int32, (rows, tokens), 0)
    column = lax.broadcasted_iota(jnp.int32, (rows, tokens), 1)
    wanted = lax.rem(row, ROWS) * length + lax.div(row, ROWS) + first_row // ROWS
    return jnp.where(column == wanted, 1.0, 0.0).astype(BF16)


def turned(pick, tokens):
    return lax.dot_general(pick, tokens, CONTRACT_LAST, preferred_element_type=F32).astype(BF16)


def first_rows(halo, size, tokens_ref, out_ref, edge_ref):
    tokens = tokens_ref.shape[1]
    row = lax.broadcasted_iota(jnp.int32, (halo, tokens), 0)
    column = lax.broadcasted_iota(jnp.int32, (halo, tokens), 1)
    last = edge_ref.shape[0]
    picks = [
        token_picker(size, size, tokens),
        jnp.where((row < last) & (column == tokens - last + row), 1.0, 0.0).astype(BF16),
    ]
    rows = turned(jnp.concatenate(picks, axis=0), tokens_ref[...])
    out_ref[...] = rows[:size]
    edge_ref[...] = rows[size : size + last]


def next_rows(firsts, tokens_ref, *chunk_refs):
    tokens = tokens_ref.shape[1]
    for row, ref in zip(firsts, chunk_refs):
        ref[...] = turned(token_picker(row, ref.shape[0], tokens), tokens_ref[...])


def load_weights(places, w_hbm, out_ref, w_ref, sem):
    copies = [
        pltpu.make_async_copy(w_hbm.at[place], w_ref.at[place], sem.at[k])
        for k, place in enumerate(places)
    ]
    for copy in copies:
        copy.start()
    for (s, part), copy in zip(places, copies):
        copy.wait()
        out_ref[s, :, part] = w_ref[s, part, :].T


def short_conv(p_ref, short_ref, s, part, rows, taps):
    width = part.stop - part.start
    total = None
    for offset in range(taps):
        start = ROWS * (taps - 1 - offset)
        term = short_ref[offset, s : s + 1, part] * p_ref[start : start + rows, :width]
        total = term if total is None else total + term
    return total


def project(normed, w_ref, s, part):
    product = jnp.dot(normed, w_ref[s, :, part], preferred_element_type=F32)
    return product.astype(BF16).astype(F32)


def signal_stage(pieces, row, taps, *refs):
    refs = list(refs)
    me_ref = refs.pop(0)
    token_refs = [refs.pop(0) for _ in range(pieces)]
    x_ref, p_ref = refs[-2:]
    halo = ROWS * (taps - 1)
    rows, share = token_refs[0].shape
    last, start = row == 0, row == rows
    fresh = last or start
    read = rows + halo if last else rows
    edge_refs = [refs.pop(0) for _ in range(pieces)] if last else []
    if not start:
        normed_in, _, _, states_in, tail_in = [refs.pop(0) for _ in range(5)]
    heads_in = refs.pop(0) if last else None
    gain_ref, w_ref, short_ref, rate_ref = refs[:4]
    normed_ref, signal_ref, marks_ref, states_ref, tail_ref = refs[4:9]
    heads_ref = refs[9] if start else None
    total_ref, sent_ref = refs[9:11] if last else (None, None)
    modes, channels = rate_ref.shape
    length = signal_ref.shape[0] // ROWS
    me = me_ref[0]

    values = [ref[...].astype(F32) for ref in token_refs]
    if last:
        preceded = jnp.where(me_ref[1] > 0, 1.0, 0.0)
        blank = jnp.zeros((ROWS - 1, share), F32)
        for s, ref in enumerate(edge_refs):
            edge = ref[...].astype(F32) * preceded
            front = [piece for k in range(taps - 1) for piece in (edge[k : k + 1], blank)]
            values[s] = jnp.concatenate(front + [values[s]], axis=0)
    for rank in range(pieces):
        chosen = values[0]
        for s in range(1, pieces):
            chosen = jnp.where(me == (rank - s) % pieces, values[s], chosen)
        x_ref[:, rank * share : (rank + 1) * share] = chosen
    features = x_ref[...]
    mean = jnp.mean(features * features, axis=1, keepdims=True)
    normed = features * lax.rsqrt(mean + 1e-06) * gain_ref[...]
    if last:
        ends = normed_in[normed_in.shape[0] - halo :, :].astype(F32)
        segment = lax.broadcasted_iota(jnp.int32, (ROWS, ends.shape[1]), 0)
        front = [
            jnp.where(segment >= 1, pltpu.roll(ends[at : at + ROWS], 1, 0), normed[at : at + ROWS])
            for at in range(0, halo, ROWS)
        ]
        normed = jnp.concatenate(front + [normed[halo:]], axis=0)
    normed = normed.astype(BF16)
    begin = 0 if last else halo + row
    normed_ref[begin : begin + read, :] = normed

    for low in range(0, channels, BLOCK):
        width = min(BLOCK, channels - low)
        part = slice(low, low + width)
        for s in (1, 2):
            if start:
                p_ref[:halo, :width] = jnp.zeros((halo, width), F32)
            elif not last:
                p_ref[:halo, :width] = tail_in[s - 1, :, part]
            p_ref[halo + rows - read : halo + rows, :width] = project(
                normed_ref[begin : begin + read, :], w_ref, s, part
            )
            if last:
                p_ref[halo + rows :, :width] = heads_in[s - 1, :, part]
            if start:
                heads_ref[s - 1, :, part] = p_ref[halo : 2 * halo, :width]
            tail_ref[s - 1, :, part] = p_ref[rows : rows + halo, :width]
            short = short_conv(p_ref, short_ref, s, part, p_ref.shape[0] - halo, taps)
            front = halo if start else 0
            there = slice(row + front, row + short.shape[0])
            if s == 1:
                signal_ref[there, part] = short[front:]
            else:
                signal_ref[there, part] = signal_ref[there, part] * short[front:]
        for lane, size in lane_groups(low, width):
            lanes = slice(lane, lane + size)
            decay = decays(rate_ref, lanes, size, 1.0)

            if fresh:
                states = (jnp.zeros((ROWS, size), F32),) * modes
            else:
                states = tuple(states_in[n, :, lanes] for n in range(modes))
                for n in range(modes):
                    marks_ref[row // rows, n, :, lanes] = states[n]

            def step(i, states):
                here = pl.ds(pl.multiple_of(row + i * ROWS, ROWS), ROWS)
                now = signal_ref[here, lanes]
                return tuple(states[n] * decay[n] + now for n in range(modes))

            steps = rows // ROWS
            skipped = taps - 1 if start else 0
            states = lax.fori_loop(skipped, steps, step, states, unroll=steps - skipped)
            if last:
                for n in range(modes):
                    marks_ref[1, n, :, lanes] = states[n]
                for at in range(rows, rows + halo, ROWS):
                    now = signal_ref[at : at + ROWS, lanes]
                    states = tuple(states[n] * decay[n] + now for n in range(modes))
                for n in range(modes):
                    marks_ref[0, n, :, lanes] = states[n]
                later = decays(rate_ref, lanes, size, float(length - steps - (taps - 1)))
                states = tuple(states_in[n, :, lanes] + later[n] * states[n] for n in range(modes))
            for n in range(modes):
                states_ref[n, :, lanes] = states[n]
            if last:
                left = lax.broadcasted_iota(jnp.int32, (ROWS, size), 0)
                left = ((ROWS - 1 - left) * length).astype(F32)
                for low_mode in range(0, modes, ROWS):
                    some = range(low_mode, min(low_mode + ROWS, modes))
                    total_ref[low_mode : low_mode + len(some), lanes] = sums_of_rows(
                        [
                            states[n] * jnp.exp(-rows_as(rate_ref[n : n + 1, lanes], size) * left)
                            for n in some
                        ]
                    )
                sent_ref[:, lanes] = total_ref[:, lanes].astype(BF16)


def local_stage(row, rows, taps, *refs):
    normed_ref, signal_ref, states_ref, w_ref, short_ref, rate_ref, mode_ref, skip_ref = refs[:8]
    q_ref, local_ref = refs[8:10]
    begin_ref, past_ref = refs[10:12] if row == 0 else (None, None)
    p_ref = refs[-1]
    modes, channels = rate_ref.shape
    length = signal_ref.shape[0] // ROWS
    for low in range(0, channels, BLOCK):
        width = min(BLOCK, channels - low)
        part = slice(low, low + width)
        normed = normed_ref[row : row + p_ref.shape[0], :]
        p_ref[:, :width] = project(normed, w_ref, 0, part)
        q_ref[:, part] = short_conv(p_ref, short_ref, 0, part, rows, taps)
        for start, size in lane_groups(low, width):
            lanes = slice(start, start + size)
            rate = [rows_as(rate_ref[n : n + 1, lanes], size) for n in range(modes)]
            segment = lax.broadcasted_iota(jnp.int32, (ROWS, size), 0)
            if row == 0:
                for n in range(modes):
                    run = states_ref[n, :, lanes]
                    for hop in (1, 2, 4):
                        weight = jnp.where(segment >= hop, jnp.exp(-rate[n] * (hop * length)), 0.0)
                        run = run + weight * pltpu.roll(run, hop, 0)
                    mode = rows_as(mode_ref[n : n + 1, lanes], size)
                    begin = jnp.where(segment >= 1, pltpu.roll(run, 1, 0), 0.0)
                    begin_ref[n, :, lanes] = mode * begin
                    past = (segment * length).astype(F32)
                    past_ref[n, :, lanes] = mode * jnp.exp(-rate[n] * past)
            lag = segment.astype(F32)
            filters = []
            for first_lag in range(0, SPAN, ROWS):
                values = tree_sum(
                    [
                        rows_as(mode_ref[n : n + 1, lanes], size)
                        * jnp.exp(-rate[n] * (lag + first_lag))
                        for n in range(modes)
                    ]
                )
                filters += [rows_as(values[j : j + 1, :], size) for j in range(ROWS)]
            filters[0] = filters[0] + skip_ref[:, lanes]

            def span(i, carry):
                base = i * (SPAN * ROWS)
                now = [
                    signal_ref[pl.ds(pl.multiple_of(row + base + k * ROWS, ROWS), ROWS), lanes]
                    for k in range(SPAN)
                ]
                for k in range(SPAN):
                    local_ref[pl.ds(pl.multiple_of(base + k * ROWS, ROWS), ROWS), lanes] = tree_sum(
                        [filters[j] * now[k - j] for j in range(k + 1)]
                    )
                return carry

            lax.fori_loop(0, rows // (SPAN * ROWS), span, 0)


def second_stage(pieces, row, rows, ahead, *refs):
    me_ref, q_ref, local_ref, begin_ref, past_ref, marks_ref, carry_ref = refs[:7]
    rate_ref, mode_ref, w_ref, send_ref, own_ref, gated_ref = refs[7:]
    modes, channels = rate_ref.shape
    for start, size in lane_groups(0, channels):
        lanes = slice(start, start + size)
        decay = decays(rate_ref, lanes, size, 1.0)
        for at in range(row, row + rows, SPAN * ROWS):
            mark = at // (SPAN * ROWS)
            states = [
                begin_ref[n, :, lanes] + past_ref[n, :, lanes] * carry_ref[n : n + 1, lanes]
                for n in range(modes)
            ]
            for known, steps in ((mark, SPAN * mark), (0, SPAN * (mark - 1) - ahead)):
                if steps <= 0:
                    continue
                less = decays(rate_ref, lanes, size, float(steps))
                mode = [mode_ref[n : n + 1, lanes] for n in range(modes)]
                if known:
                    states = [
                        mode[n] * marks_ref[known, n, :, lanes] + states[n] * less[n]
                        for n in range(modes)
                    ]
                else:
                    states = [
                        states[n] + mode[n] * marks_ref[0, n, :, lanes] * less[n]
                        for n in range(modes)
                    ]

            def step(i, states):
                here = pl.ds(pl.multiple_of(at - row + i * ROWS, ROWS), ROWS)
                states = tuple(states[n] * decay[n] for n in range(modes))
                gated_ref[here, lanes] = q_ref[here, lanes] * tree_sum(
                    [local_ref[here, lanes]] + list(states)
                )
                return states

            lax.fori_loop(0, SPAN, step, tuple(states), unroll=SPAN)
    product = jnp.dot(gated_ref[...].astype(BF16), w_ref[...], preferred_element_type=F32)
    share = own_ref.shape[1]
    me = me_ref[0]
    columns = [product[:, rank * share : (rank + 1) * share] for rank in range(pieces)]
    for s in range(pieces):
        chosen = columns[0]
        for rank in range(1, pieces):
            chosen = jnp.where(me == (rank - s) % pieces, columns[rank], chosen)
        if s == 0:
            own_ref[...] = chosen
        else:
            send_ref[(s - 1) * rows : s * rows, :] = chosen.astype(BF16)


def turned_back(rows, pick):
    return lax.dot_general(rows, pick, CONTRACT_FIRST, preferred_element_type=F32).astype(BF16)


def last_stage(pieces, sizes, row, more, *refs):
    chunks = len(sizes)
    own_refs, came_refs = refs[:chunks], refs[chunks : chunks * pieces]
    done_ref = refs[chunks * pieces] if more else None
    if more:
        out_ref, mixed_ref, rows_ref, sem = refs[-4:]
    else:
        out_ref, mixed_ref = refs[-2:]
    at = 0
    for j, size in enumerate(sizes):
        total = own_refs[j][...]
        for s in range(pieces - 1):
            total = total + came_refs[j * (pieces - 1) + s][...].astype(F32)
        mixed_ref[at : at + size, :] = total.astype(BF16)
        at += size
    if not more:
        pick = token_picker(row, at, out_ref.shape[1])
        out_ref[...] = turned_back(mixed_ref[...], pick)
        return
    share, tokens = rows_ref.shape
    pick = token_picker(row, at, tokens)
    copies = []
    for low in range(0, share, BLOCK):
        part = slice(low, min(low + BLOCK, share))
        rows_ref[part, :] = done_ref[part, :] + turned_back(mixed_ref[:, part], pick)
        copy = pltpu.make_async_copy(rows_ref.at[part], out_ref.at[part], sem.at[len(copies)])
        copy.start()
        copies.append(copy)
    for copy in copies:
        copy.wait()


def call(kernel, name, scalars, operands, outs, scratch, aliases={}, out_space=pltpu.VMEM):
    vmem = pl.BlockSpec(memory_space=pltpu.VMEM)
    smem = pl.BlockSpec(memory_space=pltpu.SMEM)
    return pl.pallas_call(
        kernel,
        out_shape=outs,
        in_specs=[smem] * len(scalars) + [vmem] * len(operands),
        out_specs=[pl.BlockSpec(memory_space=out_space)] * len(outs),
        scratch_shapes=scratch,
        input_output_aliases=aliases,
        compiler_params=pltpu.CompilerParams(vmem_limit_bytes=VMEM_LIMIT),
        cost_estimate=pl.CostEstimate(flops=1, bytes_accessed=1, transcendentals=0),
        name=name,
    )(*scalars, *operands)


def in_vmem(w):
    streams, channels, features = w.shape
    block = min(BLOCK, channels)
    places = [
        (s, slice(low, min(low + block, channels)))
        for s in (1, 2, 0)
        for low in range(0, channels, block)
    ]
    return pl.pallas_call(
        functools.partial(load_weights, places),
        out_shape=pltpu.VMEM((streams, features, channels), w.dtype),
        in_specs=[pl.BlockSpec(memory_space=pl.ANY)],
        out_specs=pl.BlockSpec(memory_space=pltpu.VMEM),
        scratch_shapes=[
            pltpu.VMEM(w.shape, w.dtype),
            pltpu.SemaphoreType.DMA((len(places),)),
        ],
        compiler_params=pltpu.CompilerParams(vmem_limit_bytes=46 * 2**20),
        cost_estimate=pl.CostEstimate(flops=1, bytes_accessed=1, transcendentals=0),
        name="load_weights",
    )(w)


def run_signal(pieces, row, rows, count, taps, place, tokens, edges, before, gain, w_in, w_short, rate):
    streams, features, channels = w_in.shape
    modes = rate.shape[0]
    halo = ROWS * (taps - 1)
    outs = [
        jax.ShapeDtypeStruct((halo + count, features), BF16),
        jax.ShapeDtypeStruct((count, channels), F32),
        jax.ShapeDtypeStruct((count // rows, modes, ROWS, channels), F32),
        jax.ShapeDtypeStruct((modes, ROWS, channels), F32),
        jax.ShapeDtypeStruct((streams - 1, halo, channels), F32),
    ]
    if row == rows:
        outs.append(outs[-1])
    if row == 0:
        outs += [jax.ShapeDtypeStruct((modes, channels), kind) for kind in (F32, BF16)]
    return call(
        functools.partial(signal_stage, pieces, row, taps),
        "signal_stage",
        [place],
        list(tokens) + list(edges) + list(before) + [gain, w_in, w_short, rate],
        outs,
        [
            pltpu.VMEM((rows + (halo if row == 0 else 0), features), F32),
            pltpu.VMEM((rows + halo * (2 if row == 0 else 1), min(BLOCK, channels)), F32),
        ],
        aliases={1 + len(tokens) + len(edges) + k: k for k in range(3)} if before else {},
    )


def run_local(row, rows, taps, normed, signal, states, w_in, w_short, rate, mode, skip):
    channels = signal.shape[1]
    out = jax.ShapeDtypeStruct((rows, channels), F32)
    begin = jax.ShapeDtypeStruct(states.shape, F32)
    return call(
        functools.partial(local_stage, row, rows, taps),
        "local_stage",
        [],
        [normed, signal, states, w_in, w_short, rate, mode, skip],
        [out, out] + ([begin, begin] if row == 0 else []),
        [pltpu.VMEM((rows + ROWS * (taps - 1), min(BLOCK, channels)), F32)],
    )


def run_second(pieces, row, rows, ahead, place, q, local, begin, past, marks, carry, rate, mode, w):
    channels, features = w.shape
    share = features // pieces
    return call(
        functools.partial(second_stage, pieces, row, rows, ahead),
        "second_stage",
        [place],
        [q, local, begin, past, marks, carry, rate, mode, w],
        [
            jax.ShapeDtypeStruct((max(1, pieces - 1) * rows, share), BF16),
            jax.ShapeDtypeStruct((rows, share), F32),
        ],
        [pltpu.VMEM((rows, channels), F32)],
    )


def run_last(pieces, sizes, row, own, came, done, count):
    share = own[0].shape[1]
    scratch = [pltpu.VMEM((sum(sizes), share), BF16)]
    if done:
        scratch += [pltpu.VMEM((share, count), BF16), pltpu.SemaphoreType.DMA((-(-share // BLOCK),))]
    (out,) = call(
        functools.partial(last_stage, pieces, sizes, row, bool(done)),
        "last_stage",
        [],
        [*own, *came, *done],
        [jax.ShapeDtypeStruct((share, count), BF16)],
        scratch,
        out_space=pl.ANY if done else pltpu.VMEM,
    )
    return out


def rotate(value, axis, steps):
    count = lax.axis_size(axis)
    return lax.ppermute(value, axis, [((i + steps) % count, i) for i in range(count)])


def combine_states(span, stride, radix, count, *refs):
    place_ref, rate_ref, total_ref = refs[:3]
    others = refs[3 : 2 + radix]
    refs = refs[2 + radix :]
    carry_in = refs[0] if stride > 1 else None
    carry_ref = refs[1] if stride > 1 else refs[0]
    position = place_ref[1]
    digit = lax.rem(lax.div(position, stride), radix)
    inner = lax.rem(position, stride)
    unit = span * stride
    rate = rate_ref[...]
    before = jnp.zeros(rate.shape, F32)
    for shift in range(1, radix):
        reached = jnp.where(digit >= shift, 1.0, 0.0)
        other = others[shift - 1][: rate.shape[0], :].astype(F32)
        before = before + jnp.exp(-rate * (unit * (shift - 1))) * (other * reached)
    if stride > 1:
        carry_ref[...] = carry_in[...] + jnp.exp(-rate * (span * inner).astype(F32)) * before
    else:
        carry_ref[...] = before
    if stride * radix < count:
        new = jnp.exp(-rate * (unit * (radix - 1 - digit)).astype(F32)) * total_ref[...]
        for shift in range(1, radix):
            at = lax.rem(digit - shift + radix, radix)
            weight = jnp.exp(-rate * (unit * (radix - 1 - at)).astype(F32))
            new = new + weight * others[shift - 1][: rate.shape[0], :].astype(F32)
        refs[-3][...] = new
        refs[-2][...] = new.astype(BF16)
        modes = new.shape[0]
        refs[-1][:modes, :] = new.astype(BF16)
        refs[-1][modes:, :] = jnp.zeros((refs[-1].shape[0] - modes, new.shape[1]), BF16)


def carried_in(state, sent, rate, span, axis, place, between):
    count = lax.axis_size(axis)
    total, stride, carry, longer = state, 1, [], None
    modes, channels = state.shape
    while stride < count:
        radix = 4 if count % (stride * 4) == 0 else 2
        assert count % (stride * radix) == 0
        group = stride * radix
        others = []
        for shift in reversed(range(1, radix)):
            pairs = []
            for i in range(count):
                digit = (i // stride) % radix
                pairs.append((i + ((digit - shift) % radix - digit) * stride, i))
            first = shift == 1 and longer is not None
            others.append(lax.ppermute(longer if first else sent, axis, pairs))
        others = between(others[::-1])
        shape = jax.ShapeDtypeStruct(state.shape, F32)
        carry = call(
            functools.partial(combine_states, span, stride, radix, count),
            "combine_states",
            [place],
            [rate, total, *others, *carry],
            [shape] if group == count else [shape, shape]
            + [jax.ShapeDtypeStruct((rows, channels), BF16) for rows in (modes, modes + ROWS)],
            [],
        )
        if group < count:
            *carry, total, sent, longer = carry
        stride = group
    return carry[0]


def body(tokens, norm_gain, w_in, w_short, decay_rate, residue, skip_gain, w_out):
    pieces, count = lax.axis_size("tp"), lax.axis_size("ctx")
    share, rows = tokens.shape
    channels = w_in.shape[1]
    taps = w_short.shape[0]
    halo = ROWS * (taps - 1)
    size = SPAN * ROWS
    assert rows == CHUNKS * size
    bf16_rows = lambda size: jax.ShapeDtypeStruct((size, share), BF16)

    place = jnp.stack([lax.axis_index("tp"), lax.axis_index("ctx")]).astype(jnp.int32)
    tokens, place = lax.optimization_barrier((tokens, place))
    x1, edge = call(
        functools.partial(first_rows, halo, size), "first_rows", [], [tokens],
        [bf16_rows(size), bf16_rows(taps - 1)], [],
    )
    edge = rotate(edge, "ctx", -1)
    tokens, x1 = lax.optimization_barrier((tokens, x1))
    x0, *others = call(
        functools.partial(next_rows, [0] + [j * size for j in range(2, CHUNKS)]), "next_rows",
        [], [tokens], [bf16_rows(size)] * (CHUNKS - 1), [],
    )
    x = [x1, *others, x0]
    residue, norm_gain, skip_gain, *_ = lax.optimization_barrier((residue, norm_gain, skip_gain, *x))
    mode = residue * jnp.sqrt(-jnp.expm1(-2.0 * decay_rate))
    gain = norm_gain[None, :]
    skip = skip_gain[None, :]
    w_in, mode, gain, skip, *_ = lax.optimization_barrier((w_in, mode, gain, skip, *x))
    w_in = in_vmem(w_in)
    edge, w_in = lax.optimization_barrier((edge, w_in))
    w_in = pltpu.with_memory_space_constraint(w_in, pltpu.VMEM)
    *parts, edges = [[part] + [rotate(part, "tp", s) for s in range(1, pieces)] for part in x + [edge]]

    before = []
    for part, j in zip(parts, list(range(1, CHUNKS)) + [0]):
        results = run_signal(
            pieces, j * size, size, rows, taps, place, part, [] if j else edges,
            before if j else [*before, heads], gain, w_in,
            w_short, decay_rate,
        )
        before = results[:5]
        if j == 1:
            heads = results[5]
    normed, signal, marks, states, _ = before
    state, sent, normed, signal, states = lax.optimization_barrier(
        (results[5], results[6], normed, signal, states)
    )
    out_sizes = [rows // 4] * 4
    out_rows = [sum(out_sizes[:j]) for j in range(4)]
    small = [w_in, w_short, decay_rate, mode, skip]
    done = []

    def local_part():
        k = len(done)
        done.append(run_local(out_rows[k], out_sizes[k], taps, normed, signal, states, *small))

    def between(others):
        if not done:
            local_part()
            others, done[-1] = lax.optimization_barrier((others, done[-1]))
        return others

    carry = carried_in(state, sent, decay_rate, rows, "ctx", place, between)
    if not done:
        local_part()
    begin, past = done[0][2:]
    own, came = [], []
    for j in range(len(out_sizes)):
        if j >= 2:
            arrived = slice((j - 2) * (pieces - 1), (j - 1) * (pieces - 1))
            normed, signal, carry, came[arrived] = lax.optimization_barrier(
                (normed, signal, carry, came[arrived])
            )
        if j > 0:
            local_part()
        send, kept = run_second(
            pieces, out_rows[j], out_sizes[j], taps - 1, place, *done[j][:2], begin, past, marks, carry,
            decay_rate, mode, w_out,
        )
        own.append(kept)
        for s in range(1, pieces):
            came.append(rotate(send[(s - 1) * out_sizes[j] : s * out_sizes[j]], "tp", -s))
    early = out_rows[-1]
    cut = (len(out_sizes) - 1) * (pieces - 1)
    done = run_last(pieces, out_sizes[:-1], 0, own[:-1], came[:cut], [], rows)
    return run_last(pieces, out_sizes[-1:], early, own[-1:], came[cut:], [done], rows)


def solution(mesh):
    placed = (
        P("tp", "ctx"),
        P(),
        P(None, "tp", None),
        P(None, None, "tp"),
        P(None, "tp"),
        P(None, "tp"),
        P("tp"),
        P("tp", None),
    )
    return jax.shard_map(
        body, mesh=mesh, in_specs=placed, out_specs=P("tp", "ctx"), check_vma=False
    )
```
